32 devices in a mesh: rep: 2 (over y), slab: 4 (over z), col: 2 (over x), pair: 2 (over core).
Axes of the slice: x: 2, y: 2, z: 4, core: 2. Of those that a mesh axis runs over, the one named last changes fastest.
Arguments:
- populations: float32 [19, 128, 32, 256], P(None, ('rep', 'slab'), 'col', 'pair'), parts along dimension 1, as said below
- solid_mask: int32 [128, 32, 256], P(('rep', 'slab'), 'col', 'pair'), parts along dimension 0, may hold values 0 or 1
- bead_owner: int32 [4096], P(('rep', 'slab', 'col', 'pair')), parts along dimension 0, may hold values from 0 to 7, as said below
- bead_base: int32 [3, 4096], P(None, ('rep', 'slab', 'col', 'pair')), parts along dimension 1, may hold values from 0 to 126, as said below
- bead_offset: float32 [3, 4096], P(None, ('rep', 'slab', 'col', 'pair')), parts along dimension 1, may hold values from 0 to 1
- bead_velocity: float32 [3, 4096], P(None, ('rep', 'slab', 'col', 'pair')), parts along dimension 1, may hold values from -0.6 to 0.6
Outputs:
- next_populations: float32 [19, 128, 32, 256], P(None, ('rep', 'slab'), 'col', 'pair'), parts along dimension 1
- bead_force: float32 [3, 4096], P(None, ('rep', 'slab', 'col', 'pair')), parts along dimension 1
The draws below stay inside these ranges and needn't reach their ends.
There are 2 independent parts, one for each index of `rep`. The reference program is written for one: setup_inputs(seed, part) draws one part's arguments, and reference() takes and returns one part's arrays. A program takes and returns all parts, laid end to end along the dimension named above; each array names one. Nothing has to cross between parts.
Inputs may be any that keep to these rules, and one draw needn't show every extreme that they name: `populations`: populations are positive. `bead_owner`: among the beads of one device each owner index appears at most 32 times; in every draw one owner index appears exactly 32 times among the beads of every device. `bead_base`: row 0 lies in 0 to 126, row 1 in 0 to 14, row 2 in 0 to 14; x is local to the x block of the bead's own pair index, y and z to the owner's block.
All inputs are finite; a program needn't handle non-finite values. No bound on the sum of `solid_mask` on one device may be relied on, other than what follows from the above.
Results may differ from the reference program's by a relative error of at most 0.0003.
Values sent between devices are 32-bit elements; how exact they have to be, the bound alone decides.
No kernel may reach another device: no remote copies, remote signals or barrier semaphores. Data moves between devices by JAX's collectives and lax.ppermute only.
A program may use at most 64 MiB of HBM per device.

```python
import jax
import jax.numpy as jnp
import numpy as np
from jax import lax

CZ = 16
CY = 16
CX = 128
OWNERS = 8
CAP = 32
BEADS_DEV = 128
BEADS = 2048
NZ = 64
NY = 32
NX = 256
N_COL = 2
N_PAIR = 2


LATTICE_STEP = np.array([[0, 0, 0], [1, 0, 0], [-1, 0, 0], [0, 1, 0], [0, -1, 0], [0, 0, 1], [0, 0, -1], [1, 1, 0], [-1, -1, 0], [1, -1, 0], [-1, 1, 0], [1, 0, 1], [-1, 0, -1], [1, 0, -1], [-1, 0, 1], [0, 1, 1], [0, -1, -1], [0, 1, -1], [0, -1, 1]], np.int32)


LATTICE_VEL = LATTICE_STEP.astype(np.float32)


LATTICE_WT = np.array([1.0 / 3.0] + [1.0 / 18.0] * 6 + [1.0 / 36.0] * 12, np.float32)


def draw_populations(key, part):
    key = jax.random.fold_in(key, 5)
    flow_key, noise_key = jax.random.split(key)
    flow = 0.04 * jax.random.truncated_normal(flow_key, -3.0, 3.0, (3, NZ, NY, NX), jnp.float32)
    noise = 0.08 * jax.random.truncated_normal(noise_key, -3.0, 3.0, (19, NZ, NY, NX), jnp.float32)
    table = jnp.asarray(LATTICE_VEL)
    along = table[:, 0, None, None, None] * flow[0] + table[:, 1, None, None, None] * flow[1] + table[:, 2, None, None, None] * flow[2]
    return (jnp.asarray(LATTICE_WT)[:, None, None, None] * (1.0 + 3.0 * along + noise)).astype(jnp.float32)


def draw_bead_owner(key, part):
    key = jax.random.fold_in(key, 11)
    busiest = jax.random.randint(jax.random.fold_in(key, 1), (), 0, OWNERS)
    others = (busiest + 1 + jnp.arange(OWNERS - 1, dtype=jnp.int32)) % OWNERS
    spares = jnp.repeat(others, CAP)
    devices = BEADS // BEADS_DEV
    block_keys = jax.random.split(jax.random.fold_in(key, 2), devices)

    def one_device(subkey):
        first_key, second_key = jax.random.split(subkey)
        rest = jax.random.permutation(first_key, spares)[:BEADS_DEV - CAP]
        listed = jnp.concatenate([jnp.full((CAP,), busiest, jnp.int32), rest.astype(jnp.int32)])
        return jax.random.permutation(second_key, listed)
    return jax.vmap(one_device)(block_keys).reshape(-1).astype(jnp.int32)


def draw_bead_base(key, part):
    key = jax.random.fold_in(key, 7)
    highest = jnp.array([[CX - 1], [CY - 1], [CZ - 1]], jnp.int32)
    return jax.random.randint(key, (3, BEADS), 0, highest).astype(jnp.int32)


def place_ends(drawn, own_key, smallest, top_value):
    index_at = [jax.random.randint(jax.random.fold_in(own_key, axis), (), 0, length) for axis, length in enumerate(drawn.shape)]
    main_axis = drawn.shape.index(max(drawn.shape))
    beside = index_at[:main_axis] + [(index_at[main_axis] + 1) % drawn.shape[main_axis]] + index_at[main_axis + 1:]
    return drawn.at[tuple(index_at)].set(smallest).at[tuple(beside)].set(top_value)


def steps_of(stream_key, shape, pieces, low, high):
    def one(dim, parts):
        heights = jax.random.uniform(jax.random.fold_in(jax.random.fold_in(stream_key, 6), dim), (parts,), jnp.float32, low / len(pieces), high / len(pieces))
        return jnp.repeat(jnp.exp(heights), shape[dim] // parts).reshape((-1,) + (1,) * (len(shape) - dim - 1))

    level = one(*pieces[0])
    for cut in pieces[1:]:
        level = level * one(*cut)
    return level


def gaussian(stream_key, shape, width, most, cuts=(), kind=jnp.bfloat16):
    loudness = steps_of(stream_key, shape, cuts, -0.22, 0.18) if cuts else 1.0
    entries = jax.random.normal(stream_key, shape, jnp.float32) * width * loudness
    return jnp.minimum(jnp.maximum(entries, -most), most).astype(kind)


def setup_inputs(seed: int = 0, part: int = 0) -> dict:
    key_list = jax.random.split(jax.random.key(seed), 7)
    own_keys = jax.random.split(jax.random.fold_in(key_list[6], part), 7)
    return {
        "populations": draw_populations(jax.random.fold_in(jax.random.fold_in(key_list[6], part), 71), part),
        "solid_mask": place_ends((jax.random.randint(own_keys[1], (NZ, NY, NX), 0, 8) < 1).astype(jnp.int32), jax.random.fold_in(own_keys[1], 1), 0, 1),
        "bead_owner": draw_bead_owner(jax.random.fold_in(jax.random.fold_in(key_list[6], part), 71), part),
        "bead_base": draw_bead_base(jax.random.fold_in(jax.random.fold_in(key_list[6], part), 71), part),
        "bead_offset": jnp.clip(1.0 * jax.random.uniform(own_keys[4], (3, BEADS), jnp.float32) ** steps_of(own_keys[4], (3, BEADS), ((1, 16),), -0.2, 0.2), 0.0, 1.0),
        "bead_velocity": gaussian(own_keys[5], (3, BEADS), 0.1, 0.6, ((1, 16),), jnp.float32),
    }


LATTICE_STEP = np.array([[0, 0, 0], [1, 0, 0], [-1, 0, 0], [0, 1, 0], [0, -1, 0], [0, 0, 1], [0, 0, -1],
                         [1, 1, 0], [-1, -1, 0], [1, -1, 0], [-1, 1, 0], [1, 0, 1], [-1, 0, -1], [1, 0, -1],
                         [-1, 0, 1], [0, 1, 1], [0, -1, -1], [0, 1, -1], [0, -1, 1]], np.int32)
LATTICE_VEL = LATTICE_STEP.astype(np.float32)
LATTICE_WT = np.array([1.0 / 3.0] + [1.0 / 18.0] * 6 + [1.0 / 36.0] * 12, np.float32)
OPPOSITE = np.array([0, 2, 1, 4, 3, 6, 5, 8, 7, 10, 9, 12, 11, 14, 13, 16, 15, 18, 17], np.int32)
TAU_PLUS = 0.8
TAU_MINUS = 0.5 + (3.0 / 16.0) / (TAU_PLUS - 0.5)
DRAG_COEF = 2.0


def moments(populations):
    density = jnp.sum(populations, axis=0)
    momentum = jnp.einsum("qd,qzyx->dzyx", jnp.asarray(LATTICE_VEL), populations, precision=lax.Precision.HIGHEST)
    return density, momentum


def collide(populations, density, momentum, solid_mask, force):
    table = jnp.asarray(LATTICE_VEL)
    weights = jnp.asarray(LATTICE_WT)[:, None, None, None]
    speed = (momentum + 0.5 * force) / density
    along = jnp.einsum("qd,dzyx->qzyx", table, speed, precision=lax.Precision.HIGHEST)
    pushed = jnp.einsum("qd,dzyx->qzyx", table, force, precision=lax.Precision.HIGHEST)
    square = jnp.sum(speed * speed, axis=0)
    power = jnp.sum(speed * force, axis=0)
    balance = weights * density * (1.0 + 3.0 * along + 4.5 * along * along - 1.5 * square)
    source = (1.0 - 0.5 / TAU_PLUS) * weights * (3.0 * (pushed - power) + 9.0 * along * pushed)
    mirror = populations[OPPOSITE]
    balance_mirror = balance[OPPOSITE]
    even_part = 0.5 * (populations + mirror) - 0.5 * (balance + balance_mirror)
    odd_part = 0.5 * (populations - mirror) - 0.5 * (balance - balance_mirror)
    relaxed = populations - even_part / TAU_PLUS - odd_part / TAU_MINUS + source
    return jnp.where(solid_mask[None] == 1, mirror, relaxed)


def reference(populations, solid_mask, bead_owner, bead_base, bead_offset, bead_velocity):
    density, momentum = moments(populations)
    flow = momentum / density
    count = bead_owner.shape[0]
    device = jnp.arange(count, dtype=jnp.int32) // BEADS_DEV
    pair_of = device % N_PAIR
    slab_of = bead_owner // N_COL
    col_of = bead_owner % N_COL
    x_cell = pair_of * CX + bead_base[0]
    y_cell = col_of * CY + bead_base[1]
    z_cell = slab_of * CZ + bead_base[2]
    corners = []
    for step_x in range(2):
        for step_y in range(2):
            for step_z in range(2):
                weight_x = bead_offset[0] if step_x else 1.0 - bead_offset[0]
                weight_y = bead_offset[1] if step_y else 1.0 - bead_offset[1]
                weight_z = bead_offset[2] if step_z else 1.0 - bead_offset[2]
                corners.append((step_x, step_y, step_z, weight_x * weight_y * weight_z))
    sampled = jnp.zeros((3, count), jnp.float32)
    for step_x, step_y, step_z, weight in corners:
        sampled = sampled + weight[None, :] * flow[:, z_cell + step_z, y_cell + step_y, x_cell + step_x]
    bead_force = DRAG_COEF * (sampled - bead_velocity)
    force_grid = jnp.zeros((3, NZ, NY, NX), jnp.float32)
    for step_x, step_y, step_z, weight in corners:
        force_grid = force_grid.at[:, z_cell + step_z, y_cell + step_y, x_cell + step_x].add(-weight[None, :] * bead_force)
    blocks = NZ // CZ

    def one_block(number):
        start = (number * CZ).astype(jnp.int32)
        return collide(lax.dynamic_slice_in_dim(populations, start, CZ, 1),
                       lax.dynamic_slice_in_dim(density, start, CZ, 0),
                       lax.dynamic_slice_in_dim(momentum, start, CZ, 1),
                       lax.dynamic_slice_in_dim(solid_mask, start, CZ, 0),
                       lax.dynamic_slice_in_dim(force_grid, start, CZ, 1))

    relaxed = lax.map(one_block, jnp.arange(blocks, dtype=jnp.int32))
    relaxed = jnp.moveaxis(relaxed, 0, 1).reshape(19, NZ, NY, NX)
    next_populations = jnp.stack([jnp.roll(relaxed[member], (int(LATTICE_STEP[member, 2]), int(LATTICE_STEP[member, 1]), int(LATTICE_STEP[member, 0])), axis=(0, 1, 2)) for member in range(19)])
    return next_populations, bead_force
```

```python
import functools

import jax
import jax.numpy as jnp
import numpy as np
from jax import lax
from jax.experimental import pallas as pl
from jax.experimental.pallas import tpu as pltpu
from jax.sharding import PartitionSpec as P

CAP = 32
GROUP = 8

STEP = np.array(
    [
        [0, 0, 0],
        [1, 0, 0],
        [-1, 0, 0],
        [0, 1, 0],
        [0, -1, 0],
        [0, 0, 1],
        [0, 0, -1],
        [1, 1, 0],
        [-1, -1, 0],
        [1, -1, 0],
        [-1, 1, 0],
        [1, 0, 1],
        [-1, 0, -1],
        [1, 0, -1],
        [-1, 0, 1],
        [0, 1, 1],
        [0, -1, -1],
        [0, 1, -1],
        [0, -1, 1],
    ],
    np.int32,
)
TAU_PLUS = 0.8
TAU_MINUS = 0.5 + (3.0 / 16.0) / (TAU_PLUS - 0.5)
KEEP_EVEN = 1.0 - 1.0 / TAU_PLUS
KEEP_ODD = 1.0 - 1.0 / TAU_MINUS
FORCE_GAIN = 1.0 - 0.5 / TAU_PLUS
DRAG_COEF = 2.0
F32 = jnp.float32
BF16 = jnp.bfloat16

X_PLUS = [i for i in range(19) if STEP[i, 0] == 1]
X_MINUS = [i for i in range(19) if STEP[i, 0] == -1]
NT = (((1,), (1,)), ((), ()))
NN = (((1,), (0,)), ((), ()))


def iota(shape, dim):
    return lax.broadcasted_iota(jnp.int32, shape, dim)


def high_low(value):
    high = value.astype(BF16)
    return high, (value - high.astype(F32)).astype(BF16)


def dot_split(left, right, dims):
    a, b = high_low(left)
    c, d = high_low(right)
    mul = functools.partial(lax.dot_general, dimension_numbers=dims, preferred_element_type=F32)
    return mul(a, c) + (mul(a, d) + mul(b, c))


def dot_select(value, choose, dims):
    first = value.astype(BF16).astype(F32)
    rest = value - first
    second = rest.astype(BF16).astype(F32)
    stacked = jnp.concatenate([first, second, rest - second], axis=0).astype(BF16)
    got = lax.dot_general(stacked, choose, dimension_numbers=dims, preferred_element_type=F32)
    rows = value.shape[0]
    return got[0:rows] + got[rows : 2 * rows] + got[2 * rows : 3 * rows]


def density_momentum(pops):
    momentum = []
    for axis in range(3):
        plus = [pops[i] for i in range(19) if STEP[i, axis] == 1]
        minus = [pops[i] for i in range(19) if STEP[i, axis] == -1]
        momentum.append(sum(plus[1:], plus[0]) - sum(minus[1:], minus[0]))
    return sum(pops[1:], pops[0]), momentum


def along(step, vector):
    terms = None
    for axis in range(3):
        if step[axis] == 0:
            continue
        if terms is None:
            terms = vector[axis] if step[axis] == 1 else -vector[axis]
        else:
            terms = terms + vector[axis] if step[axis] == 1 else terms - vector[axis]
    return terms


def collide(pops, solid, force):
    density, momentum = density_momentum(pops)
    inverse = 1.0 / density
    carried = [m + 0.5 * f for m, f in zip(momentum, force)]
    speed = [m * inverse for m in carried]
    w = 1.0 / 36.0
    bend = [(4.5 * w / TAU_PLUS) * m + (9.0 * w * FORCE_GAIN) * f for m, f in zip(carried, force)]
    push = [(3.0 * w / TAU_MINUS) * m + (3.0 * w * FORCE_GAIN) * f for m, f in zip(carried, force)]
    drop = [(1.5 * w / TAU_PLUS) * m + (3.0 * w * FORCE_GAIN) * f for m, f in zip(carried, force)]
    rest = (w / TAU_PLUS) * density - sum(
        [u * d for u, d in zip(speed[1:], drop[1:])], speed[0] * drop[0]
    )
    wall = solid == 1
    out = [None] * 19
    out[0] = jnp.where(wall, pops[0], KEEP_EVEN * pops[0] + 12.0 * rest)
    for i in range(1, 19, 2):
        a, b = pops[i], pops[i + 1]
        step = STEP[i]
        even = rest + along(step, speed) * along(step, bend)
        odd = along(step, push)
        if i < 7:
            even = even + even
            odd = odd + odd
        even = (0.5 * KEEP_EVEN) * (a + b) + even
        odd = (0.5 * KEEP_ODD) * (a - b) + odd
        out[i] = jnp.where(wall, b, even + odd)
        out[i + 1] = jnp.where(wall, a, even - odd)
    return out


def turn(value, amount, axis):
    if amount == 0:
        return value
    return pltpu.roll(value, int(amount) % value.shape[axis], axis)


def message_plan(shape):
    plan = {}
    for i in range(1, 19):
        moving = [a for a in (2, 1, 0) if STEP[i, a] != 0]
        subsets = [[a] for a in moving] + ([moving] if len(moving) == 2 else [])
        for axes in subsets:
            if axes == [0]:
                continue
            key = tuple(
                int(STEP[i, a]) % shape[k] if a in axes else 0 for k, a in enumerate((2, 1, 0))
            )
            plan.setdefault(key, []).append((i, tuple(axes)))
    return plan


def part_rows(part, span):
    return 8 if part[1] == (2, 1) else span


def message_rows(parts, span, with_drag):
    rows = 8 if with_drag else 0
    places = {}
    for part in parts:
        places[part] = rows
        rows += part_rows(part, span)
    return rows, places


def send(value, shape, offset):
    slabs, cols, pairs = shape
    perm = []
    for s in range(slabs):
        for c in range(cols):
            for p in range(pairs):
                there = (
                    ((s + offset[0]) % slabs) * cols + (c + offset[1]) % cols
                ) * pairs + (p + offset[2]) % pairs
                perm.append(((s * cols + c) * pairs + p, there))
    return lax.ppermute(value, ("slab", "col", "pair"), perm)


def wrap(value, size):
    return jnp.where(value < 0, value + size, value)


def pack_kernel(slabs, cols, count, single, owner_ref, base_ref, offset_ref, velocity_ref, target_ref, *rest):
    outs, table = rest[:-1], rest[-1]
    owner = owner_ref[...]
    owner_slab = lax.shift_right_logical(owner, cols.bit_length() - 1)
    owner_col = owner - owner_slab * cols
    relative = wrap(owner_slab - lax.axis_index("slab"), slabs) * cols + wrap(
        owner_col - lax.axis_index("col"), cols
    )
    first = 0 if single else pl.program_id(0) * GROUP
    local = relative - first
    member = (iota((GROUP, count), 0) == local).astype(F32)
    earlier = (iota((count, count), 0) < iota((count, count), 1)).astype(F32).astype(BF16)
    ahead = lax.dot_general(member.astype(BF16), earlier, NN, preferred_element_type=F32)
    rank = jnp.sum(member * ahead, axis=0, keepdims=True).astype(jnp.int32)
    inside = (local >= 0) & (local < GROUP)
    target = jnp.where(inside, local * CAP + rank, -1)
    whole_target = jnp.where(inside, relative * CAP + rank, -1)
    if single:
        target_ref[...] = whole_target
    else:

        @pl.when(pl.program_id(0) == 0)
        def _():
            target_ref[...] = whole_target

        @pl.when(pl.program_id(0) > 0)
        def _():
            target_ref[...] = jnp.maximum(target_ref[...], whole_target)

    choose = (iota((GROUP * CAP, count), 0) == target).astype(F32).astype(BF16)
    table[...] = jnp.zeros_like(table)
    table[0:3] = base_ref[...].astype(F32) + 1.0
    table[8:11] = offset_ref[...]
    table[16:19] = velocity_ref[...]
    packed = dot_select(table[...], choose, NT)
    blank = jnp.zeros((8, CAP), F32)
    for r in range(GROUP):
        lanes = slice(r * CAP, (r + 1) * CAP)
        tile = jnp.concatenate(
            [packed[0:8, lanes], packed[8:16, lanes], packed[16:24, lanes], blank], axis=1
        )
        if single:
            outs[r][...] = tile
        else:
            outs[0][r] = tile


def pack(slabs, cols, owner, base, offset, velocity):
    owners, count = slabs * cols, owner.shape[0]
    single = owners == GROUP
    tile = jax.ShapeDtypeStruct((8, 128), F32)
    target = jax.ShapeDtypeStruct((1, count), jnp.int32)
    kernel = functools.partial(pack_kernel, slabs, cols, count, single)
    scratch = [pltpu.VMEM((24, count), F32)]
    args = (owner.reshape(1, count), base, offset, velocity)
    if single:
        target, *tiles = pl.pallas_call(
            kernel, out_shape=[target] + [tile] * owners, scratch_shapes=scratch, name="pack"
        )(*args)
        return target, tiles
    return pl.pallas_call(
        kernel,
        out_shape=[target, jax.ShapeDtypeStruct((owners, 8, 128), F32)],
        grid=(owners // GROUP,),
        in_specs=[pl.BlockSpec(a.shape, lambda k: (0, 0)) for a in args],
        out_specs=[
            pl.BlockSpec((1, count), lambda k: (0, 0)),
            pl.BlockSpec((GROUP, 8, 128), lambda k: (k, 0, 0)),
        ],
        scratch_shapes=scratch,
        compiler_params=pltpu.CompilerParams(vmem_limit_bytes=48 << 20),
        name="pack",
    )(*args)


def moments_kernel(pops_ref, solid_ref, flow_ref, edge_ref, edge_solid_ref):
    depth, rows = pops_ref.shape[1], pops_ref.shape[2]

    def plane(z, carry):
        pops = [pops_ref[i, z] for i in range(19)]
        density, momentum = density_momentum(pops)
        inverse = 1.0 / density
        for axis in range(3):
            flow_ref[axis, pl.ds(pl.multiple_of(z * rows, rows), rows)] = momentum[axis] * inverse
        return carry

    lax.fori_loop(0, depth, plane, 0)
    for i in range(19):
        edge_ref[i, 0] = pops_ref[i, 0]
        edge_ref[i, 1] = pops_ref[i, depth - 1]
        edge_ref[i, 2] = pops_ref[i, :, 0, :]
        edge_ref[i, 3] = pops_ref[i, :, rows - 1, :]
    edge_solid_ref[0] = solid_ref[0]
    edge_solid_ref[1] = solid_ref[depth - 1]
    edge_solid_ref[2] = solid_ref[:, 0, :]
    edge_solid_ref[3] = solid_ref[:, rows - 1, :]


def moments(pops, solid):
    _, depth, rows, width = pops.shape
    return pl.pallas_call(
        moments_kernel,
        out_shape=[
            jax.ShapeDtypeStruct((3, depth * rows, width), F32),
            jax.ShapeDtypeStruct((19, 4, rows, width), F32),
            jax.ShapeDtypeStruct((4, rows, width), jnp.int32),
        ],
        compiler_params=pltpu.CompilerParams(vmem_limit_bytes=16 << 20),
        cost_estimate=pl.CostEstimate(flops=3000000, bytes_accessed=4000000, transcendentals=0),
        name="moments",
    )(pops, solid)


def couple_group(tiles, flow, depth, rows):
    width, slots = flow.shape[1], GROUP * CAP
    base = jnp.concatenate([t[:, 0:CAP] for t in tiles], axis=1)
    part = jnp.concatenate([t[:, CAP : 2 * CAP] for t in tiles], axis=1)
    velocity = jnp.concatenate([t[:, 2 * CAP : 3 * CAP] for t in tiles], axis=1)
    start = base.astype(jnp.int32) - 1

    def hat(axis, length):
        cell = iota((length, slots), 0)
        low, share = start[axis : axis + 1], part[axis : axis + 1]
        return jnp.where(cell == low, 1.0 - share, 0.0) + jnp.where(cell == low + 1, share, 0.0)

    hat_x, hat_y, hat_z = hat(0, width), hat(1, rows), hat(2, depth)
    weight = (hat_z[:, None, :] * hat_y[None, :, :]).reshape(depth * rows, slots)
    across = dot_split(flow, hat_x, NN)
    cells = depth * rows
    sampled = [
        jnp.sum(across[d * cells : (d + 1) * cells] * weight, axis=0, keepdims=True)
        for d in range(3)
    ]
    drag = [DRAG_COEF * (sampled[d] - velocity[d : d + 1]) for d in range(3)]
    spread = jnp.concatenate([weight * (-drag[d]) for d in range(3)], axis=0)
    return drag, dot_split(spread, hat_x, NT)


def couple_kernel(
    single, shape, plan, depth, rows, n_in, flow_ref, edge_ref, edge_solid_ref, *refs
):
    ins, force_ref, refs = refs[:n_in], refs[n_in], refs[n_in + 1 :]
    width = flow_ref.shape[2]
    flow = flow_ref[...].reshape(3 * depth * rows, width)
    blank = jnp.zeros((8, 128 - CAP), F32)
    hollow = jnp.zeros((5, GROUP * CAP), F32)

    def drag_tiles(drag):
        stacked = jnp.concatenate(drag + [hollow], axis=0)
        return [
            jnp.concatenate([stacked[:, r * CAP : (r + 1) * CAP], blank], axis=1)
            for r in range(GROUP)
        ]

    if single:
        drag, force = couple_group([t[...] for t in ins], flow, depth, rows)
        force_ref[...] = force.reshape(3, depth, rows, width)
        tiles = drag_tiles(drag)
        refs[0][...] = tiles[0]
        messages = dict(zip(sorted(plan), refs[1:]))
        for r in range(1, GROUP):
            dz, dy = divmod(r, shape[1])
            messages[((-dz) % shape[0], (-dy) % shape[1], 0)][0:8] = tiles[r]
    else:
        force_ref[...] = jnp.zeros_like(force_ref)

        def group(k, carry):
            got = [ins[0][k * GROUP + r] for r in range(GROUP)]
            drag, force = couple_group(got, flow, depth, rows)
            force_ref[...] += force.reshape(3, depth, rows, width)
            for r, tile in enumerate(drag_tiles(drag)):
                refs[0][k * GROUP + r] = tile
            return carry

        lax.fori_loop(0, ins[0].shape[0] // GROUP, group, 0)
        messages = dict(zip(sorted(plan), refs[1:]))

    places = {
        key: message_rows(parts, rows, single and key[2] == 0)[1] for key, parts in plan.items()
    }
    for side in range(4):
        pops = [edge_ref[i, side] for i in range(19)]
        if side < 2:
            force = [force_ref[d, (0, depth - 1)[side]] for d in range(3)]
        else:
            force = [force_ref[d, :, (0, rows - 1)[side - 2], :] for d in range(3)]
        out = collide(pops, edge_solid_ref[side], force)
        axis = 2 if side < 2 else 1
        leaving = -1 if side % 2 == 0 else 1
        for i in range(19):
            if STEP[i, axis] != leaving:
                continue
            moved = turn(out[i], STEP[i, 1 if axis == 2 else 2], 0)
            moved = turn(moved, STEP[i, 0], 1)
            for key, parts in plan.items():
                for part in parts:
                    if part[0] != i or part[1][0] != axis:
                        continue
                    row = places[key][part]
                    if part[1] == (2, 1):
                        kept = 0 if STEP[i, 1] == 1 else rows - 1
                        messages[key][row : row + 8] = jnp.broadcast_to(
                            moved[kept : kept + 1], (8, width)
                        )
                    else:
                        messages[key][row : row + rows] = moved


def couple(shape, plan, tiles, flow, edge, edge_solid, depth, rows, single):
    width = flow.shape[2]
    sizes = [
        message_rows(plan[key], rows, single and key[2] == 0)[0] for key in sorted(plan)
    ]
    own = (8, 128) if single else tiles[0].shape
    out_shape = [
        jax.ShapeDtypeStruct((3, depth, rows, width), F32),
        jax.ShapeDtypeStruct(own, F32),
    ] + [jax.ShapeDtypeStruct((n, width), F32) for n in sizes]
    force, drag, *messages = pl.pallas_call(
        functools.partial(couple_kernel, single, shape, plan, depth, rows, len(tiles)),
        out_shape=out_shape,
        compiler_params=pltpu.CompilerParams(vmem_limit_bytes=24 << 20),
        name="couple",
    )(flow, edge, edge_solid, *tiles)
    return force, drag, dict(zip(sorted(plan), messages))


def stream_kernel(pops_ref, solid_ref, force_ref, out_ref, column_ref):
    depth, rows, width = pops_ref.shape[1:]
    lane = iota((rows, width), 1)

    def plane(z, columns):
        pops = [pops_ref[i, z] for i in range(19)]
        out = collide(pops, solid_ref[z], [force_ref[d, z] for d in range(3)])
        columns = list(columns)
        for i in range(19):
            moved = turn(turn(out[i], STEP[i, 1], 0), STEP[i, 0], 1)
            there = z + int(STEP[i, 2])
            there = jnp.where(there < 0, depth - 1, jnp.where(there == depth, 0, there))
            out_ref[i, there] = moved
            for side, group, edge in ((0, X_PLUS, 0), (1, X_MINUS, width - 1)):
                if i in group:
                    place = group.index(i) * depth + there
                    column = jnp.broadcast_to(moved[:, edge : edge + 1], (rows, width))
                    columns[side] = jnp.where(lane == place, column, columns[side])
        return tuple(columns)

    zero = jnp.zeros((rows, width), F32)
    columns = lax.fori_loop(0, depth, plane, (zero, zero))
    column_ref[0] = columns[0]
    column_ref[1] = columns[1]


def stream(pops, solid, force):
    _, depth, rows, width = pops.shape
    return pl.pallas_call(
        stream_kernel,
        out_shape=[
            jax.ShapeDtypeStruct(pops.shape, F32),
            jax.ShapeDtypeStruct((2, rows, width), F32),
        ],
        compiler_params=pltpu.CompilerParams(vmem_limit_bytes=16 << 20),
        cost_estimate=pl.CostEstimate(flops=10000000, bytes_accessed=6000000, transcendentals=0),
        name="stream",
    )(pops, solid, force)


def finish_kernel(
    single, shape, plan, n_back, target_ref, local_ref, column_ref, *refs
):
    backs, refs = refs[:n_back], refs[n_back:]
    keys = sorted(plan)
    messages, refs = dict(zip(keys, refs[: len(keys)])), refs[len(keys) :]
    out_ref, bead_ref, held, sem = refs
    depth, rows, width = local_ref.shape[1:]
    lane = iota((rows, width), 1)
    places = {}
    for key in keys:
        for part, row in message_rows(plan[key], rows, single and key[2] == 0)[1].items():
            places[part] = (messages[key], row)

    def arrived(part):
        ref, row = places[part]
        return ref[row : row + part_rows(part, rows)]

    copies = []
    for i in range(19):
        step = STEP[i]
        side = 0 if step[0] == 1 else width - 1
        enter_z = 0 if step[2] == 1 else depth - 1
        enter_y = 0 if step[1] == 1 else rows - 1
        if step[0] != 0:
            group, which = (X_PLUS, 0) if step[0] == 1 else (X_MINUS, 1)
            columns = column_ref[which]
            for z in range(depth):
                place = group.index(i) * depth + z
                column = jnp.broadcast_to(columns[:, place : place + 1], (rows, width))
                held[i, z] = jnp.where(lane == side, column, local_ref[i, z])
        else:
            held[i] = local_ref[i]
        for axis in (2, 1):
            if step[axis] == 0:
                continue
            value = arrived((i, (axis,)))
            if step[0] != 0:
                value = jnp.where(lane == side, arrived((i, (axis, 0))), value)
            if axis == 2:
                held[i, enter_z] = value
            else:
                held[i, :, enter_y, :] = value
        if step[1] != 0 and step[2] != 0:
            held[i, enter_z, enter_y : enter_y + 1, :] = arrived((i, (2, 1)))[0:1]
        copy = pltpu.make_async_copy(held.at[i], out_ref.at[i], sem.at[i])
        copy.start()
        copies.append(copy)

    count = target_ref.shape[1]

    def gathered(tiles, first):
        slots = jnp.concatenate([t[:, 0:CAP] for t in tiles], axis=1)
        choose = (iota((GROUP * CAP, count), 0) + first == target_ref[...]).astype(F32)
        return dot_select(slots, choose.astype(BF16), NN)[0:3]

    if single:
        tiles = [backs[0][...]]
        for r in range(1, GROUP):
            dz, dy = divmod(r, shape[1])
            tiles.append(messages[((-dz) % shape[0], (-dy) % shape[1], 0)][0:8])
        bead_ref[...] = gathered(tiles, 0)
    else:

        def group(k, total):
            tiles = [backs[0][k * GROUP + r] for r in range(GROUP)]
            return total + gathered(tiles, k * (GROUP * CAP))

        bead_ref[...] = lax.fori_loop(
            0, backs[0].shape[0] // GROUP, group, jnp.zeros((3, count), F32)
        )
    for copy in copies:
        copy.wait()


def finish(shape, plan, target, local, columns, backs, messages, single):
    vmem = pl.BlockSpec(memory_space=pltpu.VMEM)
    args = [target, local, columns, *backs, *[messages[key] for key in sorted(plan)]]
    return pl.pallas_call(
        functools.partial(finish_kernel, single, shape, plan, len(backs)),
        out_shape=[
            jax.ShapeDtypeStruct(local.shape, F32),
            jax.ShapeDtypeStruct((3, target.shape[1]), F32),
        ],
        in_specs=[vmem] * len(args),
        out_specs=[pl.BlockSpec(memory_space=pl.ANY), vmem],
        scratch_shapes=[pltpu.VMEM(local.shape, F32), pltpu.SemaphoreType.DMA((19,))],
        compiler_params=pltpu.CompilerParams(vmem_limit_bytes=24 << 20),
        name="finish",
    )(*args)


def shards(populations, solid_mask, bead_owner, bead_base, bead_offset, bead_velocity):
    slabs, cols, pairs = shape = tuple(lax.axis_size(a) for a in ("slab", "col", "pair"))
    owners = slabs * cols
    depth, rows = populations.shape[1:3]
    single = owners == GROUP
    plan = message_plan(shape)
    if single:
        for r in range(1, owners):
            plan.setdefault(divmod(r, cols) + (0,), [])

    target, tiles = pack(slabs, cols, bead_owner, bead_base, bead_offset, bead_velocity)
    if single:
        tiles = [tiles[0]] + [
            send(tiles[r], shape, divmod(r, cols) + (0,)) for r in range(1, owners)
        ]
    else:
        slab, col = lax.axis_index("slab"), lax.axis_index("col")
        index = jnp.arange(owners, dtype=jnp.int32)
        away = ((index // cols - slab) % slabs) * cols + (index % cols - col) % cols
        back = ((index // cols + slab) % slabs) * cols + (index % cols + col) % cols
        swap = functools.partial(
            lax.all_to_all, axis_name=("slab", "col"), split_axis=0, concat_axis=0, tiled=True
        )
        tiles = [swap(tiles[away])]
    flow, edge, edge_solid = moments(populations, solid_mask)
    force, drag, messages = couple(
        shape, plan, tiles, flow, edge, edge_solid, depth, rows, single
    )
    messages = {key: send(value, shape, key) for key, value in messages.items()}
    if not single:
        drag = swap(drag)[back]
    local, columns = stream(populations, solid_mask, force)
    columns = send(columns, shape, (0, 0, 1))
    return finish(shape, plan, target, local, columns, [drag], messages, single)


def solution(mesh):
    return jax.shard_map(
        shards,
        mesh=mesh,
        in_specs=(
            P(None, ("rep", "slab"), "col", "pair"),
            P(("rep", "slab"), "col", "pair"),
            P(("rep", "slab", "col", "pair")),
            P(None, ("rep", "slab", "col", "pair")),
            P(None, ("rep", "slab", "col", "pair")),
            P(None, ("rep", "slab", "col", "pair")),
        ),
        out_specs=(
            P(None, ("rep", "slab"), "col", "pair"),
            P(None, ("rep", "slab", "col", "pair")),
        ),
        check_vma=False,
    )
```

```python
import functools

import jax
import jax.numpy as jnp
import numpy as np
from jax import lax
from jax.experimental import pallas as pl
from jax.experimental.pallas import tpu as pltpu
from jax.sharding import PartitionSpec as P

CAP = 32
GROUP = 8

STEP = np.array(
    [
        [0, 0, 0],
        [1, 0, 0],
        [-1, 0, 0],
        [0, 1, 0],
        [0, -1, 0],
        [0, 0, 1],
        [0, 0, -1],
        [1, 1, 0],
        [-1, -1, 0],
        [1, -1, 0],
        [-1, 1, 0],
        [1, 0, 1],
        [-1, 0, -1],
        [1, 0, -1],
        [-1, 0, 1],
        [0, 1, 1],
        [0, -1, -1],
        [0, 1, -1],
        [0, -1, 1],
    ],
    np.int32,
)
TAU_PLUS = 0.8
TAU_MINUS = 0.5 + (3.0 / 16.0) / (TAU_PLUS - 0.5)
KEEP_EVEN = 1.0 - 1.0 / TAU_PLUS
KEEP_ODD = 1.0 - 1.0 / TAU_MINUS
FORCE_GAIN = 1.0 - 0.5 / TAU_PLUS
DRAG_COEF = 2.0
F32 = jnp.float32
BF16 = jnp.bfloat16

X_PLUS = [i for i in range(19) if STEP[i, 0] == 1]
X_MINUS = [i for i in range(19) if STEP[i, 0] == -1]
NT = (((1,), (1,)), ((), ()))
NN = (((1,), (0,)), ((), ()))


def iota(shape, dim):
    return lax.broadcasted_iota(jnp.int32, shape, dim)


def high_low(value):
    high = value.astype(BF16)
    return high, (value - high.astype(F32)).astype(BF16)


def dot_split(left, right, dims):
    a, b = high_low(left)
    c, d = high_low(right)
    mul = functools.partial(lax.dot_general, dimension_numbers=dims, preferred_element_type=F32)
    return mul(a, c) + (mul(a, d) + mul(b, c))


def dot_select(value, choose, dims):
    first = value.astype(BF16).astype(F32)
    rest = value - first
    second = rest.astype(BF16).astype(F32)
    stacked = jnp.concatenate([first, second, rest - second], axis=0).astype(BF16)
    got = lax.dot_general(stacked, choose, dimension_numbers=dims, preferred_element_type=F32)
    rows = value.shape[0]
    return got[0:rows] + got[rows : 2 * rows] + got[2 * rows : 3 * rows]


def density_momentum(pops):
    momentum = []
    for axis in range(3):
        plus = [pops[i] for i in range(19) if STEP[i, axis] == 1]
        minus = [pops[i] for i in range(19) if STEP[i, axis] == -1]
        momentum.append(sum(plus[1:], plus[0]) - sum(minus[1:], minus[0]))
    return sum(pops[1:], pops[0]), momentum


def along(step, vector):
    terms = None
    for axis in range(3):
        if step[axis] == 0:
            continue
        if terms is None:
            terms = vector[axis] if step[axis] == 1 else -vector[axis]
        else:
            terms = terms + vector[axis] if step[axis] == 1 else terms - vector[axis]
    return terms


def collide(pops, solid, force):
    density, momentum = density_momentum(pops)
    inverse = 1.0 / density
    carried = [m + 0.5 * f for m, f in zip(momentum, force)]
    speed = [m * inverse for m in carried]
    w = 1.0 / 36.0
    bend = [(4.5 * w / TAU_PLUS) * m + (9.0 * w * FORCE_GAIN) * f for m, f in zip(carried, force)]
    push = [(3.0 * w / TAU_MINUS) * m + (3.0 * w * FORCE_GAIN) * f for m, f in zip(carried, force)]
    drop = [(1.5 * w / TAU_PLUS) * m + (3.0 * w * FORCE_GAIN) * f for m, f in zip(carried, force)]
    rest = (w / TAU_PLUS) * density - sum(
        [u * d for u, d in zip(speed[1:], drop[1:])], speed[0] * drop[0]
    )
    wall = solid == 1
    out = [None] * 19
    out[0] = jnp.where(wall, pops[0], KEEP_EVEN * pops[0] + 12.0 * rest)
    for i in range(1, 19, 2):
        a, b = pops[i], pops[i + 1]
        step = STEP[i]
        even = rest + along(step, speed) * along(step, bend)
        odd = along(step, push)
        if i < 7:
            even = even + even
            odd = odd + odd
        even = (0.5 * KEEP_EVEN) * (a + b) + even
        odd = (0.5 * KEEP_ODD) * (a - b) + odd
        out[i] = jnp.where(wall, b, even + odd)
        out[i + 1] = jnp.where(wall, a, even - odd)
    return out


def turn(value, amount, axis):
    if amount == 0:
        return value
    return pltpu.roll(value, int(amount) % value.shape[axis], axis)


def message_plan(shape):
    plan = {}
    for i in range(1, 19):
        moving = [a for a in (2, 1, 0) if STEP[i, a] != 0]
        subsets = [[a] for a in moving] + ([moving] if len(moving) == 2 else [])
        for axes in subsets:
            if axes == [0]:
                continue
            key = tuple(
                int(STEP[i, a]) % shape[k] if a in axes else 0 for k, a in enumerate((2, 1, 0))
            )
            plan.setdefault(key, []).append((i, tuple(axes)))
    return plan


def part_rows(part, span):
    return 8 if part[1] == (2, 1) else span


def message_rows(parts, span):
    rows = 0
    places = {}
    for part in parts:
        places[part] = rows
        rows += part_rows(part, span)
    return rows, places


def send(value, shape, offset):
    slabs, cols, pairs = shape
    perm = []
    for s in range(slabs):
        for c in range(cols):
            for p in range(pairs):
                there = (
                    ((s + offset[0]) % slabs) * cols + (c + offset[1]) % cols
                ) * pairs + (p + offset[2]) % pairs
                perm.append(((s * cols + c) * pairs + p, there))
    return lax.ppermute(value, ("slab", "col", "pair"), perm)


def wrap(value, size):
    return jnp.where(value < 0, value + size, value)


def pack_kernel(slabs, cols, count, owner_ref, base_ref, offset_ref, velocity_ref, target_ref, out_ref, table):
    owner = owner_ref[...]
    owner_slab = lax.shift_right_logical(owner, cols.bit_length() - 1)
    owner_col = owner - owner_slab * cols
    relative = wrap(owner_slab - lax.axis_index("slab"), slabs) * cols + wrap(
        owner_col - lax.axis_index("col"), cols
    )
    local = relative - pl.program_id(0) * GROUP
    member = (iota((GROUP, count), 0) == local).astype(F32)
    rank = jnp.sum(member * rank_among(member), axis=0, keepdims=True).astype(jnp.int32)
    inside = (local >= 0) & (local < GROUP)
    target = jnp.where(inside, local * CAP + rank, -1)
    whole_target = jnp.where(inside, relative * CAP + rank, -1)

    @pl.when(pl.program_id(0) == 0)
    def _():
        target_ref[...] = whole_target

    @pl.when(pl.program_id(0) > 0)
    def _():
        target_ref[...] = jnp.maximum(target_ref[...], whole_target)

    choose = (iota((GROUP * CAP, count), 0) == target).astype(F32).astype(BF16)
    table[...] = jnp.zeros_like(table)
    table[0:3] = base_ref[...].astype(F32) + 1.0
    table[8:11] = offset_ref[...]
    table[16:19] = velocity_ref[...]
    packed = dot_select(table[...], choose, NT)
    blank = jnp.zeros((8, CAP), F32)
    for r in range(GROUP):
        lanes = slice(r * CAP, (r + 1) * CAP)
        out_ref[r] = jnp.concatenate(
            [packed[0:8, lanes], packed[8:16, lanes], packed[16:24, lanes], blank], axis=1
        )


def pack(slabs, cols, owner, base, offset, velocity):
    owners, count = slabs * cols, owner.shape[0]
    args = (owner.reshape(1, count), base, offset, velocity)
    return pl.pallas_call(
        functools.partial(pack_kernel, slabs, cols, count),
        out_shape=[
            jax.ShapeDtypeStruct((1, count), jnp.int32),
            jax.ShapeDtypeStruct((owners, 8, 128), F32),
        ],
        grid=(owners // GROUP,),
        in_specs=[pl.BlockSpec(a.shape, lambda k: (0, 0)) for a in args],
        out_specs=[
            pl.BlockSpec((1, count), lambda k: (0, 0)),
            pl.BlockSpec((GROUP, 8, 128), lambda k: (k, 0, 0)),
        ],
        scratch_shapes=[pltpu.VMEM((24, count), F32)],
        compiler_params=pltpu.CompilerParams(vmem_limit_bytes=48 << 20),
        name="pack",
    )(*args)


def publish_kernel(owner_ref, base_ref, offset_ref, velocity_ref, out_ref):
    out_ref[0:1] = owner_ref[...].astype(F32)
    out_ref[1:4] = base_ref[...].astype(F32) + 1.0
    out_ref[4:7] = offset_ref[...]
    out_ref[7:10] = velocity_ref[...]
    out_ref[10:16] = jnp.zeros((6, out_ref.shape[1]), F32)


def publish(owner, base, offset, velocity):
    count = owner.shape[0]
    return pl.pallas_call(
        publish_kernel, out_shape=jax.ShapeDtypeStruct((16, count), F32), name="publish"
    )(owner.reshape(1, count), base, offset, velocity)


def rank_among(member):
    count = member.shape[1]
    earlier = (iota((count, count), 0) < iota((count, count), 1)).astype(F32).astype(BF16)
    return lax.dot_general(member.astype(BF16), earlier, NN, preferred_element_type=F32)


def own_slots(all_ref, me):
    owner = jnp.concatenate([all_ref[k, 0:1] for k in range(GROUP)], axis=0)
    member = (owner == me.astype(F32)).astype(F32)
    place = jnp.where(member > 0.0, rank_among(member), -1.0).astype(jnp.int32)
    count = owner.shape[1]
    slots = []
    for k in range(GROUP):
        choose = (iota((CAP, count), 0) == place[k : k + 1]).astype(F32).astype(BF16)
        slots.append(dot_select(all_ref[k], choose, NT))
    return jnp.concatenate(slots, axis=1)


def moments_kernel(pops_ref, solid_ref, flow_ref, edge_ref, edge_solid_ref):
    depth, rows = pops_ref.shape[1], pops_ref.shape[2]

    def plane(z, carry):
        pops = [pops_ref[i, z] for i in range(19)]
        density, momentum = density_momentum(pops)
        inverse = 1.0 / density
        for axis in range(3):
            flow_ref[axis, pl.ds(pl.multiple_of(z * rows, rows), rows)] = momentum[axis] * inverse
        return carry

    lax.fori_loop(0, depth, plane, 0)
    for i in range(19):
        edge_ref[i, 0] = pops_ref[i, 0]
        edge_ref[i, 1] = pops_ref[i, depth - 1]
        edge_ref[i, 2] = pops_ref[i, :, 0, :]
        edge_ref[i, 3] = pops_ref[i, :, rows - 1, :]
    edge_solid_ref[0] = solid_ref[0]
    edge_solid_ref[1] = solid_ref[depth - 1]
    edge_solid_ref[2] = solid_ref[:, 0, :]
    edge_solid_ref[3] = solid_ref[:, rows - 1, :]


def moments(pops, solid):
    _, depth, rows, width = pops.shape
    return pl.pallas_call(
        moments_kernel,
        out_shape=[
            jax.ShapeDtypeStruct((3, depth * rows, width), F32),
            jax.ShapeDtypeStruct((19, 4, rows, width), F32),
            jax.ShapeDtypeStruct((4, rows, width), jnp.int32),
        ],
        compiler_params=pltpu.CompilerParams(vmem_limit_bytes=16 << 20),
        cost_estimate=pl.CostEstimate(flops=3000000, bytes_accessed=4000000, transcendentals=0),
        name="moments",
    )(pops, solid)


def unpack(tiles):
    return [
        jnp.concatenate([t[0:3, g * CAP : (g + 1) * CAP] for t in tiles], axis=1)
        for g in range(3)
    ]


def couple_group(base, part, velocity, flow, depth, rows):
    width, slots = flow.shape[1], GROUP * CAP
    start = base.astype(jnp.int32) - 1

    def hat(axis, length):
        cell = iota((length, slots), 0)
        low, share = start[axis : axis + 1], part[axis : axis + 1]
        return jnp.where(cell == low, 1.0 - share, 0.0) + jnp.where(cell == low + 1, share, 0.0)

    hat_x, hat_y, hat_z = hat(0, width), hat(1, rows), hat(2, depth)
    weight = (hat_z[:, None, :] * hat_y[None, :, :]).reshape(depth * rows, slots)
    across = dot_split(flow, hat_x, NN)
    cells = depth * rows
    sampled = [
        jnp.sum(across[d * cells : (d + 1) * cells] * weight, axis=0, keepdims=True)
        for d in range(3)
    ]
    drag = [DRAG_COEF * (sampled[d] - velocity[d : d + 1]) for d in range(3)]
    spread = jnp.concatenate([weight * (-drag[d]) for d in range(3)], axis=0)
    return drag, dot_split(spread, hat_x, NT)


def couple_kernel(
    single, shape, plan, depth, rows, beads_ref, flow_ref, edge_ref, edge_solid_ref, force_ref, drag_ref, *refs
):
    width = flow_ref.shape[2]
    flow = flow_ref[...].reshape(3 * depth * rows, width)
    messages = dict(zip(sorted(plan), refs))
    blank = jnp.zeros((8, 128 - CAP), F32)
    hollow = jnp.zeros((5, GROUP * CAP), F32)

    if single:
        me = lax.axis_index("slab") * shape[1] + lax.axis_index("col")
        slots = own_slots(beads_ref, me)
        drag, force = couple_group(slots[1:4], slots[4:7], slots[7:10], flow, depth, rows)
        force_ref[...] = force.reshape(3, depth, rows, width)
        pieces = [
            jnp.concatenate([d[:, k * CAP : (k + 1) * CAP] for k in range(GROUP)], axis=0)
            for d in drag
        ]
        drag_ref[...] = jnp.concatenate(pieces + [jnp.zeros((GROUP, CAP), F32)], axis=1)
    else:
        force_ref[...] = jnp.zeros_like(force_ref)

        def group(k, carry):
            got = [beads_ref[k * GROUP + r] for r in range(GROUP)]
            drag, force = couple_group(*unpack(got), flow, depth, rows)
            force_ref[...] += force.reshape(3, depth, rows, width)
            stacked = jnp.concatenate(drag + [hollow], axis=0)
            for r in range(GROUP):
                drag_ref[k * GROUP + r] = jnp.concatenate(
                    [stacked[:, r * CAP : (r + 1) * CAP], blank], axis=1
                )
            return carry

        lax.fori_loop(0, beads_ref.shape[0] // GROUP, group, 0)

    places = {key: message_rows(parts, rows)[1] for key, parts in plan.items()}
    for side in range(4):
        pops = [edge_ref[i, side] for i in range(19)]
        if side < 2:
            force = [force_ref[d, (0, depth - 1)[side]] for d in range(3)]
        else:
            force = [force_ref[d, :, (0, rows - 1)[side - 2], :] for d in range(3)]
        out = collide(pops, edge_solid_ref[side], force)
        axis = 2 if side < 2 else 1
        leaving = -1 if side % 2 == 0 else 1
        for i in range(19):
            if STEP[i, axis] != leaving:
                continue
            moved = turn(out[i], STEP[i, 1 if axis == 2 else 2], 0)
            moved = turn(moved, STEP[i, 0], 1)
            for key, parts in plan.items():
                for part in parts:
                    if part[0] != i or part[1][0] != axis:
                        continue
                    row = places[key][part]
                    if part[1] == (2, 1):
                        kept = 0 if STEP[i, 1] == 1 else rows - 1
                        messages[key][row : row + 8] = jnp.broadcast_to(
                            moved[kept : kept + 1], (8, width)
                        )
                    else:
                        messages[key][row : row + rows] = moved


def couple(single, shape, plan, beads, flow, edge, edge_solid, depth, rows):
    width = flow.shape[2]
    sizes = [message_rows(plan[key], rows)[0] for key in sorted(plan)]
    own = (8, 128) if single else beads.shape
    out_shape = [
        jax.ShapeDtypeStruct((3, depth, rows, width), F32),
        jax.ShapeDtypeStruct(own, F32),
    ] + [jax.ShapeDtypeStruct((n, width), F32) for n in sizes]
    force, drag, *messages = pl.pallas_call(
        functools.partial(couple_kernel, single, shape, plan, depth, rows),
        out_shape=out_shape,
        compiler_params=pltpu.CompilerParams(vmem_limit_bytes=24 << 20),
        name="couple",
    )(beads, flow, edge, edge_solid)
    return force, drag, dict(zip(sorted(plan), messages))


def stream_kernel(pops_ref, solid_ref, force_ref, out_ref, column_ref):
    depth, rows, width = pops_ref.shape[1:]
    lane = iota((rows, width), 1)

    def plane(z, columns):
        pops = [pops_ref[i, z] for i in range(19)]
        out = collide(pops, solid_ref[z], [force_ref[d, z] for d in range(3)])
        columns = list(columns)
        for i in range(19):
            moved = turn(turn(out[i], STEP[i, 1], 0), STEP[i, 0], 1)
            there = z + int(STEP[i, 2])
            there = jnp.where(there < 0, depth - 1, jnp.where(there == depth, 0, there))
            out_ref[i, there] = moved
            for side, group, edge in ((0, X_PLUS, 0), (1, X_MINUS, width - 1)):
                if i in group:
                    place = group.index(i) * depth + there
                    column = jnp.broadcast_to(moved[:, edge : edge + 1], (rows, width))
                    columns[side] = jnp.where(lane == place, column, columns[side])
        return tuple(columns)

    zero = jnp.zeros((rows, width), F32)
    columns = lax.fori_loop(0, depth, plane, (zero, zero))
    column_ref[0] = columns[0]
    column_ref[1] = columns[1]


def stream(pops, solid, force):
    _, depth, rows, width = pops.shape
    return pl.pallas_call(
        stream_kernel,
        out_shape=[
            jax.ShapeDtypeStruct(pops.shape, F32),
            jax.ShapeDtypeStruct((2, rows, width), F32),
        ],
        compiler_params=pltpu.CompilerParams(vmem_limit_bytes=16 << 20),
        cost_estimate=pl.CostEstimate(flops=10000000, bytes_accessed=6000000, transcendentals=0),
        name="stream",
    )(pops, solid, force)


def finish_kernel(single, shape, plan, target_ref, local_ref, column_ref, back_ref, *refs):
    keys = sorted(plan)
    messages, refs = dict(zip(keys, refs[: len(keys)])), refs[len(keys) :]
    out_ref, bead_ref, held, sem = refs
    depth, rows, width = local_ref.shape[1:]
    lane = iota((rows, width), 1)
    places = {}
    for key in keys:
        for part, row in message_rows(plan[key], rows)[1].items():
            places[part] = (messages[key], row)

    def arrived(part):
        ref, row = places[part]
        return ref[row : row + part_rows(part, rows)]

    copies = []
    for i in range(19):
        step = STEP[i]
        side = 0 if step[0] == 1 else width - 1
        enter_z = 0 if step[2] == 1 else depth - 1
        enter_y = 0 if step[1] == 1 else rows - 1
        if step[0] != 0:
            group, which = (X_PLUS, 0) if step[0] == 1 else (X_MINUS, 1)
            columns = column_ref[which]
            for z in range(depth):
                place = group.index(i) * depth + z
                column = jnp.broadcast_to(columns[:, place : place + 1], (rows, width))
                held[i, z] = jnp.where(lane == side, column, local_ref[i, z])
        else:
            held[i] = local_ref[i]
        for axis in (2, 1):
            if step[axis] == 0:
                continue
            value = arrived((i, (axis,)))
            if step[0] != 0:
                value = jnp.where(lane == side, arrived((i, (axis, 0))), value)
            if axis == 2:
                held[i, enter_z] = value
            else:
                held[i, :, enter_y, :] = value
        if step[1] != 0 and step[2] != 0:
            held[i, enter_z, enter_y : enter_y + 1, :] = arrived((i, (2, 1)))[0:1]
        copy = pltpu.make_async_copy(held.at[i], out_ref.at[i], sem.at[i])
        copy.start()
        copies.append(copy)

    count = target_ref.shape[1]
    if single:
        me = lax.axis_index("slab") * shape[1] + lax.axis_index("col")
        mine = jnp.concatenate([back_ref[k, pl.ds(me, 1), :] for k in range(GROUP)], axis=0)
        owner = target_ref[...]
        member = (iota((GROUP, count), 0) == owner).astype(F32)
        slot = jnp.sum(member * rank_among(member), axis=0, keepdims=True).astype(jnp.int32)
        for d in range(3):
            choose = (iota((128, count), 0) == slot + d * CAP).astype(F32).astype(BF16)
            picked = dot_select(mine, choose, NN)
            bead_ref[d : d + 1] = jnp.sum(member * picked, axis=0, keepdims=True)
    else:

        def group(k, total):
            tiles = [back_ref[k * GROUP + r] for r in range(GROUP)]
            slots = jnp.concatenate([t[:, 0:CAP] for t in tiles], axis=1)
            first = k * (GROUP * CAP)
            choose = (iota((GROUP * CAP, count), 0) + first == target_ref[...]).astype(F32)
            return total + dot_select(slots, choose.astype(BF16), NN)[0:3]

        bead_ref[...] = lax.fori_loop(
            0, back_ref.shape[0] // GROUP, group, jnp.zeros((3, count), F32)
        )
    for copy in copies:
        copy.wait()


def finish(single, shape, plan, target, local, columns, back, messages):
    vmem = pl.BlockSpec(memory_space=pltpu.VMEM)
    args = [target, local, columns, back, *[messages[key] for key in sorted(plan)]]
    return pl.pallas_call(
        functools.partial(finish_kernel, single, shape, plan),
        out_shape=[
            jax.ShapeDtypeStruct(local.shape, F32),
            jax.ShapeDtypeStruct((3, target.shape[1]), F32),
        ],
        in_specs=[vmem] * len(args),
        out_specs=[pl.BlockSpec(memory_space=pl.ANY), vmem],
        scratch_shapes=[pltpu.VMEM(local.shape, F32), pltpu.SemaphoreType.DMA((19,))],
        compiler_params=pltpu.CompilerParams(vmem_limit_bytes=24 << 20),
        name="finish",
    )(*args)


def shards(populations, solid_mask, bead_owner, bead_base, bead_offset, bead_velocity):
    slabs, cols, pairs = shape = tuple(lax.axis_size(a) for a in ("slab", "col", "pair"))
    owners = slabs * cols
    depth, rows = populations.shape[1:3]
    single = owners == GROUP
    plan = message_plan(shape)
    beads = (bead_owner, bead_base, bead_offset, bead_velocity)
    group = ("slab", "col")

    if single:
        tiles = lax.all_gather(publish(*beads), group)
        target = bead_owner.reshape(1, -1)
    else:
        target, tiles = pack(slabs, cols, *beads)
        slab, col = lax.axis_index("slab"), lax.axis_index("col")
        index = jnp.arange(owners, dtype=jnp.int32)
        away = ((index // cols - slab) % slabs) * cols + (index % cols - col) % cols
        back = ((index // cols + slab) % slabs) * cols + (index % cols + col) % cols
        swap = functools.partial(
            lax.all_to_all, axis_name=group, split_axis=0, concat_axis=0, tiled=True
        )
        tiles = swap(tiles[away])
    flow, edge, edge_solid = moments(populations, solid_mask)
    force, drag, messages = couple(
        single, shape, plan, tiles, flow, edge, edge_solid, depth, rows
    )
    drag = lax.all_gather(drag, group) if single else swap(drag)[back]
    messages = {key: send(value, shape, key) for key, value in messages.items()}
    local, columns = stream(populations, solid_mask, force)
    columns = send(columns, shape, (0, 0, 1))
    return finish(single, shape, plan, target, local, columns, drag, messages)


def solution(mesh):
    return jax.shard_map(
        shards,
        mesh=mesh,
        in_specs=(
            P(None, ("rep", "slab"), "col", "pair"),
            P(("rep", "slab"), "col", "pair"),
            P(("rep", "slab", "col", "pair")),
            P(None, ("rep", "slab", "col", "pair")),
            P(None, ("rep", "slab", "col", "pair")),
            P(None, ("rep", "slab", "col", "pair")),
        ),
        out_specs=(
            P(None, ("rep", "slab"), "col", "pair"),
            P(None, ("rep", "slab", "col", "pair")),
        ),
        check_vma=False,
    )
```

```python
import functools

import jax
import jax.numpy as jnp
import numpy as np
from jax import lax
from jax.experimental import pallas as pl
from jax.experimental.pallas import tpu as pltpu
from jax.sharding import PartitionSpec as P

CAP = 32
GROUP = 8

STEP = np.array(
    [
        [0, 0, 0],
        [1, 0, 0],
        [-1, 0, 0],
        [0, 1, 0],
        [0, -1, 0],
        [0, 0, 1],
        [0, 0, -1],
        [1, 1, 0],
        [-1, -1, 0],
        [1, -1, 0],
        [-1, 1, 0],
        [1, 0, 1],
        [-1, 0, -1],
        [1, 0, -1],
        [-1, 0, 1],
        [0, 1, 1],
        [0, -1, -1],
        [0, 1, -1],
        [0, -1, 1],
    ],
    np.int32,
)
TAU_PLUS = 0.8
TAU_MINUS = 0.5 + (3.0 / 16.0) / (TAU_PLUS - 0.5)
KEEP_EVEN = 1.0 - 1.0 / TAU_PLUS
KEEP_ODD = 1.0 - 1.0 / TAU_MINUS
FORCE_GAIN = 1.0 - 0.5 / TAU_PLUS
DRAG_COEF = 2.0
F32 = jnp.float32
BF16 = jnp.bfloat16

ENTER = [[[i for i in range(19) if STEP[i, a] == sign] for sign in (1, -1)] for a in range(3)]
NT = (((1,), (1,)), ((), ()))
NN = (((1,), (0,)), ((), ()))


def iota(shape, dim):
    return lax.broadcasted_iota(jnp.int32, shape, dim)


def high_low(value):
    high = value.astype(BF16)
    return high, (value - high.astype(F32)).astype(BF16)


def dot_split(left, right, dims):
    a, b = high_low(left)
    c, d = high_low(right)
    mul = functools.partial(lax.dot_general, dimension_numbers=dims, preferred_element_type=F32)
    return mul(a, c) + (mul(a, d) + mul(b, c))


def dot_select(value, choose, dims):
    first = value.astype(BF16).astype(F32)
    rest = value - first
    second = rest.astype(BF16).astype(F32)
    stacked = jnp.concatenate([first, second, rest - second], axis=0).astype(BF16)
    got = lax.dot_general(stacked, choose, dimension_numbers=dims, preferred_element_type=F32)
    rows = value.shape[0]
    return got[0:rows] + got[rows : 2 * rows] + got[2 * rows : 3 * rows]


def density_momentum(pops):
    momentum = []
    for axis in range(3):
        plus = [pops[i] for i in range(19) if STEP[i, axis] == 1]
        minus = [pops[i] for i in range(19) if STEP[i, axis] == -1]
        momentum.append(sum(plus[1:], plus[0]) - sum(minus[1:], minus[0]))
    return sum(pops[1:], pops[0]), momentum


def along(step, vector):
    terms = None
    for axis in range(3):
        if step[axis] == 0:
            continue
        if terms is None:
            terms = vector[axis] if step[axis] == 1 else -vector[axis]
        else:
            terms = terms + vector[axis] if step[axis] == 1 else terms - vector[axis]
    return terms


def collide(pops, wall, force):
    density, momentum = density_momentum(pops)
    inverse = 1.0 / density
    carried = [m + 0.5 * f for m, f in zip(momentum, force)]
    speed = [m * inverse for m in carried]
    w = 1.0 / 36.0
    bend = [(4.5 * w / TAU_PLUS) * m + (9.0 * w * FORCE_GAIN) * f for m, f in zip(carried, force)]
    push = [(3.0 * w / TAU_MINUS) * m + (3.0 * w * FORCE_GAIN) * f for m, f in zip(carried, force)]
    drop = [(1.5 * w / TAU_PLUS) * m + (3.0 * w * FORCE_GAIN) * f for m, f in zip(carried, force)]
    rest = (w / TAU_PLUS) * density - sum(
        [u * d for u, d in zip(speed[1:], drop[1:])], speed[0] * drop[0]
    )
    out = [None] * 19
    out[0] = jnp.where(wall, pops[0], KEEP_EVEN * pops[0] + 12.0 * rest)
    for i in range(1, 19, 2):
        a, b = pops[i], pops[i + 1]
        step = STEP[i]
        even = rest + along(step, speed) * along(step, bend)
        odd = along(step, push)
        if i < 7:
            even = even + even
            odd = odd + odd
        even = (0.5 * KEEP_EVEN) * (a + b) + even
        odd = (0.5 * KEEP_ODD) * (a - b) + odd
        out[i] = jnp.where(wall, b, even + odd)
        out[i + 1] = jnp.where(wall, a, even - odd)
    return out


def turn(value, amount, axis):
    if amount == 0:
        return value
    return pltpu.roll(value, int(amount) % value.shape[axis], axis)


def send(value, shape, offset):
    slabs, cols, pairs = shape
    perm = []
    for s in range(slabs):
        for c in range(cols):
            for p in range(pairs):
                there = (
                    ((s + offset[0]) % slabs) * cols + (c + offset[1]) % cols
                ) * pairs + (p + offset[2]) % pairs
                perm.append(((s * cols + c) * pairs + p, there))
    return lax.ppermute(value, ("slab", "col", "pair"), perm)


def rank_among(member):
    count = member.shape[1]
    earlier = (iota((count, count), 0) < iota((count, count), 1)).astype(F32).astype(BF16)
    return lax.dot_general(member.astype(BF16), earlier, NN, preferred_element_type=F32)


def spread_column(tile, lane):
    return jnp.broadcast_to(tile[:, lane : lane + 1], tile.shape)


def enter_x(value, i, column):
    step = STEP[i, 0]
    if step == 0:
        return value
    side = 0 if step == 1 else value.shape[1] - 1
    return jnp.where(iota(value.shape, 1) == side, column, turn(value, step, 1))


def x_place(i):
    group = 0 if STEP[i, 0] == 1 else 1
    return group, ENTER[0][group].index(i)


def pack_kernel(owner_ref, base_ref, offset_ref, velocity_ref, target_ref, out_ref, table):
    count = owner_ref.shape[1]
    local = owner_ref[...] - pl.program_id(0) * GROUP
    member = (iota((GROUP, count), 0) == local).astype(F32)
    rank = jnp.sum(member * rank_among(member), axis=0, keepdims=True).astype(jnp.int32)
    inside = (local >= 0) & (local < GROUP)
    target = jnp.where(inside, local * CAP + rank, -1)
    whole_target = jnp.where(inside, owner_ref[...] * CAP + rank, -1)

    @pl.when(pl.program_id(0) == 0)
    def _():
        target_ref[...] = whole_target

    @pl.when(pl.program_id(0) > 0)
    def _():
        target_ref[...] = jnp.maximum(target_ref[...], whole_target)

    choose = (iota((GROUP * CAP, count), 0) == target).astype(F32).astype(BF16)
    table[...] = jnp.zeros_like(table)
    table[0:3] = base_ref[...].astype(F32) + 1.0
    table[8:11] = offset_ref[...]
    table[16:19] = velocity_ref[...]
    packed = dot_select(table[...], choose, NT)
    blank = jnp.zeros((8, CAP), F32)
    for r in range(GROUP):
        lanes = slice(r * CAP, (r + 1) * CAP)
        out_ref[r] = jnp.concatenate(
            [packed[0:8, lanes], packed[8:16, lanes], packed[16:24, lanes], blank], axis=1
        )


def pack(owners, owner, base, offset, velocity):
    count = owner.shape[0]
    args = (owner.reshape(1, count), base, offset, velocity)
    return pl.pallas_call(
        pack_kernel,
        out_shape=[
            jax.ShapeDtypeStruct((1, count), jnp.int32),
            jax.ShapeDtypeStruct((owners, 8, 128), F32),
        ],
        grid=(owners // GROUP,),
        in_specs=[pl.BlockSpec(a.shape, lambda k: (0, 0)) for a in args],
        out_specs=[
            pl.BlockSpec((1, count), lambda k: (0, 0)),
            pl.BlockSpec((GROUP, 8, 128), lambda k: (k, 0, 0)),
        ],
        scratch_shapes=[pltpu.VMEM((24, count), F32)],
        compiler_params=pltpu.CompilerParams(
            vmem_limit_bytes=(4 << 20) if owners == GROUP else (48 << 20)
        ),
        name="pack",
    )(*args)


def moments_kernel(
    pops_ref, solid_ref, flow_ref, edge_ref, edge_solid_ref, column_ref, held, held_solid, sem
):
    depth, rows, width = pops_ref.shape[1:]
    chunks = 4
    span = depth // chunks
    copies = [pltpu.make_async_copy(solid_ref, held_solid, sem.at[chunks])]
    for k in range(chunks):
        part = pl.ds(k * span, span)
        copies.append(
            pltpu.make_async_copy(pops_ref.at[:, part], held.at[:, part], sem.at[k])
        )
    for copy in copies:
        copy.start()

    def plane(z, carry):
        pops = [held[i, z] for i in range(19)]
        density, momentum = density_momentum(pops)
        inverse = 1.0 / density
        for axis in range(3):
            flow_ref[axis, pl.ds(pl.multiple_of(z * rows, rows), rows)] = momentum[axis] * inverse
        return carry

    for k in range(chunks):
        copies[1 + k].wait()
        lax.fori_loop(k * span, (k + 1) * span, plane, 0)
    copies[0].wait()
    edge_solid_ref[0] = held_solid[0]
    edge_solid_ref[1] = held_solid[depth - 1]
    edge_solid_ref[2] = held_solid[:, 0, :]
    edge_solid_ref[3] = held_solid[:, rows - 1, :]
    lane = iota((rows, 128), 1)

    def ends(planes):
        tile = jnp.ones((rows, 128), F32)
        for z, value in enumerate(planes):
            tile = jnp.where(lane == z, spread_column(value, 0), tile)
            tile = jnp.where(lane == depth + z, spread_column(value, width - 1), tile)
        return tile

    def population(i, carry):
        edge_ref[i, 0] = held[i, 0]
        edge_ref[i, 1] = held[i, depth - 1]
        edge_ref[i, 2] = held[i, :, 0, :]
        edge_ref[i, 3] = held[i, :, rows - 1, :]
        column_ref[i] = ends([held[i, z] for z in range(depth)])
        return carry

    lax.fori_loop(0, 19, population, 0)
    column_ref[19] = ends([held_solid[z].astype(F32) for z in range(depth)])


def moments(pops, solid):
    _, depth, rows, width = pops.shape
    hbm = pl.BlockSpec(memory_space=pltpu.HBM)
    return pl.pallas_call(
        moments_kernel,
        out_shape=[
            jax.ShapeDtypeStruct((3, depth * rows, width), F32),
            jax.ShapeDtypeStruct((19, 4, rows, width), F32),
            jax.ShapeDtypeStruct((4, rows, width), jnp.int32),
            jax.ShapeDtypeStruct((20, rows, 128), F32),
        ],
        in_specs=[hbm, hbm],
        scratch_shapes=[
            pltpu.VMEM(pops.shape, F32),
            pltpu.VMEM(solid.shape, jnp.int32),
            pltpu.SemaphoreType.DMA((5,)),
        ],
        compiler_params=pltpu.CompilerParams(vmem_limit_bytes=12 << 20),
        cost_estimate=pl.CostEstimate(flops=3000000, bytes_accessed=4000000, transcendentals=0),
        name="moments",
    )(pops, solid)


def unpack(tiles):
    return [
        jnp.concatenate([t[:, g * CAP : (g + 1) * CAP] for t in tiles], axis=1) for g in range(3)
    ]


def couple_group(base, part, velocity, flow, depth, rows):
    width, slots = flow.shape[1], GROUP * CAP
    start = base.astype(jnp.int32) - 1

    def hat(axis, length):
        cell = iota((length, slots), 0)
        low, share = start[axis : axis + 1], part[axis : axis + 1]
        return jnp.where(cell == low, 1.0 - share, 0.0) + jnp.where(cell == low + 1, share, 0.0)

    hat_x, hat_y, hat_z = hat(0, width), hat(1, rows), hat(2, depth)
    weight = (hat_z[:, None, :] * hat_y[None, :, :]).reshape(depth * rows, slots)
    across = dot_split(flow, hat_x, NN)
    cells = depth * rows
    sampled = [
        jnp.sum(across[d * cells : (d + 1) * cells] * weight, axis=0, keepdims=True)
        for d in range(3)
    ]
    drag = [DRAG_COEF * (sampled[d] - velocity[d : d + 1]) for d in range(3)]
    spread = jnp.concatenate([weight * (-drag[d]) for d in range(3)], axis=0)
    return drag, dot_split(spread, hat_x, NT)


def couple_kernel(shape, depth, rows, beads_ref, flow_ref, column_ref, force_ref, face_ref, *drag_refs):
    slabs, cols, _ = shape
    width = flow_ref.shape[2]
    flow = flow_ref[...].reshape(3 * depth * rows, width)
    hollow = jnp.zeros((5, GROUP * CAP), F32)

    if len(drag_refs) == 2:
        slab, col = lax.axis_index("slab"), lax.axis_index("col")
        got = []
        for r in range(GROUP):
            there = [a - b for a, b in zip((slab, col), divmod(r, cols))]
            there = [jnp.where(a < 0, a + n, a) for a, n in zip(there, (slabs, cols))]
            got.append(beads_ref[there[0] * cols + there[1]])
        drag, force = couple_group(*unpack(got), flow, depth, rows)
        force_ref[...] = force.reshape(3, depth, rows, width)
        stacked = jnp.concatenate(drag + [hollow], axis=0)
        lanes = cols * CAP
        blank = jnp.zeros((8, 128 - lanes), F32)
        for dz in range(slabs):
            tile = jnp.concatenate([stacked[:, dz * lanes : (dz + 1) * lanes], blank], axis=1)
            drag_refs[0][dz] = tile
            if dz == 2:
                drag_refs[1][...] = tile
    else:
        force_ref[...] = jnp.zeros_like(force_ref)
        blank = jnp.zeros((8, 128 - CAP), F32)

        def group(k, carry):
            got = [beads_ref[k * GROUP + r] for r in range(GROUP)]
            drag, force = couple_group(*unpack(got), flow, depth, rows)
            force_ref[...] += force.reshape(3, depth, rows, width)
            stacked = jnp.concatenate(drag + [hollow], axis=0)
            for r in range(GROUP):
                drag_refs[0][k * GROUP + r] = jnp.concatenate(
                    [stacked[:, r * CAP : (r + 1) * CAP], blank], axis=1
                )
            return carry

        lax.fori_loop(0, beads_ref.shape[0] // GROUP, group, 0)

    lane = iota((rows, 128), 1)
    force = []
    for d in range(3):
        tile = jnp.zeros((rows, 128), F32)
        for z in range(depth):
            plane = force_ref[d, z]
            tile = jnp.where(lane == z, spread_column(plane, 0), tile)
            tile = jnp.where(lane == depth + z, spread_column(plane, width - 1), tile)
        force.append(tile)
    out = collide([column_ref[i] for i in range(19)], column_ref[19] == 1.0, force)
    blank = jnp.zeros((rows, 128 - 5 * depth), F32)
    for group in range(2):
        side = slice(depth, 2 * depth) if group == 0 else slice(0, depth)
        face_ref[group] = jnp.concatenate(
            [out[i][:, side] for i in ENTER[0][group]] + [blank], axis=1
        )


def couple(shape, beads, flow, columns, depth, rows):
    width = flow.shape[2]
    single = beads.shape[0] == GROUP
    tile = jax.ShapeDtypeStruct((8, 128), F32)
    drags = [jax.ShapeDtypeStruct((shape[0], 8, 128), F32), tile] if single else [beads]
    return pl.pallas_call(
        functools.partial(couple_kernel, shape, depth, rows),
        out_shape=[
            jax.ShapeDtypeStruct((3, depth, rows, width), F32),
            jax.ShapeDtypeStruct((2, rows, 128), F32),
        ]
        + [jax.ShapeDtypeStruct(d.shape, F32) for d in drags],
        compiler_params=pltpu.CompilerParams(vmem_limit_bytes=24 << 20),
        name="couple",
    )(beads, flow, columns)


def faces_kernel(force_ref, edge_ref, edge_solid_ref, face_ref, drag_ref, up_ref, down_ref, draft_ref):
    depth, rows, width = force_ref.shape[1:]
    faces = [face_ref[0], face_ref[1]]
    turned = [f.T for f in faces]
    for side in range(4):
        pops = [edge_ref[i, side] for i in range(19)]
        first = side % 2 == 0
        if side < 2:
            force = [force_ref[d, 0 if first else depth - 1] for d in range(3)]
        else:
            force = [force_ref[d, :, 0 if first else rows - 1, :] for d in range(3)]
        out = collide(pops, edge_solid_ref[side] == 1, force)
        axis = 2 if side < 2 else 1
        group = 1 if first else 0
        for k, i in enumerate(ENTER[axis][group]):
            value = out[i]
            if STEP[i, 0] != 0:
                which, place = x_place(i)
                if axis == 2:
                    z = 0 if first else depth - 1
                    column = spread_column(faces[which], place * depth + z)
                else:
                    y = 0 if first else rows - 1
                    block = turned[which][place * depth : (place + 1) * depth]
                    column = jnp.broadcast_to(block[:, y : y + 1], (depth, width))
                value = enter_x(value, i, column)
            if axis == 2:
                (down_ref if first else up_ref)[k * rows : (k + 1) * rows] = value
            else:
                at = (group * 5 + k) * depth
                draft_ref[at : at + depth] = turn(value, STEP[i, 2], 0)
    if up_ref.shape[0] > 5 * rows:
        up_ref[5 * rows : 5 * rows + 8] = drag_ref[drag_ref.shape[0] - 1]
        down_ref[5 * rows : 5 * rows + 8] = drag_ref[1]


def faces(single, force, edge, edge_solid, face, drag):
    _, depth, rows, width = force.shape
    message = jax.ShapeDtypeStruct((5 * rows + (8 if single else 0), width), F32)
    return pl.pallas_call(
        faces_kernel,
        out_shape=[message, message, jax.ShapeDtypeStruct((10 * depth, width), F32)],
        compiler_params=pltpu.CompilerParams(vmem_limit_bytes=8 << 20),
        name="faces",
    )(force, edge, edge_solid, face, drag)


def rows_kernel(depth, rows, draft_ref, up_ref, down_ref, *refs):
    outs = refs[-1:] if len(refs) == 3 else refs
    for group in range(2):
        out_ref = outs[0] if len(outs) == 1 else outs[group]
        base = group * 5 * depth if len(outs) == 1 else 0
        y = rows - 1 if group == 0 else 0
        for k, i in enumerate(ENTER[1][group]):
            at = base + k * depth
            out_ref[at : at + depth] = draft_ref[(group * 5 + k) * depth : (group * 5 + k + 1) * depth]
            if STEP[i, 2] != 0:
                side = 0 if STEP[i, 2] == 1 else 1
                z = 0 if side == 0 else depth - 1
                row = ENTER[2][side].index(i) * rows + y
                out_ref[at + z : at + z + 1] = (up_ref, down_ref)[side][row : row + 1]
    if len(refs) == 3:
        own_ref, far_ref, out_ref = refs
        at, tail = 10 * depth, 5 * rows
        out_ref[at : at + 8] = own_ref[0]
        out_ref[at + 8 : at + 16] = down_ref[tail : tail + 8]
        out_ref[at + 16 : at + 24] = far_ref[...]
        out_ref[at + 24 : at + 32] = up_ref[tail : tail + 8]


def leaving_rows(shape, depth, rows, draft, up, down, drags):
    width = draft.shape[1]
    if drags:
        sizes = [10 * depth + 8 * shape[0]]
    else:
        sizes = [5 * depth] * 2
    return pl.pallas_call(
        functools.partial(rows_kernel, depth, rows),
        out_shape=[jax.ShapeDtypeStruct((n, width), F32) for n in sizes],
        compiler_params=pltpu.CompilerParams(vmem_limit_bytes=4 << 20),
        name="rows",
    )(draft, up, down, *drags)


def stream_kernel(pops_ref, solid_ref, force_ref, face_ref, out_ref, tile_ref, held, sem):
    depth, rows, width = pops_ref.shape[1:]
    chunks = 4
    span = depth // chunks

    def plane(z, faces):
        out = collide(
            [pops_ref[i, z] for i in range(19)],
            solid_ref[z] == 1,
            [force_ref[d, z] for d in range(3)],
        )
        for i in range(19):
            value = out[i]
            if STEP[i, 0] != 0:
                which, place = x_place(i)
                value = enter_x(value, i, spread_column(faces[which], place * depth))
            held[i, z + 1 + int(STEP[i, 2])] = turn(value, STEP[i, 1], 0)
        return tuple(pltpu.roll(f, 127, 1) for f in faces)

    runs = [(0, 5), (5, 6), (6, 7), (7, 11)] + [(i, i + 1) for i in range(11, 19)]
    copies = []
    carry = (face_ref[0], face_ref[1])
    for k in range(chunks):
        carry = lax.fori_loop(k * span, (k + 1) * span, plane, carry)
        for n, (a, b) in enumerate(runs):
            step = int(STEP[a, 2])
            low = max(k * span + step, 0)
            high = min((k + 1) * span + step, depth)
            copy = pltpu.make_async_copy(
                held.at[a:b, low + 1 : high + 1], out_ref.at[a:b, low:high], sem.at[k, n]
            )
            copy.start()
            copies.append(copy)
    for group in range(2):
        first = 0 if group == 0 else rows - 8
        for k, i in enumerate(ENTER[1][group]):
            tile_ref[group * 5 + k] = held[i, 1 : depth + 1, first : first + 8, :]
    for copy in copies:
        copy.wait()


def stream(pops, solid, force, face):
    _, depth, rows, width = pops.shape
    vmem = pl.BlockSpec(memory_space=pltpu.VMEM)
    return pl.pallas_call(
        stream_kernel,
        out_shape=[
            jax.ShapeDtypeStruct(pops.shape, F32),
            jax.ShapeDtypeStruct((10, depth, 8, width), F32),
        ],
        in_specs=[vmem] * 4,
        out_specs=[pl.BlockSpec(memory_space=pltpu.HBM), vmem],
        scratch_shapes=[
            pltpu.VMEM((19, depth + 2, rows, width), F32),
            pltpu.SemaphoreType.DMA((4, 12)),
        ],
        compiler_params=pltpu.CompilerParams(vmem_limit_bytes=16 << 20),
        cost_estimate=pl.CostEstimate(flops=10000000, bytes_accessed=6000000, transcendentals=0),
        name="stream",
    )(pops, solid, force, face)


def finish_kernel(shape, n_rows, whole_ref, target_ref, tile_ref, up_ref, down_ref, *refs):
    row_refs, refs = refs[:n_rows], refs[n_rows:]
    drag_refs, (out_ref, bead_ref, planes, tiles, sem) = refs[:-5], refs[-5:]
    depth, rows, width = whole_ref.shape[1:]

    def entering(group, k):
        if n_rows == 1:
            at = (group * 5 + k) * depth
            return row_refs[0][at : at + depth]
        return row_refs[group][k * depth : (k + 1) * depth]

    copies = []

    def leave(source, target):
        copy = pltpu.make_async_copy(source, target, sem.at[len(copies)])
        copy.start()
        copies.append(copy)

    for group in range(2):
        z = 0 if group == 0 else depth - 1
        for k, i in enumerate(ENTER[2][group]):
            value = (up_ref, down_ref)[group][k * rows : (k + 1) * rows]
            if STEP[i, 1] != 0:
                side = 0 if STEP[i, 1] == 1 else 1
                row = entering(side, ENTER[1][side].index(i))[z : z + 1]
                y = 0 if side == 0 else rows - 1
                value = jnp.where(
                    iota((rows, width), 0) == y,
                    jnp.broadcast_to(row, (rows, width)),
                    turn(value, STEP[i, 1], 0),
                )
            n = group * 5 + k
            planes[n] = value
            leave(planes.at[n], out_ref.at[i, z])
    for group in range(2):
        first = 0 if group == 0 else rows - 8
        for k, i in enumerate(ENTER[1][group]):
            n = group * 5 + k
            tiles[n] = tile_ref[n]
            tiles[n, :, 0 if group == 0 else 7, :] = entering(group, k)
            low, high = (1 if STEP[i, 2] == 1 else 0), (depth - 1 if STEP[i, 2] == -1 else depth)
            leave(tiles.at[n, low:high], out_ref.at[i, low:high, first : first + 8])

    count = target_ref.shape[1]
    target = target_ref[...]
    if n_rows == 1:
        own_ref, far_ref = drag_refs
        slabs, cols, _ = shape
        at, tail = 10 * depth, 5 * rows
        direct = jnp.concatenate(
            [own_ref[0], down_ref[tail : tail + 8], far_ref[...], up_ref[tail : tail + 8]], axis=0
        )
        passed = row_refs[0][at : at + 8 * slabs]
        table = jnp.where(iota(direct.shape, 1) < CAP, direct, passed)
        owner = lax.shift_right_logical(target, 5)
        slot = target - owner * CAP
        owner_slab = lax.shift_right_logical(owner, cols.bit_length() - 1)
        away_col = owner - owner_slab * cols - lax.axis_index("col")
        away_col = jnp.where(away_col < 0, away_col + cols, away_col)
        away_slab = owner_slab - lax.axis_index("slab")
        away_slab = jnp.where(away_slab < 0, away_slab + slabs, away_slab)
        choose = (iota((128, count), 0) == away_col * CAP + slot).astype(F32).astype(BF16)
        picked = dot_select(table, choose, NN)
        total = jnp.where(away_slab == 0, picked[0:8], 0.0)
        for dz in range(1, slabs):
            total = total + jnp.where(away_slab == dz, picked[8 * dz : 8 * dz + 8], 0.0)
        bead_ref[...] = total[0:3]
    else:
        back_ref = drag_refs[0]

        def group(k, total):
            got = [back_ref[k * GROUP + r] for r in range(GROUP)]
            slots = jnp.concatenate([t[:, 0:CAP] for t in got], axis=1)
            first = k * (GROUP * CAP)
            choose = (iota((GROUP * CAP, count), 0) + first == target).astype(F32)
            return total + dot_select(slots, choose.astype(BF16), NN)

        total = lax.fori_loop(
            0, back_ref.shape[0] // GROUP, group, jnp.zeros((8, count), F32)
        )
        bead_ref[...] = total[0:3]
    for copy in copies:
        copy.wait()


def finish(shape, whole, target, tiles, up, down, entered, drags):
    _, depth, rows, width = whole.shape
    vmem = pl.BlockSpec(memory_space=pltpu.VMEM)
    hbm = pl.BlockSpec(memory_space=pltpu.HBM)
    args = [whole, target, tiles, up, down, *entered, *drags]
    return pl.pallas_call(
        functools.partial(finish_kernel, shape, len(entered)),
        out_shape=[
            jax.ShapeDtypeStruct(whole.shape, F32),
            jax.ShapeDtypeStruct((3, target.shape[1]), F32),
        ],
        in_specs=[hbm] + [vmem] * (len(args) - 1),
        out_specs=[hbm, vmem],
        scratch_shapes=[
            pltpu.VMEM((10, rows, width), F32),
            pltpu.VMEM((10, depth, 8, width), F32),
            pltpu.SemaphoreType.DMA((20,)),
        ],
        input_output_aliases={0: 0},
        compiler_params=pltpu.CompilerParams(vmem_limit_bytes=24 << 20),
        name="finish",
    )(*args)


def shards(populations, solid_mask, bead_owner, bead_base, bead_offset, bead_velocity):
    slabs, cols, pairs = shape = tuple(lax.axis_size(a) for a in ("slab", "col", "pair"))
    owners = slabs * cols
    depth, rows = populations.shape[1:3]
    single = owners == GROUP and slabs == 4
    swap = functools.partial(
        lax.all_to_all, axis_name=("slab", "col"), split_axis=0, concat_axis=0, tiled=True
    )

    target, beads = pack(owners, bead_owner, bead_base, bead_offset, bead_velocity)
    beads = swap(beads)
    flow, edge, edge_solid, columns = moments(populations, solid_mask)
    force, face, drag, *far = couple(shape, beads, flow, columns, depth, rows)
    face = send(face, shape, (0, 0, 1))
    if single:
        far = send(far[0], shape, (2, 0, 0))
    else:
        drag = swap(drag)
    up, down, draft = faces(single, force, edge, edge_solid, face, drag)
    up = send(up, shape, (1, 0, 0))
    down = send(down, shape, (-1, 0, 0))
    whole, tiles = stream(populations, solid_mask, force, face)
    drags = [drag, far] if single else []
    leaving = leaving_rows(shape, depth, rows, draft, up, down, drags)
    entered = [send(value, shape, (0, sign, 0)) for value, sign in zip(leaving, (1, -1))]
    return tuple(finish(shape, whole, target, tiles, up, down, entered, drags or [drag]))


def solution(mesh):
    return jax.shard_map(
        shards,
        mesh=mesh,
        in_specs=(
            P(None, ("rep", "slab"), "col", "pair"),
            P(("rep", "slab"), "col", "pair"),
            P(("rep", "slab", "col", "pair")),
            P(None, ("rep", "slab", "col", "pair")),
            P(None, ("rep", "slab", "col", "pair")),
            P(None, ("rep", "slab", "col", "pair")),
        ),
        out_specs=(
            P(None, ("rep", "slab"), "col", "pair"),
            P(None, ("rep", "slab", "col", "pair")),
        ),
        check_vma=False,
    )
```

```python
import functools

import jax
import jax.numpy as jnp
import numpy as np
from jax import lax
from jax.experimental import pallas as pl
from jax.experimental.pallas import tpu as pltpu
from jax.sharding import PartitionSpec as P

CAP = 32
GROUP = 8

STEP = np.array(
    [
        [0, 0, 0],
        [1, 0, 0],
        [-1, 0, 0],
        [0, 1, 0],
        [0, -1, 0],
        [0, 0, 1],
        [0, 0, -1],
        [1, 1, 0],
        [-1, -1, 0],
        [1, -1, 0],
        [-1, 1, 0],
        [1, 0, 1],
        [-1, 0, -1],
        [1, 0, -1],
        [-1, 0, 1],
        [0, 1, 1],
        [0, -1, -1],
        [0, 1, -1],
        [0, -1, 1],
    ],
    np.int32,
)
TAU_PLUS = 0.8
TAU_MINUS = 0.5 + (3.0 / 16.0) / (TAU_PLUS - 0.5)
KEEP_EVEN = 1.0 - 1.0 / TAU_PLUS
KEEP_ODD = 1.0 - 1.0 / TAU_MINUS
FORCE_GAIN = 1.0 - 0.5 / TAU_PLUS
DRAG_COEF = 2.0
F32 = jnp.float32
BF16 = jnp.bfloat16

ENTER = [[[i for i in range(19) if STEP[i, a] == sign] for sign in (1, -1)] for a in range(3)]
NT = (((1,), (1,)), ((), ()))
NN = (((1,), (0,)), ((), ()))


def iota(shape, dim):
    return lax.broadcasted_iota(jnp.int32, shape, dim)


def high_low(value):
    high = value.astype(BF16)
    return high, (value - high.astype(F32)).astype(BF16)


def dot_split(left, right, dims):
    a, b = high_low(left)
    c, d = high_low(right)
    mul = functools.partial(lax.dot_general, dimension_numbers=dims, preferred_element_type=F32)
    return mul(a, c) + (mul(a, d) + mul(b, c))


def dot_select(value, choose, dims):
    first = value.astype(BF16).astype(F32)
    rest = value - first
    second = rest.astype(BF16).astype(F32)
    stacked = jnp.concatenate([first, second, rest - second], axis=0).astype(BF16)
    got = lax.dot_general(stacked, choose, dimension_numbers=dims, preferred_element_type=F32)
    rows = value.shape[0]
    return got[0:rows] + got[rows : 2 * rows] + got[2 * rows : 3 * rows]


def density_momentum(pops):
    momentum = []
    for axis in range(3):
        plus = [pops[i] for i in range(19) if STEP[i, axis] == 1]
        minus = [pops[i] for i in range(19) if STEP[i, axis] == -1]
        momentum.append(sum(plus[1:], plus[0]) - sum(minus[1:], minus[0]))
    return sum(pops[1:], pops[0]), momentum


def along(step, vector):
    terms = None
    for axis in range(3):
        if step[axis] == 0:
            continue
        if terms is None:
            terms = vector[axis] if step[axis] == 1 else -vector[axis]
        else:
            terms = terms + vector[axis] if step[axis] == 1 else terms - vector[axis]
    return terms


def collide(pops, wall, force):
    density, momentum = density_momentum(pops)
    inverse = 1.0 / density
    carried = [m + 0.5 * f for m, f in zip(momentum, force)]
    speed = [m * inverse for m in carried]
    w = 1.0 / 36.0
    bend = [(4.5 * w / TAU_PLUS) * m + (9.0 * w * FORCE_GAIN) * f for m, f in zip(carried, force)]
    push = [(3.0 * w / TAU_MINUS) * m + (3.0 * w * FORCE_GAIN) * f for m, f in zip(carried, force)]
    drop = [(1.5 * w / TAU_PLUS) * m + (3.0 * w * FORCE_GAIN) * f for m, f in zip(carried, force)]
    rest = (w / TAU_PLUS) * density - sum(
        [u * d for u, d in zip(speed[1:], drop[1:])], speed[0] * drop[0]
    )
    out = [None] * 19
    out[0] = jnp.where(wall, pops[0], KEEP_EVEN * pops[0] + 12.0 * rest)
    for i in range(1, 19, 2):
        a, b = pops[i], pops[i + 1]
        step = STEP[i]
        even = rest + along(step, speed) * along(step, bend)
        odd = along(step, push)
        if i < 7:
            even = even + even
            odd = odd + odd
        even = (0.5 * KEEP_EVEN) * (a + b) + even
        odd = (0.5 * KEEP_ODD) * (a - b) + odd
        out[i] = jnp.where(wall, b, even + odd)
        out[i + 1] = jnp.where(wall, a, even - odd)
    return out


def turn(value, amount, axis):
    if amount == 0:
        return value
    return pltpu.roll(value, int(amount) % value.shape[axis], axis)


def send(value, shape, offset):
    slabs, cols, pairs = shape
    perm = []
    for s in range(slabs):
        for c in range(cols):
            for p in range(pairs):
                there = (
                    ((s + offset[0]) % slabs) * cols + (c + offset[1]) % cols
                ) * pairs + (p + offset[2]) % pairs
                perm.append(((s * cols + c) * pairs + p, there))
    return lax.ppermute(value, ("slab", "col", "pair"), perm)


def rank_among(member):
    count = member.shape[1]
    earlier = (iota((count, count), 0) < iota((count, count), 1)).astype(F32).astype(BF16)
    return lax.dot_general(member.astype(BF16), earlier, NN, preferred_element_type=F32)


def spread_column(tile, lane):
    return jnp.broadcast_to(tile[:, lane : lane + 1], tile.shape)


def enter_x(value, i, column):
    step = STEP[i, 0]
    if step == 0:
        return value
    side = 0 if step == 1 else value.shape[1] - 1
    return jnp.where(iota(value.shape, 1) == side, column, turn(value, step, 1))


def x_place(i):
    group = 0 if STEP[i, 0] == 1 else 1
    place = ENTER[0][group].index(i)
    return place // 4, (place % 4) * 32 + group


def x_ends(planes):
    lane = lax.shift_right_logical(iota(planes[0].shape, 1), 1)
    tile = jnp.ones(planes[0].shape, F32)
    for z, value in enumerate(planes):
        tile = jnp.where(lane == z, pltpu.roll(value, 2 * z + 1, 1), tile)
    return tile


def pack_kernel(owner_ref, base_ref, offset_ref, velocity_ref, target_ref, out_ref, table):
    count = owner_ref.shape[1]
    local = owner_ref[...] - pl.program_id(0) * GROUP
    member = (iota((GROUP, count), 0) == local).astype(F32)
    rank = jnp.sum(member * rank_among(member), axis=0, keepdims=True).astype(jnp.int32)
    inside = (local >= 0) & (local < GROUP)
    target = jnp.where(inside, local * CAP + rank, -1)
    whole_target = jnp.where(inside, owner_ref[...] * CAP + rank, -1)

    @pl.when(pl.program_id(0) == 0)
    def _():
        target_ref[...] = whole_target

    @pl.when(pl.program_id(0) > 0)
    def _():
        target_ref[...] = jnp.maximum(target_ref[...], whole_target)

    choose = (iota((GROUP * CAP, count), 0) == target).astype(F32).astype(BF16)
    table[...] = jnp.zeros_like(table)
    table[0:3] = base_ref[...].astype(F32) + 1.0
    table[8:11] = offset_ref[...]
    table[16:19] = velocity_ref[...]
    packed = dot_select(table[...], choose, NT)
    blank = jnp.zeros((8, CAP), F32)
    for r in range(GROUP):
        lanes = slice(r * CAP, (r + 1) * CAP)
        out_ref[r] = jnp.concatenate(
            [packed[0:8, lanes], packed[8:16, lanes], packed[16:24, lanes], blank], axis=1
        )


def pack(owners, owner, base, offset, velocity):
    count = owner.shape[0]
    args = (owner.reshape(1, count), base, offset, velocity)
    return pl.pallas_call(
        pack_kernel,
        out_shape=[
            jax.ShapeDtypeStruct((1, count), jnp.int32),
            jax.ShapeDtypeStruct((owners, 8, 128), F32),
        ],
        grid=(owners // GROUP,),
        in_specs=[pl.BlockSpec(a.shape, lambda k: (0, 0)) for a in args],
        out_specs=[
            pl.BlockSpec((1, count), lambda k: (0, 0)),
            pl.BlockSpec((GROUP, 8, 128), lambda k: (k, 0, 0)),
        ],
        scratch_shapes=[pltpu.VMEM((24, count), F32)],
        compiler_params=pltpu.CompilerParams(
            vmem_limit_bytes=None if owners == GROUP else (48 << 20)
        ),
        name="pack",
    )(*args)


def moments_kernel(
    pops_ref, solid_ref, flow_ref, edge_ref, edge_solid_ref, column_ref, held, held_solid, sem
):
    depth, rows, width = pops_ref.shape[1:]
    chunks = 4
    span = depth // chunks
    copies = [pltpu.make_async_copy(solid_ref, held_solid, sem.at[chunks])]
    for k in range(chunks):
        part = pl.ds(k * span, span)
        copies.append(
            pltpu.make_async_copy(pops_ref.at[:, part], held.at[:, part], sem.at[k])
        )
    for copy in copies:
        copy.start()

    def plane(z, carry):
        pops = [held[i, z] for i in range(19)]
        density, momentum = density_momentum(pops)
        inverse = 1.0 / density
        for axis in range(3):
            flow_ref[axis, pl.ds(pl.multiple_of(z * rows, rows), rows)] = momentum[axis] * inverse
        return carry

    for k in range(chunks):
        copies[1 + k].wait()
        lax.fori_loop(k * span, (k + 1) * span, plane, 0)
    copies[0].wait()
    edge_solid_ref[0] = held_solid[0]
    edge_solid_ref[1] = held_solid[depth - 1]
    edge_solid_ref[2] = held_solid[:, 0, :]
    edge_solid_ref[3] = held_solid[:, rows - 1, :]

    def population(i, carry):
        edge_ref[i, 0] = held[i, 0]
        edge_ref[i, 1] = held[i, depth - 1]
        edge_ref[i, 2] = held[i, :, 0, :]
        edge_ref[i, 3] = held[i, :, rows - 1, :]
        column_ref[i] = x_ends([held[i, z] for z in range(depth)])
        return carry

    lax.fori_loop(0, 19, population, 0)
    column_ref[19] = x_ends([held_solid[z].astype(F32) for z in range(depth)])


def moments(pops, solid):
    _, depth, rows, width = pops.shape
    hbm = pl.BlockSpec(memory_space=pltpu.HBM)
    return pl.pallas_call(
        moments_kernel,
        out_shape=[
            jax.ShapeDtypeStruct((3, depth * rows, width), F32),
            jax.ShapeDtypeStruct((19, 4, rows, width), F32),
            jax.ShapeDtypeStruct((4, rows, width), jnp.int32),
            jax.ShapeDtypeStruct((20, rows, 128), F32),
        ],
        in_specs=[hbm, hbm],
        scratch_shapes=[
            pltpu.VMEM(pops.shape, F32),
            pltpu.VMEM(solid.shape, jnp.int32),
            pltpu.SemaphoreType.DMA((5,)),
        ],
        compiler_params=pltpu.CompilerParams(vmem_limit_bytes=64650000),
        cost_estimate=pl.CostEstimate(flops=3000000, bytes_accessed=4000000, transcendentals=0),
        name="moments",
    )(pops, solid)


def unpack(tiles):
    return [
        jnp.concatenate([t[:, g * CAP : (g + 1) * CAP] for t in tiles], axis=1) for g in range(3)
    ]


def couple_group(base, part, velocity, flow, depth, rows):
    width, slots = flow.shape[1], GROUP * CAP
    start = base.astype(jnp.int32) - 1

    def hat(axis, length):
        cell = iota((length, slots), 0)
        low, share = start[axis : axis + 1], part[axis : axis + 1]
        return jnp.where(cell == low, 1.0 - share, 0.0) + jnp.where(cell == low + 1, share, 0.0)

    hat_x, hat_y, hat_z = hat(0, width), hat(1, rows), hat(2, depth)
    weight = (hat_z[:, None, :] * hat_y[None, :, :]).reshape(depth * rows, slots)
    across = dot_split(flow, hat_x, NN)
    cells = depth * rows
    sampled = [
        jnp.sum(across[d * cells : (d + 1) * cells] * weight, axis=0, keepdims=True)
        for d in range(3)
    ]
    drag = [DRAG_COEF * (sampled[d] - velocity[d : d + 1]) for d in range(3)]
    spread = jnp.concatenate([weight * (-drag[d]) for d in range(3)], axis=0)
    return drag, dot_split(spread, hat_x, NT)


def couple_kernel(shape, depth, rows, beads_ref, flow_ref, column_ref, force_ref, face_ref, *drag_refs):
    slabs, cols, _ = shape
    width = flow_ref.shape[2]
    flow = flow_ref[...].reshape(3 * depth * rows, width)
    hollow = jnp.zeros((5, GROUP * CAP), F32)

    if len(drag_refs) == 2:
        slab, col = lax.axis_index("slab"), lax.axis_index("col")
        got = []
        for r in range(GROUP):
            there = [a - b for a, b in zip((slab, col), divmod(r, cols))]
            there = [jnp.where(a < 0, a + n, a) for a, n in zip(there, (slabs, cols))]
            got.append(beads_ref[there[0] * cols + there[1]])
        drag, force = couple_group(*unpack(got), flow, depth, rows)
        force_ref[...] = force.reshape(3, depth, rows, width)
        stacked = jnp.concatenate(drag + [hollow], axis=0)
        lanes = cols * CAP
        blank = jnp.zeros((8, 128 - lanes), F32)
        for dz in range(slabs):
            tile = jnp.concatenate([stacked[:, dz * lanes : (dz + 1) * lanes], blank], axis=1)
            drag_refs[0][dz] = tile
            if dz == 2:
                drag_refs[1][...] = tile
    else:
        force_ref[...] = jnp.zeros_like(force_ref)
        blank = jnp.zeros((8, 128 - CAP), F32)

        def group(k, carry):
            got = [beads_ref[k * GROUP + r] for r in range(GROUP)]
            drag, force = couple_group(*unpack(got), flow, depth, rows)
            force_ref[...] += force.reshape(3, depth, rows, width)
            stacked = jnp.concatenate(drag + [hollow], axis=0)
            for r in range(GROUP):
                drag_refs[0][k * GROUP + r] = jnp.concatenate(
                    [stacked[:, r * CAP : (r + 1) * CAP], blank], axis=1
                )
            return carry

        lax.fori_loop(0, beads_ref.shape[0] // GROUP, group, 0)

    force = [x_ends([force_ref[d, z] for z in range(depth)]) for d in range(3)]
    out = collide([column_ref[i] for i in range(19)], column_ref[19] == 1.0, force)
    high = lax.rem(iota((rows, 128), 1), 2) == 0
    ends = [jnp.where(high, out[i], out[j])[:, 0:32] for i, j in zip(*ENTER[0])]
    face_ref[0] = jnp.concatenate(ends[0:4], axis=1)
    face_ref[1] = jnp.concatenate([ends[4], jnp.zeros((rows, 96), F32)], axis=1)


def couple(shape, beads, flow, columns, depth, rows):
    width = flow.shape[2]
    single = beads.shape[0] == GROUP
    tile = jax.ShapeDtypeStruct((8, 128), F32)
    drags = [jax.ShapeDtypeStruct((shape[0], 8, 128), F32), tile] if single else [beads]
    return pl.pallas_call(
        functools.partial(couple_kernel, shape, depth, rows),
        out_shape=[
            jax.ShapeDtypeStruct((3, depth, rows, width), F32),
            jax.ShapeDtypeStruct((2, rows, 128), F32),
        ]
        + [jax.ShapeDtypeStruct(d.shape, F32) for d in drags],
        compiler_params=pltpu.CompilerParams(vmem_limit_bytes=ROOM),
        name="couple",
    )(beads, flow, columns)


def faces_kernel(
    force_ref, edge_ref, edge_solid_ref, face_ref, drag_ref, up_ref, down_ref, draft_ref, token_ref, turned
):
    depth, rows, width = force_ref.shape[1:]
    token_ref[...] = jnp.zeros_like(token_ref)
    tiles = [face_ref[0], face_ref[1]]
    for n in range(2):
        turned[n] = tiles[n].T
    for side in range(4):
        first = side % 2 == 0
        if side < 2:
            at = (0 if first else depth - 1, slice(None))
        else:
            at = (slice(None), 0 if first else rows - 1)
        pops = [edge_ref[i, side] for i in range(19)]
        force = [force_ref[(d,) + at] for d in range(3)]
        out = collide(pops, edge_solid_ref[side] == 1, force)
        axis = 2 if side < 2 else 1
        group = 1 if first else 0
        for k, i in enumerate(ENTER[axis][group]):
            value = out[i]
            if STEP[i, 0] != 0:
                tile, lane = x_place(i)
                if axis == 2:
                    column = spread_column(tiles[tile], lane + 2 * at[0])
                else:
                    block = turned[tile, pl.ds(lane, depth, stride=2), :]
                    column = jnp.broadcast_to(block[:, at[1] : at[1] + 1], (depth, width))
                value = enter_x(value, i, column)
            if axis == 2:
                (down_ref if first else up_ref)[k * rows : (k + 1) * rows] = value
            else:
                row = (group * 5 + k) * depth
                draft_ref[row : row + depth] = turn(value, STEP[i, 2], 0)
    if up_ref.shape[0] > 5 * rows:
        up_ref[5 * rows : 5 * rows + 8] = drag_ref[drag_ref.shape[0] - 1]
        down_ref[5 * rows : 5 * rows + 8] = drag_ref[1]


TOKEN = jax.ShapeDtypeStruct((8, 128), F32)
ROOM = 56 << 20


def faces(single, force, edge, edge_solid, face, drag):
    _, depth, rows, width = force.shape
    message = jax.ShapeDtypeStruct((5 * rows + (8 if single else 0), width), F32)
    return pl.pallas_call(
        faces_kernel,
        out_shape=[message, message, jax.ShapeDtypeStruct((10 * depth, width), F32), TOKEN],
        scratch_shapes=[pltpu.VMEM((2, 128, rows), F32)],
        compiler_params=pltpu.CompilerParams(vmem_limit_bytes=ROOM),
        name="faces",
    )(force, edge, edge_solid, face, drag)


def rows_kernel(depth, rows, before_ref, draft_ref, up_ref, down_ref, *refs):
    refs, token_ref = refs[:-1], refs[-1]
    token_ref[...] = jnp.zeros_like(token_ref)
    outs = refs[-1:] if len(refs) == 3 else refs
    for group in range(2):
        out_ref = outs[0] if len(outs) == 1 else outs[group]
        base = group * 5 * depth if len(outs) == 1 else 0
        y = rows - 1 if group == 0 else 0
        for k, i in enumerate(ENTER[1][group]):
            at = base + k * depth
            out_ref[at : at + depth] = draft_ref[(group * 5 + k) * depth : (group * 5 + k + 1) * depth]
            if STEP[i, 2] != 0:
                side = 0 if STEP[i, 2] == 1 else 1
                z = 0 if side == 0 else depth - 1
                row = ENTER[2][side].index(i) * rows + y
                out_ref[at + z : at + z + 1] = (up_ref, down_ref)[side][row : row + 1]
    if len(refs) == 3:
        own_ref, far_ref, out_ref = refs
        at, tail = 10 * depth, 5 * rows
        out_ref[at : at + 8] = own_ref[0]
        out_ref[at + 8 : at + 16] = down_ref[tail : tail + 8]
        out_ref[at + 16 : at + 24] = far_ref[...]
        out_ref[at + 24 : at + 32] = up_ref[tail : tail + 8]


def leaving_rows(shape, depth, rows, before, draft, up, down, drags):
    width = draft.shape[1]
    if drags:
        sizes = [10 * depth + 8 * shape[0]]
    else:
        sizes = [5 * depth] * 2
    args = (draft, up, down, *drags)
    return pl.pallas_call(
        functools.partial(rows_kernel, depth, rows),
        out_shape=[jax.ShapeDtypeStruct((n, width), F32) for n in sizes] + [TOKEN],
        in_specs=[pl.BlockSpec(memory_space=pl.ANY)]
        + [pl.BlockSpec(memory_space=pltpu.VMEM)] * len(args),
        compiler_params=pltpu.CompilerParams(vmem_limit_bytes=ROOM),
        name="rows",
    )(before, *args)


def stream_kernel(low, high, before_ref, *refs):
    if low > 0:
        refs = refs[1:]
    pops_ref, solid_ref, force_ref, face_ref, out_ref, tile_ref, token_ref, held, sem = refs
    depth, rows, width = pops_ref.shape[1:]
    token_ref[...] = jnp.zeros_like(token_ref)
    chunks = 2
    span = (high - low) // chunks

    def plane(z, faces):
        out = collide(
            [pops_ref[i, z] for i in range(19)],
            solid_ref[z] == 1,
            [force_ref[d, z] for d in range(3)],
        )
        for i in range(19):
            value = out[i]
            if STEP[i, 0] != 0:
                tile, lane = x_place(i)
                value = enter_x(value, i, spread_column(faces[tile], lane))
            held[i, z - low] = turn(value, STEP[i, 1], 0)
        return tuple(pltpu.roll(f, 126, 1) for f in faces)

    runs = [(0, 5), (5, 6), (6, 7), (7, 11)] + [(i, i + 1) for i in range(11, 19)]
    copies = []
    carry = (face_ref[0], face_ref[1])
    if low > 0:
        carry = tuple(pltpu.roll(f, 128 - 2 * low, 1) for f in carry)
    for k in range(chunks):
        first = low + k * span
        carry = lax.fori_loop(first, first + span, plane, carry)
        for n, (a, b) in enumerate(runs):
            step = int(STEP[a, 2])
            start, stop = max(first + step, 0), min(first + span + step, depth)
            copy = pltpu.make_async_copy(
                held.at[a:b, start - step - low : stop - step - low],
                out_ref.at[a:b, start:stop],
                sem.at[k, n],
            )
            copy.start()
            copies.append(copy)
    for group in range(2):
        first = 0 if group == 0 else rows - 8
        for k, i in enumerate(ENTER[1][group]):
            tile_ref[group * 5 + k] = held[i, :, first : first + 8, :]
    for copy in copies:
        copy.wait()


def stream(low, high, before, whole, pops, solid, force, face):
    _, depth, rows, width = pops.shape
    vmem = pl.BlockSpec(memory_space=pltpu.VMEM)
    hbm = pl.BlockSpec(memory_space=pltpu.HBM)
    whole = [] if whole is None else [whole]
    return pl.pallas_call(
        functools.partial(stream_kernel, low, high),
        out_shape=[
            jax.ShapeDtypeStruct(pops.shape, F32),
            jax.ShapeDtypeStruct((10, high - low, 8, width), F32),
            TOKEN,
        ],
        in_specs=[pl.BlockSpec(memory_space=pl.ANY)] + [hbm] * len(whole) + [vmem] * 4,
        out_specs=[hbm, vmem, vmem],
        scratch_shapes=[
            pltpu.VMEM((19, high - low, rows, width), F32),
            pltpu.SemaphoreType.DMA((2, 12)),
        ],
        input_output_aliases={1: 0} if whole else {},
        compiler_params=pltpu.CompilerParams(vmem_limit_bytes=ROOM),
        cost_estimate=pl.CostEstimate(flops=5000000, bytes_accessed=3000000, transcendentals=0),
        name="stream",
    )(before, *whole, pops, solid, force, face)


def finish_kernel(
    shape, n_rows, whole_ref, target_ref, lower_ref, upper_ref, up_ref, down_ref, *refs
):
    row_refs, refs = refs[:n_rows], refs[n_rows:]
    drag_refs, (out_ref, bead_ref, planes, tiles, sem) = refs[:-5], refs[-5:]
    depth, rows, width = whole_ref.shape[1:]

    def entering(group, k):
        if n_rows == 1:
            at = (group * 5 + k) * depth
            return row_refs[0][at : at + depth]
        return row_refs[group][k * depth : (k + 1) * depth]

    copies = []

    def leave(source, target):
        copy = pltpu.make_async_copy(source, target, sem.at[len(copies)])
        copy.start()
        copies.append(copy)

    for group in range(2):
        z = 0 if group == 0 else depth - 1
        for k, i in enumerate(ENTER[2][group]):
            value = (up_ref, down_ref)[group][k * rows : (k + 1) * rows]
            if STEP[i, 1] != 0:
                side = 0 if STEP[i, 1] == 1 else 1
                row = entering(side, ENTER[1][side].index(i))[z : z + 1]
                y = 0 if side == 0 else rows - 1
                value = jnp.where(
                    iota((rows, width), 0) == y,
                    jnp.broadcast_to(row, (rows, width)),
                    turn(value, STEP[i, 1], 0),
                )
            n = group * 5 + k
            planes[n] = value
            leave(planes.at[n], out_ref.at[i, z])
    for group in range(2):
        first = 0 if group == 0 else rows - 8
        for k, i in enumerate(ENTER[1][group]):
            n = group * 5 + k
            step = int(STEP[i, 2])
            half = lower_ref.shape[1]
            tiles[n, 1 + step : 1 + step + half] = lower_ref[n]
            tiles[n, 1 + step + half : 1 + step + depth] = upper_ref[n]
            tiles[n, 1 : 1 + depth, 0 if group == 0 else 7, :] = entering(group, k)
            low, high = max(step, 0), min(depth + step, depth)
            leave(tiles.at[n, 1 + low : 1 + high], out_ref.at[i, low:high, first : first + 8])

    count = target_ref.shape[1]
    target = target_ref[...]
    if n_rows == 1:
        own_ref, far_ref = drag_refs
        slabs, cols, _ = shape
        at, tail = 10 * depth, 5 * rows
        direct = jnp.concatenate(
            [own_ref[0], down_ref[tail : tail + 8], far_ref[...], up_ref[tail : tail + 8]], axis=0
        )
        passed = row_refs[0][at : at + 8 * slabs]
        table = jnp.where(iota(direct.shape, 1) < CAP, direct, passed)
        owner = lax.shift_right_logical(target, 5)
        slot = target - owner * CAP
        owner_slab = lax.shift_right_logical(owner, cols.bit_length() - 1)
        away_col = owner - owner_slab * cols - lax.axis_index("col")
        away_col = jnp.where(away_col < 0, away_col + cols, away_col)
        away_slab = owner_slab - lax.axis_index("slab")
        away_slab = jnp.where(away_slab < 0, away_slab + slabs, away_slab)
        choose = (iota((128, count), 0) == away_col * CAP + slot).astype(F32).astype(BF16)
        picked = dot_select(table, choose, NN)
        total = jnp.where(away_slab == 0, picked[0:8], 0.0)
        for dz in range(1, slabs):
            total = total + jnp.where(away_slab == dz, picked[8 * dz : 8 * dz + 8], 0.0)
        bead_ref[...] = total[0:3]
    else:
        back_ref = drag_refs[0]

        def group(k, total):
            got = [back_ref[k * GROUP + r] for r in range(GROUP)]
            slots = jnp.concatenate([t[:, 0:CAP] for t in got], axis=1)
            first = k * (GROUP * CAP)
            choose = (iota((GROUP * CAP, count), 0) + first == target).astype(F32)
            return total + dot_select(slots, choose.astype(BF16), NN)

        total = lax.fori_loop(
            0, back_ref.shape[0] // GROUP, group, jnp.zeros((8, count), F32)
        )
        bead_ref[...] = total[0:3]
    for copy in copies:
        copy.wait()


def finish(shape, whole, target, lower, upper, up, down, entered, drags):
    _, depth, rows, width = whole.shape
    vmem = pl.BlockSpec(memory_space=pltpu.VMEM)
    hbm = pl.BlockSpec(memory_space=pltpu.HBM)
    args = [whole, target, lower, upper, up, down, *entered, *drags]
    return pl.pallas_call(
        functools.partial(finish_kernel, shape, len(entered)),
        out_shape=[
            jax.ShapeDtypeStruct(whole.shape, F32),
            jax.ShapeDtypeStruct((3, target.shape[1]), F32),
        ],
        in_specs=[hbm] + [vmem] * (len(args) - 1),
        out_specs=[hbm, vmem],
        scratch_shapes=[
            pltpu.VMEM((10, rows, width), F32),
            pltpu.VMEM((10, depth + 2, 8, width), F32),
            pltpu.SemaphoreType.DMA((20,)),
        ],
        input_output_aliases={0: 0},
        compiler_params=pltpu.CompilerParams(vmem_limit_bytes=ROOM),
        name="finish",
    )(*args)


def shards(populations, solid_mask, bead_owner, bead_base, bead_offset, bead_velocity):
    slabs, cols, pairs = shape = tuple(lax.axis_size(a) for a in ("slab", "col", "pair"))
    owners = slabs * cols
    depth, rows = populations.shape[1:3]
    single = owners == GROUP and slabs == 4
    swap = functools.partial(
        lax.all_to_all, axis_name=("slab", "col"), split_axis=0, concat_axis=0, tiled=True
    )

    target, beads = pack(owners, bead_owner, bead_base, bead_offset, bead_velocity)
    beads = swap(beads)
    flow, edge, edge_solid, columns = moments(populations, solid_mask)
    force, face, drag, *far = couple(shape, beads, flow, columns, depth, rows)
    face = send(face, shape, (0, 0, 1))
    if single:
        far = send(far[0], shape, (2, 0, 0))
    else:
        drag = swap(drag)
    up, down, draft, token = faces(single, force, edge, edge_solid, face, drag)
    up = send(up, shape, (1, 0, 0))
    down = send(down, shape, (-1, 0, 0))
    fields = (populations, solid_mask, force, face)
    whole, lower, token = stream(0, depth // 2, token, None, *fields)
    drags = [drag, far] if single else []
    *leaving, token = leaving_rows(shape, depth, rows, token, draft, up, down, drags)
    entered = [send(value, shape, (0, sign, 0)) for value, sign in zip(leaving, (1, -1))]
    whole, upper, _ = stream(depth // 2, depth, token, whole, *fields)
    return tuple(finish(shape, whole, target, lower, upper, up, down, entered, drags or [drag]))


def solution(mesh):
    return jax.shard_map(
        shards,
        mesh=mesh,
        in_specs=(
            P(None, ("rep", "slab"), "col", "pair"),
            P(("rep", "slab"), "col", "pair"),
            P(("rep", "slab", "col", "pair")),
            P(None, ("rep", "slab", "col", "pair")),
            P(None, ("rep", "slab", "col", "pair")),
            P(None, ("rep", "slab", "col", "pair")),
        ),
        out_specs=(
            P(None, ("rep", "slab"), "col", "pair"),
            P(None, ("rep", "slab", "col", "pair")),
        ),
        check_vma=False,
    )
```

```python
import functools

import jax
import jax.numpy as jnp
import numpy as np
from jax import lax
from jax.experimental import pallas as pl
from jax.experimental.pallas import tpu as pltpu
from jax.sharding import PartitionSpec as P

CAP = 32
GROUP = 8

STEP = np.array(
    [
        [0, 0, 0],
        [1, 0, 0],
        [-1, 0, 0],
        [0, 1, 0],
        [0, -1, 0],
        [0, 0, 1],
        [0, 0, -1],
        [1, 1, 0],
        [-1, -1, 0],
        [1, -1, 0],
        [-1, 1, 0],
        [1, 0, 1],
        [-1, 0, -1],
        [1, 0, -1],
        [-1, 0, 1],
        [0, 1, 1],
        [0, -1, -1],
        [0, 1, -1],
        [0, -1, 1],
    ],
    np.int32,
)
TAU_PLUS = 0.8
TAU_MINUS = 0.5 + (3.0 / 16.0) / (TAU_PLUS - 0.5)
KEEP_EVEN = 1.0 - 1.0 / TAU_PLUS
KEEP_ODD = 1.0 - 1.0 / TAU_MINUS
FORCE_GAIN = 1.0 - 0.5 / TAU_PLUS
DRAG_COEF = 2.0
F32 = jnp.float32
BF16 = jnp.bfloat16

ENTER = [[[i for i in range(19) if STEP[i, a] == sign] for sign in (1, -1)] for a in range(3)]
NT = (((1,), (1,)), ((), ()))
NN = (((1,), (0,)), ((), ()))


def iota(shape, dim):
    return lax.broadcasted_iota(jnp.int32, shape, dim)


def high_low(value):
    high = value.astype(BF16)
    return high, (value - high.astype(F32)).astype(BF16)


def dot_split(left, right, dims):
    a, b = high_low(left)
    c, d = high_low(right)
    mul = functools.partial(lax.dot_general, dimension_numbers=dims, preferred_element_type=F32)
    return mul(a, c) + (mul(a, d) + mul(b, c))


def dot_select(value, choose, dims):
    first = value.astype(BF16).astype(F32)
    rest = value - first
    second = rest.astype(BF16).astype(F32)
    stacked = jnp.concatenate([first, second, rest - second], axis=0).astype(BF16)
    got = lax.dot_general(stacked, choose, dimension_numbers=dims, preferred_element_type=F32)
    rows = value.shape[0]
    return got[0:rows] + got[rows : 2 * rows] + got[2 * rows : 3 * rows]


def density_momentum(pops):
    momentum = []
    for axis in range(3):
        plus = [pops[i] for i in range(19) if STEP[i, axis] == 1]
        minus = [pops[i] for i in range(19) if STEP[i, axis] == -1]
        momentum.append(sum(plus[1:], plus[0]) - sum(minus[1:], minus[0]))
    return sum(pops[1:], pops[0]), momentum


def along(step, vector):
    terms = None
    for axis in range(3):
        if step[axis] == 0:
            continue
        if terms is None:
            terms = vector[axis] if step[axis] == 1 else -vector[axis]
        else:
            terms = terms + vector[axis] if step[axis] == 1 else terms - vector[axis]
    return terms


def collide(pops, wall, force):
    density, momentum = density_momentum(pops)
    inverse = 1.0 / density
    carried = [m + 0.5 * f for m, f in zip(momentum, force)]
    speed = [m * inverse for m in carried]
    w = 1.0 / 36.0
    bend = [(4.5 * w / TAU_PLUS) * m + (9.0 * w * FORCE_GAIN) * f for m, f in zip(carried, force)]
    push = [(3.0 * w / TAU_MINUS) * m + (3.0 * w * FORCE_GAIN) * f for m, f in zip(carried, force)]
    drop = [(1.5 * w / TAU_PLUS) * m + (3.0 * w * FORCE_GAIN) * f for m, f in zip(carried, force)]
    rest = (w / TAU_PLUS) * density - sum(
        [u * d for u, d in zip(speed[1:], drop[1:])], speed[0] * drop[0]
    )
    out = [None] * 19
    out[0] = jnp.where(wall, pops[0], KEEP_EVEN * pops[0] + 12.0 * rest)
    for i in range(1, 19, 2):
        a, b = pops[i], pops[i + 1]
        step = STEP[i]
        even = rest + along(step, speed) * along(step, bend)
        odd = along(step, push)
        if i < 7:
            even = even + even
            odd = odd + odd
        even = (0.5 * KEEP_EVEN) * (a + b) + even
        odd = (0.5 * KEEP_ODD) * (a - b) + odd
        out[i] = jnp.where(wall, b, even + odd)
        out[i + 1] = jnp.where(wall, a, even - odd)
    return out


def turn(value, amount, axis):
    if amount == 0:
        return value
    return pltpu.roll(value, int(amount) % value.shape[axis], axis)


def send(value, shape, offset):
    slabs, cols, pairs = shape
    perm = []
    for s in range(slabs):
        for c in range(cols):
            for p in range(pairs):
                there = (
                    ((s + offset[0]) % slabs) * cols + (c + offset[1]) % cols
                ) * pairs + (p + offset[2]) % pairs
                perm.append(((s * cols + c) * pairs + p, there))
    return lax.ppermute(value, ("slab", "col", "pair"), perm)


def rank_among(member):
    count = member.shape[1]
    earlier = (iota((count, count), 0) < iota((count, count), 1)).astype(F32).astype(BF16)
    return lax.dot_general(member.astype(BF16), earlier, NN, preferred_element_type=F32)


def spread_column(tile, lane):
    return jnp.broadcast_to(tile[:, lane : lane + 1], tile.shape)


def enter_x(value, i, column):
    step = STEP[i, 0]
    if step == 0:
        return value
    side = 0 if step == 1 else value.shape[1] - 1
    return jnp.where(iota(value.shape, 1) == side, column, turn(value, step, 1))


def x_place(i):
    group = 0 if STEP[i, 0] == 1 else 1
    place = ENTER[0][group].index(i)
    return place // 4, (place % 4) * 32 + group


def x_ends(planes):
    lane = lax.shift_right_logical(iota(planes[0].shape, 1), 1)
    tile = jnp.ones(planes[0].shape, F32)
    for z, value in enumerate(planes):
        tile = jnp.where(lane == z, pltpu.roll(value, 2 * z + 1, 1), tile)
    return tile


def pack_kernel(owner_ref, base_ref, offset_ref, velocity_ref, target_ref, out_ref, table):
    count = owner_ref.shape[1]
    local = owner_ref[...] - pl.program_id(0) * GROUP
    member = (iota((GROUP, count), 0) == local).astype(F32)
    rank = jnp.sum(member * rank_among(member), axis=0, keepdims=True).astype(jnp.int32)
    inside = (local >= 0) & (local < GROUP)
    target = jnp.where(inside, local * CAP + rank, -1)
    whole_target = jnp.where(inside, owner_ref[...] * CAP + rank, -1)

    @pl.when(pl.program_id(0) == 0)
    def _():
        target_ref[...] = whole_target

    @pl.when(pl.program_id(0) > 0)
    def _():
        target_ref[...] = jnp.maximum(target_ref[...], whole_target)

    choose = (iota((GROUP * CAP, count), 0) == target).astype(F32).astype(BF16)
    table[...] = jnp.zeros_like(table)
    table[0:3] = base_ref[...].astype(F32) + 1.0
    table[8:11] = offset_ref[...]
    table[16:19] = velocity_ref[...]
    packed = dot_select(table[...], choose, NT)
    blank = jnp.zeros((8, CAP), F32)
    for r in range(GROUP):
        lanes = slice(r * CAP, (r + 1) * CAP)
        out_ref[r] = jnp.concatenate(
            [packed[0:8, lanes], packed[8:16, lanes], packed[16:24, lanes], blank], axis=1
        )


def pack(owners, owner, base, offset, velocity):
    count = owner.shape[0]
    args = (owner.reshape(1, count), base, offset, velocity)
    return pl.pallas_call(
        pack_kernel,
        out_shape=[
            jax.ShapeDtypeStruct((1, count), jnp.int32),
            jax.ShapeDtypeStruct((owners, 8, 128), F32),
        ],
        grid=(owners // GROUP,),
        in_specs=[pl.BlockSpec(a.shape, lambda k: (0, 0)) for a in args],
        out_specs=[
            pl.BlockSpec((1, count), lambda k: (0, 0)),
            pl.BlockSpec((GROUP, 8, 128), lambda k: (k, 0, 0)),
        ],
        scratch_shapes=[pltpu.VMEM((24, count), F32)],
        compiler_params=pltpu.CompilerParams(
            vmem_limit_bytes=None if owners == GROUP else (48 << 20)
        ),
        name="pack",
    )(*args)


def moments_kernel(
    pops_ref, solid_ref, flow_ref, edge_ref, edge_solid_ref, column_ref, held, held_solid, sem
):
    depth, rows, width = pops_ref.shape[1:]
    chunks = 4
    span = depth // chunks
    copies = [pltpu.make_async_copy(solid_ref, held_solid, sem.at[chunks])]
    for k in range(chunks):
        part = pl.ds(k * span, span)
        copies.append(
            pltpu.make_async_copy(pops_ref.at[:, part], held.at[:, part], sem.at[k])
        )
    for copy in copies:
        copy.start()

    def plane(z, carry):
        pops = [held[i, z] for i in range(19)]
        density, momentum = density_momentum(pops)
        inverse = 1.0 / density
        for axis in range(3):
            flow_ref[axis, pl.ds(pl.multiple_of(z * rows, rows), rows)] = momentum[axis] * inverse
        return carry

    for k in range(chunks):
        copies[1 + k].wait()
        lax.fori_loop(k * span, (k + 1) * span, plane, 0)
    copies[0].wait()
    edge_solid_ref[0] = held_solid[0]
    edge_solid_ref[1] = held_solid[depth - 1]
    edge_solid_ref[2] = held_solid[:, 0, :]
    edge_solid_ref[3] = held_solid[:, rows - 1, :]

    def population(i, carry):
        edge_ref[i, 0] = held[i, 0]
        edge_ref[i, 1] = held[i, depth - 1]
        edge_ref[i, 2] = held[i, :, 0, :]
        edge_ref[i, 3] = held[i, :, rows - 1, :]
        column_ref[i] = x_ends([held[i, z] for z in range(depth)])
        return carry

    lax.fori_loop(0, 19, population, 0)
    column_ref[19] = x_ends([held_solid[z].astype(F32) for z in range(depth)])


def moments(pops, solid):
    _, depth, rows, width = pops.shape
    hbm = pl.BlockSpec(memory_space=pltpu.HBM)
    return pl.pallas_call(
        moments_kernel,
        out_shape=[
            jax.ShapeDtypeStruct((3, depth * rows, width), F32),
            jax.ShapeDtypeStruct((19, 4, rows, width), F32),
            jax.ShapeDtypeStruct((4, rows, width), jnp.int32),
            jax.ShapeDtypeStruct((20, rows, 128), F32),
        ],
        in_specs=[hbm, hbm],
        scratch_shapes=[
            pltpu.VMEM(pops.shape, F32),
            pltpu.VMEM(solid.shape, jnp.int32),
            pltpu.SemaphoreType.DMA((5,)),
        ],
        compiler_params=pltpu.CompilerParams(vmem_limit_bytes=54000000),
        cost_estimate=pl.CostEstimate(flops=3000000, bytes_accessed=4000000, transcendentals=0),
        name="moments",
    )(pops, solid)


def unpack(tiles):
    return [
        jnp.concatenate([t[:, g * CAP : (g + 1) * CAP] for t in tiles], axis=1) for g in range(3)
    ]


def couple_group(base, part, velocity, flow, depth, rows):
    width, slots = flow.shape[1], GROUP * CAP
    start = base.astype(jnp.int32) - 1

    def hat(axis, length):
        cell = iota((length, slots), 0)
        low, share = start[axis : axis + 1], part[axis : axis + 1]
        return jnp.where(cell == low, 1.0 - share, 0.0) + jnp.where(cell == low + 1, share, 0.0)

    hat_x, hat_y, hat_z = hat(0, width), hat(1, rows), hat(2, depth)
    weight = (hat_z[:, None, :] * hat_y[None, :, :]).reshape(depth * rows, slots)
    across = dot_split(flow, hat_x, NN)
    cells = depth * rows
    sampled = [
        jnp.sum(across[d * cells : (d + 1) * cells] * weight, axis=0, keepdims=True)
        for d in range(3)
    ]
    drag = [DRAG_COEF * (sampled[d] - velocity[d : d + 1]) for d in range(3)]
    spread = jnp.concatenate([weight * (-drag[d]) for d in range(3)], axis=0)
    return drag, dot_split(spread, hat_x, NT)


def couple_kernel(shape, depth, rows, beads_ref, flow_ref, column_ref, force_ref, face_ref, *drag_refs):
    slabs, cols, _ = shape
    width = flow_ref.shape[2]
    flow = flow_ref[...].reshape(3 * depth * rows, width)
    hollow = jnp.zeros((5, GROUP * CAP), F32)

    if len(drag_refs) == 2:
        slab, col = lax.axis_index("slab"), lax.axis_index("col")
        got = []
        for r in range(GROUP):
            there = [a - b for a, b in zip((slab, col), divmod(r, cols))]
            there = [jnp.where(a < 0, a + n, a) for a, n in zip(there, (slabs, cols))]
            got.append(beads_ref[there[0] * cols + there[1]])
        drag, force = couple_group(*unpack(got), flow, depth, rows)
        force_ref[...] = force.reshape(3, depth, rows, width)
        stacked = jnp.concatenate(drag + [hollow], axis=0)
        lanes = cols * CAP
        blank = jnp.zeros((8, 128 - lanes), F32)
        for dz in range(slabs):
            tile = jnp.concatenate([stacked[:, dz * lanes : (dz + 1) * lanes], blank], axis=1)
            drag_refs[0][dz] = tile
            if dz == 2:
                drag_refs[1][...] = tile
    else:
        force_ref[...] = jnp.zeros_like(force_ref)
        blank = jnp.zeros((8, 128 - CAP), F32)

        def group(k, carry):
            got = [beads_ref[k * GROUP + r] for r in range(GROUP)]
            drag, force = couple_group(*unpack(got), flow, depth, rows)
            force_ref[...] += force.reshape(3, depth, rows, width)
            stacked = jnp.concatenate(drag + [hollow], axis=0)
            for r in range(GROUP):
                drag_refs[0][k * GROUP + r] = jnp.concatenate(
                    [stacked[:, r * CAP : (r + 1) * CAP], blank], axis=1
                )
            return carry

        lax.fori_loop(0, beads_ref.shape[0] // GROUP, group, 0)

    force = [x_ends([force_ref[d, z] for z in range(depth)]) for d in range(3)]
    out = collide([column_ref[i] for i in range(19)], column_ref[19] == 1.0, force)
    high = lax.rem(iota((rows, 128), 1), 2) == 0
    ends = [jnp.where(high, out[i], out[j])[:, 0:32] for i, j in zip(*ENTER[0])]
    face_ref[0] = jnp.concatenate(ends[0:4], axis=1)
    face_ref[1] = jnp.concatenate([ends[4], jnp.zeros((rows, 96), F32)], axis=1)


def couple(shape, beads, flow, columns, depth, rows):
    width = flow.shape[2]
    single = beads.shape[0] == GROUP
    tile = jax.ShapeDtypeStruct((8, 128), F32)
    drags = [jax.ShapeDtypeStruct((shape[0], 8, 128), F32), tile] if single else [beads]
    return pl.pallas_call(
        functools.partial(couple_kernel, shape, depth, rows),
        out_shape=[
            jax.ShapeDtypeStruct((3, depth, rows, width), F32),
            jax.ShapeDtypeStruct((2, rows, 128), F32),
        ]
        + [jax.ShapeDtypeStruct(d.shape, F32) for d in drags],
        compiler_params=pltpu.CompilerParams(vmem_limit_bytes=ROOM),
        name="couple",
    )(beads, flow, columns)


def faces_kernel(
    force_ref, edge_ref, edge_solid_ref, face_ref, drag_ref, up_ref, down_ref, draft_ref, token_ref, turned
):
    depth, rows, width = force_ref.shape[1:]
    token_ref[...] = jnp.zeros_like(token_ref)
    tiles = [face_ref[0], face_ref[1]]
    for n in range(2):
        turned[n] = tiles[n].T
    for side in range(4):
        first = side % 2 == 0
        if side < 2:
            at = (0 if first else depth - 1, slice(None))
        else:
            at = (slice(None), 0 if first else rows - 1)
        pops = [edge_ref[i, side] for i in range(19)]
        force = [force_ref[(d,) + at] for d in range(3)]
        out = collide(pops, edge_solid_ref[side] == 1, force)
        axis = 2 if side < 2 else 1
        group = 1 if first else 0
        for k, i in enumerate(ENTER[axis][group]):
            value = out[i]
            if STEP[i, 0] != 0:
                tile, lane = x_place(i)
                if axis == 2:
                    column = spread_column(tiles[tile], lane + 2 * at[0])
                else:
                    block = turned[tile, pl.ds(lane, depth, stride=2), :]
                    column = jnp.broadcast_to(block[:, at[1] : at[1] + 1], (depth, width))
                value = enter_x(value, i, column)
            if axis == 2:
                (down_ref if first else up_ref)[k * rows : (k + 1) * rows] = value
            else:
                row = (group * 5 + k) * depth
                draft_ref[row : row + depth] = turn(value, STEP[i, 2], 0)
    if up_ref.shape[0] > 5 * rows:
        up_ref[5 * rows : 5 * rows + 8] = drag_ref[drag_ref.shape[0] - 1]
        down_ref[5 * rows : 5 * rows + 8] = drag_ref[1]


TOKEN = jax.ShapeDtypeStruct((8, 128), F32)
ROOM = 16 << 20


def faces(single, force, edge, edge_solid, face, drag):
    _, depth, rows, width = force.shape
    message = jax.ShapeDtypeStruct((5 * rows + (8 if single else 0), width), F32)
    return pl.pallas_call(
        faces_kernel,
        out_shape=[message, message, jax.ShapeDtypeStruct((10 * depth, width), F32), TOKEN],
        scratch_shapes=[pltpu.VMEM((2, 128, rows), F32)],
        compiler_params=pltpu.CompilerParams(vmem_limit_bytes=ROOM),
        name="faces",
    )(force, edge, edge_solid, face, drag)


def rows_kernel(depth, rows, before_ref, draft_ref, up_ref, down_ref, *refs):
    refs, token_ref = refs[:-1], refs[-1]
    token_ref[...] = jnp.zeros_like(token_ref)
    outs = refs[-1:] if len(refs) == 3 else refs
    for group in range(2):
        out_ref = outs[0] if len(outs) == 1 else outs[group]
        base = group * 5 * depth if len(outs) == 1 else 0
        y = rows - 1 if group == 0 else 0
        for k, i in enumerate(ENTER[1][group]):
            at = base + k * depth
            out_ref[at : at + depth] = draft_ref[(group * 5 + k) * depth : (group * 5 + k + 1) * depth]
            if STEP[i, 2] != 0:
                side = 0 if STEP[i, 2] == 1 else 1
                z = 0 if side == 0 else depth - 1
                row = ENTER[2][side].index(i) * rows + y
                out_ref[at + z : at + z + 1] = (up_ref, down_ref)[side][row : row + 1]
    if len(refs) == 3:
        own_ref, far_ref, out_ref = refs
        at, tail = 10 * depth, 5 * rows
        out_ref[at : at + 8] = own_ref[0]
        out_ref[at + 8 : at + 16] = down_ref[tail : tail + 8]
        out_ref[at + 16 : at + 24] = far_ref[...]
        out_ref[at + 24 : at + 32] = up_ref[tail : tail + 8]


def leaving_rows(shape, depth, rows, before, draft, up, down, drags):
    width = draft.shape[1]
    if drags:
        sizes = [10 * depth + 8 * shape[0]]
    else:
        sizes = [5 * depth] * 2
    args = (draft, up, down, *drags)
    return pl.pallas_call(
        functools.partial(rows_kernel, depth, rows),
        out_shape=[jax.ShapeDtypeStruct((n, width), F32) for n in sizes] + [TOKEN],
        in_specs=[pl.BlockSpec(memory_space=pl.ANY)]
        + [pl.BlockSpec(memory_space=pltpu.VMEM)] * len(args),
        compiler_params=pltpu.CompilerParams(vmem_limit_bytes=ROOM),
        name="rows",
    )(before, *args)


def stream_kernel(low, high, before_ref, *refs):
    if low > 0:
        refs = refs[1:]
    pops_ref, solid_ref, force_ref, face_ref, out_ref, tile_ref, token_ref, held, sem = refs
    depth, rows, width = pops_ref.shape[1:]
    token_ref[...] = jnp.zeros_like(token_ref)
    chunks = 2
    span = (high - low) // chunks

    def plane(z, faces):
        out = collide(
            [pops_ref[i, z] for i in range(19)],
            solid_ref[z] == 1,
            [force_ref[d, z] for d in range(3)],
        )
        for i in range(19):
            value = out[i]
            if STEP[i, 0] != 0:
                tile, lane = x_place(i)
                value = enter_x(value, i, spread_column(faces[tile], lane))
            held[i, z - low] = turn(value, STEP[i, 1], 0)
        return tuple(pltpu.roll(f, 126, 1) for f in faces)

    runs = [(0, 5), (5, 6), (6, 7), (7, 11)] + [(i, i + 1) for i in range(11, 19)]
    copies = []
    carry = (face_ref[0], face_ref[1])
    if low > 0:
        carry = tuple(pltpu.roll(f, 128 - 2 * low, 1) for f in carry)
    for k in range(chunks):
        first = low + k * span
        carry = lax.fori_loop(first, first + span, plane, carry)
        for n, (a, b) in enumerate(runs):
            step = int(STEP[a, 2])
            start, stop = max(first + step, 0), min(first + span + step, depth)
            copy = pltpu.make_async_copy(
                held.at[a:b, start - step - low : stop - step - low],
                out_ref.at[a:b, start:stop],
                sem.at[k, n],
            )
            copy.start()
            copies.append(copy)
    for group in range(2):
        first = 0 if group == 0 else rows - 8
        for k, i in enumerate(ENTER[1][group]):
            tile_ref[group * 5 + k] = held[i, :, first : first + 8, :]
    for copy in copies:
        copy.wait()


def stream(low, high, before, whole, pops, solid, force, face):
    _, depth, rows, width = pops.shape
    vmem = pl.BlockSpec(memory_space=pltpu.VMEM)
    hbm = pl.BlockSpec(memory_space=pltpu.HBM)
    whole = [] if whole is None else [whole]
    return pl.pallas_call(
        functools.partial(stream_kernel, low, high),
        out_shape=[
            jax.ShapeDtypeStruct(pops.shape, F32),
            jax.ShapeDtypeStruct((10, high - low, 8, width), F32),
            TOKEN,
        ],
        in_specs=[pl.BlockSpec(memory_space=pl.ANY)] + [hbm] * len(whole) + [vmem] * 4,
        out_specs=[hbm, vmem, vmem],
        scratch_shapes=[
            pltpu.VMEM((19, high - low, rows, width), F32),
            pltpu.SemaphoreType.DMA((2, 12)),
        ],
        input_output_aliases={1: 0} if whole else {},
        compiler_params=pltpu.CompilerParams(vmem_limit_bytes=ROOM),
        cost_estimate=pl.CostEstimate(flops=5000000, bytes_accessed=3000000, transcendentals=0),
        name="stream",
    )(before, *whole, pops, solid, force, face)


def finish_kernel(
    shape, n_rows, whole_ref, target_ref, lower_ref, upper_ref, up_ref, down_ref, *refs
):
    row_refs, refs = refs[:n_rows], refs[n_rows:]
    drag_refs, (out_ref, bead_ref, planes, tiles, sem) = refs[:-5], refs[-5:]
    depth, rows, width = whole_ref.shape[1:]

    def entering(group, k):
        if n_rows == 1:
            at = (group * 5 + k) * depth
            return row_refs[0][at : at + depth]
        return row_refs[group][k * depth : (k + 1) * depth]

    copies = []

    def leave(source, target):
        copy = pltpu.make_async_copy(source, target, sem.at[len(copies)])
        copy.start()
        copies.append(copy)

    for group in range(2):
        z = 0 if group == 0 else depth - 1
        for k, i in enumerate(ENTER[2][group]):
            value = (up_ref, down_ref)[group][k * rows : (k + 1) * rows]
            if STEP[i, 1] != 0:
                side = 0 if STEP[i, 1] == 1 else 1
                row = entering(side, ENTER[1][side].index(i))[z : z + 1]
                y = 0 if side == 0 else rows - 1
                value = jnp.where(
                    iota((rows, width), 0) == y,
                    jnp.broadcast_to(row, (rows, width)),
                    turn(value, STEP[i, 1], 0),
                )
            n = group * 5 + k
            planes[n] = value
            leave(planes.at[n], out_ref.at[i, z])
    for group in range(2):
        first = 0 if group == 0 else rows - 8
        for k, i in enumerate(ENTER[1][group]):
            n = group * 5 + k
            step = int(STEP[i, 2])
            half = lower_ref.shape[1]
            tiles[n, 1 + step : 1 + step + half] = lower_ref[n]
            tiles[n, 1 + step + half : 1 + step + depth] = upper_ref[n]
            tiles[n, 1 : 1 + depth, 0 if group == 0 else 7, :] = entering(group, k)
            low, high = max(step, 0), min(depth + step, depth)
            leave(tiles.at[n, 1 + low : 1 + high], out_ref.at[i, low:high, first : first + 8])

    count = target_ref.shape[1]
    target = target_ref[...]
    if n_rows == 1:
        own_ref, far_ref = drag_refs
        slabs, cols, _ = shape
        at, tail = 10 * depth, 5 * rows
        direct = jnp.concatenate(
            [own_ref[0], down_ref[tail : tail + 8], far_ref[...], up_ref[tail : tail + 8]], axis=0
        )
        passed = row_refs[0][at : at + 8 * slabs]
        table = jnp.where(iota(direct.shape, 1) < CAP, direct, passed)
        owner = lax.shift_right_logical(target, 5)
        slot = target - owner * CAP
        owner_slab = lax.shift_right_logical(owner, cols.bit_length() - 1)
        away_col = owner - owner_slab * cols - lax.axis_index("col")
        away_col = jnp.where(away_col < 0, away_col + cols, away_col)
        away_slab = owner_slab - lax.axis_index("slab")
        away_slab = jnp.where(away_slab < 0, away_slab + slabs, away_slab)
        choose = (iota((128, count), 0) == away_col * CAP + slot).astype(F32).astype(BF16)
        picked = dot_select(table, choose, NN)
        total = jnp.where(away_slab == 0, picked[0:8], 0.0)
        for dz in range(1, slabs):
            total = total + jnp.where(away_slab == dz, picked[8 * dz : 8 * dz + 8], 0.0)
        bead_ref[...] = total[0:3]
    else:
        back_ref = drag_refs[0]

        def group(k, total):
            got = [back_ref[k * GROUP + r] for r in range(GROUP)]
            slots = jnp.concatenate([t[:, 0:CAP] for t in got], axis=1)
            first = k * (GROUP * CAP)
            choose = (iota((GROUP * CAP, count), 0) + first == target).astype(F32)
            return total + dot_select(slots, choose.astype(BF16), NN)

        total = lax.fori_loop(
            0, back_ref.shape[0] // GROUP, group, jnp.zeros((8, count), F32)
        )
        bead_ref[...] = total[0:3]
    for copy in copies:
        copy.wait()


def finish(shape, whole, target, lower, upper, up, down, entered, drags):
    _, depth, rows, width = whole.shape
    vmem = pl.BlockSpec(memory_space=pltpu.VMEM)
    hbm = pl.BlockSpec(memory_space=pltpu.HBM)
    args = [whole, target, lower, upper, up, down, *entered, *drags]
    return pl.pallas_call(
        functools.partial(finish_kernel, shape, len(entered)),
        out_shape=[
            jax.ShapeDtypeStruct(whole.shape, F32),
            jax.ShapeDtypeStruct((3, target.shape[1]), F32),
        ],
        in_specs=[hbm] + [vmem] * (len(args) - 1),
        out_specs=[hbm, vmem],
        scratch_shapes=[
            pltpu.VMEM((10, rows, width), F32),
            pltpu.VMEM((10, depth + 2, 8, width), F32),
            pltpu.SemaphoreType.DMA((20,)),
        ],
        input_output_aliases={0: 0},
        compiler_params=pltpu.CompilerParams(vmem_limit_bytes=ROOM),
        name="finish",
    )(*args)


def shards(populations, solid_mask, bead_owner, bead_base, bead_offset, bead_velocity):
    slabs, cols, pairs = shape = tuple(lax.axis_size(a) for a in ("slab", "col", "pair"))
    owners = slabs * cols
    depth, rows = populations.shape[1:3]
    single = owners == GROUP and slabs == 4
    swap = functools.partial(
        lax.all_to_all, axis_name=("slab", "col"), split_axis=0, concat_axis=0, tiled=True
    )

    target, beads = pack(owners, bead_owner, bead_base, bead_offset, bead_velocity)
    beads = swap(beads)
    flow, edge, edge_solid, columns = moments(populations, solid_mask)
    force, face, drag, *far = couple(shape, beads, flow, columns, depth, rows)
    face = send(face, shape, (0, 0, 1))
    if single:
        far = send(far[0], shape, (2, 0, 0))
    else:
        drag = swap(drag)
    up, down, draft, token = faces(single, force, edge, edge_solid, face, drag)
    up = send(up, shape, (1, 0, 0))
    down = send(down, shape, (-1, 0, 0))
    fields = (populations, solid_mask, force, face)
    whole, lower, token = stream(0, depth // 2, token, None, *fields)
    drags = [drag, far] if single else []
    *leaving, token = leaving_rows(shape, depth, rows, token, draft, up, down, drags)
    entered = [send(value, shape, (0, sign, 0)) for value, sign in zip(leaving, (1, -1))]
    whole, upper, _ = stream(depth // 2, depth, token, whole, *fields)
    return tuple(finish(shape, whole, target, lower, upper, up, down, entered, drags or [drag]))


def solution(mesh):
    return jax.shard_map(
        shards,
        mesh=mesh,
        in_specs=(
            P(None, ("rep", "slab"), "col", "pair"),
            P(("rep", "slab"), "col", "pair"),
            P(("rep", "slab", "col", "pair")),
            P(None, ("rep", "slab", "col", "pair")),
            P(None, ("rep", "slab", "col", "pair")),
            P(None, ("rep", "slab", "col", "pair")),
        ),
        out_specs=(
            P(None, ("rep", "slab"), "col", "pair"),
            P(None, ("rep", "slab", "col", "pair")),
        ),
        check_vma=False,
    )
```

```python
import functools

import jax
import jax.numpy as jnp
import numpy as np
from jax import lax
from jax.experimental import pallas as pl
from jax.experimental.pallas import tpu as pltpu
from jax.sharding import PartitionSpec as P

CAP = 32
GROUP = 8

STEP = np.array(
    [
        [0, 0, 0],
        [1, 0, 0],
        [-1, 0, 0],
        [0, 1, 0],
        [0, -1, 0],
        [0, 0, 1],
        [0, 0, -1],
        [1, 1, 0],
        [-1, -1, 0],
        [1, -1, 0],
        [-1, 1, 0],
        [1, 0, 1],
        [-1, 0, -1],
        [1, 0, -1],
        [-1, 0, 1],
        [0, 1, 1],
        [0, -1, -1],
        [0, 1, -1],
        [0, -1, 1],
    ],
    np.int32,
)
TAU_PLUS = 0.8
TAU_MINUS = 0.5 + (3.0 / 16.0) / (TAU_PLUS - 0.5)
KEEP_EVEN = 1.0 - 1.0 / TAU_PLUS
KEEP_ODD = 1.0 - 1.0 / TAU_MINUS
FORCE_GAIN = 1.0 - 0.5 / TAU_PLUS
DRAG_COEF = 2.0
F32 = jnp.float32
BF16 = jnp.bfloat16

ENTER = [[[i for i in range(19) if STEP[i, a] == sign] for sign in (1, -1)] for a in range(3)]
NT = (((1,), (1,)), ((), ()))
NN = (((1,), (0,)), ((), ()))


def iota(shape, dim):
    return lax.broadcasted_iota(jnp.int32, shape, dim)


def high_low(value):
    high = value.astype(BF16)
    return high, (value - high.astype(F32)).astype(BF16)


def dot_split(left, right, dims):
    a, b = high_low(left)
    c, d = high_low(right)
    mul = functools.partial(lax.dot_general, dimension_numbers=dims, preferred_element_type=F32)
    return mul(a, c) + (mul(a, d) + mul(b, c))


def dot_select(value, choose, dims):
    first = value.astype(BF16).astype(F32)
    rest = value - first
    second = rest.astype(BF16).astype(F32)
    stacked = jnp.concatenate([first, second, rest - second], axis=0).astype(BF16)
    got = lax.dot_general(stacked, choose, dimension_numbers=dims, preferred_element_type=F32)
    rows = value.shape[0]
    return got[0:rows] + got[rows : 2 * rows] + got[2 * rows : 3 * rows]


def density_momentum(pops):
    momentum = []
    for axis in range(3):
        plus = [pops[i] for i in range(19) if STEP[i, axis] == 1]
        minus = [pops[i] for i in range(19) if STEP[i, axis] == -1]
        momentum.append(sum(plus[1:], plus[0]) - sum(minus[1:], minus[0]))
    return sum(pops[1:], pops[0]), momentum


def along(step, vector):
    terms = None
    for axis in range(3):
        if step[axis] == 0:
            continue
        if terms is None:
            terms = vector[axis] if step[axis] == 1 else -vector[axis]
        else:
            terms = terms + vector[axis] if step[axis] == 1 else terms - vector[axis]
    return terms


def collide(pops, wall, force):
    density, momentum = density_momentum(pops)
    inverse = 1.0 / density
    carried = [m + 0.5 * f for m, f in zip(momentum, force)]
    speed = [m * inverse for m in carried]
    w = 1.0 / 36.0
    bend = [(4.5 * w / TAU_PLUS) * m + (9.0 * w * FORCE_GAIN) * f for m, f in zip(carried, force)]
    push = [(3.0 * w / TAU_MINUS) * m + (3.0 * w * FORCE_GAIN) * f for m, f in zip(carried, force)]
    drop = [(1.5 * w / TAU_PLUS) * m + (3.0 * w * FORCE_GAIN) * f for m, f in zip(carried, force)]
    rest = (w / TAU_PLUS) * density - sum(
        [u * d for u, d in zip(speed[1:], drop[1:])], speed[0] * drop[0]
    )
    out = [None] * 19
    out[0] = jnp.where(wall, pops[0], KEEP_EVEN * pops[0] + 12.0 * rest)
    for i in range(1, 19, 2):
        a, b = pops[i], pops[i + 1]
        step = STEP[i]
        even = rest + along(step, speed) * along(step, bend)
        odd = along(step, push)
        if i < 7:
            even = even + even
            odd = odd + odd
        even = (0.5 * KEEP_EVEN) * (a + b) + even
        odd = (0.5 * KEEP_ODD) * (a - b) + odd
        out[i] = jnp.where(wall, b, even + odd)
        out[i + 1] = jnp.where(wall, a, even - odd)
    return out


def turn(value, amount, axis):
    if amount == 0:
        return value
    return pltpu.roll(value, int(amount) % value.shape[axis], axis)


def send(value, shape, offset):
    slabs, cols, pairs = shape
    perm = []
    for s in range(slabs):
        for c in range(cols):
            for p in range(pairs):
                there = (
                    ((s + offset[0]) % slabs) * cols + (c + offset[1]) % cols
                ) * pairs + (p + offset[2]) % pairs
                perm.append(((s * cols + c) * pairs + p, there))
    return lax.ppermute(value, ("slab", "col", "pair"), perm)


def rank_among(member):
    count = member.shape[1]
    earlier = (iota((count, count), 0) < iota((count, count), 1)).astype(F32).astype(BF16)
    return lax.dot_general(member.astype(BF16), earlier, NN, preferred_element_type=F32)


def spread_column(tile, lane):
    return jnp.broadcast_to(tile[:, lane : lane + 1], tile.shape)


def enter_x(value, i, column):
    step = STEP[i, 0]
    if step == 0:
        return value
    side = 0 if step == 1 else value.shape[1] - 1
    return jnp.where(iota(value.shape, 1) == side, column, turn(value, step, 1))


def x_place(i):
    group = 0 if STEP[i, 0] == 1 else 1
    place = ENTER[0][group].index(i)
    return place // 4, (place % 4) * 32 + group


def x_ends(planes):
    lane = lax.shift_right_logical(iota(planes[0].shape, 1), 1)
    tile = jnp.ones(planes[0].shape, F32)
    for z, value in enumerate(planes):
        tile = jnp.where(lane == z, pltpu.roll(value, 2 * z + 1, 1), tile)
    return tile


def pack_kernel(owner_ref, base_ref, offset_ref, velocity_ref, target_ref, out_ref, table):
    count = owner_ref.shape[1]
    local = owner_ref[...] - pl.program_id(0) * GROUP
    member = (iota((GROUP, count), 0) == local).astype(F32)
    rank = jnp.sum(member * rank_among(member), axis=0, keepdims=True).astype(jnp.int32)
    inside = (local >= 0) & (local < GROUP)
    target = jnp.where(inside, local * CAP + rank, -1)
    whole_target = jnp.where(inside, owner_ref[...] * CAP + rank, -1)

    @pl.when(pl.program_id(0) == 0)
    def _():
        target_ref[...] = whole_target

    @pl.when(pl.program_id(0) > 0)
    def _():
        target_ref[...] = jnp.maximum(target_ref[...], whole_target)

    choose = (iota((GROUP * CAP, count), 0) == target).astype(F32).astype(BF16)
    table[...] = jnp.zeros_like(table)
    table[0:3] = base_ref[...].astype(F32) + 1.0
    table[8:11] = offset_ref[...]
    table[16:19] = velocity_ref[...]
    packed = dot_select(table[...], choose, NT)
    blank = jnp.zeros((8, CAP), F32)
    for r in range(GROUP):
        lanes = slice(r * CAP, (r + 1) * CAP)
        out_ref[r] = jnp.concatenate(
            [packed[0:8, lanes], packed[8:16, lanes], packed[16:24, lanes], blank], axis=1
        )


def pack(owners, owner, base, offset, velocity):
    count = owner.shape[0]
    args = (owner.reshape(1, count), base, offset, velocity)
    return pl.pallas_call(
        pack_kernel,
        out_shape=[
            jax.ShapeDtypeStruct((1, count), jnp.int32),
            jax.ShapeDtypeStruct((owners, 8, 128), F32),
        ],
        grid=(owners // GROUP,),
        in_specs=[pl.BlockSpec(a.shape, lambda k: (0, 0)) for a in args],
        out_specs=[
            pl.BlockSpec((1, count), lambda k: (0, 0)),
            pl.BlockSpec((GROUP, 8, 128), lambda k: (k, 0, 0)),
        ],
        scratch_shapes=[pltpu.VMEM((24, count), F32)],
        compiler_params=pltpu.CompilerParams(
            vmem_limit_bytes=None if owners == GROUP else (48 << 20)
        ),
        name="pack",
    )(*args)


def moments_kernel(
    pops_ref, solid_ref, flow_ref, column_ref, held, held_solid, sem
):
    depth, rows, width = pops_ref.shape[1:]
    chunks = 4
    span = depth // chunks
    copies = [pltpu.make_async_copy(solid_ref, held_solid, sem.at[chunks])]
    for k in range(chunks):
        part = pl.ds(k * span, span)
        copies.append(
            pltpu.make_async_copy(pops_ref.at[:, part], held.at[:, part], sem.at[k])
        )
    for copy in copies:
        copy.start()

    def plane(z, carry):
        pops = [held[i, z] for i in range(19)]
        density, momentum = density_momentum(pops)
        inverse = 1.0 / density
        for axis in range(3):
            flow_ref[axis, pl.ds(pl.multiple_of(z * rows, rows), rows)] = momentum[axis] * inverse
        return carry

    for k in range(chunks):
        copies[1 + k].wait()
        lax.fori_loop(k * span, (k + 1) * span, plane, 0, unroll=2)
    copies[0].wait()
    for i in range(19):
        column_ref[i] = x_ends([held[i, z] for z in range(depth)])
    column_ref[19] = x_ends([held_solid[z].astype(F32) for z in range(depth)])


def moments(pops, solid):
    _, depth, rows, width = pops.shape
    hbm = pl.BlockSpec(memory_space=pltpu.HBM)
    return pl.pallas_call(
        moments_kernel,
        out_shape=[
            jax.ShapeDtypeStruct((3, depth * rows, width), F32),
            jax.ShapeDtypeStruct((20, rows, 128), F32),
        ],
        in_specs=[hbm, hbm],
        scratch_shapes=[
            pltpu.VMEM(pops.shape, F32),
            pltpu.VMEM(solid.shape, jnp.int32),
            pltpu.SemaphoreType.DMA((5,)),
        ],
        compiler_params=pltpu.CompilerParams(vmem_limit_bytes=54000000),
        cost_estimate=pl.CostEstimate(flops=3000000, bytes_accessed=4000000, transcendentals=0),
        name="moments",
    )(pops, solid)


def unpack(tiles):
    return [
        jnp.concatenate([t[:, g * CAP : (g + 1) * CAP] for t in tiles], axis=1) for g in range(3)
    ]


def couple_group(base, part, velocity, flow, depth, rows):
    width, slots = flow.shape[1], GROUP * CAP
    start = base.astype(jnp.int32) - 1

    def hat(axis, length):
        cell = iota((length, slots), 0)
        low, share = start[axis : axis + 1], part[axis : axis + 1]
        return jnp.where(cell == low, 1.0 - share, 0.0) + jnp.where(cell == low + 1, share, 0.0)

    hat_x, hat_y, hat_z = hat(0, width), hat(1, rows), hat(2, depth)
    weight = (hat_z[:, None, :] * hat_y[None, :, :]).reshape(depth * rows, slots)
    across = dot_split(flow, hat_x, NN)
    cells = depth * rows
    sampled = [
        jnp.sum(across[d * cells : (d + 1) * cells] * weight, axis=0, keepdims=True)
        for d in range(3)
    ]
    drag = [DRAG_COEF * (sampled[d] - velocity[d : d + 1]) for d in range(3)]
    spread = jnp.concatenate([weight * (-drag[d]) for d in range(3)], axis=0)
    return drag, dot_split(spread, hat_x, NT)


def couple_kernel(shape, depth, rows, beads_ref, flow_ref, column_ref, force_ref, face_ref, *drag_refs):
    slabs, cols, _ = shape
    width = flow_ref.shape[2]
    flow = flow_ref[...].reshape(3 * depth * rows, width)
    hollow = jnp.zeros((5, GROUP * CAP), F32)

    if len(drag_refs) == 2:
        slab, col = lax.axis_index("slab"), lax.axis_index("col")
        got = []
        for r in range(GROUP):
            there = [a - b for a, b in zip((slab, col), divmod(r, cols))]
            there = [jnp.where(a < 0, a + n, a) for a, n in zip(there, (slabs, cols))]
            got.append(beads_ref[there[0] * cols + there[1]])
        drag, force = couple_group(*unpack(got), flow, depth, rows)
        force_ref[...] = force.reshape(3, depth, rows, width)
        stacked = jnp.concatenate(drag + [hollow], axis=0)
        lanes = cols * CAP
        blank = jnp.zeros((8, 128 - lanes), F32)
        for dz in range(slabs):
            tile = jnp.concatenate([stacked[:, dz * lanes : (dz + 1) * lanes], blank], axis=1)
            drag_refs[0][dz] = tile
            if dz == 2:
                drag_refs[1][...] = tile
    else:
        force_ref[...] = jnp.zeros_like(force_ref)
        blank = jnp.zeros((8, 128 - CAP), F32)

        def group(k, carry):
            got = [beads_ref[k * GROUP + r] for r in range(GROUP)]
            drag, force = couple_group(*unpack(got), flow, depth, rows)
            force_ref[...] += force.reshape(3, depth, rows, width)
            stacked = jnp.concatenate(drag + [hollow], axis=0)
            for r in range(GROUP):
                drag_refs[0][k * GROUP + r] = jnp.concatenate(
                    [stacked[:, r * CAP : (r + 1) * CAP], blank], axis=1
                )
            return carry

        lax.fori_loop(0, beads_ref.shape[0] // GROUP, group, 0)

    force = [x_ends([force_ref[d, z] for z in range(depth)]) for d in range(3)]
    out = collide([column_ref[i] for i in range(19)], column_ref[19] == 1.0, force)
    high = lax.rem(iota((rows, 128), 1), 2) == 0
    ends = [jnp.where(high, out[i], out[j])[:, 0:32] for i, j in zip(*ENTER[0])]
    face_ref[0] = jnp.concatenate(ends[0:4], axis=1)
    face_ref[1] = jnp.concatenate([ends[4], jnp.zeros((rows, 96), F32)], axis=1)


def couple(shape, beads, flow, columns, depth, rows):
    width = flow.shape[2]
    single = beads.shape[0] == GROUP
    tile = jax.ShapeDtypeStruct((8, 128), F32)
    drags = [jax.ShapeDtypeStruct((shape[0], 8, 128), F32), tile] if single else [beads]
    return pl.pallas_call(
        functools.partial(couple_kernel, shape, depth, rows),
        out_shape=[
            jax.ShapeDtypeStruct((3, depth, rows, width), F32),
            jax.ShapeDtypeStruct((2, rows, 128), F32),
        ]
        + [jax.ShapeDtypeStruct(d.shape, F32) for d in drags],
        compiler_params=pltpu.CompilerParams(vmem_limit_bytes=ROOM),
        name="couple",
    )(beads, flow, columns)


def faces_kernel(
    force_ref, pops_ref, solid_ref, face_ref, drag_ref, up_ref, down_ref, draft_ref, token_ref, turned
):
    depth, rows, width = force_ref.shape[1:]
    token_ref[...] = jnp.zeros_like(token_ref)
    tiles = [face_ref[0], face_ref[1]]
    for n in range(2):
        turned[n] = tiles[n].T
    for side in range(4):
        first = side % 2 == 0
        if side < 2:
            at = (0 if first else depth - 1, slice(None))
        else:
            at = (slice(None), 0 if first else rows - 1)
        pops = [pops_ref[(i,) + at] for i in range(19)]
        force = [force_ref[(d,) + at] for d in range(3)]
        out = collide(pops, solid_ref[at] == 1, force)
        axis = 2 if side < 2 else 1
        group = 1 if first else 0
        for k, i in enumerate(ENTER[axis][group]):
            value = out[i]
            if STEP[i, 0] != 0:
                tile, lane = x_place(i)
                if axis == 2:
                    column = spread_column(tiles[tile], lane + 2 * at[0])
                else:
                    block = turned[tile, pl.ds(lane, depth, stride=2), :]
                    column = jnp.broadcast_to(block[:, at[1] : at[1] + 1], (depth, width))
                value = enter_x(value, i, column)
            if axis == 2:
                (down_ref if first else up_ref)[k * rows : (k + 1) * rows] = value
            else:
                row = (group * 5 + k) * depth
                draft_ref[row : row + depth] = turn(value, STEP[i, 2], 0)
    if up_ref.shape[0] > 5 * rows:
        up_ref[5 * rows : 5 * rows + 8] = drag_ref[drag_ref.shape[0] - 1]
        down_ref[5 * rows : 5 * rows + 8] = drag_ref[1]


TOKEN = jax.ShapeDtypeStruct((8, 128), F32)
ROOM = 16 << 20


def faces(single, force, pops, solid, face, drag):
    _, depth, rows, width = force.shape
    message = jax.ShapeDtypeStruct((5 * rows + (8 if single else 0), width), F32)
    return pl.pallas_call(
        faces_kernel,
        out_shape=[message, message, jax.ShapeDtypeStruct((10 * depth, width), F32), TOKEN],
        scratch_shapes=[pltpu.VMEM((2, 128, rows), F32)],
        compiler_params=pltpu.CompilerParams(vmem_limit_bytes=ROOM),
        name="faces",
    )(force, pops, solid, face, drag)


def rows_kernel(depth, rows, before_ref, draft_ref, up_ref, down_ref, *refs):
    refs, token_ref = refs[:-1], refs[-1]
    token_ref[...] = jnp.zeros_like(token_ref)
    outs = refs[-1:] if len(refs) == 3 else refs
    for group in range(2):
        out_ref = outs[0] if len(outs) == 1 else outs[group]
        base = group * 5 * depth if len(outs) == 1 else 0
        y = rows - 1 if group == 0 else 0
        for k, i in enumerate(ENTER[1][group]):
            at = base + k * depth
            out_ref[at : at + depth] = draft_ref[(group * 5 + k) * depth : (group * 5 + k + 1) * depth]
            if STEP[i, 2] != 0:
                side = 0 if STEP[i, 2] == 1 else 1
                z = 0 if side == 0 else depth - 1
                row = ENTER[2][side].index(i) * rows + y
                out_ref[at + z : at + z + 1] = (up_ref, down_ref)[side][row : row + 1]
    if len(refs) == 3:
        own_ref, far_ref, out_ref = refs
        at, tail = 10 * depth, 5 * rows
        out_ref[at : at + 8] = own_ref[0]
        out_ref[at + 8 : at + 16] = down_ref[tail : tail + 8]
        out_ref[at + 16 : at + 24] = far_ref[...]
        out_ref[at + 24 : at + 32] = up_ref[tail : tail + 8]


def leaving_rows(shape, depth, rows, before, draft, up, down, drags):
    width = draft.shape[1]
    if drags:
        sizes = [10 * depth + 8 * shape[0]]
    else:
        sizes = [5 * depth] * 2
    args = (draft, up, down, *drags)
    return pl.pallas_call(
        functools.partial(rows_kernel, depth, rows),
        out_shape=[jax.ShapeDtypeStruct((n, width), F32) for n in sizes] + [TOKEN],
        in_specs=[pl.BlockSpec(memory_space=pl.ANY)]
        + [pl.BlockSpec(memory_space=pltpu.VMEM)] * len(args),
        compiler_params=pltpu.CompilerParams(vmem_limit_bytes=ROOM),
        name="rows",
    )(before, *args)


def stream_kernel(low, high, before_ref, *refs):
    if low > 0:
        refs = refs[1:]
    pops_ref, solid_ref, force_ref, face_ref, out_ref, tile_ref, token_ref, held, sem = refs
    depth, rows, width = pops_ref.shape[1:]
    token_ref[...] = jnp.zeros_like(token_ref)
    chunks = 2
    span = (high - low) // chunks

    def plane(z, faces):
        out = collide(
            [pops_ref[i, z] for i in range(19)],
            solid_ref[z] == 1,
            [force_ref[d, z] for d in range(3)],
        )
        for i in range(19):
            value = out[i]
            if STEP[i, 0] != 0:
                tile, lane = x_place(i)
                value = enter_x(value, i, spread_column(faces[tile], lane))
            held[i, z - low] = turn(value, STEP[i, 1], 0)
        return tuple(pltpu.roll(f, 126, 1) for f in faces)

    runs = [(0, 5), (5, 6), (6, 7), (7, 11)] + [(i, i + 1) for i in range(11, 19)]
    copies = []
    carry = (face_ref[0], face_ref[1])
    if low > 0:
        carry = tuple(pltpu.roll(f, 128 - 2 * low, 1) for f in carry)
    for k in range(chunks):
        first = low + k * span
        carry = lax.fori_loop(first, first + span, plane, carry, unroll=2)
        for n, (a, b) in enumerate(runs):
            step = int(STEP[a, 2])
            start, stop = max(first + step, 0), min(first + span + step, depth)
            copy = pltpu.make_async_copy(
                held.at[a:b, start - step - low : stop - step - low],
                out_ref.at[a:b, start:stop],
                sem.at[k, n],
            )
            copy.start()
            copies.append(copy)
    for group in range(2):
        first = 0 if group == 0 else rows - 8
        for k, i in enumerate(ENTER[1][group]):
            tile_ref[group * 5 + k] = held[i, :, first : first + 8, :]
    for copy in copies:
        copy.wait()


def stream(low, high, before, whole, pops, solid, force, face):
    _, depth, rows, width = pops.shape
    vmem = pl.BlockSpec(memory_space=pltpu.VMEM)
    hbm = pl.BlockSpec(memory_space=pltpu.HBM)
    whole = [] if whole is None else [whole]
    return pl.pallas_call(
        functools.partial(stream_kernel, low, high),
        out_shape=[
            jax.ShapeDtypeStruct(pops.shape, F32),
            jax.ShapeDtypeStruct((10, high - low, 8, width), F32),
            TOKEN,
        ],
        in_specs=[pl.BlockSpec(memory_space=pl.ANY)] + [hbm] * len(whole) + [vmem] * 4,
        out_specs=[hbm, vmem, vmem],
        scratch_shapes=[
            pltpu.VMEM((19, high - low, rows, width), F32),
            pltpu.SemaphoreType.DMA((2, 12)),
        ],
        input_output_aliases={1: 0} if whole else {},
        compiler_params=pltpu.CompilerParams(vmem_limit_bytes=ROOM),
        cost_estimate=pl.CostEstimate(flops=5000000, bytes_accessed=3000000, transcendentals=0),
        name="stream",
    )(before, *whole, pops, solid, force, face)


def finish_kernel(
    shape, n_rows, whole_ref, target_ref, lower_ref, upper_ref, up_ref, down_ref, *refs
):
    row_refs, refs = refs[:n_rows], refs[n_rows:]
    drag_refs, (out_ref, bead_ref, planes, tiles, sem) = refs[:-5], refs[-5:]
    depth, rows, width = whole_ref.shape[1:]

    def entering(group, k):
        if n_rows == 1:
            at = (group * 5 + k) * depth
            return row_refs[0][at : at + depth]
        return row_refs[group][k * depth : (k + 1) * depth]

    copies = []

    def leave(source, target):
        copy = pltpu.make_async_copy(source, target, sem.at[len(copies)])
        copy.start()
        copies.append(copy)

    for group in range(2):
        z = 0 if group == 0 else depth - 1
        for k, i in enumerate(ENTER[2][group]):
            value = (up_ref, down_ref)[group][k * rows : (k + 1) * rows]
            if STEP[i, 1] != 0:
                side = 0 if STEP[i, 1] == 1 else 1
                row = entering(side, ENTER[1][side].index(i))[z : z + 1]
                y = 0 if side == 0 else rows - 1
                value = jnp.where(
                    iota((rows, width), 0) == y,
                    jnp.broadcast_to(row, (rows, width)),
                    turn(value, STEP[i, 1], 0),
                )
            n = group * 5 + k
            planes[n] = value
            leave(planes.at[n], out_ref.at[i, z])
    for group in range(2):
        first = 0 if group == 0 else rows - 8
        for k, i in enumerate(ENTER[1][group]):
            n = group * 5 + k
            step = int(STEP[i, 2])
            half = lower_ref.shape[1]
            tiles[n, 1 + step : 1 + step + half] = lower_ref[n]
            tiles[n, 1 + step + half : 1 + step + depth] = upper_ref[n]
            tiles[n, 1 : 1 + depth, 0 if group == 0 else 7, :] = entering(group, k)
            low, high = max(step, 0), min(depth + step, depth)
            leave(tiles.at[n, 1 + low : 1 + high], out_ref.at[i, low:high, first : first + 8])

    count = target_ref.shape[1]
    target = target_ref[...]
    if n_rows == 1:
        own_ref, far_ref = drag_refs
        slabs, cols, _ = shape
        at, tail = 10 * depth, 5 * rows
        direct = jnp.concatenate(
            [own_ref[0], down_ref[tail : tail + 8], far_ref[...], up_ref[tail : tail + 8]], axis=0
        )
        passed = row_refs[0][at : at + 8 * slabs]
        table = jnp.where(iota(direct.shape, 1) < CAP, direct, passed)
        owner = lax.shift_right_logical(target, 5)
        slot = target - owner * CAP
        owner_slab = lax.shift_right_logical(owner, cols.bit_length() - 1)
        away_col = owner - owner_slab * cols - lax.axis_index("col")
        away_col = jnp.where(away_col < 0, away_col + cols, away_col)
        away_slab = owner_slab - lax.axis_index("slab")
        away_slab = jnp.where(away_slab < 0, away_slab + slabs, away_slab)
        choose = (iota((128, count), 0) == away_col * CAP + slot).astype(F32).astype(BF16)
        picked = dot_select(table, choose, NN)
        total = jnp.where(away_slab == 0, picked[0:8], 0.0)
        for dz in range(1, slabs):
            total = total + jnp.where(away_slab == dz, picked[8 * dz : 8 * dz + 8], 0.0)
        bead_ref[...] = total[0:3]
    else:
        back_ref = drag_refs[0]

        def group(k, total):
            got = [back_ref[k * GROUP + r] for r in range(GROUP)]
            slots = jnp.concatenate([t[:, 0:CAP] for t in got], axis=1)
            first = k * (GROUP * CAP)
            choose = (iota((GROUP * CAP, count), 0) + first == target).astype(F32)
            return total + dot_select(slots, choose.astype(BF16), NN)

        total = lax.fori_loop(
            0, back_ref.shape[0] // GROUP, group, jnp.zeros((8, count), F32)
        )
        bead_ref[...] = total[0:3]
    for copy in copies:
        copy.wait()


def finish(shape, whole, target, lower, upper, up, down, entered, drags):
    _, depth, rows, width = whole.shape
    vmem = pl.BlockSpec(memory_space=pltpu.VMEM)
    hbm = pl.BlockSpec(memory_space=pltpu.HBM)
    args = [whole, target, lower, upper, up, down, *entered, *drags]
    return pl.pallas_call(
        functools.partial(finish_kernel, shape, len(entered)),
        out_shape=[
            jax.ShapeDtypeStruct(whole.shape, F32),
            jax.ShapeDtypeStruct((3, target.shape[1]), F32),
        ],
        in_specs=[hbm] + [vmem] * (len(args) - 1),
        out_specs=[hbm, vmem],
        scratch_shapes=[
            pltpu.VMEM((10, rows, width), F32),
            pltpu.VMEM((10, depth + 2, 8, width), F32),
            pltpu.SemaphoreType.DMA((20,)),
        ],
        input_output_aliases={0: 0},
        compiler_params=pltpu.CompilerParams(vmem_limit_bytes=ROOM),
        name="finish",
    )(*args)


def shards(populations, solid_mask, bead_owner, bead_base, bead_offset, bead_velocity):
    slabs, cols, pairs = shape = tuple(lax.axis_size(a) for a in ("slab", "col", "pair"))
    owners = slabs * cols
    depth, rows = populations.shape[1:3]
    single = owners == GROUP and slabs == 4
    swap = functools.partial(
        lax.all_to_all, axis_name=("slab", "col"), split_axis=0, concat_axis=0, tiled=True
    )

    target, beads = pack(owners, bead_owner, bead_base, bead_offset, bead_velocity)
    beads = swap(beads)
    flow, columns = moments(populations, solid_mask)
    force, face, drag, *far = couple(shape, beads, flow, columns, depth, rows)
    face = send(face, shape, (0, 0, 1))
    if single:
        far = send(far[0], shape, (2, 0, 0))
    else:
        drag = swap(drag)
    up, down, draft, token = faces(single, force, populations, solid_mask, face, drag)
    up = send(up, shape, (1, 0, 0))
    down = send(down, shape, (-1, 0, 0))
    fields = (populations, solid_mask, force, face)
    whole, lower, token = stream(0, depth // 2, token, None, *fields)
    drags = [drag, far] if single else []
    *leaving, token = leaving_rows(shape, depth, rows, token, draft, up, down, drags)
    entered = [send(value, shape, (0, sign, 0)) for value, sign in zip(leaving, (1, -1))]
    whole, upper, _ = stream(depth // 2, depth, token, whole, *fields)
    return tuple(finish(shape, whole, target, lower, upper, up, down, entered, drags or [drag]))


def solution(mesh):
    return jax.shard_map(
        shards,
        mesh=mesh,
        in_specs=(
            P(None, ("rep", "slab"), "col", "pair"),
            P(("rep", "slab"), "col", "pair"),
            P(("rep", "slab", "col", "pair")),
            P(None, ("rep", "slab", "col", "pair")),
            P(None, ("rep", "slab", "col", "pair")),
            P(None, ("rep", "slab", "col", "pair")),
        ),
        out_specs=(
            P(None, ("rep", "slab"), "col", "pair"),
            P(None, ("rep", "slab", "col", "pair")),
        ),
        check_vma=False,
    )
```

```python
import functools

import jax
import jax.numpy as jnp
import numpy as np
from jax import lax
from jax.experimental import pallas as pl
from jax.experimental.pallas import tpu as pltpu
from jax.sharding import PartitionSpec as P

CAP = 32
GROUP = 8

STEP = np.array(
    [
        [0, 0, 0],
        [1, 0, 0],
        [-1, 0, 0],
        [0, 1, 0],
        [0, -1, 0],
        [0, 0, 1],
        [0, 0, -1],
        [1, 1, 0],
        [-1, -1, 0],
        [1, -1, 0],
        [-1, 1, 0],
        [1, 0, 1],
        [-1, 0, -1],
        [1, 0, -1],
        [-1, 0, 1],
        [0, 1, 1],
        [0, -1, -1],
        [0, 1, -1],
        [0, -1, 1],
    ],
    np.int32,
)
TAU_PLUS = 0.8
TAU_MINUS = 0.5 + (3.0 / 16.0) / (TAU_PLUS - 0.5)
KEEP_EVEN = 1.0 - 1.0 / TAU_PLUS
KEEP_ODD = 1.0 - 1.0 / TAU_MINUS
FORCE_GAIN = 1.0 - 0.5 / TAU_PLUS
DRAG_COEF = 2.0
F32 = jnp.float32
BF16 = jnp.bfloat16

ENTER = [[[i for i in range(19) if STEP[i, a] == sign] for sign in (1, -1)] for a in range(3)]
TOKEN = jax.ShapeDtypeStruct((8, 128), F32)
ROOM = 16 << 20
NT = (((1,), (1,)), ((), ()))
NN = (((1,), (0,)), ((), ()))


def iota(shape, dim):
    return lax.broadcasted_iota(jnp.int32, shape, dim)


def high_low(value):
    high = value.astype(BF16)
    return high, (value - high.astype(F32)).astype(BF16)


def dot_split(left, right, dims):
    a, b = high_low(left)
    c, d = high_low(right)
    mul = functools.partial(lax.dot_general, dimension_numbers=dims, preferred_element_type=F32)
    return mul(a, c) + (mul(a, d) + mul(b, c))


def dot_select(value, choose, dims):
    first = value.astype(BF16).astype(F32)
    rest = value - first
    second = rest.astype(BF16).astype(F32)
    stacked = jnp.concatenate([first, second, rest - second], axis=0).astype(BF16)
    got = lax.dot_general(stacked, choose, dimension_numbers=dims, preferred_element_type=F32)
    rows = value.shape[0]
    return got[0:rows] + got[rows : 2 * rows] + got[2 * rows : 3 * rows]


def density_momentum(pops):
    momentum = []
    for axis in range(3):
        plus = [pops[i] for i in range(19) if STEP[i, axis] == 1]
        minus = [pops[i] for i in range(19) if STEP[i, axis] == -1]
        momentum.append(sum(plus[1:], plus[0]) - sum(minus[1:], minus[0]))
    return sum(pops[1:], pops[0]), momentum


def along(step, vector):
    terms = None
    for axis in range(3):
        if step[axis] == 0:
            continue
        if terms is None:
            terms = vector[axis] if step[axis] == 1 else -vector[axis]
        else:
            terms = terms + vector[axis] if step[axis] == 1 else terms - vector[axis]
    return terms


def collide(pops, wall, force):
    density, momentum = density_momentum(pops)
    inverse = 1.0 / density
    carried = [m + 0.5 * f for m, f in zip(momentum, force)]
    speed = [m * inverse for m in carried]
    w = 1.0 / 36.0
    bend = [(4.5 * w / TAU_PLUS) * m + (9.0 * w * FORCE_GAIN) * f for m, f in zip(carried, force)]
    push = [(3.0 * w / TAU_MINUS) * m + (3.0 * w * FORCE_GAIN) * f for m, f in zip(carried, force)]
    drop = [(1.5 * w / TAU_PLUS) * m + (3.0 * w * FORCE_GAIN) * f for m, f in zip(carried, force)]
    rest = (w / TAU_PLUS) * density - sum(
        [u * d for u, d in zip(speed[1:], drop[1:])], speed[0] * drop[0]
    )
    out = [None] * 19
    out[0] = jnp.where(wall, pops[0], KEEP_EVEN * pops[0] + 12.0 * rest)
    for i in range(1, 19, 2):
        a, b = pops[i], pops[i + 1]
        step = STEP[i]
        even = rest + along(step, speed) * along(step, bend)
        odd = along(step, push)
        if i < 7:
            even = even + even
            odd = odd + odd
        even = (0.5 * KEEP_EVEN) * (a + b) + even
        odd = (0.5 * KEEP_ODD) * (a - b) + odd
        out[i] = jnp.where(wall, b, even + odd)
        out[i + 1] = jnp.where(wall, a, even - odd)
    return out


def turn(value, amount, axis):
    if amount == 0:
        return value
    return pltpu.roll(value, int(amount) % value.shape[axis], axis)


def send(value, shape, offset):
    return permute(value, shape, lambda at: [(a + b) % n for a, b, n in zip(at, offset, shape)])


def exchange(value, shape, bits):
    return permute(value, shape, lambda at: [a ^ b for a, b in zip(at, bits)])


def permute(value, shape, target):
    def flat(at):
        return (at[0] * shape[1] + at[1]) * shape[2] + at[2]

    perm = [(flat(at), flat(target(at))) for at in np.ndindex(*shape)]
    return lax.ppermute(value, ("slab", "col", "pair"), perm)


def rank_among(member):
    count = member.shape[1]
    earlier = (iota((count, count), 0) < iota((count, count), 1)).astype(F32).astype(BF16)
    return lax.dot_general(member.astype(BF16), earlier, NN, preferred_element_type=F32)


def spread_column(tile, lane):
    return jnp.broadcast_to(tile[:, lane : lane + 1], tile.shape)


def enter_x(value, i, column):
    step = STEP[i, 0]
    if step == 0:
        return value
    side = 0 if step == 1 else value.shape[1] - 1
    return jnp.where(iota(value.shape, 1) == side, column, turn(value, step, 1))


def x_place(i):
    group = 0 if STEP[i, 0] == 1 else 1
    place = ENTER[0][group].index(i)
    return place // 4, (place % 4) * 32 + group


def x_ends(planes):
    lane = lax.shift_right_logical(iota(planes[0].shape, 1), 1)
    tile = jnp.ones(planes[0].shape, F32)
    for z, value in enumerate(planes):
        tile = jnp.where(lane == z, pltpu.roll(value, 2 * z + 1, 1), tile)
    return tile


def pack_kernel(owner_ref, base_ref, offset_ref, velocity_ref, target_ref, out_ref, table):
    count = owner_ref.shape[1]
    local = owner_ref[...] - pl.program_id(0) * GROUP
    member = (iota((GROUP, count), 0) == local).astype(F32)
    rank = jnp.sum(member * rank_among(member), axis=0, keepdims=True).astype(jnp.int32)
    inside = (local >= 0) & (local < GROUP)
    target = jnp.where(inside, local * CAP + rank, -1)
    whole_target = jnp.where(inside, owner_ref[...] * CAP + rank, -1)

    @pl.when(pl.program_id(0) == 0)
    def _():
        target_ref[...] = whole_target

    @pl.when(pl.program_id(0) > 0)
    def _():
        target_ref[...] = jnp.maximum(target_ref[...], whole_target)

    choose = (iota((GROUP * CAP, count), 0) == target).astype(F32).astype(BF16)
    table[...] = jnp.zeros_like(table)
    table[0:3] = base_ref[...].astype(F32) + 1.0
    table[8:11] = offset_ref[...]
    table[16:19] = velocity_ref[...]
    packed = dot_select(table[...], choose, NT)
    blank = jnp.zeros((8, CAP), F32)
    for r in range(GROUP):
        lanes = slice(r * CAP, (r + 1) * CAP)
        out_ref[r] = jnp.concatenate(
            [packed[0:8, lanes], packed[8:16, lanes], packed[16:24, lanes], blank], axis=1
        )


def pack(owners, owner, base, offset, velocity):
    count = owner.shape[0]
    args = (owner.reshape(1, count), base, offset, velocity)
    return pl.pallas_call(
        pack_kernel,
        out_shape=[
            jax.ShapeDtypeStruct((1, count), jnp.int32),
            jax.ShapeDtypeStruct((owners, 8, 128), F32),
        ],
        grid=(owners // GROUP,),
        in_specs=[pl.BlockSpec(a.shape, lambda k: (0, 0)) for a in args],
        out_specs=[
            pl.BlockSpec((1, count), lambda k: (0, 0)),
            pl.BlockSpec((GROUP, 8, 128), lambda k: (k, 0, 0)),
        ],
        scratch_shapes=[pltpu.VMEM((24, count), F32)],
        compiler_params=pltpu.CompilerParams(
            vmem_limit_bytes=None if owners == GROUP else (48 << 20)
        ),
        name="pack",
    )(*args)


def publish_kernel(owner_ref, base_ref, offset_ref, velocity_ref, out_ref):
    out_ref[0:1] = owner_ref[...].astype(F32)
    out_ref[1:4] = base_ref[...].astype(F32) + 1.0
    out_ref[4:7] = offset_ref[...]
    out_ref[7:10] = velocity_ref[...]
    out_ref[10:16] = jnp.zeros((6, out_ref.shape[1]), F32)


def publish(owner, base, offset, velocity):
    count = owner.shape[0]
    return pl.pallas_call(
        publish_kernel, out_shape=jax.ShapeDtypeStruct((16, count), F32), name="publish"
    )(owner.reshape(1, count), base, offset, velocity)


def join_kernel(before_ref, *refs):
    refs, out_ref, token_ref = refs[:-2], refs[-2], refs[-1]
    row = 0
    for ref in refs:
        out_ref[row : row + ref.shape[0]] = ref[...]
        row += ref.shape[0]
    token_ref[...] = jnp.zeros_like(token_ref)


def join(before, *parts):
    rows = sum(p.shape[0] for p in parts)
    return pl.pallas_call(
        join_kernel,
        out_shape=[jax.ShapeDtypeStruct((rows, parts[0].shape[1]), F32), TOKEN],
        in_specs=[pl.BlockSpec(memory_space=pl.ANY)]
        + [pl.BlockSpec(memory_space=pltpu.VMEM)] * len(parts),
        compiler_params=pltpu.CompilerParams(vmem_limit_bytes=ROOM),
        name="join",
    )(before, *parts)


def own_slots(blocks, me):
    owner = jnp.concatenate([block[0:1] for block in blocks], axis=0)
    member = (owner == me.astype(F32)).astype(F32)
    place = jnp.where(member > 0.0, rank_among(member), -1.0).astype(jnp.int32)
    slots = []
    for k, block in enumerate(blocks):
        choose = (iota((CAP, owner.shape[1]), 0) == place[k : k + 1]).astype(F32).astype(BF16)
        slots.append(dot_select(block, choose, NT))
    return jnp.concatenate(slots, axis=1)


def flow_kernel(low, high, before_ref, pops_ref, flow_ref, token_ref, *own):
    rows = pops_ref.shape[2]
    copies = []
    if own:
        held, sem = own
        span = (high - low) // sem.shape[0]
        for k in range(sem.shape[0]):
            part = pl.ds(low + k * span, span)
            copies.append(
                pltpu.make_async_copy(
                    pops_ref.at[:, part], held.at[:, pl.ds(k * span, span)], sem.at[k]
                )
            )
            copies[-1].start()
    else:
        held, span = pops_ref, high - low

    def plane(z, carry):
        density, momentum = density_momentum([held[i, z] for i in range(19)])
        inverse = 1.0 / density
        first = 0 if own else low
        at = pl.ds(pl.multiple_of((z - first) * rows, rows), rows)
        for axis in range(3):
            flow_ref[axis, at] = momentum[axis] * inverse
        return carry

    if own:
        for k, copy in enumerate(copies):
            copy.wait()
            lax.fori_loop(k * span, (k + 1) * span, plane, 0, unroll=2)
    else:
        lax.fori_loop(low, high, plane, 0, unroll=2)
    token_ref[...] = jnp.zeros_like(token_ref)


def flow_of(low, high, before, pops, own):
    _, _, rows, width = pops.shape
    kind = pltpu.HBM if own else pltpu.VMEM
    scratch = [
        pltpu.VMEM((19, high - low, rows, width), F32),
        pltpu.SemaphoreType.DMA((2,)),
    ]
    return pl.pallas_call(
        functools.partial(flow_kernel, low, high),
        out_shape=[jax.ShapeDtypeStruct((3, (high - low) * rows, width), F32), TOKEN],
        in_specs=[pl.BlockSpec(memory_space=pl.ANY), pl.BlockSpec(memory_space=kind)],
        scratch_shapes=scratch if own else [],
        compiler_params=pltpu.CompilerParams(vmem_limit_bytes=54000000 if own else ROOM),
        cost_estimate=pl.CostEstimate(flops=1000000, bytes_accessed=1500000, transcendentals=0),
        name="flow",
    )(before, pops)


def edges_kernel(before_ref, pops_ref, solid_ref, owner_ref, column_ref, side_ref, wall_ref, target_ref):
    depth, rows = pops_ref.shape[1:3]
    for i in range(19):
        column_ref[i] = x_ends([pops_ref[i, z] for z in range(depth)])
        side_ref[i, 0] = pops_ref[i, :, 0, :]
        side_ref[i, 1] = pops_ref[i, :, rows - 1, :]
    column_ref[19] = x_ends([solid_ref[z].astype(F32) for z in range(depth)])
    wall_ref[0] = solid_ref[:, 0, :]
    wall_ref[1] = solid_ref[:, rows - 1, :]
    owner = owner_ref[...]
    member = (iota((GROUP, owner.shape[1]), 0) == owner).astype(F32)
    rank = jnp.sum(member * rank_among(member), axis=0, keepdims=True)
    target_ref[...] = owner * CAP + rank.astype(jnp.int32)


def edges(before, pops, solid, owner):
    _, depth, rows, width = pops.shape
    count = owner.shape[0]
    return pl.pallas_call(
        edges_kernel,
        out_shape=[
            jax.ShapeDtypeStruct((20, rows, 128), F32),
            jax.ShapeDtypeStruct((19, 2, depth, width), F32),
            jax.ShapeDtypeStruct((2, depth, width), jnp.int32),
            jax.ShapeDtypeStruct((1, count), jnp.int32),
        ],
        in_specs=[pl.BlockSpec(memory_space=pl.ANY)] + [pl.BlockSpec(memory_space=pltpu.VMEM)] * 3,
        compiler_params=pltpu.CompilerParams(vmem_limit_bytes=ROOM),
        cost_estimate=pl.CostEstimate(flops=1000000, bytes_accessed=3000000, transcendentals=0),
        name="edges",
    )(before, pops, solid, owner.reshape(1, count))


def unpack(tiles):
    return [
        jnp.concatenate([t[:, g * CAP : (g + 1) * CAP] for t in tiles], axis=1) for g in range(3)
    ]


def couple_group(base, part, velocity, flow, depth, rows):
    width, slots = flow.shape[1], GROUP * CAP
    start = base.astype(jnp.int32) - 1

    def hat(axis, length):
        cell = iota((length, slots), 0)
        low, share = start[axis : axis + 1], part[axis : axis + 1]
        return jnp.where(cell == low, 1.0 - share, 0.0) + jnp.where(cell == low + 1, share, 0.0)

    hat_x, hat_y, hat_z = hat(0, width), hat(1, rows), hat(2, depth)
    weight = (hat_z[:, None, :] * hat_y[None, :, :]).reshape(depth * rows, slots)
    across = dot_split(flow, hat_x, NN)
    cells = depth * rows
    sampled = [
        jnp.sum(across[d * cells : (d + 1) * cells] * weight, axis=0, keepdims=True)
        for d in range(3)
    ]
    drag = [DRAG_COEF * (sampled[d] - velocity[d : d + 1]) for d in range(3)]
    spread = jnp.concatenate([weight * (-drag[d]) for d in range(3)], axis=0)
    return drag, dot_split(spread, hat_x, NT)


def couple_kernel(single, shape, depth, rows, n_beads, *refs):
    bead_refs, refs = refs[:n_beads], refs[n_beads:]
    lower_ref, upper_ref, column_ref, force_ref, face_ref, *drag_refs = refs
    slabs, cols, _ = shape
    width = lower_ref.shape[2]
    halves = (lower_ref, upper_ref)
    flow = jnp.concatenate([ref[d] for d in range(3) for ref in halves], axis=0)
    hollow = jnp.zeros((5, GROUP * CAP), F32)

    if single:
        slab, col = lax.axis_index("slab"), lax.axis_index("col")
        blocks = [
            ref[k : k + 16] for ref in bead_refs for k in range(0, ref.shape[0], 16)
        ]
        slots = own_slots(blocks, slab * cols + col)
        drag, force = couple_group(slots[1:4], slots[4:7], slots[7:10], flow, depth, rows)
        force_ref[...] = force.reshape(3, depth, rows, width)
        stacked = jnp.concatenate(drag + [hollow], axis=0)
        lanes = cols * CAP
        blank = jnp.zeros((8, 128 - lanes), F32)
        tiles = [
            jnp.concatenate([stacked[:, k * lanes : (k + 1) * lanes], blank], axis=1)
            for k in range(slabs)
        ]
        even = lax.rem(slab, 2) == 0
        drag_refs[0][0] = tiles[0]
        drag_refs[0][1] = jnp.where(even, tiles[3], tiles[1])
        drag_refs[0][2] = tiles[2]
        drag_refs[0][3] = jnp.where(even, tiles[1], tiles[3])
        drag_refs[1][...] = tiles[2]
    else:
        force_ref[...] = jnp.zeros_like(force_ref)
        blank = jnp.zeros((8, 128 - CAP), F32)

        def group(k, carry):
            got = [bead_refs[0][k * GROUP + r] for r in range(GROUP)]
            drag, force = couple_group(*unpack(got), flow, depth, rows)
            force_ref[...] += force.reshape(3, depth, rows, width)
            stacked = jnp.concatenate(drag + [hollow], axis=0)
            for r in range(GROUP):
                drag_refs[0][k * GROUP + r] = jnp.concatenate(
                    [stacked[:, r * CAP : (r + 1) * CAP], blank], axis=1
                )
            return carry

        lax.fori_loop(0, bead_refs[0].shape[0] // GROUP, group, 0)

    force = [x_ends([force_ref[d, z] for z in range(depth)]) for d in range(3)]
    out = collide([column_ref[i] for i in range(19)], column_ref[19] == 1.0, force)
    high = lax.rem(iota((rows, 128), 1), 2) == 0
    ends = [jnp.where(high, out[i], out[j])[:, 0:32] for i, j in zip(*ENTER[0])]
    face_ref[0] = jnp.concatenate(ends[0:4], axis=1)
    face_ref[1] = jnp.concatenate([ends[4], jnp.zeros((rows, 96), F32)], axis=1)


def couple(single, shape, beads, flow, columns, depth, rows):
    width = flow[0].shape[2]
    tile = jax.ShapeDtypeStruct((8, 128), F32)
    drags = [jax.ShapeDtypeStruct((shape[0], 8, 128), F32), tile] if single else beads
    return pl.pallas_call(
        functools.partial(couple_kernel, single, shape, depth, rows, len(beads)),
        out_shape=[
            jax.ShapeDtypeStruct((3, depth, rows, width), F32),
            jax.ShapeDtypeStruct((2, rows, 128), F32),
        ]
        + [jax.ShapeDtypeStruct(d.shape, F32) for d in drags],
        compiler_params=pltpu.CompilerParams(vmem_limit_bytes=ROOM),
        name="couple",
    )(*beads, *flow, columns)


def faces_kernel(
    force_ref, pops_ref, solid_ref, side_ref, wall_ref, face_ref, drag_ref, up_ref, down_ref, draft_ref, token_ref, turned
):
    depth, rows, width = force_ref.shape[1:]
    token_ref[...] = jnp.zeros_like(token_ref)
    tiles = [face_ref[0], face_ref[1]]
    for n in range(2):
        turned[n] = tiles[n].T
    for side in range(4):
        first = side % 2 == 0
        if side < 2:
            at = (0 if first else depth - 1, slice(None))
        else:
            at = (slice(None), 0 if first else rows - 1)
        force = [force_ref[(d,) + at] for d in range(3)]
        if side < 2:
            pops, wall = [pops_ref[i, at[0]] for i in range(19)], solid_ref[at[0]]
        else:
            pops, wall = [side_ref[i, side - 2] for i in range(19)], wall_ref[side - 2]
        out = collide(pops, wall == 1, force)
        axis = 2 if side < 2 else 1
        group = 1 if first else 0
        for k, i in enumerate(ENTER[axis][group]):
            value = out[i]
            if STEP[i, 0] != 0:
                tile, lane = x_place(i)
                if axis == 2:
                    column = spread_column(tiles[tile], lane + 2 * at[0])
                else:
                    block = turned[tile, pl.ds(lane, depth, stride=2), :]
                    column = jnp.broadcast_to(block[:, at[1] : at[1] + 1], (depth, width))
                value = enter_x(value, i, column)
            if axis == 2:
                (down_ref if first else up_ref)[k * rows : (k + 1) * rows] = value
            else:
                row = (group * 5 + k) * depth
                draft_ref[row : row + depth] = turn(value, STEP[i, 2], 0)
    if up_ref.shape[0] > 5 * rows:
        up_ref[5 * rows : 5 * rows + 8] = drag_ref[drag_ref.shape[0] - 1]
        down_ref[5 * rows : 5 * rows + 8] = drag_ref[1]


def faces(single, force, pops, solid, sides, walls, face, drag):
    _, depth, rows, width = force.shape
    message = jax.ShapeDtypeStruct((5 * rows + (8 if single else 0), width), F32)
    return pl.pallas_call(
        faces_kernel,
        out_shape=[message, message, jax.ShapeDtypeStruct((10 * depth, width), F32), TOKEN],
        scratch_shapes=[pltpu.VMEM((2, 128, rows), F32)],
        compiler_params=pltpu.CompilerParams(vmem_limit_bytes=ROOM),
        name="faces",
    )(force, pops, solid, sides, walls, face, drag)


def rows_kernel(depth, rows, before_ref, draft_ref, up_ref, down_ref, *refs):
    refs, token_ref = refs[:-1], refs[-1]
    token_ref[...] = jnp.zeros_like(token_ref)
    outs = refs[-1:] if len(refs) == 3 else refs
    for group in range(2):
        out_ref = outs[0] if len(outs) == 1 else outs[group]
        base = group * 5 * depth if len(outs) == 1 else 0
        y = rows - 1 if group == 0 else 0
        for k, i in enumerate(ENTER[1][group]):
            at = base + k * depth
            out_ref[at : at + depth] = draft_ref[(group * 5 + k) * depth : (group * 5 + k + 1) * depth]
            if STEP[i, 2] != 0:
                side = 0 if STEP[i, 2] == 1 else 1
                z = 0 if side == 0 else depth - 1
                row = ENTER[2][side].index(i) * rows + y
                out_ref[at + z : at + z + 1] = (up_ref, down_ref)[side][row : row + 1]
    if len(refs) == 3:
        own_ref, far_ref, out_ref = refs
        at, tail = 10 * depth, 5 * rows
        out_ref[at : at + 8] = own_ref[0]
        out_ref[at + 8 : at + 16] = down_ref[tail : tail + 8]
        out_ref[at + 16 : at + 24] = far_ref[...]
        out_ref[at + 24 : at + 32] = up_ref[tail : tail + 8]


def leaving_rows(shape, depth, rows, before, draft, up, down, drags):
    width = draft.shape[1]
    if drags:
        sizes = [10 * depth + 8 * shape[0]]
    else:
        sizes = [5 * depth] * 2
    args = (draft, up, down, *drags)
    return pl.pallas_call(
        functools.partial(rows_kernel, depth, rows),
        out_shape=[jax.ShapeDtypeStruct((n, width), F32) for n in sizes] + [TOKEN],
        in_specs=[pl.BlockSpec(memory_space=pl.ANY)]
        + [pl.BlockSpec(memory_space=pltpu.VMEM)] * len(args),
        compiler_params=pltpu.CompilerParams(vmem_limit_bytes=ROOM),
        name="rows",
    )(before, *args)


def stream_kernel(low, high, before_ref, *refs):
    if low > 0:
        refs = refs[1:]
    pops_ref, solid_ref, force_ref, face_ref, out_ref, tile_ref, token_ref, held, sem = refs
    depth, rows, width = pops_ref.shape[1:]
    token_ref[...] = jnp.zeros_like(token_ref)
    chunks = 2
    span = (high - low) // chunks

    def plane(z, faces):
        out = collide(
            [pops_ref[i, z] for i in range(19)],
            solid_ref[z] == 1,
            [force_ref[d, z] for d in range(3)],
        )
        for i in range(19):
            value = out[i]
            if STEP[i, 0] != 0:
                tile, lane = x_place(i)
                value = enter_x(value, i, spread_column(faces[tile], lane))
            held[i, z - low] = turn(value, STEP[i, 1], 0)
        return tuple(pltpu.roll(f, 126, 1) for f in faces)

    runs = [(0, 5), (5, 6), (6, 7), (7, 11)] + [(i, i + 1) for i in range(11, 19)]
    copies = []
    carry = (face_ref[0], face_ref[1])
    if low > 0:
        carry = tuple(pltpu.roll(f, 128 - 2 * low, 1) for f in carry)
    for k in range(chunks):
        first = low + k * span
        carry = lax.fori_loop(first, first + span, plane, carry, unroll=2)
        for n, (a, b) in enumerate(runs):
            step = int(STEP[a, 2])
            start, stop = max(first + step, 0), min(first + span + step, depth)
            copy = pltpu.make_async_copy(
                held.at[a:b, start - step - low : stop - step - low],
                out_ref.at[a:b, start:stop],
                sem.at[k, n],
            )
            copy.start()
            copies.append(copy)
    for group in range(2):
        first = 0 if group == 0 else rows - 8
        for k, i in enumerate(ENTER[1][group]):
            tile_ref[group * 5 + k] = held[i, :, first : first + 8, :]
    for copy in copies:
        copy.wait()


def stream(low, high, before, whole, pops, solid, force, face):
    _, depth, rows, width = pops.shape
    vmem = pl.BlockSpec(memory_space=pltpu.VMEM)
    hbm = pl.BlockSpec(memory_space=pltpu.HBM)
    whole = [] if whole is None else [whole]
    return pl.pallas_call(
        functools.partial(stream_kernel, low, high),
        out_shape=[
            jax.ShapeDtypeStruct(pops.shape, F32),
            jax.ShapeDtypeStruct((10, high - low, 8, width), F32),
            TOKEN,
        ],
        in_specs=[pl.BlockSpec(memory_space=pl.ANY)] + [hbm] * len(whole) + [vmem] * 4,
        out_specs=[hbm, vmem, vmem],
        scratch_shapes=[
            pltpu.VMEM((19, high - low, rows, width), F32),
            pltpu.SemaphoreType.DMA((2, 12)),
        ],
        input_output_aliases={1: 0} if whole else {},
        compiler_params=pltpu.CompilerParams(vmem_limit_bytes=ROOM),
        cost_estimate=pl.CostEstimate(flops=5000000, bytes_accessed=3000000, transcendentals=0),
        name="stream",
    )(before, *whole, pops, solid, force, face)


def finish_kernel(
    shape, n_rows, whole_ref, target_ref, lower_ref, upper_ref, up_ref, down_ref, *refs
):
    row_refs, refs = refs[:n_rows], refs[n_rows:]
    drag_refs, (out_ref, bead_ref, planes, tiles, sem) = refs[:-5], refs[-5:]
    depth, rows, width = whole_ref.shape[1:]

    def entering(group, k):
        if n_rows == 1:
            at = (group * 5 + k) * depth
            return row_refs[0][at : at + depth]
        return row_refs[group][k * depth : (k + 1) * depth]

    copies = []

    def leave(source, target):
        copy = pltpu.make_async_copy(source, target, sem.at[len(copies)])
        copy.start()
        copies.append(copy)

    for group in range(2):
        z = 0 if group == 0 else depth - 1
        for k, i in enumerate(ENTER[2][group]):
            value = (up_ref, down_ref)[group][k * rows : (k + 1) * rows]
            if STEP[i, 1] != 0:
                side = 0 if STEP[i, 1] == 1 else 1
                row = entering(side, ENTER[1][side].index(i))[z : z + 1]
                y = 0 if side == 0 else rows - 1
                value = jnp.where(
                    iota((rows, width), 0) == y,
                    jnp.broadcast_to(row, (rows, width)),
                    turn(value, STEP[i, 1], 0),
                )
            n = group * 5 + k
            planes[n] = value
            leave(planes.at[n], out_ref.at[i, z])
    for group in range(2):
        first = 0 if group == 0 else rows - 8
        for k, i in enumerate(ENTER[1][group]):
            n = group * 5 + k
            step = int(STEP[i, 2])
            half = lower_ref.shape[1]
            tiles[n, 1 + step : 1 + step + half] = lower_ref[n]
            tiles[n, 1 + step + half : 1 + step + depth] = upper_ref[n]
            tiles[n, 1 : 1 + depth, 0 if group == 0 else 7, :] = entering(group, k)
            low, high = max(step, 0), min(depth + step, depth)
            leave(tiles.at[n, 1 + low : 1 + high], out_ref.at[i, low:high, first : first + 8])

    count = target_ref.shape[1]
    target = target_ref[...]
    if n_rows == 1:
        own_ref, far_ref = drag_refs
        slabs, cols, _ = shape
        at, tail = 10 * depth, 5 * rows
        direct = jnp.concatenate(
            [own_ref[0], down_ref[tail : tail + 8], far_ref[...], up_ref[tail : tail + 8]], axis=0
        )
        passed = row_refs[0][at : at + 8 * slabs]
        table = jnp.where(iota(direct.shape, 1) < CAP, direct, passed)
        owner = lax.shift_right_logical(target, 5)
        slot = target - owner * CAP
        owner_slab = lax.shift_right_logical(owner, cols.bit_length() - 1)
        away_col = owner - owner_slab * cols - lax.axis_index("col")
        away_col = jnp.where(away_col < 0, away_col + cols, away_col)
        away_slab = owner_slab - lax.axis_index("slab")
        away_slab = jnp.where(away_slab < 0, away_slab + slabs, away_slab)
        choose = (iota((128, count), 0) == away_col * CAP + slot).astype(F32).astype(BF16)
        picked = dot_select(table, choose, NN)
        total = jnp.where(away_slab == 0, picked[0:8], 0.0)
        for dz in range(1, slabs):
            total = total + jnp.where(away_slab == dz, picked[8 * dz : 8 * dz + 8], 0.0)
        bead_ref[...] = total[0:3]
    else:
        back_ref = drag_refs[0]

        def group(k, total):
            got = [back_ref[k * GROUP + r] for r in range(GROUP)]
            slots = jnp.concatenate([t[:, 0:CAP] for t in got], axis=1)
            first = k * (GROUP * CAP)
            choose = (iota((GROUP * CAP, count), 0) + first == target).astype(F32)
            return total + dot_select(slots, choose.astype(BF16), NN)

        total = lax.fori_loop(
            0, back_ref.shape[0] // GROUP, group, jnp.zeros((8, count), F32)
        )
        bead_ref[...] = total[0:3]
    for copy in copies:
        copy.wait()


def finish(shape, whole, target, lower, upper, up, down, entered, drags):
    _, depth, rows, width = whole.shape
    vmem = pl.BlockSpec(memory_space=pltpu.VMEM)
    hbm = pl.BlockSpec(memory_space=pltpu.HBM)
    args = [whole, target, lower, upper, up, down, *entered, *drags]
    return pl.pallas_call(
        functools.partial(finish_kernel, shape, len(entered)),
        out_shape=[
            jax.ShapeDtypeStruct(whole.shape, F32),
            jax.ShapeDtypeStruct((3, target.shape[1]), F32),
        ],
        in_specs=[hbm] + [vmem] * (len(args) - 1),
        out_specs=[hbm, vmem],
        scratch_shapes=[
            pltpu.VMEM((10, rows, width), F32),
            pltpu.VMEM((10, depth + 2, 8, width), F32),
            pltpu.SemaphoreType.DMA((20,)),
        ],
        input_output_aliases={0: 0},
        compiler_params=pltpu.CompilerParams(vmem_limit_bytes=ROOM),
        name="finish",
    )(*args)


def shards(populations, solid_mask, bead_owner, bead_base, bead_offset, bead_velocity):
    slabs, cols, pairs = shape = tuple(lax.axis_size(a) for a in ("slab", "col", "pair"))
    owners = slabs * cols
    depth, rows = populations.shape[1:3]
    single = owners == GROUP and slabs == 4
    swap = functools.partial(
        lax.all_to_all, axis_name=("slab", "col"), split_axis=0, concat_axis=0, tiled=True
    )

    beads = (bead_owner, bead_base, bead_offset, bead_velocity)
    half = depth // 2
    if single:
        token = own = publish(*beads)
        first = exchange(own, shape, (0, 1, 0))
        lower, token = flow_of(0, half, token, populations, True)
        pair, token = join(token, own, first)
        second = exchange(pair, shape, (1, 0, 0))
        upper, token = flow_of(half, depth, token, populations, False)
        four, token = join(token, pair, second)
        third = exchange(four, shape, (2, 0, 0))
        beads = [four, third]
    else:
        token = jnp.zeros(TOKEN.shape, F32)
        target, messages = pack(owners, *beads)
        beads = [swap(messages)]
        lower, _ = flow_of(0, half, token, populations, True)
        upper, _ = flow_of(half, depth, token, populations, False)
    columns, sides, walls, slots = edges(token, populations, solid_mask, bead_owner)
    if single:
        target = slots
    force, face, drag, *far = couple(
        single, shape, beads, (lower, upper), columns, depth, rows
    )
    face = send(face, shape, (0, 0, 1))
    if single:
        far = send(far[0], shape, (2, 0, 0))
    else:
        drag = swap(drag)
    up, down, draft, token = faces(
        single, force, populations, solid_mask, sides, walls, face, drag
    )
    up = send(up, shape, (1, 0, 0))
    down = send(down, shape, (-1, 0, 0))
    fields = (populations, solid_mask, force, face)
    whole, lower, token = stream(0, depth // 2, token, None, *fields)
    drags = [drag, far] if single else []
    *leaving, token = leaving_rows(shape, depth, rows, token, draft, up, down, drags)
    entered = [send(value, shape, (0, sign, 0)) for value, sign in zip(leaving, (1, -1))]
    whole, upper, _ = stream(depth // 2, depth, token, whole, *fields)
    return tuple(finish(shape, whole, target, lower, upper, up, down, entered, drags or [drag]))


def solution(mesh):
    return jax.shard_map(
        shards,
        mesh=mesh,
        in_specs=(
            P(None, ("rep", "slab"), "col", "pair"),
            P(("rep", "slab"), "col", "pair"),
            P(("rep", "slab", "col", "pair")),
            P(None, ("rep", "slab", "col", "pair")),
            P(None, ("rep", "slab", "col", "pair")),
            P(None, ("rep", "slab", "col", "pair")),
        ),
        out_specs=(
            P(None, ("rep", "slab"), "col", "pair"),
            P(None, ("rep", "slab", "col", "pair")),
        ),
        check_vma=False,
    )
```

```python
import functools

import jax
import jax.numpy as jnp
import numpy as np
from jax import lax
from jax.experimental import pallas as pl
from jax.experimental.pallas import tpu as pltpu
from jax.sharding import PartitionSpec as P

CAP = 32
GROUP = 8

STEP = np.array(
    [
        [0, 0, 0],
        [1, 0, 0],
        [-1, 0, 0],
        [0, 1, 0],
        [0, -1, 0],
        [0, 0, 1],
        [0, 0, -1],
        [1, 1, 0],
        [-1, -1, 0],
        [1, -1, 0],
        [-1, 1, 0],
        [1, 0, 1],
        [-1, 0, -1],
        [1, 0, -1],
        [-1, 0, 1],
        [0, 1, 1],
        [0, -1, -1],
        [0, 1, -1],
        [0, -1, 1],
    ],
    np.int32,
)
TAU_PLUS = 0.8
TAU_MINUS = 0.5 + (3.0 / 16.0) / (TAU_PLUS - 0.5)
KEEP_EVEN = 1.0 - 1.0 / TAU_PLUS
KEEP_ODD = 1.0 - 1.0 / TAU_MINUS
FORCE_GAIN = 1.0 - 0.5 / TAU_PLUS
DRAG_COEF = 2.0
F32 = jnp.float32
BF16 = jnp.bfloat16

ENTER = [[[i for i in range(19) if STEP[i, a] == sign] for sign in (1, -1)] for a in range(3)]
TOKEN = jax.ShapeDtypeStruct((8, 128), F32)
ROOM = 16 << 20
NT = (((1,), (1,)), ((), ()))
NN = (((1,), (0,)), ((), ()))


def iota(shape, dim):
    return lax.broadcasted_iota(jnp.int32, shape, dim)


def high_low(value):
    high = value.astype(BF16)
    return high, (value - high.astype(F32)).astype(BF16)


def dot_split(left, right, dims):
    a, b = high_low(left)
    c, d = high_low(right)
    mul = functools.partial(lax.dot_general, dimension_numbers=dims, preferred_element_type=F32)
    return mul(a, c) + (mul(a, d) + mul(b, c))


def dot_select(value, choose, dims):
    first = value.astype(BF16).astype(F32)
    rest = value - first
    second = rest.astype(BF16).astype(F32)
    stacked = jnp.concatenate([first, second, rest - second], axis=0).astype(BF16)
    got = lax.dot_general(stacked, choose, dimension_numbers=dims, preferred_element_type=F32)
    rows = value.shape[0]
    return got[0:rows] + got[rows : 2 * rows] + got[2 * rows : 3 * rows]


def density_momentum(pops):
    momentum = []
    for axis in range(3):
        plus = [pops[i] for i in range(19) if STEP[i, axis] == 1]
        minus = [pops[i] for i in range(19) if STEP[i, axis] == -1]
        momentum.append(sum(plus[1:], plus[0]) - sum(minus[1:], minus[0]))
    return sum(pops[1:], pops[0]), momentum


def along(step, vector):
    terms = None
    for axis in range(3):
        if step[axis] == 0:
            continue
        if terms is None:
            terms = vector[axis] if step[axis] == 1 else -vector[axis]
        else:
            terms = terms + vector[axis] if step[axis] == 1 else terms - vector[axis]
    return terms


def collide(pops, wall, force):
    density, momentum = density_momentum(pops)
    inverse = 1.0 / density
    carried = [m + 0.5 * f for m, f in zip(momentum, force)]
    speed = [m * inverse for m in carried]
    w = 1.0 / 36.0
    bend = [(4.5 * w / TAU_PLUS) * m + (9.0 * w * FORCE_GAIN) * f for m, f in zip(carried, force)]
    push = [(3.0 * w / TAU_MINUS) * m + (3.0 * w * FORCE_GAIN) * f for m, f in zip(carried, force)]
    drop = [(1.5 * w / TAU_PLUS) * m + (3.0 * w * FORCE_GAIN) * f for m, f in zip(carried, force)]
    rest = (w / TAU_PLUS) * density - sum(
        [u * d for u, d in zip(speed[1:], drop[1:])], speed[0] * drop[0]
    )
    out = [None] * 19
    out[0] = jnp.where(wall, pops[0], KEEP_EVEN * pops[0] + 12.0 * rest)
    for i in range(1, 19, 2):
        a, b = pops[i], pops[i + 1]
        step = STEP[i]
        even = rest + along(step, speed) * along(step, bend)
        odd = along(step, push)
        if i < 7:
            even = even + even
            odd = odd + odd
        even = (0.5 * KEEP_EVEN) * (a + b) + even
        odd = (0.5 * KEEP_ODD) * (a - b) + odd
        out[i] = jnp.where(wall, b, even + odd)
        out[i + 1] = jnp.where(wall, a, even - odd)
    return out


def turn(value, amount, axis):
    if amount == 0:
        return value
    return pltpu.roll(value, int(amount) % value.shape[axis], axis)


def send(value, shape, target):
    def flat(at):
        return (at[0] * shape[1] + at[1]) * shape[2] + at[2]

    perm = [(flat(at), flat(target(*at))) for at in np.ndindex(*shape)]
    return lax.ppermute(value, ("slab", "col", "pair"), perm)


def send_slab(value, shape, which):
    def target(s, c, p):
        return ((s + (1 if s % 2 == which else -1)) % shape[0], c, p)

    return send(value, shape, target)


def even_slab():
    return lax.rem(lax.axis_index("slab"), 2) == 0


def rank_among(member):
    count = member.shape[1]
    earlier = (iota((count, count), 0) < iota((count, count), 1)).astype(F32).astype(BF16)
    return lax.dot_general(member.astype(BF16), earlier, NN, preferred_element_type=F32)


def spread_column(tile, lane):
    return jnp.broadcast_to(tile[:, lane : lane + 1], tile.shape)


def enter_x(value, i, column):
    step = STEP[i, 0]
    if step == 0:
        return value
    side = 0 if step == 1 else value.shape[1] - 1
    return jnp.where(iota(value.shape, 1) == side, column, turn(value, step, 1))


def x_place(i):
    group = 0 if STEP[i, 0] == 1 else 1
    place = ENTER[0][group].index(i)
    return place // 4, (place % 4) * 32 + group


def x_ends(planes):
    lane = lax.shift_right_logical(iota(planes[0].shape, 1), 1)
    tile = jnp.ones(planes[0].shape, F32)
    for z, value in enumerate(planes):
        tile = jnp.where(lane == z, pltpu.roll(value, 2 * z + 1, 1), tile)
    return tile


def pack_kernel(
    steps, owner_ref, base_ref, offset_ref, velocity_ref, target_ref, out_ref, table
):
    count = owner_ref.shape[1]
    step = 0 if steps == 1 else pl.program_id(0)
    local = owner_ref[...] - step * GROUP
    member = (iota((GROUP, count), 0) == local).astype(F32)
    rank = jnp.sum(member * rank_among(member), axis=0, keepdims=True).astype(jnp.int32)
    inside = (local >= 0) & (local < GROUP)
    target = jnp.where(inside, local * CAP + rank, -1)
    whole_target = jnp.where(inside, owner_ref[...] * CAP + rank, -1)

    if steps == 1:
        target_ref[...] = whole_target
    else:
        known = jnp.where(step == 0, -1, target_ref[...])
        target_ref[...] = jnp.maximum(known, whole_target)

    choose = (iota((GROUP * CAP, count), 0) == target).astype(F32).astype(BF16)
    table[...] = jnp.zeros_like(table)
    table[0:3] = base_ref[...].astype(F32) + 1.0
    table[8:11] = offset_ref[...]
    table[16:19] = velocity_ref[...]
    packed = dot_select(table[...], choose, NT)
    blank = jnp.zeros((8, CAP), F32)
    for r in range(GROUP):
        lanes = slice(r * CAP, (r + 1) * CAP)
        out_ref[r] = jnp.concatenate(
            [packed[0:8, lanes], packed[8:16, lanes], packed[16:24, lanes], blank], axis=1
        )


def pack(owners, owner, base, offset, velocity):
    count, steps = owner.shape[0], owners // GROUP
    args = (owner.reshape(1, count), base, offset, velocity)
    blocks = {}
    if steps > 1:
        blocks = dict(
            grid=(steps,),
            in_specs=[pl.BlockSpec(a.shape, lambda k: (0, 0)) for a in args],
            out_specs=[
                pl.BlockSpec((1, count), lambda k: (0, 0)),
                pl.BlockSpec((GROUP, 8, 128), lambda k: (k, 0, 0)),
            ],
            compiler_params=pltpu.CompilerParams(vmem_limit_bytes=48 << 20),
        )
    return pl.pallas_call(
        functools.partial(pack_kernel, steps),
        out_shape=[
            jax.ShapeDtypeStruct((1, count), jnp.int32),
            jax.ShapeDtypeStruct((owners, 8, 128), F32),
        ],
        scratch_shapes=[pltpu.VMEM((24, count), F32)],
        name="pack",
        **blocks,
    )(*args)


def moments_kernel(
    pops_ref, solid_ref, flow_ref, column_ref, side_ref, wall_ref, held, held_solid, sem
):
    depth, rows, width = pops_ref.shape[1:]
    chunks = 4
    span = depth // chunks
    copies = [pltpu.make_async_copy(solid_ref, held_solid, sem.at[chunks])]
    for k in range(chunks):
        part = pl.ds(k * span, span)
        copies.append(
            pltpu.make_async_copy(pops_ref.at[:, part], held.at[:, part], sem.at[k])
        )
    for copy in copies:
        copy.start()

    def plane(z, carry):
        pops = [held[i, z] for i in range(19)]
        density, momentum = density_momentum(pops)
        inverse = 1.0 / density
        for axis in range(3):
            flow_ref[axis, pl.ds(pl.multiple_of(z * rows, rows), rows)] = momentum[axis] * inverse
        return carry

    for k in range(chunks):
        copies[1 + k].wait()
        lax.fori_loop(k * span, (k + 1) * span, plane, 0, unroll=2)
    copies[0].wait()
    for i in range(19):
        column_ref[i] = x_ends([held[i, z] for z in range(depth)])
        side_ref[i, 0] = held[i, :, 0, :]
        side_ref[i, 1] = held[i, :, rows - 1, :]
    wall_ref[0] = held_solid[:, 0, :]
    wall_ref[1] = held_solid[:, rows - 1, :]
    column_ref[19] = x_ends([held_solid[z].astype(F32) for z in range(depth)])


def moments(pops, solid):
    _, depth, rows, width = pops.shape
    hbm = pl.BlockSpec(memory_space=pltpu.HBM)
    return pl.pallas_call(
        moments_kernel,
        out_shape=[
            jax.ShapeDtypeStruct((3, depth * rows, width), F32),
            jax.ShapeDtypeStruct((20, rows, 128), F32),
            jax.ShapeDtypeStruct((19, 2, depth, width), F32),
            jax.ShapeDtypeStruct((2, depth, width), jnp.int32),
        ],
        in_specs=[hbm, hbm],
        scratch_shapes=[
            pltpu.VMEM(pops.shape, F32),
            pltpu.VMEM(solid.shape, jnp.int32),
            pltpu.SemaphoreType.DMA((5,)),
        ],
        compiler_params=pltpu.CompilerParams(vmem_limit_bytes=54000000),
        cost_estimate=pl.CostEstimate(flops=3000000, bytes_accessed=4000000, transcendentals=0),
        name="moments",
    )(pops, solid)


def unpack(tiles):
    return [
        jnp.concatenate([t[:, g * CAP : (g + 1) * CAP] for t in tiles], axis=1) for g in range(3)
    ]


def couple_group(base, part, velocity, flow, depth, rows):
    width, slots = flow.shape[1], GROUP * CAP
    start = base.astype(jnp.int32) - 1

    def hat(axis, length):
        cell = iota((length, slots), 0)
        low, share = start[axis : axis + 1], part[axis : axis + 1]
        return jnp.where(cell == low, 1.0 - share, 0.0) + jnp.where(cell == low + 1, share, 0.0)

    hat_x, hat_y, hat_z = hat(0, width), hat(1, rows), hat(2, depth)
    weight = (hat_z[:, None, :] * hat_y[None, :, :]).reshape(depth * rows, slots)
    across = dot_split(flow, hat_x, NN)
    cells = depth * rows
    sampled = [
        jnp.sum(across[d * cells : (d + 1) * cells] * weight, axis=0, keepdims=True)
        for d in range(3)
    ]
    drag = [DRAG_COEF * (sampled[d] - velocity[d : d + 1]) for d in range(3)]
    spread = jnp.concatenate([weight * (-drag[d]) for d in range(3)], axis=0)
    return drag, dot_split(spread, hat_x, NT)


def couple_kernel(shape, depth, rows, beads_ref, flow_ref, column_ref, force_ref, face_ref, *drag_refs):
    slabs, cols, _ = shape
    width = flow_ref.shape[2]
    flow = flow_ref[...].reshape(3 * depth * rows, width)
    hollow = jnp.zeros((5, GROUP * CAP), F32)

    if len(drag_refs) == 2:
        slab, col = lax.axis_index("slab"), lax.axis_index("col")
        got = []
        for r in range(GROUP):
            there = [a - b for a, b in zip((slab, col), divmod(r, cols))]
            there = [jnp.where(a < 0, a + n, a) for a, n in zip(there, (slabs, cols))]
            got.append(beads_ref[there[0] * cols + there[1]])
        drag, force = couple_group(*unpack(got), flow, depth, rows)
        force_ref[...] = force.reshape(3, depth, rows, width)
        stacked = jnp.concatenate(drag + [hollow], axis=0)
        lanes = cols * CAP
        blank = jnp.zeros((8, 128 - lanes), F32)
        for dz in range(slabs):
            tile = jnp.concatenate([stacked[:, dz * lanes : (dz + 1) * lanes], blank], axis=1)
            drag_refs[0][dz] = tile
            if dz == 2:
                drag_refs[1][...] = tile
    else:
        force_ref[...] = jnp.zeros_like(force_ref)
        blank = jnp.zeros((8, 128 - CAP), F32)

        def group(k, carry):
            got = [beads_ref[k * GROUP + r] for r in range(GROUP)]
            drag, force = couple_group(*unpack(got), flow, depth, rows)
            force_ref[...] += force.reshape(3, depth, rows, width)
            stacked = jnp.concatenate(drag + [hollow], axis=0)
            for r in range(GROUP):
                drag_refs[0][k * GROUP + r] = jnp.concatenate(
                    [stacked[:, r * CAP : (r + 1) * CAP], blank], axis=1
                )
            return carry

        lax.fori_loop(0, beads_ref.shape[0] // GROUP, group, 0)

    force = [x_ends([force_ref[d, z] for z in range(depth)]) for d in range(3)]
    out = collide([column_ref[i] for i in range(19)], column_ref[19] == 1.0, force)
    high = lax.rem(iota((rows, 128), 1), 2) == 0
    ends = [jnp.where(high, out[i], out[j])[:, 0:32] for i, j in zip(*ENTER[0])]
    face_ref[0] = jnp.concatenate(ends[0:4], axis=1)
    face_ref[1] = jnp.concatenate([ends[4], jnp.zeros((rows, 96), F32)], axis=1)


def couple(shape, beads, flow, columns, depth, rows):
    width = flow.shape[2]
    single = beads.shape[0] == GROUP
    tile = jax.ShapeDtypeStruct((8, 128), F32)
    drags = [jax.ShapeDtypeStruct((shape[0], 8, 128), F32), tile] if single else [beads]
    return pl.pallas_call(
        functools.partial(couple_kernel, shape, depth, rows),
        out_shape=[
            jax.ShapeDtypeStruct((3, depth, rows, width), F32),
            jax.ShapeDtypeStruct((2, rows, 128), F32),
        ]
        + [jax.ShapeDtypeStruct(d.shape, F32) for d in drags],
        compiler_params=pltpu.CompilerParams(vmem_limit_bytes=ROOM),
        name="couple",
    )(beads, flow, columns)


def faces_kernel(
    force_ref, pops_ref, solid_ref, side_ref, wall_ref, face_ref, drag_ref, *refs
):
    first_ref, second_ref, draft_ref, token_ref, turned, leaving = refs
    depth, rows, width = force_ref.shape[1:]
    token_ref[...] = jnp.zeros_like(token_ref)
    tiles = [face_ref[0], face_ref[1]]
    for n in range(2):
        turned[n] = tiles[n].T
    for side in range(4):
        first = side % 2 == 0
        if side < 2:
            at = (0 if first else depth - 1, slice(None))
        else:
            at = (slice(None), 0 if first else rows - 1)
        force = [force_ref[(d,) + at] for d in range(3)]
        if side < 2:
            pops, wall = [pops_ref[i, at[0]] for i in range(19)], solid_ref[at[0]]
        else:
            pops, wall = [side_ref[i, side - 2] for i in range(19)], wall_ref[side - 2]
        out = collide(pops, wall == 1, force)
        axis = 2 if side < 2 else 1
        group = 1 if first else 0
        for k, i in enumerate(ENTER[axis][group]):
            value = out[i]
            if STEP[i, 0] != 0:
                tile, lane = x_place(i)
                if axis == 2:
                    column = spread_column(tiles[tile], lane + 2 * at[0])
                else:
                    block = turned[tile, pl.ds(lane, depth, stride=2), :]
                    column = jnp.broadcast_to(block[:, at[1] : at[1] + 1], (depth, width))
                value = enter_x(value, i, column)
            if axis == 2:
                leaving[group, k * rows : (k + 1) * rows] = value
            else:
                row = (group * 5 + k) * depth
                draft_ref[row : row + depth] = turn(value, STEP[i, 2], 0)
    if leaving.shape[1] > 5 * rows:
        leaving[0, 5 * rows : 5 * rows + 8] = drag_ref[drag_ref.shape[0] - 1]
        leaving[1, 5 * rows : 5 * rows + 8] = drag_ref[1]
    even = even_slab()
    first_ref[...] = jnp.where(even, leaving[0], leaving[1])
    second_ref[...] = jnp.where(even, leaving[1], leaving[0])


def faces(single, force, pops, solid, sides, walls, face, drag):
    _, depth, rows, width = force.shape
    message = jax.ShapeDtypeStruct((5 * rows + (8 if single else 0), width), F32)
    return pl.pallas_call(
        faces_kernel,
        out_shape=[message, message, jax.ShapeDtypeStruct((10 * depth, width), F32), TOKEN],
        scratch_shapes=[pltpu.VMEM((2, 128, rows), F32), pltpu.VMEM((2, *message.shape), F32)],
        compiler_params=pltpu.CompilerParams(vmem_limit_bytes=ROOM),
        name="faces",
    )(force, pops, solid, sides, walls, face, drag)


def entered_z(first_ref, second_ref, side, rows):
    even = even_slab() if side == 0 else jnp.logical_not(even_slab())
    return jnp.where(even, second_ref[rows], first_ref[rows])


def rows_kernel(depth, rows, before_ref, draft_ref, first_ref, second_ref, *refs):
    refs, token_ref = refs[:-1], refs[-1]
    token_ref[...] = jnp.zeros_like(token_ref)
    outs = refs[-1:] if len(refs) == 3 else refs
    for group in range(2):
        out_ref = outs[0] if len(outs) == 1 else outs[group]
        base = group * 5 * depth if len(outs) == 1 else 0
        y = rows - 1 if group == 0 else 0
        for k, i in enumerate(ENTER[1][group]):
            at = base + k * depth
            out_ref[at : at + depth] = draft_ref[(group * 5 + k) * depth : (group * 5 + k + 1) * depth]
            if STEP[i, 2] != 0:
                side = 0 if STEP[i, 2] == 1 else 1
                z = 0 if side == 0 else depth - 1
                row = ENTER[2][side].index(i) * rows + y
                out_ref[at + z : at + z + 1] = entered_z(
                    first_ref, second_ref, side, slice(row, row + 1)
                )
    if len(refs) == 3:
        own_ref, far_ref, out_ref = refs
        at, tail = 10 * depth, 5 * rows
        out_ref[at : at + 8] = own_ref[0]
        out_ref[at + 8 : at + 16] = entered_z(first_ref, second_ref, 1, slice(tail, tail + 8))
        out_ref[at + 16 : at + 24] = far_ref[...]
        out_ref[at + 24 : at + 32] = entered_z(first_ref, second_ref, 0, slice(tail, tail + 8))


def leaving_rows(shape, depth, rows, before, draft, first, second, drags):
    width = draft.shape[1]
    if drags:
        sizes = [10 * depth + 8 * shape[0]]
    else:
        sizes = [5 * depth] * 2
    args = (draft, first, second, *drags)
    return pl.pallas_call(
        functools.partial(rows_kernel, depth, rows),
        out_shape=[jax.ShapeDtypeStruct((n, width), F32) for n in sizes] + [TOKEN],
        in_specs=[pl.BlockSpec(memory_space=pl.ANY)]
        + [pl.BlockSpec(memory_space=pltpu.VMEM)] * len(args),
        compiler_params=pltpu.CompilerParams(vmem_limit_bytes=ROOM),
        name="rows",
    )(before, *args)


def stream_kernel(low, high, before_ref, *refs):
    if low > 0:
        refs = refs[1:]
    pops_ref, solid_ref, force_ref, face_ref, out_ref, tile_ref, token_ref, held, sem = refs
    depth, rows, width = pops_ref.shape[1:]
    token_ref[...] = jnp.zeros_like(token_ref)
    chunks = 2
    span = (high - low) // chunks

    def plane(z, faces):
        out = collide(
            [pops_ref[i, z] for i in range(19)],
            solid_ref[z] == 1,
            [force_ref[d, z] for d in range(3)],
        )
        for i in range(19):
            value = out[i]
            if STEP[i, 0] != 0:
                tile, lane = x_place(i)
                value = enter_x(value, i, spread_column(faces[tile], lane))
            held[i, z - low] = turn(value, STEP[i, 1], 0)
        return tuple(pltpu.roll(f, 126, 1) for f in faces)

    runs = [(0, 5), (5, 6), (6, 7), (7, 11)] + [(i, i + 1) for i in range(11, 19)]
    copies = []
    carry = (face_ref[0], face_ref[1])
    if low > 0:
        carry = tuple(pltpu.roll(f, 128 - 2 * low, 1) for f in carry)
    for k in range(chunks):
        first = low + k * span
        carry = lax.fori_loop(first, first + span, plane, carry, unroll=2)
        for n, (a, b) in enumerate(runs):
            step = int(STEP[a, 2])
            start, stop = max(first + step, 0), min(first + span + step, depth)
            copy = pltpu.make_async_copy(
                held.at[a:b, start - step - low : stop - step - low],
                out_ref.at[a:b, start:stop],
                sem.at[k, n],
            )
            copy.start()
            copies.append(copy)
    for group in range(2):
        first = 0 if group == 0 else rows - 8
        for k, i in enumerate(ENTER[1][group]):
            tile_ref[group * 5 + k] = held[i, :, first : first + 8, :]
    for copy in copies:
        copy.wait()


def stream(low, high, before, whole, pops, solid, force, face):
    _, depth, rows, width = pops.shape
    vmem = pl.BlockSpec(memory_space=pltpu.VMEM)
    hbm = pl.BlockSpec(memory_space=pltpu.HBM)
    whole = [] if whole is None else [whole]
    return pl.pallas_call(
        functools.partial(stream_kernel, low, high),
        out_shape=[
            jax.ShapeDtypeStruct(pops.shape, F32),
            jax.ShapeDtypeStruct((10, high - low, 8, width), F32),
            TOKEN,
        ],
        in_specs=[pl.BlockSpec(memory_space=pl.ANY)] + [hbm] * len(whole) + [vmem] * 4,
        out_specs=[hbm, vmem, vmem],
        scratch_shapes=[
            pltpu.VMEM((19, high - low, rows, width), F32),
            pltpu.SemaphoreType.DMA((2, 12)),
        ],
        input_output_aliases={1: 0} if whole else {},
        compiler_params=pltpu.CompilerParams(vmem_limit_bytes=ROOM),
        cost_estimate=pl.CostEstimate(flops=5000000, bytes_accessed=3000000, transcendentals=0),
        name="stream",
    )(before, *whole, pops, solid, force, face)


def finish_kernel(
    shape, n_rows, whole_ref, target_ref, lower_ref, upper_ref, first_ref, second_ref, *refs
):
    row_refs, refs = refs[:n_rows], refs[n_rows:]
    drag_refs, (out_ref, bead_ref, planes, tiles, sem) = refs[:-5], refs[-5:]
    depth, rows, width = whole_ref.shape[1:]

    def entering(group, k):
        if n_rows == 1:
            at = (group * 5 + k) * depth
            return row_refs[0][at : at + depth]
        return row_refs[group][k * depth : (k + 1) * depth]

    copies = []

    def leave(source, target):
        copy = pltpu.make_async_copy(source, target, sem.at[len(copies)])
        copy.start()
        copies.append(copy)

    for group in range(2):
        z = 0 if group == 0 else depth - 1
        for k, i in enumerate(ENTER[2][group]):
            value = entered_z(first_ref, second_ref, group, slice(k * rows, (k + 1) * rows))
            if STEP[i, 1] != 0:
                side = 0 if STEP[i, 1] == 1 else 1
                row = entering(side, ENTER[1][side].index(i))[z : z + 1]
                y = 0 if side == 0 else rows - 1
                value = jnp.where(
                    iota((rows, width), 0) == y,
                    jnp.broadcast_to(row, (rows, width)),
                    turn(value, STEP[i, 1], 0),
                )
            n = group * 5 + k
            planes[n] = value
            leave(planes.at[n], out_ref.at[i, z])
    for group in range(2):
        first = 0 if group == 0 else rows - 8
        for k, i in enumerate(ENTER[1][group]):
            n = group * 5 + k
            step = int(STEP[i, 2])
            half = lower_ref.shape[1]
            tiles[n, 1 + step : 1 + step + half] = lower_ref[n]
            tiles[n, 1 + step + half : 1 + step + depth] = upper_ref[n]
            tiles[n, 1 : 1 + depth, 0 if group == 0 else 7, :] = entering(group, k)
            low, high = max(step, 0), min(depth + step, depth)
            leave(tiles.at[n, 1 + low : 1 + high], out_ref.at[i, low:high, first : first + 8])

    count = target_ref.shape[1]
    target = target_ref[...]
    if n_rows == 1:
        own_ref, far_ref = drag_refs
        slabs, cols, _ = shape
        at, tail = 10 * depth, 5 * rows
        came = [
            entered_z(first_ref, second_ref, side, slice(tail, tail + 8)) for side in range(2)
        ]
        direct = jnp.concatenate([own_ref[0], came[1], far_ref[...], came[0]], axis=0)
        passed = row_refs[0][at : at + 8 * slabs]
        table = jnp.where(iota(direct.shape, 1) < CAP, direct, passed)
        owner = lax.shift_right_logical(target, 5)
        slot = target - owner * CAP
        owner_slab = lax.shift_right_logical(owner, cols.bit_length() - 1)
        away_col = owner - owner_slab * cols - lax.axis_index("col")
        away_col = jnp.where(away_col < 0, away_col + cols, away_col)
        away_slab = owner_slab - lax.axis_index("slab")
        away_slab = jnp.where(away_slab < 0, away_slab + slabs, away_slab)
        choose = (iota((128, count), 0) == away_col * CAP + slot).astype(F32).astype(BF16)
        picked = dot_select(table, choose, NN)
        total = jnp.where(away_slab == 0, picked[0:8], 0.0)
        for dz in range(1, slabs):
            total = total + jnp.where(away_slab == dz, picked[8 * dz : 8 * dz + 8], 0.0)
        bead_ref[...] = total[0:3]
    else:
        back_ref = drag_refs[0]

        def group(k, total):
            got = [back_ref[k * GROUP + r] for r in range(GROUP)]
            slots = jnp.concatenate([t[:, 0:CAP] for t in got], axis=1)
            first = k * (GROUP * CAP)
            choose = (iota((GROUP * CAP, count), 0) + first == target).astype(F32)
            return total + dot_select(slots, choose.astype(BF16), NN)

        total = lax.fori_loop(
            0, back_ref.shape[0] // GROUP, group, jnp.zeros((8, count), F32)
        )
        bead_ref[...] = total[0:3]
    for copy in copies:
        copy.wait()


def finish(shape, whole, target, lower, upper, first, second, entered, drags):
    _, depth, rows, width = whole.shape
    vmem = pl.BlockSpec(memory_space=pltpu.VMEM)
    hbm = pl.BlockSpec(memory_space=pltpu.HBM)
    args = [whole, target, lower, upper, first, second, *entered, *drags]
    return pl.pallas_call(
        functools.partial(finish_kernel, shape, len(entered)),
        out_shape=[
            jax.ShapeDtypeStruct(whole.shape, F32),
            jax.ShapeDtypeStruct((3, target.shape[1]), F32),
        ],
        in_specs=[hbm] + [vmem] * (len(args) - 1),
        out_specs=[hbm, vmem],
        scratch_shapes=[
            pltpu.VMEM((10, rows, width), F32),
            pltpu.VMEM((10, depth + 2, 8, width), F32),
            pltpu.SemaphoreType.DMA((20,)),
        ],
        input_output_aliases={0: 0},
        compiler_params=pltpu.CompilerParams(vmem_limit_bytes=ROOM),
        name="finish",
    )(*args)


def shards(populations, solid_mask, bead_owner, bead_base, bead_offset, bead_velocity):
    slabs, cols, pairs = shape = tuple(lax.axis_size(a) for a in ("slab", "col", "pair"))
    owners = slabs * cols
    depth, rows = populations.shape[1:3]
    single = owners == GROUP and slabs == 4
    swap = functools.partial(
        lax.all_to_all, axis_name=("slab", "col"), split_axis=0, concat_axis=0, tiled=True
    )

    target, messages = pack(owners, bead_owner, bead_base, bead_offset, bead_velocity)
    messages = swap(messages)
    flow, columns, sides, walls = moments(populations, solid_mask)
    force, face, drag, *far = couple(shape, messages, flow, columns, depth, rows)
    face = send(face, shape, lambda s, c, p: (s, c, (p + 1) % pairs))
    if single:
        far = send(far[0], shape, lambda s, c, p: ((s + 2) % slabs, c, p))
    else:
        drag = swap(drag)
    first, second, draft, token = faces(
        single, force, populations, solid_mask, sides, walls, face, drag
    )
    first, second = send_slab(first, shape, 0), send_slab(second, shape, 1)
    fields = (populations, solid_mask, force, face)
    whole, lower, token = stream(0, depth // 2, token, None, *fields)
    drags = [drag, far] if single else []
    *leaving, token = leaving_rows(shape, depth, rows, token, draft, first, second, drags)
    entered = [
        send(value, shape, lambda s, c, p, sign=sign: (s, (c + sign) % cols, p))
        for value, sign in zip(leaving, (1, -1))
    ]
    whole, upper, _ = stream(depth // 2, depth, token, whole, *fields)
    return tuple(
        finish(shape, whole, target, lower, upper, first, second, entered, drags or [drag])
    )


def solution(mesh):
    return jax.shard_map(
        shards,
        mesh=mesh,
        in_specs=(
            P(None, ("rep", "slab"), "col", "pair"),
            P(("rep", "slab"), "col", "pair"),
            P(("rep", "slab", "col", "pair")),
            P(None, ("rep", "slab", "col", "pair")),
            P(None, ("rep", "slab", "col", "pair")),
            P(None, ("rep", "slab", "col", "pair")),
        ),
        out_specs=(
            P(None, ("rep", "slab"), "col", "pair"),
            P(None, ("rep", "slab", "col", "pair")),
        ),
        check_vma=False,
    )
```

```python
import functools

import jax
import jax.numpy as jnp
import numpy as np
from jax import lax
from jax.experimental import pallas as pl
from jax.experimental.pallas import tpu as pltpu
from jax.sharding import PartitionSpec as P

CAP = 32
GROUP = 8

STEP = np.array(
    [
        [0, 0, 0],
        [1, 0, 0],
        [-1, 0, 0],
        [0, 1, 0],
        [0, -1, 0],
        [0, 0, 1],
        [0, 0, -1],
        [1, 1, 0],
        [-1, -1, 0],
        [1, -1, 0],
        [-1, 1, 0],
        [1, 0, 1],
        [-1, 0, -1],
        [1, 0, -1],
        [-1, 0, 1],
        [0, 1, 1],
        [0, -1, -1],
        [0, 1, -1],
        [0, -1, 1],
    ],
    np.int32,
)
TAU_PLUS = 0.8
TAU_MINUS = 0.5 + (3.0 / 16.0) / (TAU_PLUS - 0.5)
KEEP_EVEN = 1.0 - 1.0 / TAU_PLUS
KEEP_ODD = 1.0 - 1.0 / TAU_MINUS
FORCE_GAIN = 1.0 - 0.5 / TAU_PLUS
DRAG_COEF = 2.0
F32 = jnp.float32
BF16 = jnp.bfloat16

ENTER = [[[i for i in range(19) if STEP[i, a] == sign] for sign in (1, -1)] for a in range(3)]
TOKEN = jax.ShapeDtypeStruct((8, 128), F32)
ROOM = 16 << 20
NT = (((1,), (1,)), ((), ()))
NN = (((1,), (0,)), ((), ()))


def iota(shape, dim):
    return lax.broadcasted_iota(jnp.int32, shape, dim)


def high_low(value):
    high = value.astype(BF16)
    return high, (value - high.astype(F32)).astype(BF16)


def dot_split(left, right, dims):
    (a, b), (c, d) = left, right
    mul = functools.partial(lax.dot_general, dimension_numbers=dims, preferred_element_type=F32)
    return mul(a, c) + (mul(a, d) + mul(b, c))


def dot_select(value, choose, dims):
    first = value.astype(BF16).astype(F32)
    rest = value - first
    second = rest.astype(BF16).astype(F32)
    stacked = jnp.concatenate([first, second, rest - second], axis=0).astype(BF16)
    got = lax.dot_general(stacked, choose, dimension_numbers=dims, preferred_element_type=F32)
    rows = value.shape[0]
    return got[0:rows] + got[rows : 2 * rows] + got[2 * rows : 3 * rows]


def density_momentum(pops):
    momentum = []
    for axis in range(3):
        plus = [pops[i] for i in range(19) if STEP[i, axis] == 1]
        minus = [pops[i] for i in range(19) if STEP[i, axis] == -1]
        momentum.append(sum(plus[1:], plus[0]) - sum(minus[1:], minus[0]))
    return sum(pops[1:], pops[0]), momentum


def along(step, vector):
    terms = None
    for axis in range(3):
        if step[axis] == 0:
            continue
        if terms is None:
            terms = vector[axis] if step[axis] == 1 else -vector[axis]
        else:
            terms = terms + vector[axis] if step[axis] == 1 else terms - vector[axis]
    return terms


def collide(pops, wall, force):
    density, momentum = density_momentum(pops)
    inverse = 1.0 / density
    carried = [m + 0.5 * f for m, f in zip(momentum, force)]
    speed = [m * inverse for m in carried]
    w = 1.0 / 36.0
    bend = [(4.5 * w / TAU_PLUS) * m + (9.0 * w * FORCE_GAIN) * f for m, f in zip(carried, force)]
    push = [(3.0 * w / TAU_MINUS) * m + (3.0 * w * FORCE_GAIN) * f for m, f in zip(carried, force)]
    drop = [(1.5 * w / TAU_PLUS) * m + (3.0 * w * FORCE_GAIN) * f for m, f in zip(carried, force)]
    rest = (w / TAU_PLUS) * density - sum(
        [u * d for u, d in zip(speed[1:], drop[1:])], speed[0] * drop[0]
    )
    out = [None] * 19
    out[0] = jnp.where(wall, pops[0], KEEP_EVEN * pops[0] + 12.0 * rest)
    for i in range(1, 19, 2):
        a, b = pops[i], pops[i + 1]
        step = STEP[i]
        even = rest + along(step, speed) * along(step, bend)
        odd = along(step, push)
        if i < 7:
            even = even + even
            odd = odd + odd
        even = (0.5 * KEEP_EVEN) * (a + b) + even
        odd = (0.5 * KEEP_ODD) * (a - b) + odd
        out[i] = jnp.where(wall, b, even + odd)
        out[i + 1] = jnp.where(wall, a, even - odd)
    return out


def turn(value, amount, axis):
    if amount == 0:
        return value
    return pltpu.roll(value, int(amount) % value.shape[axis], axis)


def send(value, shape, target):
    def flat(at):
        return (at[0] * shape[1] + at[1]) * shape[2] + at[2]

    perm = [(flat(at), flat(target(*at))) for at in np.ndindex(*shape)]
    return lax.ppermute(value, ("slab", "col", "pair"), perm)


def send_slab(value, shape, which):
    def target(s, c, p):
        return ((s + (1 if s % 2 == which else -1)) % shape[0], c, p)

    return send(value, shape, target)


def even_slab():
    return lax.rem(lax.axis_index("slab"), 2) == 0


def rank_among(member):
    count = member.shape[1]
    earlier = (iota((count, count), 0) < iota((count, count), 1)).astype(F32).astype(BF16)
    return lax.dot_general(member.astype(BF16), earlier, NN, preferred_element_type=F32)


def spread_column(tile, lane):
    return jnp.broadcast_to(tile[:, lane : lane + 1], tile.shape)


def patch_x(value, i, column):
    side = 0 if STEP[i, 0] == 1 else value.shape[1] - 1
    return jnp.where(iota(value.shape, 1) == side, column, value)


def x_place(i):
    group = 0 if STEP[i, 0] == 1 else 1
    place = ENTER[0][group].index(i)
    return place // 4, (place % 4) * 32 + group


def x_ends(planes):
    lane = lax.shift_right_logical(iota(planes[0].shape, 1), 1)
    tile = jnp.ones(planes[0].shape, F32)
    for z, value in enumerate(planes):
        tile = jnp.where(lane == z, pltpu.roll(value, 2 * z + 1, 1), tile)
    return tile


def pack_kernel(
    steps, owner_ref, base_ref, offset_ref, velocity_ref, target_ref, out_ref, table
):
    count = owner_ref.shape[1]
    step = 0 if steps == 1 else pl.program_id(0)
    local = owner_ref[...] - step * GROUP
    member = (iota((GROUP, count), 0) == local).astype(F32)
    rank = jnp.sum(member * rank_among(member), axis=0, keepdims=True).astype(jnp.int32)
    inside = (local >= 0) & (local < GROUP)
    target = jnp.where(inside, local * CAP + rank, -1)
    whole_target = jnp.where(inside, owner_ref[...] * CAP + rank, -1)

    if steps == 1:
        target_ref[...] = whole_target
    else:
        known = jnp.where(step == 0, -1, target_ref[...])
        target_ref[...] = jnp.maximum(known, whole_target)

    choose = (iota((GROUP * CAP, count), 0) == target).astype(F32).astype(BF16)
    table[...] = jnp.zeros_like(table)
    table[0:3] = base_ref[...].astype(F32) + 1.0
    table[8:11] = offset_ref[...]
    table[16:19] = velocity_ref[...]
    packed = dot_select(table[...], choose, NT)
    blank = jnp.zeros((8, CAP), F32)
    for r in range(GROUP):
        lanes = slice(r * CAP, (r + 1) * CAP)
        out_ref[r] = jnp.concatenate(
            [packed[0:8, lanes], packed[8:16, lanes], packed[16:24, lanes], blank], axis=1
        )


def pack(owners, owner, base, offset, velocity):
    count, steps = owner.shape[0], owners // GROUP
    args = (owner.reshape(1, count), base, offset, velocity)
    blocks = {}
    if steps > 1:
        blocks = dict(
            grid=(steps,),
            in_specs=[pl.BlockSpec(a.shape, lambda k: (0, 0)) for a in args],
            out_specs=[
                pl.BlockSpec((1, count), lambda k: (0, 0)),
                pl.BlockSpec((GROUP, 8, 128), lambda k: (k, 0, 0)),
            ],
            compiler_params=pltpu.CompilerParams(vmem_limit_bytes=48 << 20),
        )
    return pl.pallas_call(
        functools.partial(pack_kernel, steps),
        out_shape=[
            jax.ShapeDtypeStruct((1, count), jnp.int32),
            jax.ShapeDtypeStruct((owners, 8, 128), F32),
        ],
        scratch_shapes=[pltpu.VMEM((24, count), F32)],
        name="pack",
        **blocks,
    )(*args)


def moments_kernel(
    pops_ref, solid_ref, high_ref, low_ref, column_ref, side_ref, wall_ref, held, held_solid, sem
):
    depth, rows, width = pops_ref.shape[1:]
    chunks = 4
    span = depth // chunks
    copies = [pltpu.make_async_copy(solid_ref, held_solid, sem.at[chunks])]
    for k in range(chunks):
        part = pl.ds(k * span, span)
        copies.append(
            pltpu.make_async_copy(pops_ref.at[:, part], held.at[:, part], sem.at[k])
        )
    for copy in copies:
        copy.start()

    def plane(z, carry):
        pops = [held[i, z] for i in range(19)]
        density, momentum = density_momentum(pops)
        inverse = 1.0 / density
        for axis in range(3):
            at = pl.ds(pl.multiple_of(axis * depth * rows + z * rows, rows), rows)
            high_ref[at], low_ref[at] = high_low(momentum[axis] * inverse)
        return carry

    for k in range(chunks):
        copies[1 + k].wait()
        lax.fori_loop(k * span, (k + 1) * span, plane, 0, unroll=2)
    copies[0].wait()
    for i in range(19):
        column_ref[i] = x_ends([held[i, z] for z in range(depth)])
        side_ref[i, 0] = held[i, :, 0, :]
        side_ref[i, 1] = held[i, :, rows - 1, :]
    wall_ref[0] = held_solid[:, 0, :]
    wall_ref[1] = held_solid[:, rows - 1, :]
    column_ref[19] = x_ends([held_solid[z].astype(F32) for z in range(depth)])


def moments(pops, solid):
    _, depth, rows, width = pops.shape
    hbm = pl.BlockSpec(memory_space=pltpu.HBM)
    return pl.pallas_call(
        moments_kernel,
        out_shape=[
            jax.ShapeDtypeStruct((3 * depth * rows, width), BF16),
            jax.ShapeDtypeStruct((3 * depth * rows, width), BF16),
            jax.ShapeDtypeStruct((20, rows, 128), F32),
            jax.ShapeDtypeStruct((19, 2, depth, width), F32),
            jax.ShapeDtypeStruct((2, depth, width), jnp.int32),
        ],
        in_specs=[hbm, hbm],
        scratch_shapes=[
            pltpu.VMEM(pops.shape, F32),
            pltpu.VMEM(solid.shape, jnp.int32),
            pltpu.SemaphoreType.DMA((5,)),
        ],
        compiler_params=pltpu.CompilerParams(vmem_limit_bytes=54000000),
        cost_estimate=pl.CostEstimate(flops=3000000, bytes_accessed=4000000, transcendentals=0),
        name="moments",
    )(pops, solid)


def unpack(tiles):
    return [
        jnp.concatenate([t[:, g * CAP : (g + 1) * CAP] for t in tiles], axis=1) for g in range(3)
    ]


def couple_group(base, part, velocity, flow, depth, rows):
    width, slots = flow[0].shape[1], GROUP * CAP
    start = base.astype(jnp.int32) - 1

    def hat(axis, length):
        cell = iota((length, slots), 0)
        low, share = start[axis : axis + 1], part[axis : axis + 1]
        return jnp.where(cell == low, 1.0 - share, 0.0) + jnp.where(cell == low + 1, share, 0.0)

    hat_x, hat_y, hat_z = high_low(hat(0, width)), hat(1, rows), hat(2, depth)
    weight = (hat_z[:, None, :] * hat_y[None, :, :]).reshape(depth * rows, slots)
    across = dot_split(flow, hat_x, NN)
    cells = depth * rows
    sampled = [
        jnp.sum(across[d * cells : (d + 1) * cells] * weight, axis=0, keepdims=True)
        for d in range(3)
    ]
    drag = [DRAG_COEF * (sampled[d] - velocity[d : d + 1]) for d in range(3)]
    spread = jnp.concatenate([weight * (-drag[d]) for d in range(3)], axis=0)
    return drag, dot_split(high_low(spread), hat_x, NT)


def couple_kernel(shape, depth, rows, beads_ref, high_ref, low_ref, *refs):
    slabs, cols, _ = shape
    column_ref, force_ref, face_ref, *drag_refs = refs
    width = high_ref.shape[1]
    flow = (high_ref[...], low_ref[...])
    hollow = jnp.zeros((5, GROUP * CAP), F32)

    if len(drag_refs) == 2:
        slab, col = lax.axis_index("slab"), lax.axis_index("col")
        got = []
        for r in range(GROUP):
            there = [a - b for a, b in zip((slab, col), divmod(r, cols))]
            there = [jnp.where(a < 0, a + n, a) for a, n in zip(there, (slabs, cols))]
            got.append(beads_ref[there[0] * cols + there[1]])
        drag, force = couple_group(*unpack(got), flow, depth, rows)
        force_ref[...] = force.reshape(3, depth, rows, width)
        stacked = jnp.concatenate(drag + [hollow], axis=0)
        lanes = cols * CAP
        blank = jnp.zeros((8, 128 - lanes), F32)
        for dz in range(slabs):
            tile = jnp.concatenate([stacked[:, dz * lanes : (dz + 1) * lanes], blank], axis=1)
            drag_refs[0][dz] = tile
            if dz == 2:
                drag_refs[1][...] = tile
    else:
        force_ref[...] = jnp.zeros_like(force_ref)
        blank = jnp.zeros((8, 128 - CAP), F32)

        def group(k, carry):
            got = [beads_ref[k * GROUP + r] for r in range(GROUP)]
            drag, force = couple_group(*unpack(got), flow, depth, rows)
            force_ref[...] += force.reshape(3, depth, rows, width)
            stacked = jnp.concatenate(drag + [hollow], axis=0)
            for r in range(GROUP):
                drag_refs[0][k * GROUP + r] = jnp.concatenate(
                    [stacked[:, r * CAP : (r + 1) * CAP], blank], axis=1
                )
            return carry

        lax.fori_loop(0, beads_ref.shape[0] // GROUP, group, 0)

    force = [x_ends([force_ref[d, z] for z in range(depth)]) for d in range(3)]
    out = collide([column_ref[i] for i in range(19)], column_ref[19] == 1.0, force)
    high = lax.rem(iota((rows, 128), 1), 2) == 0
    ends = [jnp.where(high, out[i], out[j])[:, 0:32] for i, j in zip(*ENTER[0])]
    face_ref[0] = jnp.concatenate(ends[0:4], axis=1)
    face_ref[1] = jnp.concatenate([ends[4], jnp.zeros((rows, 96), F32)], axis=1)


def couple(shape, beads, flow, columns, depth, rows):
    width = flow[0].shape[1]
    single = beads.shape[0] == GROUP
    tile = jax.ShapeDtypeStruct((8, 128), F32)
    drags = [jax.ShapeDtypeStruct((shape[0], 8, 128), F32), tile] if single else [beads]
    return pl.pallas_call(
        functools.partial(couple_kernel, shape, depth, rows),
        out_shape=[
            jax.ShapeDtypeStruct((3, depth, rows, width), F32),
            jax.ShapeDtypeStruct((2, rows, 128), F32),
        ]
        + [jax.ShapeDtypeStruct(d.shape, F32) for d in drags],
        compiler_params=pltpu.CompilerParams(vmem_limit_bytes=ROOM),
        name="couple",
    )(beads, *flow, columns)


def faces_kernel(force_ref, pops_ref, solid_ref, side_ref, wall_ref, leaving_ref, draft_ref, token_ref):
    depth, rows, width = force_ref.shape[1:]
    token_ref[...] = jnp.zeros_like(token_ref)
    for side in range(4):
        first = side % 2 == 0
        group = 1 if first else 0
        if side < 2:
            z = 0 if first else depth - 1
            force = [force_ref[d, z] for d in range(3)]
            pops, wall = [pops_ref[i, z] for i in range(19)], solid_ref[z]
        else:
            force = [force_ref[d, :, 0 if first else rows - 1, :] for d in range(3)]
            pops, wall = [side_ref[i, side - 2] for i in range(19)], wall_ref[side - 2]
        out = collide(pops, wall == 1, force)
        for k, i in enumerate(ENTER[2 if side < 2 else 1][group]):
            value = turn(out[i], STEP[i, 0], 1)
            if side < 2:
                leaving_ref[group, k * rows : (k + 1) * rows] = value
            else:
                row = (group * 5 + k) * depth
                draft_ref[row : row + depth] = turn(value, STEP[i, 2], 0)


def faces(force, pops, solid, sides, walls):
    _, depth, rows, width = force.shape
    return pl.pallas_call(
        faces_kernel,
        out_shape=[
            jax.ShapeDtypeStruct((2, 5 * rows, width), F32),
            jax.ShapeDtypeStruct((10 * depth, width), F32),
            TOKEN,
        ],
        compiler_params=pltpu.CompilerParams(vmem_limit_bytes=ROOM),
        name="faces",
    )(force, pops, solid, sides, walls)


def planes_kernel(depth, rows, leaving_ref, face_ref, drag_ref, first_ref, second_ref, token_ref):
    width = leaving_ref.shape[2]
    token_ref[...] = jnp.zeros_like(token_ref)
    tiles = [face_ref[0], face_ref[1]]
    even = even_slab()
    for k in range(5):
        at = slice(k * rows, (k + 1) * rows)
        both = []
        for group in range(2):
            i = ENTER[2][group][k]
            value = leaving_ref[group, at]
            if STEP[i, 0] != 0:
                tile, lane = x_place(i)
                z = depth - 1 if group == 0 else 0
                value = patch_x(value, i, spread_column(tiles[tile], lane + 2 * z))
            both.append(value)
        first_ref[at] = jnp.where(even, both[0], both[1])
        second_ref[at] = jnp.where(even, both[1], both[0])
    if first_ref.shape[0] > 5 * rows:
        up, down = drag_ref[drag_ref.shape[0] - 1], drag_ref[1]
        first_ref[5 * rows : 5 * rows + 8] = jnp.where(even, up, down)
        second_ref[5 * rows : 5 * rows + 8] = jnp.where(even, down, up)


def planes(single, rows, depth, leaving, face, drag):
    message = jax.ShapeDtypeStruct((5 * rows + (8 if single else 0), leaving.shape[2]), F32)
    return pl.pallas_call(
        functools.partial(planes_kernel, depth, rows),
        out_shape=[message, message, TOKEN],
        compiler_params=pltpu.CompilerParams(vmem_limit_bytes=ROOM),
        name="planes",
    )(leaving, face, drag)


def entered_z(first_ref, second_ref, side, rows):
    even = even_slab() if side == 0 else jnp.logical_not(even_slab())
    return jnp.where(even, second_ref[rows], first_ref[rows])


def rows_kernel(depth, rows, before_ref, draft_ref, face_ref, first_ref, second_ref, *refs):
    refs, token_ref, turned = refs[:-2], refs[-2], refs[-1]
    token_ref[...] = jnp.zeros_like(token_ref)
    outs = refs[-1:] if len(refs) == 3 else refs
    for n in range(2):
        turned[n] = face_ref[n].T
    for group in range(2):
        out_ref = outs[0] if len(outs) == 1 else outs[group]
        base = group * 5 * depth if len(outs) == 1 else 0
        y = rows - 1 if group == 0 else 0
        for k, i in enumerate(ENTER[1][group]):
            at = base + k * depth
            value = draft_ref[(group * 5 + k) * depth : (group * 5 + k + 1) * depth]
            if STEP[i, 0] != 0:
                tile, lane = x_place(i)
                column = turned[tile, pl.ds(lane, depth, stride=2), :][:, y : y + 1]
                value = patch_x(value, i, jnp.broadcast_to(column, value.shape))
            out_ref[at : at + depth] = value
            if STEP[i, 2] != 0:
                side = 0 if STEP[i, 2] == 1 else 1
                z = 0 if side == 0 else depth - 1
                row = ENTER[2][side].index(i) * rows + y
                out_ref[at + z : at + z + 1] = entered_z(
                    first_ref, second_ref, side, slice(row, row + 1)
                )
    if len(refs) == 3:
        own_ref, far_ref, out_ref = refs
        came = arrived_drag(own_ref, far_ref, first_ref, second_ref, 5 * rows)
        out_ref[10 * depth : 10 * depth + 8] = one_tile(came, 1)


def arrived_drag(own_ref, far_ref, first_ref, second_ref, tail):
    at = slice(tail, tail + 8)
    up, down = [entered_z(first_ref, second_ref, side, at) for side in range(2)]
    return [own_ref[0], down, far_ref[...], up]


def one_tile(tiles, col):
    return jnp.concatenate([t[:, col * CAP : (col + 1) * CAP] for t in tiles], axis=1)


def leaving_rows(depth, rows, before, draft, face, first, second, drags):
    width = draft.shape[1]
    if drags:
        sizes = [10 * depth + 8]
    else:
        sizes = [5 * depth] * 2
    args = (draft, face, first, second, *drags)
    return pl.pallas_call(
        functools.partial(rows_kernel, depth, rows),
        out_shape=[jax.ShapeDtypeStruct((n, width), F32) for n in sizes] + [TOKEN],
        in_specs=[pl.BlockSpec(memory_space=pl.ANY)]
        + [pl.BlockSpec(memory_space=pltpu.VMEM)] * len(args),
        scratch_shapes=[pltpu.VMEM((2, 128, rows), F32)],
        compiler_params=pltpu.CompilerParams(vmem_limit_bytes=ROOM),
        name="rows",
    )(before, *args)


def stream_kernel(low, high, before_ref, *refs):
    if low > 0:
        refs = refs[1:]
    pops_ref, solid_ref, force_ref, face_ref, out_ref, tile_ref, token_ref, held, sem = refs
    depth, rows, width = pops_ref.shape[1:]
    token_ref[...] = jnp.zeros_like(token_ref)
    chunks = 2
    span = (high - low) // chunks

    def plane(z, faces):
        out = collide(
            [pops_ref[i, z] for i in range(19)],
            solid_ref[z] == 1,
            [force_ref[d, z] for d in range(3)],
        )
        for i in range(19):
            value = out[i]
            if STEP[i, 0] != 0:
                tile, lane = x_place(i)
                value = turn(value, STEP[i, 0], 1)
                value = patch_x(value, i, spread_column(faces[tile], lane))
            held[i, z - low] = turn(value, STEP[i, 1], 0)
        return tuple(pltpu.roll(f, 126, 1) for f in faces)

    runs = [(0, 5), (5, 6), (6, 7), (7, 11)] + [(i, i + 1) for i in range(11, 19)]
    copies = []
    carry = (face_ref[0], face_ref[1])
    if low > 0:
        carry = tuple(pltpu.roll(f, 128 - 2 * low, 1) for f in carry)
    for k in range(chunks):
        first = low + k * span
        carry = lax.fori_loop(first, first + span, plane, carry, unroll=2)
        for n, (a, b) in enumerate(runs):
            step = int(STEP[a, 2])
            start, stop = max(first + step, 0), min(first + span + step, depth)
            copy = pltpu.make_async_copy(
                held.at[a:b, start - step - low : stop - step - low],
                out_ref.at[a:b, start:stop],
                sem.at[k, n],
            )
            copy.start()
            copies.append(copy)
    for group in range(2):
        first = 0 if group == 0 else rows - 8
        for k, i in enumerate(ENTER[1][group]):
            tile_ref[group * 5 + k] = held[i, :, first : first + 8, :]
    for copy in copies:
        copy.wait()


def stream(low, high, before, whole, pops, solid, force, face):
    _, depth, rows, width = pops.shape
    vmem = pl.BlockSpec(memory_space=pltpu.VMEM)
    hbm = pl.BlockSpec(memory_space=pltpu.HBM)
    whole = [] if whole is None else [whole]
    return pl.pallas_call(
        functools.partial(stream_kernel, low, high),
        out_shape=[
            jax.ShapeDtypeStruct(pops.shape, F32),
            jax.ShapeDtypeStruct((10, high - low, 8, width), F32),
            TOKEN,
        ],
        in_specs=[pl.BlockSpec(memory_space=pl.ANY)] + [hbm] * len(whole) + [vmem] * 4,
        out_specs=[hbm, vmem, vmem],
        scratch_shapes=[
            pltpu.VMEM((19, high - low, rows, width), F32),
            pltpu.SemaphoreType.DMA((2, 12)),
        ],
        input_output_aliases={1: 0} if whole else {},
        compiler_params=pltpu.CompilerParams(vmem_limit_bytes=ROOM),
        cost_estimate=pl.CostEstimate(flops=5000000, bytes_accessed=3000000, transcendentals=0),
        name="stream",
    )(before, *whole, pops, solid, force, face)


def finish_kernel(
    shape, n_rows, whole_ref, target_ref, lower_ref, upper_ref, first_ref, second_ref, *refs
):
    row_refs, refs = refs[:n_rows], refs[n_rows:]
    drag_refs, (out_ref, bead_ref, planes, tiles, bead, sem) = refs[:-6], refs[-6:]
    depth, rows, width = whole_ref.shape[1:]

    def entering(group, k):
        if n_rows == 1:
            at = (group * 5 + k) * depth
            return row_refs[0][at : at + depth]
        return row_refs[group][k * depth : (k + 1) * depth]

    copies = []

    def leave(source, target):
        copy = pltpu.make_async_copy(source, target, sem.at[len(copies)])
        copy.start()
        copies.append(copy)

    for group in range(2):
        z = 0 if group == 0 else depth - 1
        for k, i in enumerate(ENTER[2][group]):
            value = entered_z(first_ref, second_ref, group, slice(k * rows, (k + 1) * rows))
            if STEP[i, 1] != 0:
                side = 0 if STEP[i, 1] == 1 else 1
                row = entering(side, ENTER[1][side].index(i))[z : z + 1]
                y = 0 if side == 0 else rows - 1
                value = jnp.where(
                    iota((rows, width), 0) == y,
                    jnp.broadcast_to(row, (rows, width)),
                    turn(value, STEP[i, 1], 0),
                )
            n = group * 5 + k
            planes[n] = value
            leave(planes.at[n], out_ref.at[i, z])
    for group in range(2):
        first = 0 if group == 0 else rows - 8
        for k, i in enumerate(ENTER[1][group]):
            n = group * 5 + k
            step = int(STEP[i, 2])
            half = lower_ref.shape[1]
            tiles[n, 1 + step : 1 + step + half] = lower_ref[n]
            tiles[n, 1 + step + half : 1 + step + depth] = upper_ref[n]
            tiles[n, 1 : 1 + depth, 0 if group == 0 else 7, :] = entering(group, k)
            low, high = max(step, 0), min(depth + step, depth)
            leave(tiles.at[n, 1 + low : 1 + high], out_ref.at[i, low:high, first : first + 8])

    count = target_ref.shape[1]
    target = target_ref[...]
    if n_rows == 1:
        slabs, cols, _ = shape
        came = arrived_drag(*drag_refs, first_ref, second_ref, 5 * rows)
        passed = row_refs[0][10 * depth : 10 * depth + 8]
        table = jnp.concatenate([one_tile(came, 0), passed], axis=1)
        owner = lax.shift_right_logical(target, 5)
        owner_slab = lax.shift_right_logical(owner, cols.bit_length() - 1)
        away_col = owner - owner_slab * cols - lax.axis_index("col")
        away_col = jnp.where(away_col < 0, away_col + cols, away_col)
        away_slab = owner_slab - lax.axis_index("slab")
        away_slab = jnp.where(away_slab < 0, away_slab + slabs, away_slab)
        place = away_col * 128 + away_slab * CAP + target - owner * CAP
        choose = (iota((256, count), 0) == place).astype(F32).astype(BF16)
        total = dot_select(table, choose, NN)
    else:
        back_ref = drag_refs[0]

        def group(k, total):
            got = [back_ref[k * GROUP + r] for r in range(GROUP)]
            slots = jnp.concatenate([t[:, 0:CAP] for t in got], axis=1)
            first = k * (GROUP * CAP)
            choose = (iota((GROUP * CAP, count), 0) + first == target).astype(F32)
            return total + dot_select(slots, choose.astype(BF16), NN)

        total = lax.fori_loop(
            0, back_ref.shape[0] // GROUP, group, jnp.zeros((8, count), F32)
        )
    bead[...] = total[0:3]
    leave(bead, bead_ref)
    for copy in copies:
        copy.wait()


def finish(shape, whole, target, lower, upper, first, second, entered, drags):
    _, depth, rows, width = whole.shape
    vmem = pl.BlockSpec(memory_space=pltpu.VMEM)
    hbm = pl.BlockSpec(memory_space=pltpu.HBM)
    args = [whole, target, lower, upper, first, second, *entered, *drags]
    return pl.pallas_call(
        functools.partial(finish_kernel, shape, len(entered)),
        out_shape=[
            jax.ShapeDtypeStruct(whole.shape, F32),
            jax.ShapeDtypeStruct((3, target.shape[1]), F32),
        ],
        in_specs=[hbm] + [vmem] * (len(args) - 1),
        out_specs=[hbm, hbm],
        scratch_shapes=[
            pltpu.VMEM((10, rows, width), F32),
            pltpu.VMEM((10, depth + 2, 8, width), F32),
            pltpu.VMEM((3, target.shape[1]), F32),
            pltpu.SemaphoreType.DMA((21,)),
        ],
        input_output_aliases={0: 0},
        compiler_params=pltpu.CompilerParams(vmem_limit_bytes=ROOM),
        name="finish",
    )(*args)


def shards(populations, solid_mask, bead_owner, bead_base, bead_offset, bead_velocity):
    slabs, cols, pairs = shape = tuple(lax.axis_size(a) for a in ("slab", "col", "pair"))
    owners = slabs * cols
    depth, rows = populations.shape[1:3]
    single = owners == GROUP and slabs == 4
    swap = functools.partial(
        lax.all_to_all, axis_name=("slab", "col"), split_axis=0, concat_axis=0, tiled=True
    )

    target, messages = pack(owners, bead_owner, bead_base, bead_offset, bead_velocity)
    messages = swap(messages)
    *flow, columns, sides, walls = moments(populations, solid_mask)
    force, face, drag, *far = couple(shape, messages, flow, columns, depth, rows)
    leaving, draft, token = faces(force, populations, solid_mask, sides, walls)
    face = send(face, shape, lambda s, c, p: (s, c, (p + 1) % pairs))
    if single:
        far = send(far[0], shape, lambda s, c, p: ((s + 2) % slabs, c, p))
    else:
        drag = swap(drag)
    first, second, token = planes(single, rows, depth, leaving, face, drag)
    first, second = send_slab(first, shape, 0), send_slab(second, shape, 1)
    fields = (populations, solid_mask, force, face)
    whole, lower, token = stream(0, depth // 2, token, None, *fields)
    drags = [drag, far] if single else []
    *leaving, token = leaving_rows(depth, rows, token, draft, face, first, second, drags)
    entered = [
        send(value, shape, lambda s, c, p, sign=sign: (s, (c + sign) % cols, p))
        for value, sign in zip(leaving, (1, -1))
    ]
    whole, upper, _ = stream(depth // 2, depth, token, whole, *fields)
    return tuple(
        finish(shape, whole, target, lower, upper, first, second, entered, drags or [drag])
    )


def solution(mesh):
    return jax.shard_map(
        shards,
        mesh=mesh,
        in_specs=(
            P(None, ("rep", "slab"), "col", "pair"),
            P(("rep", "slab"), "col", "pair"),
            P(("rep", "slab", "col", "pair")),
            P(None, ("rep", "slab", "col", "pair")),
            P(None, ("rep", "slab", "col", "pair")),
            P(None, ("rep", "slab", "col", "pair")),
        ),
        out_specs=(
            P(None, ("rep", "slab"), "col", "pair"),
            P(None, ("rep", "slab", "col", "pair")),
        ),
        check_vma=False,
    )
```

```python
import functools

import jax
import jax.numpy as jnp
import numpy as np
from jax import lax
from jax.experimental import pallas as pl
from jax.experimental.pallas import tpu as pltpu
from jax.sharding import PartitionSpec as P

CAP = 32
GROUP = 8

STEP = np.array(
    [
        [0, 0, 0],
        [1, 0, 0],
        [-1, 0, 0],
        [0, 1, 0],
        [0, -1, 0],
        [0, 0, 1],
        [0, 0, -1],
        [1, 1, 0],
        [-1, -1, 0],
        [1, -1, 0],
        [-1, 1, 0],
        [1, 0, 1],
        [-1, 0, -1],
        [1, 0, -1],
        [-1, 0, 1],
        [0, 1, 1],
        [0, -1, -1],
        [0, 1, -1],
        [0, -1, 1],
    ],
    np.int32,
)
TAU_PLUS = 0.8
TAU_MINUS = 0.5 + (3.0 / 16.0) / (TAU_PLUS - 0.5)
KEEP_EVEN = 1.0 - 1.0 / TAU_PLUS
KEEP_ODD = 1.0 - 1.0 / TAU_MINUS
FORCE_GAIN = 1.0 - 0.5 / TAU_PLUS
DRAG_COEF = 2.0
F32 = jnp.float32
BF16 = jnp.bfloat16

ENTER = [[[i for i in range(19) if STEP[i, a] == sign] for sign in (1, -1)] for a in range(3)]
TOKEN = jax.ShapeDtypeStruct((8, 128), F32)
ROOM = 16 << 20
NT = (((1,), (1,)), ((), ()))
NN = (((1,), (0,)), ((), ()))


def iota(shape, dim):
    return lax.broadcasted_iota(jnp.int32, shape, dim)


def high_low(value):
    high = value.astype(BF16)
    return high, (value - high.astype(F32)).astype(BF16)


def dot_split(left, right, dims):
    (a, b), (c, d) = left, right
    mul = functools.partial(lax.dot_general, dimension_numbers=dims, preferred_element_type=F32)
    return mul(a, c) + (mul(a, d) + mul(b, c))


def dot_select(value, choose, dims):
    first = value.astype(BF16).astype(F32)
    rest = value - first
    second = rest.astype(BF16).astype(F32)
    stacked = jnp.concatenate([first, second, rest - second], axis=0).astype(BF16)
    got = lax.dot_general(stacked, choose, dimension_numbers=dims, preferred_element_type=F32)
    rows = value.shape[0]
    return got[0:rows] + got[rows : 2 * rows] + got[2 * rows : 3 * rows]


def density_momentum(pops):
    momentum = []
    for axis in range(3):
        plus = [pops[i] for i in range(19) if STEP[i, axis] == 1]
        minus = [pops[i] for i in range(19) if STEP[i, axis] == -1]
        momentum.append(sum(plus[1:], plus[0]) - sum(minus[1:], minus[0]))
    return sum(pops[1:], pops[0]), momentum


def along(step, vector):
    terms = None
    for axis in range(3):
        if step[axis] == 0:
            continue
        if terms is None:
            terms = vector[axis] if step[axis] == 1 else -vector[axis]
        else:
            terms = terms + vector[axis] if step[axis] == 1 else terms - vector[axis]
    return terms


def collide(pops, wall, force):
    density, momentum = density_momentum(pops)
    inverse = 1.0 / density
    carried = [m + 0.5 * f for m, f in zip(momentum, force)]
    speed = [m * inverse for m in carried]
    w = 1.0 / 36.0
    bend = [(4.5 * w / TAU_PLUS) * m + (9.0 * w * FORCE_GAIN) * f for m, f in zip(carried, force)]
    push = [(3.0 * w / TAU_MINUS) * m + (3.0 * w * FORCE_GAIN) * f for m, f in zip(carried, force)]
    drop = [(1.5 * w / TAU_PLUS) * m + (3.0 * w * FORCE_GAIN) * f for m, f in zip(carried, force)]
    rest = (w / TAU_PLUS) * density - sum(
        [u * d for u, d in zip(speed[1:], drop[1:])], speed[0] * drop[0]
    )
    out = [None] * 19
    out[0] = jnp.where(wall, pops[0], KEEP_EVEN * pops[0] + 12.0 * rest)
    for i in range(1, 19, 2):
        a, b = pops[i], pops[i + 1]
        step = STEP[i]
        even = rest + along(step, speed) * along(step, bend)
        odd = along(step, push)
        if i < 7:
            even = even + even
            odd = odd + odd
        even = (0.5 * KEEP_EVEN) * (a + b) + even
        odd = (0.5 * KEEP_ODD) * (a - b) + odd
        out[i] = jnp.where(wall, b, even + odd)
        out[i + 1] = jnp.where(wall, a, even - odd)
    return out


def turn(value, amount, axis):
    if amount == 0:
        return value
    return pltpu.roll(value, int(amount) % value.shape[axis], axis)


def send(value, shape, target):
    def flat(at):
        return (at[0] * shape[1] + at[1]) * shape[2] + at[2]

    perm = [(flat(at), flat(target(*at))) for at in np.ndindex(*shape)]
    return lax.ppermute(value, ("slab", "col", "pair"), perm)


def send_slab(value, shape, which):
    def target(s, c, p):
        return ((s + (1 if s % 2 == which else -1)) % shape[0], c, p)

    return send(value, shape, target)


def even_slab():
    return lax.rem(lax.axis_index("slab"), 2) == 0


def rank_among(member):
    count = member.shape[1]
    earlier = (iota((count, count), 0) < iota((count, count), 1)).astype(F32).astype(BF16)
    return lax.dot_general(member.astype(BF16), earlier, NN, preferred_element_type=F32)


def spread_column(tile, lane):
    return jnp.broadcast_to(tile[:, lane : lane + 1], tile.shape)


def patch_x(value, i, column):
    side = 0 if STEP[i, 0] == 1 else value.shape[1] - 1
    return jnp.where(iota(value.shape, 1) == side, column, value)


def x_place(i):
    group = 0 if STEP[i, 0] == 1 else 1
    place = ENTER[0][group].index(i)
    return place // 4, (place % 4) * 32 + group


def x_ends(planes):
    lane = lax.shift_right_logical(iota(planes[0].shape, 1), 1)
    tile = jnp.ones(planes[0].shape, F32)
    for z, value in enumerate(planes):
        tile = jnp.where(lane == z, pltpu.roll(value, 2 * z + 1, 1), tile)
    return tile


def pack_kernel(
    steps, owner_ref, base_ref, offset_ref, velocity_ref, target_ref, out_ref, table
):
    count = owner_ref.shape[1]
    step = 0 if steps == 1 else pl.program_id(0)
    local = owner_ref[...] - step * GROUP
    member = (iota((GROUP, count), 0) == local).astype(F32)
    rank = jnp.sum(member * rank_among(member), axis=0, keepdims=True).astype(jnp.int32)
    inside = (local >= 0) & (local < GROUP)
    target = jnp.where(inside, local * CAP + rank, -1)
    whole_target = jnp.where(inside, owner_ref[...] * CAP + rank, -1)

    if steps == 1:
        target_ref[...] = whole_target
    else:
        known = jnp.where(step == 0, -1, target_ref[...])
        target_ref[...] = jnp.maximum(known, whole_target)

    choose = (iota((GROUP * CAP, count), 0) == target).astype(F32).astype(BF16)
    table[...] = jnp.zeros_like(table)
    table[0:3] = base_ref[...].astype(F32) + 1.0
    table[8:11] = offset_ref[...]
    table[16:19] = velocity_ref[...]
    packed = dot_select(table[...], choose, NT)
    blank = jnp.zeros((8, CAP), F32)
    for r in range(GROUP):
        lanes = slice(r * CAP, (r + 1) * CAP)
        out_ref[r] = jnp.concatenate(
            [packed[0:8, lanes], packed[8:16, lanes], packed[16:24, lanes], blank], axis=1
        )


def pack(owners, owner, base, offset, velocity):
    count, steps = owner.shape[0], owners // GROUP
    args = (owner.reshape(1, count), base, offset, velocity)
    blocks = {}
    if steps > 1:
        blocks = dict(
            grid=(steps,),
            in_specs=[pl.BlockSpec(a.shape, lambda k: (0, 0)) for a in args],
            out_specs=[
                pl.BlockSpec((1, count), lambda k: (0, 0)),
                pl.BlockSpec((GROUP, 8, 128), lambda k: (k, 0, 0)),
            ],
            compiler_params=pltpu.CompilerParams(vmem_limit_bytes=48 << 20),
        )
    return pl.pallas_call(
        functools.partial(pack_kernel, steps),
        out_shape=[
            jax.ShapeDtypeStruct((1, count), jnp.int32),
            jax.ShapeDtypeStruct((owners, 8, 128), F32),
        ],
        scratch_shapes=[pltpu.VMEM((24, count), F32)],
        name="pack",
        **blocks,
    )(*args)


def moments_kernel(
    pops_ref, solid_ref, high_ref, low_ref, column_ref, side_ref, wall_ref, held, held_solid, sem
):
    depth, rows, width = pops_ref.shape[1:]
    chunks = 4
    span = depth // chunks
    copies = [pltpu.make_async_copy(solid_ref, held_solid, sem.at[chunks])]
    for k in range(chunks):
        part = pl.ds(k * span, span)
        copies.append(
            pltpu.make_async_copy(pops_ref.at[:, part], held.at[:, part], sem.at[k])
        )
    for copy in copies:
        copy.start()

    def plane(z, carry):
        pops = [held[i, z] for i in range(19)]
        density, momentum = density_momentum(pops)
        inverse = 1.0 / density
        for axis in range(3):
            at = pl.ds(pl.multiple_of(axis * depth * rows + z * rows, rows), rows)
            high_ref[at], low_ref[at] = high_low(momentum[axis] * inverse)
        return carry

    for k in range(chunks):
        copies[1 + k].wait()
        lax.fori_loop(k * span, (k + 1) * span, plane, 0, unroll=2)
    copies[0].wait()
    for i in range(19):
        column_ref[i] = x_ends([held[i, z] for z in range(depth)])
        side_ref[i, 0] = held[i, :, 0, :]
        side_ref[i, 1] = held[i, :, rows - 1, :]
    wall_ref[0] = held_solid[:, 0, :]
    wall_ref[1] = held_solid[:, rows - 1, :]
    column_ref[19] = x_ends([held_solid[z].astype(F32) for z in range(depth)])


def moments(pops, solid):
    _, depth, rows, width = pops.shape
    hbm = pl.BlockSpec(memory_space=pltpu.HBM)
    return pl.pallas_call(
        moments_kernel,
        out_shape=[
            jax.ShapeDtypeStruct((3 * depth * rows, width), BF16),
            jax.ShapeDtypeStruct((3 * depth * rows, width), BF16),
            jax.ShapeDtypeStruct((20, rows, 128), F32),
            jax.ShapeDtypeStruct((19, 2, depth, width), F32),
            jax.ShapeDtypeStruct((2, depth, width), jnp.int32),
        ],
        in_specs=[hbm, hbm],
        scratch_shapes=[
            pltpu.VMEM(pops.shape, F32),
            pltpu.VMEM(solid.shape, jnp.int32),
            pltpu.SemaphoreType.DMA((5,)),
        ],
        compiler_params=pltpu.CompilerParams(vmem_limit_bytes=54000000),
        cost_estimate=pl.CostEstimate(flops=3000000, bytes_accessed=4000000, transcendentals=0),
        name="moments",
    )(pops, solid)


def unpack(tiles):
    return [
        jnp.concatenate([t[:, g * CAP : (g + 1) * CAP] for t in tiles], axis=1) for g in range(3)
    ]


def couple_group(base, part, velocity, flow, depth, rows):
    width, slots = flow[0].shape[1], GROUP * CAP
    start = base.astype(jnp.int32) - 1

    def hat(axis, length):
        cell = iota((length, slots), 0)
        low, share = start[axis : axis + 1], part[axis : axis + 1]
        return jnp.where(cell == low, 1.0 - share, 0.0) + jnp.where(cell == low + 1, share, 0.0)

    hat_x, hat_y, hat_z = high_low(hat(0, width)), hat(1, rows), hat(2, depth)
    weight = (hat_z[:, None, :] * hat_y[None, :, :]).reshape(depth * rows, slots)
    across = dot_split(flow, hat_x, NN)
    cells = depth * rows
    sampled = [
        jnp.sum(across[d * cells : (d + 1) * cells] * weight, axis=0, keepdims=True)
        for d in range(3)
    ]
    drag = [DRAG_COEF * (sampled[d] - velocity[d : d + 1]) for d in range(3)]
    spread = jnp.concatenate([weight * (-drag[d]) for d in range(3)], axis=0)
    return drag, dot_split(high_low(spread), hat_x, NT)


def couple_kernel(shape, depth, rows, n_drags, beads_ref, high_ref, low_ref, *refs):
    slabs, cols, _ = shape
    column_ref, pops_ref, solid_ref, force_ref, face_ref, first_ref, second_ref, *refs = refs
    drag_refs, token_ref = refs[:-1], refs[-1]
    token_ref[...] = jnp.zeros_like(token_ref)
    width = high_ref.shape[1]
    flow = (high_ref[...], low_ref[...])
    hollow = jnp.zeros((5, GROUP * CAP), F32)

    if n_drags == 2:
        slab, col = lax.axis_index("slab"), lax.axis_index("col")
        got = []
        for r in range(GROUP):
            there = [a - b for a, b in zip((slab, col), divmod(r, cols))]
            there = [jnp.where(a < 0, a + n, a) for a, n in zip(there, (slabs, cols))]
            got.append(beads_ref[there[0] * cols + there[1]])
        drag, force = couple_group(*unpack(got), flow, depth, rows)
        force_ref[...] = force.reshape(3, depth, rows, width)
        stacked = jnp.concatenate(drag + [hollow], axis=0)
        lanes = cols * CAP
        blank = jnp.zeros((8, 128 - lanes), F32)
        for dz in range(slabs):
            tile = jnp.concatenate([stacked[:, dz * lanes : (dz + 1) * lanes], blank], axis=1)
            drag_refs[0][dz] = tile
            if dz == 2:
                drag_refs[1][...] = tile
            if dz == 1:
                down = tile
        up = tile
    else:
        force_ref[...] = jnp.zeros_like(force_ref)
        blank = jnp.zeros((8, 128 - CAP), F32)

        def group(k, carry):
            got = [beads_ref[k * GROUP + r] for r in range(GROUP)]
            drag, force = couple_group(*unpack(got), flow, depth, rows)
            force_ref[...] += force.reshape(3, depth, rows, width)
            stacked = jnp.concatenate(drag + [hollow], axis=0)
            for r in range(GROUP):
                drag_refs[0][k * GROUP + r] = jnp.concatenate(
                    [stacked[:, r * CAP : (r + 1) * CAP], blank], axis=1
                )
            return carry

        lax.fori_loop(0, beads_ref.shape[0] // GROUP, group, 0)

    force = [x_ends([force_ref[d, z] for z in range(depth)]) for d in range(3)]
    out = collide([column_ref[i] for i in range(19)], column_ref[19] == 1.0, force)
    high = lax.rem(iota((rows, 128), 1), 2) == 0
    ends = [jnp.where(high, out[i], out[j])[:, 0:32] for i, j in zip(*ENTER[0])]
    face_ref[0] = jnp.concatenate(ends[0:4], axis=1)
    face_ref[1] = jnp.concatenate([ends[4], jnp.zeros((rows, 96), F32)], axis=1)


    even = even_slab()
    leaving = []
    for group, z in ((0, depth - 1), (1, 0)):
        out = collide(
            [pops_ref[i, z] for i in range(19)],
            solid_ref[z] == 1,
            [force_ref[d, z] for d in range(3)],
        )
        leaving.append([turn(out[i], STEP[i, 0], 1) for i in ENTER[2][group]])
    if n_drags == 2:
        leaving[0].append(up)
        leaving[1].append(down)
    row = 0
    for a, b in zip(*leaving):
        at = slice(row, row + a.shape[0])
        first_ref[at] = jnp.where(even, a, b)
        second_ref[at] = jnp.where(even, b, a)
        row += a.shape[0]


def couple(shape, beads, flow, columns, pops, solid, depth, rows):
    width = flow[0].shape[1]
    single = beads.shape[0] == GROUP
    tile = jax.ShapeDtypeStruct((8, 128), F32)
    drags = [jax.ShapeDtypeStruct((shape[0], 8, 128), F32), tile] if single else [beads]
    message = jax.ShapeDtypeStruct((5 * rows + (8 if single else 0), width), F32)
    return pl.pallas_call(
        functools.partial(couple_kernel, shape, depth, rows, len(drags)),
        out_shape=[
            jax.ShapeDtypeStruct((3, depth, rows, width), F32),
            jax.ShapeDtypeStruct((2, rows, 128), F32),
            message,
            message,
        ]
        + [jax.ShapeDtypeStruct(d.shape, F32) for d in drags]
        + [TOKEN],
        compiler_params=pltpu.CompilerParams(vmem_limit_bytes=ROOM),
        name="couple",
    )(beads, *flow, columns, pops, solid)


def entered_z(first_ref, second_ref, side, rows):
    even = even_slab() if side == 0 else jnp.logical_not(even_slab())
    return jnp.where(even, second_ref[rows], first_ref[rows])


X_EDGES = [i for side in range(2) for i in ENTER[2][side] if STEP[i, 0] != 0]


def rows_kernel(depth, rows, before_ref, draft_ref, face_ref, first_ref, second_ref, *refs):
    refs, (cross_ref, token_ref, turned) = refs[:-3], refs[-3:]
    token_ref[...] = jnp.zeros_like(token_ref)
    outs = refs[-1:] if len(refs) == 3 else refs
    for n in range(2):
        turned[n] = face_ref[n].T
    for group in range(2):
        out_ref = outs[0] if len(outs) == 1 else outs[group]
        base = group * 5 * depth if len(outs) == 1 else 0
        y = rows - 1 if group == 0 else 0
        for k, i in enumerate(ENTER[1][group]):
            at = base + k * depth
            value = draft_ref[(group * 5 + k) * depth : (group * 5 + k + 1) * depth]
            if STEP[i, 0] != 0:
                tile, lane = x_place(i)
                column = turned[tile, pl.ds(lane, depth, stride=2), :][:, y : y + 1]
                value = patch_x(value, i, jnp.broadcast_to(column, value.shape))
            out_ref[at : at + depth] = value
            if STEP[i, 2] != 0:
                side = 0 if STEP[i, 2] == 1 else 1
                z = 0 if side == 0 else depth - 1
                row = ENTER[2][side].index(i) * rows + y
                out_ref[at + z : at + z + 1] = entered_z(
                    first_ref, second_ref, side, slice(row, row + 1)
                )
    if len(refs) == 3:
        own_ref, far_ref, out_ref = refs
        came = arrived_drag(own_ref, far_ref, first_ref, second_ref, 5 * rows)
        out_ref[10 * depth : 10 * depth + 8] = one_tile(came, 1)
    for k, i in enumerate(X_EDGES):
        side = 0 if STEP[i, 2] == 1 else 1
        at = ENTER[2][side].index(i) * rows
        cross_ref[k * rows : (k + 1) * rows] = entered_z(
            first_ref, second_ref, side, slice(at, at + rows)
        )


def arrived_drag(own_ref, far_ref, first_ref, second_ref, tail):
    at = slice(tail, tail + 8)
    up, down = [entered_z(first_ref, second_ref, side, at) for side in range(2)]
    return [own_ref[0], down, far_ref[...], up]


def one_tile(tiles, col):
    return jnp.concatenate([t[:, col * CAP : (col + 1) * CAP] for t in tiles], axis=1)


def leaving_rows(depth, rows, before, draft, face, first, second, drags):
    width = draft.shape[1]
    if drags:
        sizes = [10 * depth + 8]
    else:
        sizes = [5 * depth] * 2
    args = (draft, face, first, second, *drags)
    return pl.pallas_call(
        functools.partial(rows_kernel, depth, rows),
        out_shape=[jax.ShapeDtypeStruct((n, width), F32) for n in sizes + [4 * rows]] + [TOKEN],
        in_specs=[pl.BlockSpec(memory_space=pl.ANY)]
        + [pl.BlockSpec(memory_space=pltpu.VMEM)] * len(args),
        scratch_shapes=[pltpu.VMEM((2, 128, rows), F32)],
        compiler_params=pltpu.CompilerParams(vmem_limit_bytes=ROOM),
        name="rows",
    )(before, *args)


def runs(members):
    found = []
    for i in members:
        if found and found[-1][1] == i and STEP[i, 2] == STEP[i - 1, 2]:
            found[-1] = (found[-1][0], i + 1)
        else:
            found.append((i, i + 1))
    return found


def stream_planes(low, high, faces, pops_ref, solid_ref, force_ref, held):
    def plane(z, faces):
        out = collide(
            [pops_ref[i, z] for i in range(19)],
            solid_ref[z] == 1,
            [force_ref[d, z] for d in range(3)],
        )
        for i in range(19):
            value = turn(out[i], STEP[i, 0], 1)
            if STEP[i, 0] != 0 and faces:
                tile, lane = x_place(i)
                value = patch_x(value, i, spread_column(faces[tile], lane))
            held[i, z] = turn(value, STEP[i, 1], 0)
        return tuple(pltpu.roll(f, 126, 1) for f in faces)

    return lax.fori_loop(low, high, plane, faces, unroll=2)


def lower_kernel(
    before_ref, pops_ref, solid_ref, force_ref, side_ref, wall_ref, held, draft_ref, token_ref
):
    depth, rows, _ = pops_ref.shape[1:]
    token_ref[...] = jnp.zeros_like(token_ref)
    for group in range(2):
        force = [force_ref[d, :, 0 if group else rows - 1, :] for d in range(3)]
        out = collide([side_ref[i, 1 - group] for i in range(19)], wall_ref[1 - group] == 1, force)
        for k, i in enumerate(ENTER[1][group]):
            row = (group * 5 + k) * depth
            value = turn(out[i], STEP[i, 0], 1)
            draft_ref[row : row + depth] = turn(value, STEP[i, 2], 0)
    stream_planes(0, held.shape[1], (), pops_ref, solid_ref, force_ref, held)


def upper_kernel(
    before_ref, lower_ref, pops_ref, solid_ref, force_ref, face_ref, out_ref, tile_ref, held, sem
):
    depth, rows, width = pops_ref.shape[1:]
    half = lower_ref.shape[1]
    copies = []

    def leave(source, members, low, high):
        for a, b in runs(members):
            step = int(STEP[a, 2])
            start, stop = max(low + step, 0), min(high + step, depth)
            copy = pltpu.make_async_copy(
                source.at[a:b, start - step : stop - step],
                out_ref.at[a:b, start:stop],
                sem.at[len(copies)],
            )
            copy.start()
            copies.append(copy)

    straight = [i for i in range(19) if STEP[i, 0] == 0]
    across = [i for i in range(19) if STEP[i, 0] != 0]
    leave(lower_ref, straight, 0, half)
    faces = (face_ref[0], face_ref[1])
    for i in across:
        tile, lane = x_place(i)
        for z in range(half):
            column = turn(spread_column(faces[tile], lane + 2 * z), STEP[i, 1], 0)
            held[i, z] = patch_x(lower_ref[i, z], i, column)
    leave(held, across, 0, half)
    faces = tuple(pltpu.roll(f, 128 - 2 * half, 1) for f in faces)
    marks = upper_marks(half, depth)
    for low, high in zip(marks, marks[1:]):
        faces = stream_planes(low, high, faces, pops_ref, solid_ref, force_ref, held)
        leave(held, range(19), low, high)
    for group in range(2):
        first = slice(0, 8) if group == 0 else slice(rows - 8, rows)
        for k, i in enumerate(ENTER[1][group]):
            source = lower_ref if i in straight else held
            tile_ref[group * 5 + k, 0:half] = source[i, 0:half, first, :]
            tile_ref[group * 5 + k, half:depth] = held[i, half:depth, first, :]
    for copy in copies:
        copy.wait()


def upper_marks(half, depth):
    return list(range(half, depth - 2, 4)) + ([depth - 2] if (depth - half) % 4 else []) + [depth]


def stream_lower(half, before, pops, solid, force, sides, walls):
    _, depth, rows, width = pops.shape
    vmem = pl.BlockSpec(memory_space=pltpu.VMEM)
    return pl.pallas_call(
        lower_kernel,
        out_shape=[
            jax.ShapeDtypeStruct((19, half, rows, width), F32),
            jax.ShapeDtypeStruct((10 * depth, width), F32),
            TOKEN,
        ],
        in_specs=[pl.BlockSpec(memory_space=pl.ANY)] + [vmem] * 5,
        compiler_params=pltpu.CompilerParams(vmem_limit_bytes=ROOM),
        cost_estimate=pl.CostEstimate(flops=3000000, bytes_accessed=2000000, transcendentals=0),
        name="lower",
    )(before, pops, solid, force, sides, walls)


def stream_upper(before, lower, pops, solid, force, face):
    _, depth, rows, width = pops.shape
    vmem = pl.BlockSpec(memory_space=pltpu.VMEM)
    return pl.pallas_call(
        upper_kernel,
        out_shape=[
            jax.ShapeDtypeStruct(pops.shape, F32),
            jax.ShapeDtypeStruct((10, depth, 8, width), F32),
        ],
        in_specs=[pl.BlockSpec(memory_space=pl.ANY)] + [vmem] * 5,
        out_specs=[pl.BlockSpec(memory_space=pltpu.HBM), vmem],
        scratch_shapes=[
            pltpu.VMEM(pops.shape, F32),
            pltpu.SemaphoreType.DMA((20 * len(upper_marks(lower.shape[1], depth)),)),
        ],
        compiler_params=pltpu.CompilerParams(vmem_limit_bytes=ROOM),
        cost_estimate=pl.CostEstimate(flops=5000000, bytes_accessed=3000000, transcendentals=0),
        name="upper",
    )(before, lower, pops, solid, force, face)


def finish_kernel(shape, n_rows, whole_ref, target_ref, tile_ref, first_ref, second_ref, *refs):
    row_refs, cross_ref, refs = refs[:n_rows], refs[n_rows], refs[n_rows + 1 :]
    drag_refs, (out_ref, bead_ref, planes, tiles, bead, sem) = refs[:-6], refs[-6:]
    depth, rows, width = whole_ref.shape[1:]

    def entering(group, k):
        at = (group * 5 + k) * depth if n_rows == 1 else k * depth
        return row_refs[group % n_rows][at : at + depth]

    copies = []

    def leave(source, target):
        copy = pltpu.make_async_copy(source, target, sem.at[len(copies)])
        copy.start()
        copies.append(copy)

    for group in range(2):
        z = 0 if group == 0 else depth - 1
        for k, i in enumerate(ENTER[2][group]):
            value = entered_z(first_ref, second_ref, group, slice(k * rows, (k + 1) * rows))
            if STEP[i, 1] != 0:
                side = 0 if STEP[i, 1] == 1 else 1
                y = 0 if side == 0 else rows - 1
                row = entering(side, ENTER[1][side].index(i))[z : z + 1]
                value = jnp.where(
                    iota((rows, width), 0) == y,
                    jnp.broadcast_to(row, (rows, width)),
                    turn(value, STEP[i, 1], 0),
                )
            if STEP[i, 0] != 0:
                at = X_EDGES.index(i) * rows
                value = patch_x(value, i, cross_ref[at : at + rows])
            n = group * 5 + k
            planes[n] = value
            leave(planes.at[n], out_ref.at[i, z])
    for group in range(2):
        first = 0 if group == 0 else rows - 8
        for k, i in enumerate(ENTER[1][group]):
            n = group * 5 + k
            step = int(STEP[i, 2])
            tiles[n, 1 + step : 1 + step + depth] = tile_ref[n]
            tiles[n, 1 : 1 + depth, 0 if group == 0 else 7, :] = entering(group, k)
            low, high = max(step, 0), min(depth + step, depth)
            leave(tiles.at[n, 1 + low : 1 + high], out_ref.at[i, low:high, first : first + 8])

    count = target_ref.shape[1]
    target = target_ref[...]
    if len(drag_refs) == 2:
        slabs, cols, _ = shape
        came = arrived_drag(*drag_refs, first_ref, second_ref, 5 * rows)
        passed = row_refs[0][10 * depth : 10 * depth + 8]
        table = jnp.concatenate([one_tile(came, 0), passed], axis=1)
        owner = lax.shift_right_logical(target, 5)
        owner_slab = lax.shift_right_logical(owner, cols.bit_length() - 1)
        away_col = owner - owner_slab * cols - lax.axis_index("col")
        away_col = jnp.where(away_col < 0, away_col + cols, away_col)
        away_slab = owner_slab - lax.axis_index("slab")
        away_slab = jnp.where(away_slab < 0, away_slab + slabs, away_slab)
        place = away_col * 128 + away_slab * CAP + target - owner * CAP
        choose = (iota((256, count), 0) == place).astype(F32).astype(BF16)
        total = dot_select(table, choose, NN)
    else:
        back_ref = drag_refs[0]

        def group(k, total):
            got = [back_ref[k * GROUP + r] for r in range(GROUP)]
            slots = jnp.concatenate([t[:, 0:CAP] for t in got], axis=1)
            first = k * (GROUP * CAP)
            choose = (iota((GROUP * CAP, count), 0) + first == target).astype(F32)
            return total + dot_select(slots, choose.astype(BF16), NN)

        total = lax.fori_loop(
            0, back_ref.shape[0] // GROUP, group, jnp.zeros((8, count), F32)
        )
    bead[...] = total[0:3]
    leave(bead, bead_ref)
    for copy in copies:
        copy.wait()


def finish(shape, whole, target, tiles, first, second, entered, cross, drags):
    _, depth, rows, width = whole.shape
    vmem = pl.BlockSpec(memory_space=pltpu.VMEM)
    hbm = pl.BlockSpec(memory_space=pltpu.HBM)
    args = [whole, target, tiles, first, second, *entered, cross, *drags]
    return pl.pallas_call(
        functools.partial(finish_kernel, shape, len(entered)),
        out_shape=[
            jax.ShapeDtypeStruct(whole.shape, F32),
            jax.ShapeDtypeStruct((3, target.shape[1]), F32),
        ],
        in_specs=[hbm] + [vmem] * (len(args) - 1),
        out_specs=[hbm, hbm],
        scratch_shapes=[
            pltpu.VMEM((10, rows, width), F32),
            pltpu.VMEM((10, depth + 2, 8, width), F32),
            pltpu.VMEM((3, target.shape[1]), F32),
            pltpu.SemaphoreType.DMA((21,)),
        ],
        input_output_aliases={0: 0},
        compiler_params=pltpu.CompilerParams(vmem_limit_bytes=ROOM),
        name="finish",
    )(*args)


def shards(populations, solid_mask, bead_owner, bead_base, bead_offset, bead_velocity):
    slabs, cols, pairs = shape = tuple(lax.axis_size(a) for a in ("slab", "col", "pair"))
    owners = slabs * cols
    depth, rows = populations.shape[1:3]
    single = owners == GROUP and slabs == 4
    swap = functools.partial(
        lax.all_to_all, axis_name=("slab", "col"), split_axis=0, concat_axis=0, tiled=True
    )

    target, messages = pack(owners, bead_owner, bead_base, bead_offset, bead_velocity)
    messages = swap(messages)
    *flow, columns, sides, walls = moments(populations, solid_mask)
    force, face, first, second, drag, *far, token = couple(
        shape, messages, flow, columns, populations, solid_mask, depth, rows
    )

    def send_pair(value):
        return send(value, shape, lambda s, c, p: (s, c, (p + 1) % pairs))

    def send_col(values):
        return [
            send(value, shape, lambda s, c, p, sign=sign: (s, (c + sign) % cols, p))
            for value, sign in zip(values, (1, -1))
        ]

    face = send_pair(face)
    first, second = send_slab(first, shape, 0), send_slab(second, shape, 1)
    if single:
        drags = [drag, send(far[0], shape, lambda s, c, p: ((s + 2) % slabs, c, p))]
    else:
        drags = []
        drag = swap(drag)
    fields = (populations, solid_mask, force)
    lower, draft, token = stream_lower(depth // 2, token, *fields, sides, walls)
    *leaving, cross, token = leaving_rows(depth, rows, token, draft, face, first, second, drags)
    entered, cross = send_col(leaving), send_pair(cross)
    whole, tiles = stream_upper(token, lower, *fields, face)
    return tuple(
        finish(shape, whole, target, tiles, first, second, entered, cross, drags or [drag])
    )


def solution(mesh):
    return jax.shard_map(
        shards,
        mesh=mesh,
        in_specs=(
            P(None, ("rep", "slab"), "col", "pair"),
            P(("rep", "slab"), "col", "pair"),
            P(("rep", "slab", "col", "pair")),
            P(None, ("rep", "slab", "col", "pair")),
            P(None, ("rep", "slab", "col", "pair")),
            P(None, ("rep", "slab", "col", "pair")),
        ),
        out_specs=(
            P(None, ("rep", "slab"), "col", "pair"),
            P(None, ("rep", "slab", "col", "pair")),
        ),
        check_vma=False,
    )
```

```python
import functools

import jax
import jax.numpy as jnp
import numpy as np
from jax import lax
from jax.experimental import pallas as pl
from jax.experimental.pallas import tpu as pltpu
from jax.sharding import PartitionSpec as P

CAP = 32
GROUP = 8

STEP = np.array(
    [
        [0, 0, 0],
        [1, 0, 0],
        [-1, 0, 0],
        [0, 1, 0],
        [0, -1, 0],
        [0, 0, 1],
        [0, 0, -1],
        [1, 1, 0],
        [-1, -1, 0],
        [1, -1, 0],
        [-1, 1, 0],
        [1, 0, 1],
        [-1, 0, -1],
        [1, 0, -1],
        [-1, 0, 1],
        [0, 1, 1],
        [0, -1, -1],
        [0, 1, -1],
        [0, -1, 1],
    ],
    np.int32,
)
TAU_PLUS = 0.8
TAU_MINUS = 0.5 + (3.0 / 16.0) / (TAU_PLUS - 0.5)
KEEP_EVEN = 1.0 - 1.0 / TAU_PLUS
KEEP_ODD = 1.0 - 1.0 / TAU_MINUS
FORCE_GAIN = 1.0 - 0.5 / TAU_PLUS
DRAG_COEF = 2.0
F32 = jnp.float32
BF16 = jnp.bfloat16

ENTER = [[[i for i in range(19) if STEP[i, a] == sign] for sign in (1, -1)] for a in range(3)]
TOKEN = jax.ShapeDtypeStruct((8, 128), F32)
ROOM = 16 << 20
NT = (((1,), (1,)), ((), ()))
NN = (((1,), (0,)), ((), ()))


def iota(shape, dim):
    return lax.broadcasted_iota(jnp.int32, shape, dim)


def high_low(value):
    high = value.astype(BF16)
    return high, (value - high.astype(F32)).astype(BF16)


def dot_split(left, right, dims):
    (a, b), (c, d) = left, right
    mul = functools.partial(lax.dot_general, dimension_numbers=dims, preferred_element_type=F32)
    return mul(a, c) + (mul(a, d) + mul(b, c))


def dot_select(value, choose, dims):
    first = value.astype(BF16).astype(F32)
    rest = value - first
    second = rest.astype(BF16).astype(F32)
    stacked = jnp.concatenate([first, second, rest - second], axis=0).astype(BF16)
    got = lax.dot_general(stacked, choose, dimension_numbers=dims, preferred_element_type=F32)
    rows = value.shape[0]
    return got[0:rows] + got[rows : 2 * rows] + got[2 * rows : 3 * rows]


def density_momentum(pops):
    momentum = []
    for axis in range(3):
        plus = [pops[i] for i in range(19) if STEP[i, axis] == 1]
        minus = [pops[i] for i in range(19) if STEP[i, axis] == -1]
        momentum.append(sum(plus[1:], plus[0]) - sum(minus[1:], minus[0]))
    return sum(pops[1:], pops[0]), momentum


def along(step, vector):
    terms = None
    for axis in range(3):
        if step[axis] == 0:
            continue
        if terms is None:
            terms = vector[axis] if step[axis] == 1 else -vector[axis]
        else:
            terms = terms + vector[axis] if step[axis] == 1 else terms - vector[axis]
    return terms


def collide(pops, wall, force):
    density, momentum = density_momentum(pops)
    inverse = 1.0 / density
    carried = [m + 0.5 * f for m, f in zip(momentum, force)]
    speed = [m * inverse for m in carried]
    w = 1.0 / 36.0
    bend = [(4.5 * w / TAU_PLUS) * m + (9.0 * w * FORCE_GAIN) * f for m, f in zip(carried, force)]
    push = [(3.0 * w / TAU_MINUS) * m + (3.0 * w * FORCE_GAIN) * f for m, f in zip(carried, force)]
    drop = [(1.5 * w / TAU_PLUS) * m + (3.0 * w * FORCE_GAIN) * f for m, f in zip(carried, force)]
    rest = (w / TAU_PLUS) * density - sum(
        [u * d for u, d in zip(speed[1:], drop[1:])], speed[0] * drop[0]
    )
    out = [None] * 19
    out[0] = jnp.where(wall, pops[0], KEEP_EVEN * pops[0] + 12.0 * rest)
    for i in range(1, 19, 2):
        a, b = pops[i], pops[i + 1]
        step = STEP[i]
        even = rest + along(step, speed) * along(step, bend)
        odd = along(step, push)
        if i < 7:
            even = even + even
            odd = odd + odd
        even = (0.5 * KEEP_EVEN) * (a + b) + even
        odd = (0.5 * KEEP_ODD) * (a - b) + odd
        out[i] = jnp.where(wall, b, even + odd)
        out[i + 1] = jnp.where(wall, a, even - odd)
    return out


def turn(value, amount, axis):
    if amount == 0:
        return value
    return pltpu.roll(value, int(amount) % value.shape[axis], axis)


def send(value, shape, target):
    def flat(at):
        return (at[0] * shape[1] + at[1]) * shape[2] + at[2]

    perm = [(flat(at), flat(target(*at))) for at in np.ndindex(*shape)]
    return lax.ppermute(value, ("slab", "col", "pair"), perm)


def send_slab(value, shape, which):
    def target(s, c, p):
        return ((s + (1 if s % 2 == which else -1)) % shape[0], c, p)

    return send(value, shape, target)


def odd_slab():
    return lax.rem(lax.axis_index("slab"), 2) == 1


def rank_among(member):
    count = member.shape[1]
    earlier = (iota((count, count), 0) < iota((count, count), 1)).astype(F32).astype(BF16)
    return lax.dot_general(member.astype(BF16), earlier, NN, preferred_element_type=F32)


def spread_column(tile, lane):
    return jnp.broadcast_to(tile[:, lane : lane + 1], tile.shape)


def patch_x(value, i, column):
    side = 0 if STEP[i, 0] == 1 else value.shape[1] - 1
    return jnp.where(iota(value.shape, 1) == side, column, value)


def x_place(i):
    group = 0 if STEP[i, 0] == 1 else 1
    place = ENTER[0][group].index(i)
    return place // 4, (place % 4) * 32 + group


def x_ends(planes):
    lane = lax.shift_right_logical(iota(planes[0].shape, 1), 1)
    tile = jnp.ones(planes[0].shape, F32)
    for z, value in enumerate(planes):
        tile = jnp.where(lane == z, pltpu.roll(value, 2 * z + 1, 1), tile)
    return tile


def pack_kernel(
    steps, owner_ref, base_ref, offset_ref, velocity_ref, target_ref, out_ref, table
):
    count = owner_ref.shape[1]
    step = 0 if steps == 1 else pl.program_id(0)
    local = owner_ref[...] - step * GROUP
    member = (iota((GROUP, count), 0) == local).astype(F32)
    rank = jnp.sum(member * rank_among(member), axis=0, keepdims=True).astype(jnp.int32)
    inside = (local >= 0) & (local < GROUP)
    target = jnp.where(inside, local * CAP + rank, -1)
    whole_target = jnp.where(inside, owner_ref[...] * CAP + rank, -1)

    if steps == 1:
        target_ref[...] = whole_target
    else:
        known = jnp.where(step == 0, -1, target_ref[...])
        target_ref[...] = jnp.maximum(known, whole_target)

    choose = (iota((GROUP * CAP, count), 0) == target).astype(F32).astype(BF16)
    table[...] = jnp.zeros_like(table)
    table[0:3] = base_ref[...].astype(F32) + 1.0
    table[8:11] = offset_ref[...]
    table[16:19] = velocity_ref[...]
    packed = dot_select(table[...], choose, NT)
    blank = jnp.zeros((8, CAP), F32)
    for r in range(GROUP):
        lanes = slice(r * CAP, (r + 1) * CAP)
        out_ref[r] = jnp.concatenate(
            [packed[0:8, lanes], packed[8:16, lanes], packed[16:24, lanes], blank], axis=1
        )


def pack(owners, owner, base, offset, velocity):
    count, steps = owner.shape[0], owners // GROUP
    args = (owner.reshape(1, count), base, offset, velocity)
    blocks = {}
    if steps > 1:
        blocks = dict(
            grid=(steps,),
            in_specs=[pl.BlockSpec(a.shape, lambda k: (0, 0)) for a in args],
            out_specs=[
                pl.BlockSpec((1, count), lambda k: (0, 0)),
                pl.BlockSpec((GROUP, 8, 128), lambda k: (k, 0, 0)),
            ],
            compiler_params=pltpu.CompilerParams(vmem_limit_bytes=48 << 20),
        )
    return pl.pallas_call(
        functools.partial(pack_kernel, steps),
        out_shape=[
            jax.ShapeDtypeStruct((1, count), jnp.int32),
            jax.ShapeDtypeStruct((owners, 8, 128), F32),
        ],
        scratch_shapes=[pltpu.VMEM((24, count), F32)],
        name="pack",
        **blocks,
    )(*args)


def moments_kernel(
    pops_ref, solid_ref, high_ref, low_ref, column_ref, side_ref, wall_ref, held, held_solid, sem
):
    depth, rows, width = pops_ref.shape[1:]
    chunks = 4
    span = depth // chunks
    copies = [pltpu.make_async_copy(solid_ref, held_solid, sem.at[chunks])]
    for k in range(chunks):
        part = pl.ds(k * span, span)
        copies.append(
            pltpu.make_async_copy(pops_ref.at[:, part], held.at[:, part], sem.at[k])
        )
    for copy in copies:
        copy.start()

    def plane(z, carry):
        pops = [held[i, z] for i in range(19)]
        density, momentum = density_momentum(pops)
        inverse = 1.0 / density
        for axis in range(3):
            at = pl.ds(pl.multiple_of(axis * depth * rows + z * rows, rows), rows)
            high_ref[at], low_ref[at] = high_low(momentum[axis] * inverse)
        return carry

    for k in range(chunks):
        copies[1 + k].wait()
        lax.fori_loop(k * span, (k + 1) * span, plane, 0, unroll=2)
    copies[0].wait()
    for i in range(19):
        column_ref[i] = x_ends([held[i, z] for z in range(depth)])
        side_ref[i, 0] = held[i, :, 0, :]
        side_ref[i, 1] = held[i, :, rows - 1, :]
    wall_ref[0] = held_solid[:, 0, :]
    wall_ref[1] = held_solid[:, rows - 1, :]
    column_ref[19] = x_ends([held_solid[z].astype(F32) for z in range(depth)])


def moments(pops, solid):
    _, depth, rows, width = pops.shape
    hbm = pl.BlockSpec(memory_space=pltpu.HBM)
    return pl.pallas_call(
        moments_kernel,
        out_shape=[
            jax.ShapeDtypeStruct((3 * depth * rows, width), BF16),
            jax.ShapeDtypeStruct((3 * depth * rows, width), BF16),
            jax.ShapeDtypeStruct((20, rows, 128), F32),
            jax.ShapeDtypeStruct((19, 2, depth, width), F32),
            jax.ShapeDtypeStruct((2, depth, width), jnp.int32),
        ],
        in_specs=[hbm, hbm],
        scratch_shapes=[
            pltpu.VMEM(pops.shape, F32),
            pltpu.VMEM(solid.shape, jnp.int32),
            pltpu.SemaphoreType.DMA((5,)),
        ],
        compiler_params=pltpu.CompilerParams(vmem_limit_bytes=54000000),
        cost_estimate=pl.CostEstimate(flops=3000000, bytes_accessed=4000000, transcendentals=0),
        name="moments",
    )(pops, solid)


def unpack(tiles):
    return [
        jnp.concatenate([t[:, g * CAP : (g + 1) * CAP] for t in tiles], axis=1) for g in range(3)
    ]


def couple_group(base, part, velocity, flow, depth, rows):
    width, slots = flow[0].shape[1], GROUP * CAP
    start = base.astype(jnp.int32) - 1

    def hat(axis, length):
        cell = iota((length, slots), 0)
        low, share = start[axis : axis + 1], part[axis : axis + 1]
        return jnp.where(cell == low, 1.0 - share, 0.0) + jnp.where(cell == low + 1, share, 0.0)

    hat_x, hat_y, hat_z = high_low(hat(0, width)), hat(1, rows), hat(2, depth)
    weight = (hat_z[:, None, :] * hat_y[None, :, :]).reshape(depth * rows, slots)
    across = dot_split(flow, hat_x, NN)
    cells = depth * rows
    sampled = [
        jnp.sum(across[d * cells : (d + 1) * cells] * weight, axis=0, keepdims=True)
        for d in range(3)
    ]
    drag = [DRAG_COEF * (sampled[d] - velocity[d : d + 1]) for d in range(3)]
    spread = jnp.concatenate([weight * (-drag[d]) for d in range(3)], axis=0)
    return drag, dot_split(high_low(spread), hat_x, NT)


def couple_kernel(shape, depth, rows, n_drags, beads_ref, high_ref, low_ref, *refs):
    slabs, cols, _ = shape
    pops_ref, solid_ref, force_ref, first_ref, second_ref, *refs = refs
    drag_refs, token_ref = refs[:-1], refs[-1]
    token_ref[...] = jnp.zeros_like(token_ref)
    width = high_ref.shape[1]
    flow = (high_ref[...], low_ref[...])
    hollow = jnp.zeros((5, GROUP * CAP), F32)

    if n_drags == 2:
        slab, col = lax.axis_index("slab"), lax.axis_index("col")
        got = []
        for r in range(GROUP):
            there = [a - b for a, b in zip((slab, col), divmod(r, cols))]
            there = [jnp.where(a < 0, a + n, a) for a, n in zip(there, (slabs, cols))]
            got.append(beads_ref[there[0] * cols + there[1]])
        drag, force = couple_group(*unpack(got), flow, depth, rows)
        force_ref[...] = force.reshape(3, depth, rows, width)
        stacked = jnp.concatenate(drag + [hollow], axis=0)
        lanes = cols * CAP
        blank = jnp.zeros((8, 128 - lanes), F32)
        for dz in range(slabs):
            tile = jnp.concatenate([stacked[:, dz * lanes : (dz + 1) * lanes], blank], axis=1)
            drag_refs[0][dz] = tile
            if dz == 2:
                drag_refs[1][...] = tile
            if dz == 1:
                down = tile
        up = tile
    else:
        force_ref[...] = jnp.zeros_like(force_ref)
        blank = jnp.zeros((8, 128 - CAP), F32)

        def group(k, carry):
            got = [beads_ref[k * GROUP + r] for r in range(GROUP)]
            drag, force = couple_group(*unpack(got), flow, depth, rows)
            force_ref[...] += force.reshape(3, depth, rows, width)
            stacked = jnp.concatenate(drag + [hollow], axis=0)
            for r in range(GROUP):
                drag_refs[0][k * GROUP + r] = jnp.concatenate(
                    [stacked[:, r * CAP : (r + 1) * CAP], blank], axis=1
                )
            return carry

        lax.fori_loop(0, beads_ref.shape[0] // GROUP, group, 0)

    odd = odd_slab()
    leaving = []
    for group, z in ((0, depth - 1), (1, 0)):
        out = collide(
            [pops_ref[i, z] for i in range(19)],
            solid_ref[z] == 1,
            [force_ref[d, z] for d in range(3)],
        )
        leaving.append([turn(out[i], STEP[i, 0], 1) for i in ENTER[2][group]])
    if n_drags == 2:
        leaving[0].append(up)
        leaving[1].append(down)
    row = 0
    for a, b in zip(*leaving):
        at = slice(row, row + a.shape[0])
        first_ref[at] = jnp.where(odd, a, b)
        second_ref[at] = jnp.where(odd, b, a)
        row += a.shape[0]


def couple(shape, beads, flow, pops, solid, depth, rows):
    width = flow[0].shape[1]
    single = beads.shape[0] == GROUP
    tile = jax.ShapeDtypeStruct((8, 128), F32)
    drags = [jax.ShapeDtypeStruct((shape[0], 8, 128), F32), tile] if single else [beads]
    message = jax.ShapeDtypeStruct((5 * rows + (8 if single else 0), width), F32)
    return pl.pallas_call(
        functools.partial(couple_kernel, shape, depth, rows, len(drags)),
        out_shape=[
            jax.ShapeDtypeStruct((3, depth, rows, width), F32),
            message,
            message,
        ]
        + [jax.ShapeDtypeStruct(d.shape, F32) for d in drags]
        + [TOKEN],
        compiler_params=pltpu.CompilerParams(vmem_limit_bytes=ROOM),
        name="couple",
    )(beads, *flow, pops, solid)


def x_faces_kernel(force_ref, column_ref, face_ref):
    _, depth, rows, _ = force_ref.shape
    force = [x_ends([force_ref[d, z] for z in range(depth)]) for d in range(3)]
    out = collide([column_ref[i] for i in range(19)], column_ref[19] == 1.0, force)
    high = lax.rem(iota((rows, 128), 1), 2) == 0
    ends = [jnp.where(high, out[i], out[j])[:, 0:32] for i, j in zip(*ENTER[0])]
    face_ref[0] = jnp.concatenate(ends[0:4], axis=1)
    face_ref[1] = jnp.concatenate([ends[4], jnp.zeros((rows, 96), F32)], axis=1)


def x_faces(force, columns):
    return pl.pallas_call(
        x_faces_kernel,
        out_shape=jax.ShapeDtypeStruct((2, *columns.shape[1:]), F32),
        compiler_params=pltpu.CompilerParams(vmem_limit_bytes=ROOM),
        name="x_faces",
    )(force, columns)


def entered_z(first_ref, second_ref, side, rows):
    odd = odd_slab() if side == 0 else jnp.logical_not(odd_slab())
    return jnp.where(odd, second_ref[rows], first_ref[rows])


X_EDGES = [i for side in range(2) for i in ENTER[2][side] if STEP[i, 0] != 0]


def rows_kernel(depth, rows, before_ref, draft_ref, face_ref, first_ref, second_ref, *refs):
    refs, (cross_ref, token_ref, turned) = refs[:-3], refs[-3:]
    token_ref[...] = jnp.zeros_like(token_ref)
    outs = refs[-1:] if len(refs) == 3 else refs
    for n in range(2):
        turned[n] = face_ref[n].T
    for group in range(2):
        out_ref = outs[0] if len(outs) == 1 else outs[group]
        base = group * 5 * depth if len(outs) == 1 else 0
        y = rows - 1 if group == 0 else 0
        for k, i in enumerate(ENTER[1][group]):
            at = base + k * depth
            value = draft_ref[(group * 5 + k) * depth : (group * 5 + k + 1) * depth]
            if STEP[i, 0] != 0:
                tile, lane = x_place(i)
                column = turned[tile, pl.ds(lane, depth, stride=2), :][:, y : y + 1]
                value = patch_x(value, i, jnp.broadcast_to(column, value.shape))
            out_ref[at : at + depth] = value
            if STEP[i, 2] != 0:
                side = 0 if STEP[i, 2] == 1 else 1
                z = 0 if side == 0 else depth - 1
                row = ENTER[2][side].index(i) * rows + y
                out_ref[at + z : at + z + 1] = entered_z(
                    first_ref, second_ref, side, slice(row, row + 1)
                )
    if len(refs) == 3:
        own_ref, far_ref, out_ref = refs
        came = arrived_drag(own_ref, far_ref, first_ref, second_ref, 5 * rows)
        out_ref[10 * depth : 10 * depth + 8] = one_tile(came, 1)
    for k, i in enumerate(X_EDGES):
        side = 0 if STEP[i, 2] == 1 else 1
        at = ENTER[2][side].index(i) * rows
        cross_ref[k * rows : (k + 1) * rows] = entered_z(
            first_ref, second_ref, side, slice(at, at + rows)
        )


def arrived_drag(own_ref, far_ref, first_ref, second_ref, tail):
    at = slice(tail, tail + 8)
    up, down = [entered_z(first_ref, second_ref, side, at) for side in range(2)]
    return [own_ref[0], down, far_ref[...], up]


def one_tile(tiles, col):
    return jnp.concatenate([t[:, col * CAP : (col + 1) * CAP] for t in tiles], axis=1)


def leaving_rows(depth, rows, before, draft, face, first, second, drags):
    width = draft.shape[1]
    if drags:
        sizes = [10 * depth + 8]
    else:
        sizes = [5 * depth] * 2
    args = (draft, face, first, second, *drags)
    return pl.pallas_call(
        functools.partial(rows_kernel, depth, rows),
        out_shape=[jax.ShapeDtypeStruct((n, width), F32) for n in sizes + [4 * rows]] + [TOKEN],
        in_specs=[pl.BlockSpec(memory_space=pl.ANY)]
        + [pl.BlockSpec(memory_space=pltpu.VMEM)] * len(args),
        scratch_shapes=[pltpu.VMEM((2, 128, rows), F32)],
        compiler_params=pltpu.CompilerParams(vmem_limit_bytes=ROOM),
        name="rows",
    )(before, *args)


def runs(members):
    found = []
    for i in members:
        if found and found[-1][1] == i and STEP[i, 2] == STEP[i - 1, 2]:
            found[-1] = (found[-1][0], i + 1)
        else:
            found.append((i, i + 1))
    return found


def stream_planes(low, high, faces, pops_ref, solid_ref, force_ref, held):
    def plane(z, faces):
        out = collide(
            [pops_ref[i, z] for i in range(19)],
            solid_ref[z] == 1,
            [force_ref[d, z] for d in range(3)],
        )
        for i in range(19):
            value = turn(out[i], STEP[i, 0], 1)
            if STEP[i, 0] != 0 and faces:
                tile, lane = x_place(i)
                value = patch_x(value, i, spread_column(faces[tile], lane))
            held[i, z] = turn(value, STEP[i, 1], 0)
        return tuple(pltpu.roll(f, 126, 1) for f in faces)

    return lax.fori_loop(low, high, plane, faces, unroll=2)


def lower_kernel(
    before_ref, pops_ref, solid_ref, force_ref, side_ref, wall_ref, held, draft_ref, token_ref
):
    depth, rows, _ = pops_ref.shape[1:]
    token_ref[...] = jnp.zeros_like(token_ref)
    for group in range(2):
        force = [force_ref[d, :, 0 if group else rows - 1, :] for d in range(3)]
        out = collide([side_ref[i, 1 - group] for i in range(19)], wall_ref[1 - group] == 1, force)
        for k, i in enumerate(ENTER[1][group]):
            row = (group * 5 + k) * depth
            value = turn(out[i], STEP[i, 0], 1)
            draft_ref[row : row + depth] = turn(value, STEP[i, 2], 0)
    stream_planes(0, held.shape[1], (), pops_ref, solid_ref, force_ref, held)


def upper_kernel(
    before_ref, lower_ref, pops_ref, solid_ref, force_ref, face_ref, out_ref, tile_ref, held, sem
):
    depth, rows, width = pops_ref.shape[1:]
    half = lower_ref.shape[1]
    copies = []

    def leave(source, members, low, high):
        for a, b in runs(members):
            step = int(STEP[a, 2])
            start, stop = max(low + step, 0), min(high + step, depth)
            copy = pltpu.make_async_copy(
                source.at[a:b, start - step : stop - step],
                out_ref.at[a:b, start:stop],
                sem.at[len(copies)],
            )
            copy.start()
            copies.append(copy)

    straight = [i for i in range(19) if STEP[i, 0] == 0]
    across = [i for i in range(19) if STEP[i, 0] != 0]
    leave(lower_ref, straight, 0, half)
    faces = (face_ref[0], face_ref[1])
    for i in across:
        tile, lane = x_place(i)
        for z in range(half):
            column = turn(spread_column(faces[tile], lane + 2 * z), STEP[i, 1], 0)
            held[i, z] = patch_x(lower_ref[i, z], i, column)
    leave(held, across, 0, half)
    faces = tuple(pltpu.roll(f, 128 - 2 * half, 1) for f in faces)
    marks = upper_marks(half, depth)
    for low, high in zip(marks, marks[1:]):
        faces = stream_planes(low, high, faces, pops_ref, solid_ref, force_ref, held)
        leave(held, range(19), low, high)
    for group in range(2):
        first = slice(0, 8) if group == 0 else slice(rows - 8, rows)
        for k, i in enumerate(ENTER[1][group]):
            source = lower_ref if i in straight else held
            tile_ref[group * 5 + k, 0:half] = source[i, 0:half, first, :]
            tile_ref[group * 5 + k, half:depth] = held[i, half:depth, first, :]
    for copy in copies:
        copy.wait()


def upper_marks(half, depth):
    return list(range(half, depth - 2, 4)) + ([depth - 2] if (depth - half) % 4 else []) + [depth]


def stream_lower(half, before, pops, solid, force, sides, walls):
    _, depth, rows, width = pops.shape
    vmem = pl.BlockSpec(memory_space=pltpu.VMEM)
    return pl.pallas_call(
        lower_kernel,
        out_shape=[
            jax.ShapeDtypeStruct((19, half, rows, width), F32),
            jax.ShapeDtypeStruct((10 * depth, width), F32),
            TOKEN,
        ],
        in_specs=[pl.BlockSpec(memory_space=pl.ANY)] + [vmem] * 5,
        compiler_params=pltpu.CompilerParams(vmem_limit_bytes=ROOM),
        cost_estimate=pl.CostEstimate(flops=3000000, bytes_accessed=2000000, transcendentals=0),
        name="lower",
    )(before, pops, solid, force, sides, walls)


def stream_upper(before, lower, pops, solid, force, face):
    _, depth, rows, width = pops.shape
    vmem = pl.BlockSpec(memory_space=pltpu.VMEM)
    return pl.pallas_call(
        upper_kernel,
        out_shape=[
            jax.ShapeDtypeStruct(pops.shape, F32),
            jax.ShapeDtypeStruct((10, depth, 8, width), F32),
        ],
        in_specs=[pl.BlockSpec(memory_space=pl.ANY)] + [vmem] * 5,
        out_specs=[pl.BlockSpec(memory_space=pltpu.HBM), vmem],
        scratch_shapes=[
            pltpu.VMEM(pops.shape, F32),
            pltpu.SemaphoreType.DMA((20 * len(upper_marks(lower.shape[1], depth)),)),
        ],
        compiler_params=pltpu.CompilerParams(vmem_limit_bytes=ROOM),
        cost_estimate=pl.CostEstimate(flops=5000000, bytes_accessed=3000000, transcendentals=0),
        name="upper",
    )(before, lower, pops, solid, force, face)


def finish_kernel(shape, n_rows, whole_ref, target_ref, tile_ref, first_ref, second_ref, *refs):
    row_refs, cross_ref, refs = refs[:n_rows], refs[n_rows], refs[n_rows + 1 :]
    drag_refs, (out_ref, bead_ref, planes, tiles, bead, sem) = refs[:-6], refs[-6:]
    depth, rows, width = whole_ref.shape[1:]

    def entering(group, k):
        at = (group * 5 + k) * depth if n_rows == 1 else k * depth
        return row_refs[group % n_rows][at : at + depth]

    copies = []

    def leave(source, target):
        copy = pltpu.make_async_copy(source, target, sem.at[len(copies)])
        copy.start()
        copies.append(copy)

    for group in range(2):
        z = 0 if group == 0 else depth - 1
        for k, i in enumerate(ENTER[2][group]):
            value = entered_z(first_ref, second_ref, group, slice(k * rows, (k + 1) * rows))
            if STEP[i, 1] != 0:
                side = 0 if STEP[i, 1] == 1 else 1
                y = 0 if side == 0 else rows - 1
                row = entering(side, ENTER[1][side].index(i))[z : z + 1]
                value = jnp.where(
                    iota((rows, width), 0) == y,
                    jnp.broadcast_to(row, (rows, width)),
                    turn(value, STEP[i, 1], 0),
                )
            if STEP[i, 0] != 0:
                at = X_EDGES.index(i) * rows
                value = patch_x(value, i, cross_ref[at : at + rows])
            n = group * 5 + k
            planes[n] = value
            leave(planes.at[n], out_ref.at[i, z])
    for group in range(2):
        first = 0 if group == 0 else rows - 8
        for k, i in enumerate(ENTER[1][group]):
            n = group * 5 + k
            step = int(STEP[i, 2])
            tiles[n, 1 + step : 1 + step + depth] = tile_ref[n]
            tiles[n, 1 : 1 + depth, 0 if group == 0 else 7, :] = entering(group, k)
            low, high = max(step, 0), min(depth + step, depth)
            leave(tiles.at[n, 1 + low : 1 + high], out_ref.at[i, low:high, first : first + 8])

    count = target_ref.shape[1]
    target = target_ref[...]
    if len(drag_refs) == 2:
        slabs, cols, _ = shape
        came = arrived_drag(*drag_refs, first_ref, second_ref, 5 * rows)
        passed = row_refs[0][10 * depth : 10 * depth + 8]
        table = jnp.concatenate([one_tile(came, 0), passed], axis=1)
        owner = lax.shift_right_logical(target, 5)
        owner_slab = lax.shift_right_logical(owner, cols.bit_length() - 1)
        away_col = owner - owner_slab * cols - lax.axis_index("col")
        away_col = jnp.where(away_col < 0, away_col + cols, away_col)
        away_slab = owner_slab - lax.axis_index("slab")
        away_slab = jnp.where(away_slab < 0, away_slab + slabs, away_slab)
        place = away_col * 128 + away_slab * CAP + target - owner * CAP
        choose = (iota((256, count), 0) == place).astype(F32).astype(BF16)
        total = dot_select(table, choose, NN)
    else:
        back_ref = drag_refs[0]

        def group(k, total):
            got = [back_ref[k * GROUP + r] for r in range(GROUP)]
            slots = jnp.concatenate([t[:, 0:CAP] for t in got], axis=1)
            first = k * (GROUP * CAP)
            choose = (iota((GROUP * CAP, count), 0) + first == target).astype(F32)
            return total + dot_select(slots, choose.astype(BF16), NN)

        total = lax.fori_loop(
            0, back_ref.shape[0] // GROUP, group, jnp.zeros((8, count), F32)
        )
    bead[...] = total[0:3]
    leave(bead, bead_ref)
    for copy in copies:
        copy.wait()


def finish(shape, whole, target, tiles, first, second, entered, cross, drags):
    _, depth, rows, width = whole.shape
    vmem = pl.BlockSpec(memory_space=pltpu.VMEM)
    hbm = pl.BlockSpec(memory_space=pltpu.HBM)
    args = [whole, target, tiles, first, second, *entered, cross, *drags]
    return pl.pallas_call(
        functools.partial(finish_kernel, shape, len(entered)),
        out_shape=[
            jax.ShapeDtypeStruct(whole.shape, F32),
            jax.ShapeDtypeStruct((3, target.shape[1]), F32),
        ],
        in_specs=[hbm] + [vmem] * (len(args) - 1),
        out_specs=[hbm, hbm],
        scratch_shapes=[
            pltpu.VMEM((10, rows, width), F32),
            pltpu.VMEM((10, depth + 2, 8, width), F32),
            pltpu.VMEM((3, target.shape[1]), F32),
            pltpu.SemaphoreType.DMA((21,)),
        ],
        input_output_aliases={0: 0},
        compiler_params=pltpu.CompilerParams(vmem_limit_bytes=ROOM),
        name="finish",
    )(*args)


def shards(populations, solid_mask, bead_owner, bead_base, bead_offset, bead_velocity):
    slabs, cols, pairs = shape = tuple(lax.axis_size(a) for a in ("slab", "col", "pair"))
    owners = slabs * cols
    depth, rows = populations.shape[1:3]
    single = owners == GROUP and slabs == 4
    swap = functools.partial(
        lax.all_to_all, axis_name=("slab", "col"), split_axis=0, concat_axis=0, tiled=True
    )

    target, messages = pack(owners, bead_owner, bead_base, bead_offset, bead_velocity)
    messages = swap(messages)
    *flow, columns, sides, walls = moments(populations, solid_mask)
    force, first, second, drag, *far, token = couple(
        shape, messages, flow, populations, solid_mask, depth, rows
    )

    def send_pair(value):
        return send(value, shape, lambda s, c, p: (s, c, (p + 1) % pairs))

    def send_col(values):
        return [
            send(value, shape, lambda s, c, p, sign=sign: (s, (c + sign) % cols, p))
            for value, sign in zip(values, (1, -1))
        ]

    face = send_pair(x_faces(force, columns))
    first, second = send_slab(first, shape, 1), send_slab(second, shape, 0)
    if single:
        drags = [drag, send(far[0], shape, lambda s, c, p: ((s + 2) % slabs, c, p))]
    else:
        drags = []
        drag = swap(drag)
    fields = (populations, solid_mask, force)
    lower, draft, token = stream_lower(10, token, *fields, sides, walls)
    *leaving, cross, token = leaving_rows(depth, rows, token, draft, face, first, second, drags)
    entered, cross = send_col(leaving), send_pair(cross)
    whole, tiles = stream_upper(token, lower, *fields, face)
    return tuple(
        finish(shape, whole, target, tiles, first, second, entered, cross, drags or [drag])
    )


def solution(mesh):
    return jax.shard_map(
        shards,
        mesh=mesh,
        in_specs=(
            P(None, ("rep", "slab"), "col", "pair"),
            P(("rep", "slab"), "col", "pair"),
            P(("rep", "slab", "col", "pair")),
            P(None, ("rep", "slab", "col", "pair")),
            P(None, ("rep", "slab", "col", "pair")),
            P(None, ("rep", "slab", "col", "pair")),
        ),
        out_specs=(
            P(None, ("rep", "slab"), "col", "pair"),
            P(None, ("rep", "slab", "col", "pair")),
        ),
        check_vma=False,
    )
```

```python
import functools

import jax
import jax.numpy as jnp
import numpy as np
from jax import lax
from jax.experimental import pallas as pl
from jax.experimental.pallas import tpu as pltpu
from jax.sharding import PartitionSpec as P

CAP = 32
GROUP = 8

STEP = np.array(
    [
        [0, 0, 0],
        [1, 0, 0],
        [-1, 0, 0],
        [0, 1, 0],
        [0, -1, 0],
        [0, 0, 1],
        [0, 0, -1],
        [1, 1, 0],
        [-1, -1, 0],
        [1, -1, 0],
        [-1, 1, 0],
        [1, 0, 1],
        [-1, 0, -1],
        [1, 0, -1],
        [-1, 0, 1],
        [0, 1, 1],
        [0, -1, -1],
        [0, 1, -1],
        [0, -1, 1],
    ],
    np.int32,
)
TAU_PLUS = 0.8
TAU_MINUS = 0.5 + (3.0 / 16.0) / (TAU_PLUS - 0.5)
KEEP_EVEN = 1.0 - 1.0 / TAU_PLUS
KEEP_ODD = 1.0 - 1.0 / TAU_MINUS
FORCE_GAIN = 1.0 - 0.5 / TAU_PLUS
DRAG_COEF = 2.0
F32 = jnp.float32
BF16 = jnp.bfloat16

ENTER = [[[i for i in range(19) if STEP[i, a] == sign] for sign in (1, -1)] for a in range(3)]
TOKEN = jax.ShapeDtypeStruct((8, 128), F32)
ROOM = 16 << 20
NT = (((1,), (1,)), ((), ()))
NN = (((1,), (0,)), ((), ()))


def iota(shape, dim):
    return lax.broadcasted_iota(jnp.int32, shape, dim)


def high_low(value):
    high = value.astype(BF16)
    return high, (value - high.astype(F32)).astype(BF16)


def dot_split(left, right, dims):
    (a, b), (c, d) = left, right
    mul = functools.partial(lax.dot_general, dimension_numbers=dims, preferred_element_type=F32)
    return mul(a, c) + (mul(a, d) + mul(b, c))


def dot_select(value, choose, dims):
    first = value.astype(BF16).astype(F32)
    rest = value - first
    second = rest.astype(BF16).astype(F32)
    stacked = jnp.concatenate([first, second, rest - second], axis=0).astype(BF16)
    got = lax.dot_general(stacked, choose, dimension_numbers=dims, preferred_element_type=F32)
    rows = value.shape[0]
    return got[0:rows] + got[rows : 2 * rows] + got[2 * rows : 3 * rows]


def density_momentum(pops):
    momentum = []
    for axis in range(3):
        plus = [pops[i] for i in range(19) if STEP[i, axis] == 1]
        minus = [pops[i] for i in range(19) if STEP[i, axis] == -1]
        momentum.append(sum(plus[1:], plus[0]) - sum(minus[1:], minus[0]))
    return sum(pops[1:], pops[0]), momentum


def along(step, vector):
    terms = None
    for axis in range(3):
        if step[axis] == 0:
            continue
        if terms is None:
            terms = vector[axis] if step[axis] == 1 else -vector[axis]
        else:
            terms = terms + vector[axis] if step[axis] == 1 else terms - vector[axis]
    return terms


def collide(pops, wall, force):
    density, momentum = density_momentum(pops)
    inverse = 1.0 / density
    carried = [m + 0.5 * f for m, f in zip(momentum, force)]
    speed = [m * inverse for m in carried]
    w = 1.0 / 36.0
    bend = [(4.5 * w / TAU_PLUS) * m + (9.0 * w * FORCE_GAIN) * f for m, f in zip(carried, force)]
    push = [(3.0 * w / TAU_MINUS) * m + (3.0 * w * FORCE_GAIN) * f for m, f in zip(carried, force)]
    drop = [(1.5 * w / TAU_PLUS) * m + (3.0 * w * FORCE_GAIN) * f for m, f in zip(carried, force)]
    rest = (w / TAU_PLUS) * density - sum(
        [u * d for u, d in zip(speed[1:], drop[1:])], speed[0] * drop[0]
    )
    out = [None] * 19
    out[0] = jnp.where(wall, pops[0], KEEP_EVEN * pops[0] + 12.0 * rest)
    for i in range(1, 19, 2):
        a, b = pops[i], pops[i + 1]
        step = STEP[i]
        even = rest + along(step, speed) * along(step, bend)
        odd = along(step, push)
        if i < 7:
            even = even + even
            odd = odd + odd
        even = (0.5 * KEEP_EVEN) * (a + b) + even
        odd = (0.5 * KEEP_ODD) * (a - b) + odd
        out[i] = jnp.where(wall, b, even + odd)
        out[i + 1] = jnp.where(wall, a, even - odd)
    return out


def turn(value, amount, axis):
    if amount == 0:
        return value
    return pltpu.roll(value, int(amount) % value.shape[axis], axis)


def send(value, shape, target):
    def flat(at):
        return (at[0] * shape[1] + at[1]) * shape[2] + at[2]

    perm = [(flat(at), flat(target(*at))) for at in np.ndindex(*shape)]
    return lax.ppermute(value, ("slab", "col", "pair"), perm)


def send_slab(value, shape, which):
    def target(s, c, p):
        return ((s + (1 if s % 2 == which else -1)) % shape[0], c, p)

    return send(value, shape, target)


def odd_slab():
    return lax.rem(lax.axis_index("slab"), 2) == 1


def rank_among(member):
    count = member.shape[1]
    earlier = (iota((count, count), 0) < iota((count, count), 1)).astype(F32).astype(BF16)
    return lax.dot_general(member.astype(BF16), earlier, NN, preferred_element_type=F32)


def spread_column(tile, lane):
    return jnp.broadcast_to(tile[:, lane : lane + 1], tile.shape)


def patch_x(value, i, column):
    side = 0 if STEP[i, 0] == 1 else value.shape[1] - 1
    return jnp.where(iota(value.shape, 1) == side, column, value)


def x_place(i):
    group = 0 if STEP[i, 0] == 1 else 1
    place = ENTER[0][group].index(i)
    return place // 4, (place % 4) * 32 + group


def x_ends(planes):
    lane = lax.shift_right_logical(iota(planes[0].shape, 1), 1)
    tile = jnp.ones(planes[0].shape, F32)
    for z, value in enumerate(planes):
        tile = jnp.where(lane == z, pltpu.roll(value, 2 * z + 1, 1), tile)
    return tile


def pack_kernel(
    steps, owner_ref, base_ref, offset_ref, velocity_ref, target_ref, out_ref, table
):
    count = owner_ref.shape[1]
    step = 0 if steps == 1 else pl.program_id(0)
    local = owner_ref[...] - step * GROUP
    member = (iota((GROUP, count), 0) == local).astype(F32)
    rank = jnp.sum(member * rank_among(member), axis=0, keepdims=True).astype(jnp.int32)
    inside = (local >= 0) & (local < GROUP)
    target = jnp.where(inside, local * CAP + rank, -1)
    whole_target = jnp.where(inside, owner_ref[...] * CAP + rank, -1)

    if steps == 1:
        target_ref[...] = whole_target
    else:
        known = jnp.where(step == 0, -1, target_ref[...])
        target_ref[...] = jnp.maximum(known, whole_target)

    choose = (iota((GROUP * CAP, count), 0) == target).astype(F32).astype(BF16)
    table[...] = jnp.zeros_like(table)
    table[0:3] = base_ref[...].astype(F32) + 1.0
    table[8:11] = offset_ref[...]
    table[16:19] = velocity_ref[...]
    packed = dot_select(table[...], choose, NT)
    blank = jnp.zeros((8, CAP), F32)
    for r in range(GROUP):
        lanes = slice(r * CAP, (r + 1) * CAP)
        out_ref[r] = jnp.concatenate(
            [packed[0:8, lanes], packed[8:16, lanes], packed[16:24, lanes], blank], axis=1
        )


def pack(owners, owner, base, offset, velocity):
    count, steps = owner.shape[0], owners // GROUP
    args = (owner.reshape(1, count), base, offset, velocity)
    blocks = {}
    if steps > 1:
        blocks = dict(
            grid=(steps,),
            in_specs=[pl.BlockSpec(a.shape, lambda k: (0, 0)) for a in args],
            out_specs=[
                pl.BlockSpec((1, count), lambda k: (0, 0)),
                pl.BlockSpec((GROUP, 8, 128), lambda k: (k, 0, 0)),
            ],
            compiler_params=pltpu.CompilerParams(vmem_limit_bytes=48 << 20),
        )
    return pl.pallas_call(
        functools.partial(pack_kernel, steps),
        out_shape=[
            jax.ShapeDtypeStruct((1, count), jnp.int32),
            jax.ShapeDtypeStruct((owners, 8, 128), F32),
        ],
        scratch_shapes=[pltpu.VMEM((24, count), F32)],
        name="pack",
        **blocks,
    )(*args)


def moments_kernel(
    pops_ref, solid_ref, high_ref, low_ref, column_ref, side_ref, wall_ref, held, held_solid, flow, sem
):
    depth, rows, width = pops_ref.shape[1:]
    chunks = 4
    span = depth // chunks
    copies = [pltpu.make_async_copy(solid_ref, held_solid, sem.at[chunks])]
    for k in range(chunks):
        part = pl.ds(k * span, span)
        copies.append(
            pltpu.make_async_copy(pops_ref.at[:, part], held.at[:, part], sem.at[k])
        )
    for copy in copies:
        copy.start()

    def plane(z, carry):
        pops = [held[i, z] for i in range(19)]
        density, momentum = density_momentum(pops)
        inverse = 1.0 / density
        for axis in range(3):
            flow[axis, pl.ds(pl.multiple_of(z * rows, rows), rows)] = momentum[axis] * inverse
        return carry

    for k in range(chunks):
        copies[1 + k].wait()
        lax.fori_loop(k * span, (k + 1) * span, plane, 0, unroll=2)
    copies[0].wait()
    for axis in range(3):
        at = slice(axis * width, (axis + 1) * width)
        high_ref[at], low_ref[at] = high_low(flow[axis].T)
    for i in range(19):
        column_ref[i] = x_ends([held[i, z] for z in range(depth)])
        side_ref[i, 0] = held[i, :, 0, :]
        side_ref[i, 1] = held[i, :, rows - 1, :]
    wall_ref[0] = held_solid[:, 0, :]
    wall_ref[1] = held_solid[:, rows - 1, :]
    column_ref[19] = x_ends([held_solid[z].astype(F32) for z in range(depth)])


def moments(pops, solid):
    _, depth, rows, width = pops.shape
    hbm = pl.BlockSpec(memory_space=pltpu.HBM)
    return pl.pallas_call(
        moments_kernel,
        out_shape=[
            jax.ShapeDtypeStruct((3 * width, depth * rows), BF16),
            jax.ShapeDtypeStruct((3 * width, depth * rows), BF16),
            jax.ShapeDtypeStruct((20, rows, 128), F32),
            jax.ShapeDtypeStruct((19, 2, depth, width), F32),
            jax.ShapeDtypeStruct((2, depth, width), jnp.int32),
        ],
        in_specs=[hbm, hbm],
        scratch_shapes=[
            pltpu.VMEM(pops.shape, F32),
            pltpu.VMEM(solid.shape, jnp.int32),
            pltpu.VMEM((3, depth * rows, width), F32),
            pltpu.SemaphoreType.DMA((5,)),
        ],
        compiler_params=pltpu.CompilerParams(vmem_limit_bytes=54000000),
        cost_estimate=pl.CostEstimate(flops=3000000, bytes_accessed=4000000, transcendentals=0),
        name="moments",
    )(pops, solid)


def unpack(tiles):
    return [
        jnp.concatenate([t[:, g * CAP : (g + 1) * CAP] for t in tiles], axis=1) for g in range(3)
    ]


def couple_group(base, part, velocity, flow, depth, rows, width):
    slots = GROUP * CAP
    start = base.astype(jnp.int32) - 1

    def hat(axis, length):
        cell = iota((length, slots), 0)
        low, share = start[axis : axis + 1], part[axis : axis + 1]
        return jnp.where(cell == low, 1.0 - share, 0.0) + jnp.where(cell == low + 1, share, 0.0)

    hat_x, hat_y, hat_z = hat(0, width), hat(1, rows), hat(2, depth)
    weight = high_low((hat_z[:, None, :] * hat_y[None, :, :]).reshape(depth * rows, slots))
    across = dot_split(flow, weight, NN)
    drag = []
    for d in range(3):
        sampled = jnp.sum(across[d * width : (d + 1) * width] * hat_x, axis=0, keepdims=True)
        drag.append(DRAG_COEF * (sampled - velocity[d : d + 1]))
    spread = jnp.concatenate([hat_x * (-drag[d]) for d in range(3)], axis=0)
    return drag, dot_split(weight, high_low(spread), NT)


def couple_kernel(shape, n_drags, beads_ref, high_ref, low_ref, *refs):
    slabs, cols, _ = shape
    column_ref, pops_ref, solid_ref, force_ref, face_ref, first_ref, second_ref, *refs = refs
    drag_refs, token_ref = refs[:-1], refs[-1]
    token_ref[...] = jnp.zeros_like(token_ref)
    depth, rows, width = pops_ref.shape[1:]
    flow = (high_ref[...], low_ref[...])

    def grid(force):
        return [
            force[:, d * width : (d + 1) * width].reshape(depth, rows, width) for d in range(3)
        ]

    hollow = jnp.zeros((5, GROUP * CAP), F32)

    if n_drags == 2:
        slab, col = lax.axis_index("slab"), lax.axis_index("col")
        got = []
        for r in range(GROUP):
            there = [a - b for a, b in zip((slab, col), divmod(r, cols))]
            there = [jnp.where(a < 0, a + n, a) for a, n in zip(there, (slabs, cols))]
            got.append(beads_ref[there[0] * cols + there[1]])
        drag, force = couple_group(*unpack(got), flow, depth, rows, width)
        for d, value in enumerate(grid(force)):
            force_ref[d] = value
        stacked = jnp.concatenate(drag + [hollow], axis=0)
        lanes = cols * CAP
        blank = jnp.zeros((8, 128 - lanes), F32)
        for dz in range(slabs):
            tile = jnp.concatenate([stacked[:, dz * lanes : (dz + 1) * lanes], blank], axis=1)
            drag_refs[0][dz] = tile
            if dz == 2:
                drag_refs[1][...] = tile
            if dz == 1:
                down = tile
        up = tile
    else:
        force_ref[...] = jnp.zeros_like(force_ref)
        blank = jnp.zeros((8, 128 - CAP), F32)

        def group(k, carry):
            got = [beads_ref[k * GROUP + r] for r in range(GROUP)]
            drag, force = couple_group(*unpack(got), flow, depth, rows, width)
            for d, value in enumerate(grid(force)):
                force_ref[d] += value
            stacked = jnp.concatenate(drag + [hollow], axis=0)
            for r in range(GROUP):
                drag_refs[0][k * GROUP + r] = jnp.concatenate(
                    [stacked[:, r * CAP : (r + 1) * CAP], blank], axis=1
                )
            return carry

        lax.fori_loop(0, beads_ref.shape[0] // GROUP, group, 0)

    force = [x_ends([force_ref[d, z] for z in range(depth)]) for d in range(3)]
    out = collide([column_ref[i] for i in range(19)], column_ref[19] == 1.0, force)
    high = lax.rem(iota((rows, 128), 1), 2) == 0
    ends = [jnp.where(high, out[i], out[j])[:, 0:32] for i, j in zip(*ENTER[0])]
    face_ref[0] = jnp.concatenate(ends[0:4], axis=1)
    face_ref[1] = jnp.concatenate([ends[4], jnp.zeros((rows, 96), F32)], axis=1)
    odd = odd_slab()
    leaving = []
    for group, z in ((0, depth - 1), (1, 0)):
        out = collide(
            [pops_ref[i, z] for i in range(19)],
            solid_ref[z] == 1,
            [force_ref[d, z] for d in range(3)],
        )
        leaving.append([turn(out[i], STEP[i, 0], 1) for i in ENTER[2][group]])
    if n_drags == 2:
        leaving[0].append(up)
        leaving[1].append(down)
    row = 0
    for a, b in zip(*leaving):
        at = slice(row, row + a.shape[0])
        first_ref[at] = jnp.where(odd, a, b)
        second_ref[at] = jnp.where(odd, b, a)
        row += a.shape[0]


def couple(shape, beads, flow, columns, pops, solid):
    _, depth, rows, width = pops.shape
    single = beads.shape[0] == GROUP
    tile = jax.ShapeDtypeStruct((8, 128), F32)
    drags = [jax.ShapeDtypeStruct((shape[0], 8, 128), F32), tile] if single else [beads]
    message = jax.ShapeDtypeStruct((5 * rows + (8 if single else 0), width), F32)
    return pl.pallas_call(
        functools.partial(couple_kernel, shape, len(drags)),
        out_shape=[
            jax.ShapeDtypeStruct((3, depth, rows, width), F32),
            jax.ShapeDtypeStruct((2, rows, 128), F32),
            message,
            message,
        ]
        + [jax.ShapeDtypeStruct(d.shape, F32) for d in drags]
        + [TOKEN],
        compiler_params=pltpu.CompilerParams(vmem_limit_bytes=ROOM),
        name="couple",
    )(beads, *flow, columns, pops, solid)


def entered_z(first_ref, second_ref, side, rows):
    odd = odd_slab() if side == 0 else jnp.logical_not(odd_slab())
    return jnp.where(odd, second_ref[rows], first_ref[rows])


X_EDGES = [i for side in range(2) for i in ENTER[2][side] if STEP[i, 0] != 0]


def rows_kernel(depth, rows, before_ref, draft_ref, face_ref, first_ref, second_ref, *refs):
    refs, (cross_ref, token_ref, turned) = refs[:-3], refs[-3:]
    token_ref[...] = jnp.zeros_like(token_ref)
    outs = refs[-1:] if len(refs) == 3 else refs
    for n in range(2):
        turned[n] = face_ref[n].T
    for group in range(2):
        out_ref = outs[0] if len(outs) == 1 else outs[group]
        base = group * 5 * depth if len(outs) == 1 else 0
        y = rows - 1 if group == 0 else 0
        for k, i in enumerate(ENTER[1][group]):
            at = base + k * depth
            value = draft_ref[(group * 5 + k) * depth : (group * 5 + k + 1) * depth]
            if STEP[i, 0] != 0:
                tile, lane = x_place(i)
                column = turned[tile, pl.ds(lane, depth, stride=2), :][:, y : y + 1]
                value = patch_x(value, i, jnp.broadcast_to(column, value.shape))
            out_ref[at : at + depth] = value
            if STEP[i, 2] != 0:
                side = 0 if STEP[i, 2] == 1 else 1
                z = 0 if side == 0 else depth - 1
                row = ENTER[2][side].index(i) * rows + y
                out_ref[at + z : at + z + 1] = entered_z(
                    first_ref, second_ref, side, slice(row, row + 1)
                )
    if len(refs) == 3:
        own_ref, far_ref, out_ref = refs
        came = arrived_drag(own_ref, far_ref, first_ref, second_ref, 5 * rows)
        out_ref[10 * depth : 10 * depth + 8] = one_tile(came, 1)
    for k, i in enumerate(X_EDGES):
        side = 0 if STEP[i, 2] == 1 else 1
        at = ENTER[2][side].index(i) * rows
        cross_ref[k * rows : (k + 1) * rows] = entered_z(
            first_ref, second_ref, side, slice(at, at + rows)
        )


def arrived_drag(own_ref, far_ref, first_ref, second_ref, tail):
    at = slice(tail, tail + 8)
    up, down = [entered_z(first_ref, second_ref, side, at) for side in range(2)]
    return [own_ref[0], down, far_ref[...], up]


def one_tile(tiles, col):
    return jnp.concatenate([t[:, col * CAP : (col + 1) * CAP] for t in tiles], axis=1)


def leaving_rows(depth, rows, before, draft, face, first, second, drags):
    width = draft.shape[1]
    if drags:
        sizes = [10 * depth + 8]
    else:
        sizes = [5 * depth] * 2
    args = (draft, face, first, second, *drags)
    return pl.pallas_call(
        functools.partial(rows_kernel, depth, rows),
        out_shape=[jax.ShapeDtypeStruct((n, width), F32) for n in sizes + [4 * rows]] + [TOKEN],
        in_specs=[pl.BlockSpec(memory_space=pl.ANY)]
        + [pl.BlockSpec(memory_space=pltpu.VMEM)] * len(args),
        scratch_shapes=[pltpu.VMEM((2, 128, rows), F32)],
        compiler_params=pltpu.CompilerParams(vmem_limit_bytes=ROOM),
        name="rows",
    )(before, *args)


def runs(members):
    found = []
    for i in members:
        if found and found[-1][1] == i and STEP[i, 2] == STEP[i - 1, 2]:
            found[-1] = (found[-1][0], i + 1)
        else:
            found.append((i, i + 1))
    return found


def stream_planes(low, high, faces, pops_ref, solid_ref, force_ref, held):
    def plane(z, faces):
        out = collide(
            [pops_ref[i, z] for i in range(19)],
            solid_ref[z] == 1,
            [force_ref[d, z] for d in range(3)],
        )
        for i in range(19):
            value = turn(out[i], STEP[i, 0], 1)
            if STEP[i, 0] != 0 and faces:
                tile, lane = x_place(i)
                value = patch_x(value, i, spread_column(faces[tile], lane))
            held[i, z] = turn(value, STEP[i, 1], 0)
        return tuple(pltpu.roll(f, 126, 1) for f in faces)

    return lax.fori_loop(low, high, plane, faces, unroll=2)


def lower_kernel(
    before_ref, pops_ref, solid_ref, force_ref, side_ref, wall_ref, held, draft_ref, token_ref
):
    depth, rows, _ = pops_ref.shape[1:]
    token_ref[...] = jnp.zeros_like(token_ref)
    for group in range(2):
        force = [force_ref[d, :, 0 if group else rows - 1, :] for d in range(3)]
        out = collide([side_ref[i, 1 - group] for i in range(19)], wall_ref[1 - group] == 1, force)
        for k, i in enumerate(ENTER[1][group]):
            row = (group * 5 + k) * depth
            value = turn(out[i], STEP[i, 0], 1)
            draft_ref[row : row + depth] = turn(value, STEP[i, 2], 0)
    stream_planes(0, held.shape[1], (), pops_ref, solid_ref, force_ref, held)


def upper_kernel(
    before_ref, lower_ref, pops_ref, solid_ref, force_ref, face_ref, out_ref, tile_ref, held, sem
):
    depth, rows, width = pops_ref.shape[1:]
    half = lower_ref.shape[1]
    copies = []

    def leave(source, members, low, high):
        for a, b in runs(members):
            step = int(STEP[a, 2])
            start, stop = max(low + step, 0), min(high + step, depth)
            copy = pltpu.make_async_copy(
                source.at[a:b, start - step : stop - step],
                out_ref.at[a:b, start:stop],
                sem.at[len(copies)],
            )
            copy.start()
            copies.append(copy)

    straight = [i for i in range(19) if STEP[i, 0] == 0]
    across = [i for i in range(19) if STEP[i, 0] != 0]
    leave(lower_ref, straight, 0, half)
    faces = (face_ref[0], face_ref[1])
    for i in across:
        tile, lane = x_place(i)
        for z in range(half):
            column = turn(spread_column(faces[tile], lane + 2 * z), STEP[i, 1], 0)
            held[i, z] = patch_x(lower_ref[i, z], i, column)
    leave(held, across, 0, half)
    faces = tuple(pltpu.roll(f, 128 - 2 * half, 1) for f in faces)
    marks = upper_marks(half, depth)
    for low, high in zip(marks, marks[1:]):
        faces = stream_planes(low, high, faces, pops_ref, solid_ref, force_ref, held)
        leave(held, range(19), low, high)
    for group in range(2):
        first = slice(0, 8) if group == 0 else slice(rows - 8, rows)
        for k, i in enumerate(ENTER[1][group]):
            source = lower_ref if i in straight else held
            tile_ref[group * 5 + k, 0:half] = source[i, 0:half, first, :]
            tile_ref[group * 5 + k, half:depth] = held[i, half:depth, first, :]
    for copy in copies:
        copy.wait()


def upper_marks(half, depth):
    return list(range(half, depth - 2, 4)) + ([depth - 2] if (depth - half) % 4 else []) + [depth]


def stream_lower(half, before, pops, solid, force, sides, walls):
    _, depth, rows, width = pops.shape
    vmem = pl.BlockSpec(memory_space=pltpu.VMEM)
    return pl.pallas_call(
        lower_kernel,
        out_shape=[
            jax.ShapeDtypeStruct((19, half, rows, width), F32),
            jax.ShapeDtypeStruct((10 * depth, width), F32),
            TOKEN,
        ],
        in_specs=[pl.BlockSpec(memory_space=pl.ANY)] + [vmem] * 5,
        compiler_params=pltpu.CompilerParams(vmem_limit_bytes=ROOM),
        cost_estimate=pl.CostEstimate(flops=3000000, bytes_accessed=2000000, transcendentals=0),
        name="lower",
    )(before, pops, solid, force, sides, walls)


def stream_upper(before, lower, pops, solid, force, face):
    _, depth, rows, width = pops.shape
    vmem = pl.BlockSpec(memory_space=pltpu.VMEM)
    return pl.pallas_call(
        upper_kernel,
        out_shape=[
            jax.ShapeDtypeStruct(pops.shape, F32),
            jax.ShapeDtypeStruct((10, depth, 8, width), F32),
        ],
        in_specs=[pl.BlockSpec(memory_space=pl.ANY)] + [vmem] * 5,
        out_specs=[pl.BlockSpec(memory_space=pltpu.HBM), vmem],
        scratch_shapes=[
            pltpu.VMEM(pops.shape, F32),
            pltpu.SemaphoreType.DMA((20 * len(upper_marks(lower.shape[1], depth)),)),
        ],
        compiler_params=pltpu.CompilerParams(vmem_limit_bytes=ROOM),
        cost_estimate=pl.CostEstimate(flops=5000000, bytes_accessed=3000000, transcendentals=0),
        name="upper",
    )(before, lower, pops, solid, force, face)


def finish_kernel(shape, n_rows, whole_ref, target_ref, tile_ref, first_ref, second_ref, *refs):
    row_refs, cross_ref, refs = refs[:n_rows], refs[n_rows], refs[n_rows + 1 :]
    drag_refs, (out_ref, bead_ref, planes, tiles, bead, sem) = refs[:-6], refs[-6:]
    depth, rows, width = whole_ref.shape[1:]

    def entering(group, k):
        at = (group * 5 + k) * depth if n_rows == 1 else k * depth
        return row_refs[group % n_rows][at : at + depth]

    copies = []

    def leave(source, target):
        copy = pltpu.make_async_copy(source, target, sem.at[len(copies)])
        copy.start()
        copies.append(copy)

    for group in range(2):
        z = 0 if group == 0 else depth - 1
        for k, i in enumerate(ENTER[2][group]):
            value = entered_z(first_ref, second_ref, group, slice(k * rows, (k + 1) * rows))
            if STEP[i, 1] != 0:
                side = 0 if STEP[i, 1] == 1 else 1
                y = 0 if side == 0 else rows - 1
                row = entering(side, ENTER[1][side].index(i))[z : z + 1]
                value = jnp.where(
                    iota((rows, width), 0) == y,
                    jnp.broadcast_to(row, (rows, width)),
                    turn(value, STEP[i, 1], 0),
                )
            if STEP[i, 0] != 0:
                at = X_EDGES.index(i) * rows
                value = patch_x(value, i, cross_ref[at : at + rows])
            n = group * 5 + k
            planes[n] = value
            leave(planes.at[n], out_ref.at[i, z])
    for group in range(2):
        first = 0 if group == 0 else rows - 8
        for k, i in enumerate(ENTER[1][group]):
            n = group * 5 + k
            step = int(STEP[i, 2])
            tiles[n, 1 + step : 1 + step + depth] = tile_ref[n]
            tiles[n, 1 : 1 + depth, 0 if group == 0 else 7, :] = entering(group, k)
            low, high = max(step, 0), min(depth + step, depth)
            leave(tiles.at[n, 1 + low : 1 + high], out_ref.at[i, low:high, first : first + 8])

    count = target_ref.shape[1]
    target = target_ref[...]
    if len(drag_refs) == 2:
        slabs, cols, _ = shape
        came = arrived_drag(*drag_refs, first_ref, second_ref, 5 * rows)
        passed = row_refs[0][10 * depth : 10 * depth + 8]
        table = jnp.concatenate([one_tile(came, 0), passed], axis=1)
        owner = lax.shift_right_logical(target, 5)
        owner_slab = lax.shift_right_logical(owner, cols.bit_length() - 1)
        away_col = owner - owner_slab * cols - lax.axis_index("col")
        away_col = jnp.where(away_col < 0, away_col + cols, away_col)
        away_slab = owner_slab - lax.axis_index("slab")
        away_slab = jnp.where(away_slab < 0, away_slab + slabs, away_slab)
        place = away_col * 128 + away_slab * CAP + target - owner * CAP
        choose = (iota((256, count), 0) == place).astype(F32).astype(BF16)
        total = dot_select(table, choose, NN)
    else:
        back_ref = drag_refs[0]

        def group(k, total):
            got = [back_ref[k * GROUP + r] for r in range(GROUP)]
            slots = jnp.concatenate([t[:, 0:CAP] for t in got], axis=1)
            first = k * (GROUP * CAP)
            choose = (iota((GROUP * CAP, count), 0) + first == target).astype(F32)
            return total + dot_select(slots, choose.astype(BF16), NN)

        total = lax.fori_loop(
            0, back_ref.shape[0] // GROUP, group, jnp.zeros((8, count), F32)
        )
    bead[...] = total[0:3]
    leave(bead, bead_ref)
    for copy in copies:
        copy.wait()


def finish(shape, whole, target, tiles, first, second, entered, cross, drags):
    _, depth, rows, width = whole.shape
    vmem = pl.BlockSpec(memory_space=pltpu.VMEM)
    hbm = pl.BlockSpec(memory_space=pltpu.HBM)
    args = [whole, target, tiles, first, second, *entered, cross, *drags]
    return pl.pallas_call(
        functools.partial(finish_kernel, shape, len(entered)),
        out_shape=[
            jax.ShapeDtypeStruct(whole.shape, F32),
            jax.ShapeDtypeStruct((3, target.shape[1]), F32),
        ],
        in_specs=[hbm] + [vmem] * (len(args) - 1),
        out_specs=[hbm, hbm],
        scratch_shapes=[
            pltpu.VMEM((10, rows, width), F32),
            pltpu.VMEM((10, depth + 2, 8, width), F32),
            pltpu.VMEM((3, target.shape[1]), F32),
            pltpu.SemaphoreType.DMA((21,)),
        ],
        input_output_aliases={0: 0},
        compiler_params=pltpu.CompilerParams(vmem_limit_bytes=ROOM),
        name="finish",
    )(*args)


def shards(populations, solid_mask, bead_owner, bead_base, bead_offset, bead_velocity):
    slabs, cols, pairs = shape = tuple(lax.axis_size(a) for a in ("slab", "col", "pair"))
    owners = slabs * cols
    depth, rows = populations.shape[1:3]
    single = owners == GROUP and slabs == 4
    swap = functools.partial(
        lax.all_to_all, axis_name=("slab", "col"), split_axis=0, concat_axis=0, tiled=True
    )

    target, messages = pack(owners, bead_owner, bead_base, bead_offset, bead_velocity)
    messages = swap(messages)
    *flow, columns, sides, walls = moments(populations, solid_mask)
    force, face, first, second, drag, *far, token = couple(
        shape, messages, flow, columns, populations, solid_mask
    )

    def send_pair(value):
        return send(value, shape, lambda s, c, p: (s, c, (p + 1) % pairs))

    def send_col(values):
        return [
            send(value, shape, lambda s, c, p, sign=sign: (s, (c + sign) % cols, p))
            for value, sign in zip(values, (1, -1))
        ]

    face = send_pair(face)
    first, second = send_slab(first, shape, 1), send_slab(second, shape, 0)
    if single:
        drags = [drag, send(far[0], shape, lambda s, c, p: ((s + 2) % slabs, c, p))]
    else:
        drags = []
        drag = swap(drag)
    fields = (populations, solid_mask, force)
    lower, draft, token = stream_lower(10, token, *fields, sides, walls)
    *leaving, cross, token = leaving_rows(depth, rows, token, draft, face, first, second, drags)
    entered, cross = send_col(leaving), send_pair(cross)
    whole, tiles = stream_upper(token, lower, *fields, face)
    return tuple(
        finish(shape, whole, target, tiles, first, second, entered, cross, drags or [drag])
    )


def solution(mesh):
    return jax.shard_map(
        shards,
        mesh=mesh,
        in_specs=(
            P(None, ("rep", "slab"), "col", "pair"),
            P(("rep", "slab"), "col", "pair"),
            P(("rep", "slab", "col", "pair")),
            P(None, ("rep", "slab", "col", "pair")),
            P(None, ("rep", "slab", "col", "pair")),
            P(None, ("rep", "slab", "col", "pair")),
        ),
        out_specs=(
            P(None, ("rep", "slab"), "col", "pair"),
            P(None, ("rep", "slab", "col", "pair")),
        ),
        check_vma=False,
    )
```

```python
import functools

import jax
import jax.numpy as jnp
import numpy as np
from jax import lax
from jax.experimental import pallas as pl
from jax.experimental.pallas import tpu as pltpu
from jax.sharding import PartitionSpec as P

CAP = 32
GROUP = 8

STEP = np.array(
    [
        [0, 0, 0],
        [1, 0, 0],
        [-1, 0, 0],
        [0, 1, 0],
        [0, -1, 0],
        [0, 0, 1],
        [0, 0, -1],
        [1, 1, 0],
        [-1, -1, 0],
        [1, -1, 0],
        [-1, 1, 0],
        [1, 0, 1],
        [-1, 0, -1],
        [1, 0, -1],
        [-1, 0, 1],
        [0, 1, 1],
        [0, -1, -1],
        [0, 1, -1],
        [0, -1, 1],
    ],
    np.int32,
)
TAU_PLUS = 0.8
TAU_MINUS = 0.5 + (3.0 / 16.0) / (TAU_PLUS - 0.5)
KEEP_EVEN = 1.0 - 1.0 / TAU_PLUS
KEEP_ODD = 1.0 - 1.0 / TAU_MINUS
FORCE_GAIN = 1.0 - 0.5 / TAU_PLUS
DRAG_COEF = 2.0
F32 = jnp.float32
BF16 = jnp.bfloat16

ENTER = [[[i for i in range(19) if STEP[i, a] == sign] for sign in (1, -1)] for a in range(3)]
TOKEN = jax.ShapeDtypeStruct((8, 128), F32)
LONG = pl.CostEstimate(flops=5000000000, bytes_accessed=1000000000, transcendentals=0)
ROOM = 16 << 20
NT = (((1,), (1,)), ((), ()))
NN = (((1,), (0,)), ((), ()))


def iota(shape, dim):
    return lax.broadcasted_iota(jnp.int32, shape, dim)


def high_low(value):
    high = value.astype(BF16)
    return high, (value - high.astype(F32)).astype(BF16)


def dot_split(left, right, dims):
    (a, b), (c, d) = left, right
    mul = functools.partial(lax.dot_general, dimension_numbers=dims, preferred_element_type=F32)
    return mul(a, c) + (mul(a, d) + mul(b, c))


def dot_select(value, choose, dims):
    first = value.astype(BF16).astype(F32)
    rest = value - first
    second = rest.astype(BF16).astype(F32)
    stacked = jnp.concatenate([first, second, rest - second], axis=0).astype(BF16)
    got = lax.dot_general(stacked, choose, dimension_numbers=dims, preferred_element_type=F32)
    rows = value.shape[0]
    return got[0:rows] + got[rows : 2 * rows] + got[2 * rows : 3 * rows]


def density_momentum(pops):
    momentum = []
    for axis in range(3):
        plus = [pops[i] for i in range(19) if STEP[i, axis] == 1]
        minus = [pops[i] for i in range(19) if STEP[i, axis] == -1]
        momentum.append(sum(plus[1:], plus[0]) - sum(minus[1:], minus[0]))
    return sum(pops[1:], pops[0]), momentum


def along(step, vector):
    terms = None
    for axis in range(3):
        if step[axis] == 0:
            continue
        if terms is None:
            terms = vector[axis] if step[axis] == 1 else -vector[axis]
        else:
            terms = terms + vector[axis] if step[axis] == 1 else terms - vector[axis]
    return terms


def collide(pops, wall, force):
    density, momentum = density_momentum(pops)
    inverse = 1.0 / density
    carried = [m + 0.5 * f for m, f in zip(momentum, force)]
    speed = [m * inverse for m in carried]
    w = 1.0 / 36.0
    bend = [(4.5 * w / TAU_PLUS) * m + (9.0 * w * FORCE_GAIN) * f for m, f in zip(carried, force)]
    push = [(3.0 * w / TAU_MINUS) * m + (3.0 * w * FORCE_GAIN) * f for m, f in zip(carried, force)]
    drop = [(1.5 * w / TAU_PLUS) * m + (3.0 * w * FORCE_GAIN) * f for m, f in zip(carried, force)]
    rest = (w / TAU_PLUS) * density - sum(
        [u * d for u, d in zip(speed[1:], drop[1:])], speed[0] * drop[0]
    )
    out = [None] * 19
    out[0] = jnp.where(wall, pops[0], KEEP_EVEN * pops[0] + 12.0 * rest)
    for i in range(1, 19, 2):
        a, b = pops[i], pops[i + 1]
        step = STEP[i]
        even = rest + along(step, speed) * along(step, bend)
        odd = along(step, push)
        if i < 7:
            even = even + even
            odd = odd + odd
        even = (0.5 * KEEP_EVEN) * (a + b) + even
        odd = (0.5 * KEEP_ODD) * (a - b) + odd
        out[i] = jnp.where(wall, b, even + odd)
        out[i + 1] = jnp.where(wall, a, even - odd)
    return out


def turn(value, amount, axis):
    if amount == 0:
        return value
    return pltpu.roll(value, int(amount) % value.shape[axis], axis)


def send(value, shape, target):
    def flat(at):
        return (at[0] * shape[1] + at[1]) * shape[2] + at[2]

    perm = [(flat(at), flat(target(*at))) for at in np.ndindex(*shape)]
    return lax.ppermute(value, ("slab", "col", "pair"), perm)


def send_slab(value, shape, which):
    def target(s, c, p):
        return ((s + (1 if s % 2 == which else -1)) % shape[0], c, p)

    return send(value, shape, target)


def odd_slab():
    return lax.rem(lax.axis_index("slab"), 2) == 1


def rank_among(member):
    count = member.shape[1]
    earlier = (iota((count, count), 0) < iota((count, count), 1)).astype(F32).astype(BF16)
    return lax.dot_general(member.astype(BF16), earlier, NN, preferred_element_type=F32)


def spread_column(tile, lane):
    return jnp.broadcast_to(tile[:, lane : lane + 1], tile.shape)


def patch_x(value, i, column):
    side = 0 if STEP[i, 0] == 1 else value.shape[1] - 1
    return jnp.where(iota(value.shape, 1) == side, column, value)


def x_place(i):
    group = 0 if STEP[i, 0] == 1 else 1
    place = ENTER[0][group].index(i)
    return place // 4, (place % 4) * 32 + group


def x_ends(planes):
    lane = lax.shift_right_logical(iota(planes[0].shape, 1), 1)
    tile = jnp.ones(planes[0].shape, F32)
    for z, value in enumerate(planes):
        tile = jnp.where(lane == z, pltpu.roll(value, 2 * z + 1, 1), tile)
    return tile


def pack_kernel(
    steps, owner_ref, base_ref, offset_ref, velocity_ref, target_ref, out_ref, table
):
    count = owner_ref.shape[1]
    step = 0 if steps == 1 else pl.program_id(0)
    local = owner_ref[...] - step * GROUP
    member = (iota((GROUP, count), 0) == local).astype(F32)
    rank = jnp.sum(member * rank_among(member), axis=0, keepdims=True).astype(jnp.int32)
    inside = (local >= 0) & (local < GROUP)
    target = jnp.where(inside, local * CAP + rank, -1)
    whole_target = jnp.where(inside, owner_ref[...] * CAP + rank, -1)

    if steps == 1:
        target_ref[...] = whole_target
    else:
        known = jnp.where(step == 0, -1, target_ref[...])
        target_ref[...] = jnp.maximum(known, whole_target)

    choose = (iota((GROUP * CAP, count), 0) == target).astype(F32).astype(BF16)
    table[...] = jnp.zeros_like(table)
    table[0:3] = base_ref[...].astype(F32) + 1.0
    table[8:11] = offset_ref[...]
    table[16:19] = velocity_ref[...]
    packed = dot_select(table[...], choose, NT)
    blank = jnp.zeros((8, CAP), F32)
    for r in range(GROUP):
        lanes = slice(r * CAP, (r + 1) * CAP)
        out_ref[r] = jnp.concatenate(
            [packed[0:8, lanes], packed[8:16, lanes], packed[16:24, lanes], blank], axis=1
        )


def pack(owners, owner, base, offset, velocity):
    count, steps = owner.shape[0], owners // GROUP
    args = (owner.reshape(1, count), base, offset, velocity)
    blocks = {}
    if steps > 1:
        blocks = dict(
            grid=(steps,),
            in_specs=[pl.BlockSpec(a.shape, lambda k: (0, 0)) for a in args],
            out_specs=[
                pl.BlockSpec((1, count), lambda k: (0, 0)),
                pl.BlockSpec((GROUP, 8, 128), lambda k: (k, 0, 0)),
            ],
            compiler_params=pltpu.CompilerParams(vmem_limit_bytes=48 << 20),
        )
    return pl.pallas_call(
        functools.partial(pack_kernel, steps),
        out_shape=[
            jax.ShapeDtypeStruct((1, count), jnp.int32),
            jax.ShapeDtypeStruct((owners, 8, 128), F32),
        ],
        scratch_shapes=[pltpu.VMEM((24, count), F32)],
        name="pack",
        **blocks,
    )(*args)


def moments_kernel(
    pops_ref, solid_ref, high_ref, low_ref, column_ref, side_ref, wall_ref, held, held_solid, flow, sem
):
    depth, rows, width = pops_ref.shape[1:]
    chunks = 4
    span = depth // chunks
    copies = [pltpu.make_async_copy(solid_ref, held_solid, sem.at[chunks])]
    for k in range(chunks):
        part = pl.ds(k * span, span)
        copies.append(
            pltpu.make_async_copy(pops_ref.at[:, part], held.at[:, part], sem.at[k])
        )
    for copy in copies:
        copy.start()

    def plane(z, carry):
        pops = [held[i, z] for i in range(19)]
        density, momentum = density_momentum(pops)
        inverse = 1.0 / density
        for axis in range(3):
            flow[axis, pl.ds(pl.multiple_of(z * rows, rows), rows)] = momentum[axis] * inverse
        return carry

    for k in range(chunks):
        copies[1 + k].wait()
        lax.fori_loop(k * span, (k + 1) * span, plane, 0, unroll=2)
    copies[0].wait()
    for axis in range(3):
        at = slice(axis * width, (axis + 1) * width)
        high_ref[at], low_ref[at] = high_low(flow[axis].T)
    for i in range(19):
        column_ref[i] = x_ends([held[i, z] for z in range(depth)])
        side_ref[i, 0] = held[i, :, 0, :]
        side_ref[i, 1] = held[i, :, rows - 1, :]
    wall_ref[0] = held_solid[:, 0, :]
    wall_ref[1] = held_solid[:, rows - 1, :]
    column_ref[19] = x_ends([held_solid[z].astype(F32) for z in range(depth)])


def moments(pops, solid):
    _, depth, rows, width = pops.shape
    hbm = pl.BlockSpec(memory_space=pltpu.HBM)
    return pl.pallas_call(
        moments_kernel,
        out_shape=[
            jax.ShapeDtypeStruct((3 * width, depth * rows), BF16),
            jax.ShapeDtypeStruct((3 * width, depth * rows), BF16),
            jax.ShapeDtypeStruct((20, rows, 128), F32),
            jax.ShapeDtypeStruct((19, 2, depth, width), F32),
            jax.ShapeDtypeStruct((2, depth, width), jnp.int32),
        ],
        in_specs=[hbm, hbm],
        scratch_shapes=[
            pltpu.VMEM(pops.shape, F32),
            pltpu.VMEM(solid.shape, jnp.int32),
            pltpu.VMEM((3, depth * rows, width), F32),
            pltpu.SemaphoreType.DMA((5,)),
        ],
        compiler_params=pltpu.CompilerParams(vmem_limit_bytes=54000000),
        cost_estimate=pl.CostEstimate(flops=3000000, bytes_accessed=4000000, transcendentals=0),
        name="moments",
    )(pops, solid)


def unpack(tiles):
    return [
        jnp.concatenate([t[:, g * CAP : (g + 1) * CAP] for t in tiles], axis=1) for g in range(3)
    ]


def couple_group(base, part, velocity, flow, depth, rows, width):
    slots = GROUP * CAP
    start = base.astype(jnp.int32) - 1

    def hat(axis, length):
        cell = iota((length, slots), 0)
        low, share = start[axis : axis + 1], part[axis : axis + 1]
        return jnp.where(cell == low, 1.0 - share, 0.0) + jnp.where(cell == low + 1, share, 0.0)

    hat_x, hat_y, hat_z = hat(0, width), hat(1, rows), hat(2, depth)
    weight = high_low((hat_z[:, None, :] * hat_y[None, :, :]).reshape(depth * rows, slots))
    across = dot_split(flow, weight, NN)
    drag = []
    for d in range(3):
        sampled = jnp.sum(across[d * width : (d + 1) * width] * hat_x, axis=0, keepdims=True)
        drag.append(DRAG_COEF * (sampled - velocity[d : d + 1]))
    spread = jnp.concatenate([hat_x * (-drag[d]) for d in range(3)], axis=0)
    return drag, dot_split(weight, high_low(spread), NT)


def couple_kernel(shape, n_drags, beads_ref, high_ref, low_ref, *refs):
    slabs, cols, _ = shape
    column_ref, pops_ref, solid_ref, force_ref, face_ref, first_ref, second_ref, *refs = refs
    drag_refs, token_ref = refs[:-1], refs[-1]
    token_ref[...] = jnp.zeros_like(token_ref)
    depth, rows, width = pops_ref.shape[1:]
    flow = (high_ref[...], low_ref[...])

    def grid(force):
        return [
            force[:, d * width : (d + 1) * width].reshape(depth, rows, width) for d in range(3)
        ]

    hollow = jnp.zeros((5, GROUP * CAP), F32)

    if n_drags == 2:
        slab, col = lax.axis_index("slab"), lax.axis_index("col")
        got = []
        for r in range(GROUP):
            there = [a - b for a, b in zip((slab, col), divmod(r, cols))]
            there = [jnp.where(a < 0, a + n, a) for a, n in zip(there, (slabs, cols))]
            got.append(beads_ref[there[0] * cols + there[1]])
        drag, force = couple_group(*unpack(got), flow, depth, rows, width)
        for d, value in enumerate(grid(force)):
            force_ref[d] = value
        stacked = jnp.concatenate(drag + [hollow], axis=0)
        lanes = cols * CAP
        blank = jnp.zeros((8, 128 - lanes), F32)
        for dz in range(slabs):
            tile = jnp.concatenate([stacked[:, dz * lanes : (dz + 1) * lanes], blank], axis=1)
            drag_refs[0][dz] = tile
            if dz == 2:
                drag_refs[1][...] = tile
            if dz == 1:
                down = tile
        up = tile
    else:
        force_ref[...] = jnp.zeros_like(force_ref)
        blank = jnp.zeros((8, 128 - CAP), F32)

        def group(k, carry):
            got = [beads_ref[k * GROUP + r] for r in range(GROUP)]
            drag, force = couple_group(*unpack(got), flow, depth, rows, width)
            for d, value in enumerate(grid(force)):
                force_ref[d] += value
            stacked = jnp.concatenate(drag + [hollow], axis=0)
            for r in range(GROUP):
                drag_refs[0][k * GROUP + r] = jnp.concatenate(
                    [stacked[:, r * CAP : (r + 1) * CAP], blank], axis=1
                )
            return carry

        lax.fori_loop(0, beads_ref.shape[0] // GROUP, group, 0)

    force = [x_ends([force_ref[d, z] for z in range(depth)]) for d in range(3)]
    out = collide([column_ref[i] for i in range(19)], column_ref[19] == 1.0, force)
    high = lax.rem(iota((rows, 128), 1), 2) == 0
    ends = [jnp.where(high, out[i], out[j])[:, 0:32] for i, j in zip(*ENTER[0])]
    face_ref[0] = jnp.concatenate(ends[0:4], axis=1)
    face_ref[1] = jnp.concatenate([ends[4], jnp.zeros((rows, 96), F32)], axis=1)
    odd = odd_slab()
    leaving = []
    for group, z in ((0, depth - 1), (1, 0)):
        out = collide(
            [pops_ref[i, z] for i in range(19)],
            solid_ref[z] == 1,
            [force_ref[d, z] for d in range(3)],
        )
        leaving.append([turn(out[i], STEP[i, 0], 1) for i in ENTER[2][group]])
    if n_drags == 2:
        leaving[0].append(up)
        leaving[1].append(down)
    row = 0
    for a, b in zip(*leaving):
        at = slice(row, row + a.shape[0])
        first_ref[at] = jnp.where(odd, a, b)
        second_ref[at] = jnp.where(odd, b, a)
        row += a.shape[0]


def couple(shape, beads, flow, columns, pops, solid):
    _, depth, rows, width = pops.shape
    single = beads.shape[0] == GROUP
    tile = jax.ShapeDtypeStruct((8, 128), F32)
    drags = [jax.ShapeDtypeStruct((shape[0], 8, 128), F32), tile] if single else [beads]
    message = jax.ShapeDtypeStruct((5 * rows + (8 if single else 0), width), F32)
    return pl.pallas_call(
        functools.partial(couple_kernel, shape, len(drags)),
        out_shape=[
            jax.ShapeDtypeStruct((3, depth, rows, width), F32),
            jax.ShapeDtypeStruct((2, rows, 128), F32),
            message,
            message,
        ]
        + [jax.ShapeDtypeStruct(d.shape, F32) for d in drags]
        + [TOKEN],
        compiler_params=pltpu.CompilerParams(vmem_limit_bytes=ROOM),
        name="couple",
    )(beads, *flow, columns, pops, solid)


def sides_kernel(before_ref, force_ref, side_ref, wall_ref, face_ref, *refs):
    outs, token_ref, turned = refs[:-2], refs[-2], refs[-1]
    depth, rows = force_ref.shape[1:3]
    token_ref[...] = jnp.zeros_like(token_ref)
    for n in range(2):
        turned[n] = face_ref[n].T
    for group in range(2):
        y = rows - 1 if group == 0 else 0
        force = [force_ref[d, :, y, :] for d in range(3)]
        out = collide([side_ref[i, 1 - group] for i in range(19)], wall_ref[1 - group] == 1, force)
        for k, i in enumerate(ENTER[1][group]):
            value = turn(out[i], STEP[i, 0], 1)
            if STEP[i, 0] != 0:
                tile, lane = x_place(i)
                column = turned[tile, pl.ds(lane, depth, stride=2), :][:, y : y + 1]
                value = patch_x(value, i, jnp.broadcast_to(column, value.shape))
            out_ref, base = (outs[0], 5 * depth * group) if len(outs) == 1 else (outs[group], 0)
            at = base + k * depth
            out_ref[at : at + depth] = turn(value, STEP[i, 2], 0)


def side_rows(cols, before, force, sides, walls, face):
    _, depth, rows, width = force.shape
    sizes = [10 * depth] if cols == 2 else [5 * depth] * 2
    return pl.pallas_call(
        sides_kernel,
        out_shape=[jax.ShapeDtypeStruct((n, width), F32) for n in sizes] + [TOKEN],
        in_specs=[pl.BlockSpec(memory_space=pl.ANY)] + [pl.BlockSpec(memory_space=pltpu.VMEM)] * 4,
        scratch_shapes=[pltpu.VMEM((2, 128, rows), F32)],
        compiler_params=pltpu.CompilerParams(vmem_limit_bytes=ROOM),
        name="sides",
    )(before, force, sides, walls, face)


def entered_z(first_ref, second_ref, side, rows):
    odd = odd_slab() if side == 0 else jnp.logical_not(odd_slab())
    return jnp.where(odd, second_ref[rows], first_ref[rows])


X_EDGES = [i for side in range(2) for i in ENTER[2][side] if STEP[i, 0] != 0]
Y_EDGES = [[i for i in ENTER[1][side] if STEP[i, 2] != 0] for side in range(2)]


def z_side(i):
    return 0 if STEP[i, 2] == 1 else 1


def edges_kernel(rows, before_ref, first_ref, second_ref, *refs):
    cross_ref, token_ref = refs[-2:]
    token_ref[...] = jnp.zeros_like(token_ref)
    own_ref, far_ref = refs[:2] if len(refs) == 5 else (None, None)
    outs = refs[:-2] if own_ref is None else refs[2:-2]
    for group in range(2):
        y = rows - 1 if group == 0 else 0
        out_ref, row = (outs[0], 2 * group) if len(outs) == 1 else (outs[group], 0)
        for k, i in enumerate(Y_EDGES[group]):
            at = ENTER[2][z_side(i)].index(i) * rows + y
            out_ref[row + k : row + k + 1] = entered_z(
                first_ref, second_ref, z_side(i), slice(at, at + 1)
            )
    if own_ref is not None:
        came = arrived_drag(own_ref, far_ref, first_ref, second_ref, 5 * rows)
        outs[0][8:16] = one_tile(came, 1)
    for k, i in enumerate(X_EDGES):
        at = ENTER[2][z_side(i)].index(i) * rows
        cross_ref[k * rows : (k + 1) * rows] = entered_z(
            first_ref, second_ref, z_side(i), slice(at, at + rows)
        )


def arrived_drag(own_ref, far_ref, first_ref, second_ref, tail):
    at = slice(tail, tail + 8)
    up, down = [entered_z(first_ref, second_ref, side, at) for side in range(2)]
    return [own_ref[0], down, far_ref[...], up]


def one_tile(tiles, col):
    return jnp.concatenate([t[:, col * CAP : (col + 1) * CAP] for t in tiles], axis=1)


def edges(cols, rows, before, first, second, drags):
    width = first.shape[1]
    sizes = ([16] if drags else [8]) if cols == 2 else [8, 8]
    args = (first, second, *drags)
    return pl.pallas_call(
        functools.partial(edges_kernel, rows),
        out_shape=[jax.ShapeDtypeStruct((n, width), F32) for n in sizes + [4 * rows]] + [TOKEN],
        in_specs=[pl.BlockSpec(memory_space=pl.ANY)]
        + [pl.BlockSpec(memory_space=pltpu.VMEM)] * len(args),
        compiler_params=pltpu.CompilerParams(vmem_limit_bytes=ROOM),
        name="edges",
    )(before, *args)


def runs(members):
    found = []
    for i in members:
        if found and found[-1][1] == i and STEP[i, 2] == STEP[i - 1, 2]:
            found[-1] = (found[-1][0], i + 1)
        else:
            found.append((i, i + 1))
    return found


def stream_planes(low, high, faces, pops_ref, solid_ref, force_ref, held):
    def plane(z, faces):
        out = collide(
            [pops_ref[i, z] for i in range(19)],
            solid_ref[z] == 1,
            [force_ref[d, z] for d in range(3)],
        )
        for i in range(19):
            value = turn(out[i], STEP[i, 0], 1)
            if STEP[i, 0] != 0 and faces:
                tile, lane = x_place(i)
                value = patch_x(value, i, spread_column(faces[tile], lane))
            held[i, z] = turn(value, STEP[i, 1], 0)
        return tuple(pltpu.roll(f, 126, 1) for f in faces)

    return lax.fori_loop(low, high, plane, faces, unroll=2)


def lower_kernel(before_ref, pops_ref, solid_ref, force_ref, held, token_ref):
    token_ref[...] = jnp.zeros_like(token_ref)
    stream_planes(0, held.shape[1], (), pops_ref, solid_ref, force_ref, held)


def upper_kernel(
    before_ref, lower_ref, pops_ref, solid_ref, force_ref, face_ref, out_ref, tile_ref, held, sem
):
    depth, rows, width = pops_ref.shape[1:]
    half = lower_ref.shape[1]
    copies = []

    def leave(source, members, low, high):
        for a, b in runs(members):
            step = int(STEP[a, 2])
            start, stop = max(low + step, 0), min(high + step, depth)
            copy = pltpu.make_async_copy(
                source.at[a:b, start - step : stop - step],
                out_ref.at[a:b, start:stop],
                sem.at[len(copies)],
            )
            copy.start()
            copies.append(copy)

    straight = [i for i in range(19) if STEP[i, 0] == 0]
    across = [i for i in range(19) if STEP[i, 0] != 0]
    leave(lower_ref, straight, 0, half)
    faces = (face_ref[0], face_ref[1])
    for i in across:
        tile, lane = x_place(i)
        for z in range(half):
            column = turn(spread_column(faces[tile], lane + 2 * z), STEP[i, 1], 0)
            held[i, z] = patch_x(lower_ref[i, z], i, column)
    leave(held, across, 0, half)
    faces = tuple(pltpu.roll(f, 128 - 2 * half, 1) for f in faces)
    marks = upper_marks(half, depth)
    for low, high in zip(marks, marks[1:]):
        faces = stream_planes(low, high, faces, pops_ref, solid_ref, force_ref, held)
        leave(held, range(19), low, high)
    for group in range(2):
        first = slice(0, 8) if group == 0 else slice(rows - 8, rows)
        for k, i in enumerate(ENTER[1][group]):
            source = lower_ref if i in straight else held
            tile_ref[group * 5 + k, 0:half] = source[i, 0:half, first, :]
            tile_ref[group * 5 + k, half:depth] = held[i, half:depth, first, :]
    for copy in copies:
        copy.wait()


def upper_marks(half, depth):
    return list(range(half, depth - 2, 4)) + ([depth - 2] if (depth - half) % 4 else []) + [depth]


def stream_lower(half, before, pops, solid, force):
    _, _, rows, width = pops.shape
    vmem = pl.BlockSpec(memory_space=pltpu.VMEM)
    return pl.pallas_call(
        lower_kernel,
        out_shape=[jax.ShapeDtypeStruct((19, half, rows, width), F32), TOKEN],
        in_specs=[pl.BlockSpec(memory_space=pl.ANY)] + [vmem] * 3,
        compiler_params=pltpu.CompilerParams(vmem_limit_bytes=ROOM),
        cost_estimate=pl.CostEstimate(flops=300000000, bytes_accessed=100000000, transcendentals=0),
        name="lower",
    )(before, pops, solid, force)


def stream_upper(before, lower, pops, solid, force, face):
    _, depth, rows, width = pops.shape
    vmem = pl.BlockSpec(memory_space=pltpu.VMEM)
    return pl.pallas_call(
        upper_kernel,
        out_shape=[
            jax.ShapeDtypeStruct(pops.shape, F32),
            jax.ShapeDtypeStruct((10, depth, 8, width), F32),
        ],
        in_specs=[pl.BlockSpec(memory_space=pl.ANY)] + [vmem] * 5,
        out_specs=[pl.BlockSpec(memory_space=pltpu.HBM), vmem],
        scratch_shapes=[
            pltpu.VMEM(pops.shape, F32),
            pltpu.SemaphoreType.DMA((20 * len(upper_marks(lower.shape[1], depth)),)),
        ],
        compiler_params=pltpu.CompilerParams(vmem_limit_bytes=ROOM),
        cost_estimate=LONG,
        name="upper",
    )(before, lower, pops, solid, force, face)


def finish_kernel(shape, n_rows, whole_ref, target_ref, tile_ref, first_ref, second_ref, *refs):
    row_refs, edge_refs, refs = refs[:n_rows], refs[n_rows : 2 * n_rows], refs[2 * n_rows :]
    cross_ref, refs = refs[0], refs[1:]
    drag_refs, (out_ref, bead_ref, planes, tiles, bead, sem) = refs[:-6], refs[-6:]
    depth, rows, width = whole_ref.shape[1:]

    def entering(group, k):
        at = (group * 5 + k) * depth if n_rows == 1 else k * depth
        value = row_refs[group % n_rows][at : at + depth]
        i = ENTER[1][group][k]
        if STEP[i, 2] == 0:
            return value
        z = 0 if STEP[i, 2] == 1 else depth - 1
        edge = jnp.broadcast_to(edge_row(group, i), value.shape)
        return jnp.where(iota(value.shape, 0) == z, edge, value)

    def edge_row(group, i):
        row = Y_EDGES[group].index(i) + (2 * group if n_rows == 1 else 0)
        return edge_refs[group % n_rows][row : row + 1]

    copies = []

    def leave(source, target):
        copy = pltpu.make_async_copy(source, target, sem.at[len(copies)])
        copy.start()
        copies.append(copy)

    for group in range(2):
        z = 0 if group == 0 else depth - 1
        for k, i in enumerate(ENTER[2][group]):
            value = entered_z(first_ref, second_ref, group, slice(k * rows, (k + 1) * rows))
            if STEP[i, 1] != 0:
                side = 0 if STEP[i, 1] == 1 else 1
                y = 0 if side == 0 else rows - 1
                value = jnp.where(
                    iota((rows, width), 0) == y,
                    jnp.broadcast_to(edge_row(side, i), (rows, width)),
                    turn(value, STEP[i, 1], 0),
                )
            if STEP[i, 0] != 0:
                at = X_EDGES.index(i) * rows
                value = patch_x(value, i, cross_ref[at : at + rows])
            n = group * 5 + k
            planes[n] = value
            leave(planes.at[n], out_ref.at[i, z])
    for group in range(2):
        first = 0 if group == 0 else rows - 8
        for k, i in enumerate(ENTER[1][group]):
            n = group * 5 + k
            step = int(STEP[i, 2])
            tiles[n, 1 + step : 1 + step + depth] = tile_ref[n]
            tiles[n, 1 : 1 + depth, 0 if group == 0 else 7, :] = entering(group, k)
            low, high = max(step, 0), min(depth + step, depth)
            leave(tiles.at[n, 1 + low : 1 + high], out_ref.at[i, low:high, first : first + 8])

    count = target_ref.shape[1]
    target = target_ref[...]
    if len(drag_refs) == 2:
        slabs, cols, _ = shape
        came = arrived_drag(*drag_refs, first_ref, second_ref, 5 * rows)
        passed = edge_refs[0][8:16]
        table = jnp.concatenate([one_tile(came, 0), passed], axis=1)
        owner = lax.shift_right_logical(target, 5)
        owner_slab = lax.shift_right_logical(owner, cols.bit_length() - 1)
        away_col = owner - owner_slab * cols - lax.axis_index("col")
        away_col = jnp.where(away_col < 0, away_col + cols, away_col)
        away_slab = owner_slab - lax.axis_index("slab")
        away_slab = jnp.where(away_slab < 0, away_slab + slabs, away_slab)
        place = away_col * 128 + away_slab * CAP + target - owner * CAP
        choose = (iota((256, count), 0) == place).astype(F32).astype(BF16)
        total = dot_select(table, choose, NN)
    else:
        back_ref = drag_refs[0]

        def group(k, total):
            got = [back_ref[k * GROUP + r] for r in range(GROUP)]
            slots = jnp.concatenate([t[:, 0:CAP] for t in got], axis=1)
            first = k * (GROUP * CAP)
            choose = (iota((GROUP * CAP, count), 0) + first == target).astype(F32)
            return total + dot_select(slots, choose.astype(BF16), NN)

        total = lax.fori_loop(
            0, back_ref.shape[0] // GROUP, group, jnp.zeros((8, count), F32)
        )
    bead[...] = total[0:3]
    leave(bead, bead_ref)
    for copy in copies:
        copy.wait()


def finish(shape, whole, target, tiles, first, second, entered, late, cross, drags):
    _, depth, rows, width = whole.shape
    vmem = pl.BlockSpec(memory_space=pltpu.VMEM)
    hbm = pl.BlockSpec(memory_space=pltpu.HBM)
    args = [whole, target, tiles, first, second, *entered, *late, cross, *drags]
    return pl.pallas_call(
        functools.partial(finish_kernel, shape, len(entered)),
        out_shape=[
            jax.ShapeDtypeStruct(whole.shape, F32),
            jax.ShapeDtypeStruct((3, target.shape[1]), F32),
        ],
        in_specs=[hbm] + [vmem] * (len(args) - 1),
        out_specs=[hbm, hbm],
        scratch_shapes=[
            pltpu.VMEM((10, rows, width), F32),
            pltpu.VMEM((10, depth + 2, 8, width), F32),
            pltpu.VMEM((3, target.shape[1]), F32),
            pltpu.SemaphoreType.DMA((21,)),
        ],
        input_output_aliases={0: 0},
        compiler_params=pltpu.CompilerParams(vmem_limit_bytes=ROOM),
        name="finish",
    )(*args)


def shards(populations, solid_mask, bead_owner, bead_base, bead_offset, bead_velocity):
    slabs, cols, pairs = shape = tuple(lax.axis_size(a) for a in ("slab", "col", "pair"))
    owners = slabs * cols
    depth, rows = populations.shape[1:3]
    single = owners == GROUP and slabs == 4
    swap = functools.partial(
        lax.all_to_all, axis_name=("slab", "col"), split_axis=0, concat_axis=0, tiled=True
    )

    target, messages = pack(owners, bead_owner, bead_base, bead_offset, bead_velocity)
    messages = swap(messages)
    *flow, columns, sides, walls = moments(populations, solid_mask)
    force, face, first, second, drag, *far, token = couple(
        shape, messages, flow, columns, populations, solid_mask
    )

    def send_pair(value):
        return send(value, shape, lambda s, c, p: (s, c, (p + 1) % pairs))

    def send_col(values):
        return [
            send(value, shape, lambda s, c, p, sign=sign: (s, (c + sign) % cols, p))
            for value, sign in zip(values, (1, -1))
        ]

    face = send_pair(face)
    first, second = send_slab(first, shape, 1), send_slab(second, shape, 0)
    if single:
        drags = [drag, send(far[0], shape, lambda s, c, p: ((s + 2) % slabs, c, p))]
    else:
        drags = []
        drag = swap(drag)
    fields = (populations, solid_mask, force)
    lower, token = stream_lower(4, token, *fields)
    *entered, token = side_rows(cols, token, force, sides, walls, face)
    entered = send_col(entered)
    *late, cross, token = edges(cols, rows, token, first, second, drags)
    late, cross = send_col(late), send_pair(cross)
    whole, tiles = stream_upper(token, lower, *fields, face)
    return tuple(
        finish(
            shape, whole, target, tiles, first, second, entered, late, cross, drags or [drag]
        )
    )


def solution(mesh):
    return jax.shard_map(
        shards,
        mesh=mesh,
        in_specs=(
            P(None, ("rep", "slab"), "col", "pair"),
            P(("rep", "slab"), "col", "pair"),
            P(("rep", "slab", "col", "pair")),
            P(None, ("rep", "slab", "col", "pair")),
            P(None, ("rep", "slab", "col", "pair")),
            P(None, ("rep", "slab", "col", "pair")),
        ),
        out_specs=(
            P(None, ("rep", "slab"), "col", "pair"),
            P(None, ("rep", "slab", "col", "pair")),
        ),
        check_vma=False,
    )
```

```python
import functools

import jax
import jax.numpy as jnp
import numpy as np
from jax import lax
from jax.experimental import pallas as pl
from jax.experimental.pallas import tpu as pltpu
from jax.sharding import PartitionSpec as P

CAP = 32
GROUP = 8

STEP = np.array(
    [
        [0, 0, 0],
        [1, 0, 0],
        [-1, 0, 0],
        [0, 1, 0],
        [0, -1, 0],
        [0, 0, 1],
        [0, 0, -1],
        [1, 1, 0],
        [-1, -1, 0],
        [1, -1, 0],
        [-1, 1, 0],
        [1, 0, 1],
        [-1, 0, -1],
        [1, 0, -1],
        [-1, 0, 1],
        [0, 1, 1],
        [0, -1, -1],
        [0, 1, -1],
        [0, -1, 1],
    ],
    np.int32,
)
TAU_PLUS = 0.8
TAU_MINUS = 0.5 + (3.0 / 16.0) / (TAU_PLUS - 0.5)
KEEP_EVEN = 1.0 - 1.0 / TAU_PLUS
KEEP_ODD = 1.0 - 1.0 / TAU_MINUS
FORCE_GAIN = 1.0 - 0.5 / TAU_PLUS
DRAG_COEF = 2.0
F32 = jnp.float32
BF16 = jnp.bfloat16

ENTER = [[[i for i in range(19) if STEP[i, a] == sign] for sign in (1, -1)] for a in range(3)]
TOKEN = jax.ShapeDtypeStruct((8, 128), F32)
LONG = pl.CostEstimate(flops=5000000000, bytes_accessed=1000000000, transcendentals=0)
ROOM = 16 << 20
NT = (((1,), (1,)), ((), ()))
NN = (((1,), (0,)), ((), ()))


def iota(shape, dim):
    return lax.broadcasted_iota(jnp.int32, shape, dim)


def high_low(value):
    high = value.astype(BF16)
    return high, (value - high.astype(F32)).astype(BF16)


def dot_split(left, right, dims):
    (a, b), (c, d) = left, right
    mul = functools.partial(lax.dot_general, dimension_numbers=dims, preferred_element_type=F32)
    return mul(a, c) + (mul(a, d) + mul(b, c))


def dot_select(value, choose, dims):
    first = value.astype(BF16).astype(F32)
    rest = value - first
    second = rest.astype(BF16).astype(F32)
    stacked = jnp.concatenate([first, second, rest - second], axis=0).astype(BF16)
    got = lax.dot_general(stacked, choose, dimension_numbers=dims, preferred_element_type=F32)
    rows = value.shape[0]
    return got[0:rows] + got[rows : 2 * rows] + got[2 * rows : 3 * rows]


def density_momentum(pops):
    momentum = []
    for axis in range(3):
        plus = [pops[i] for i in range(19) if STEP[i, axis] == 1]
        minus = [pops[i] for i in range(19) if STEP[i, axis] == -1]
        momentum.append(sum(plus[1:], plus[0]) - sum(minus[1:], minus[0]))
    return sum(pops[1:], pops[0]), momentum


def along(step, vector):
    terms = None
    for axis in range(3):
        if step[axis] == 0:
            continue
        if terms is None:
            terms = vector[axis] if step[axis] == 1 else -vector[axis]
        else:
            terms = terms + vector[axis] if step[axis] == 1 else terms - vector[axis]
    return terms


def collide(pops, wall, force):
    density, momentum = density_momentum(pops)
    inverse = 1.0 / density
    carried = [m + 0.5 * f for m, f in zip(momentum, force)]
    speed = [m * inverse for m in carried]
    w = 1.0 / 36.0
    bend = [(4.5 * w / TAU_PLUS) * m + (9.0 * w * FORCE_GAIN) * f for m, f in zip(carried, force)]
    push = [(3.0 * w / TAU_MINUS) * m + (3.0 * w * FORCE_GAIN) * f for m, f in zip(carried, force)]
    drop = [(1.5 * w / TAU_PLUS) * m + (3.0 * w * FORCE_GAIN) * f for m, f in zip(carried, force)]
    rest = (w / TAU_PLUS) * density - sum(
        [u * d for u, d in zip(speed[1:], drop[1:])], speed[0] * drop[0]
    )
    out = [None] * 19
    out[0] = jnp.where(wall, pops[0], KEEP_EVEN * pops[0] + 12.0 * rest)
    for i in range(1, 19, 2):
        a, b = pops[i], pops[i + 1]
        step = STEP[i]
        even = rest + along(step, speed) * along(step, bend)
        odd = along(step, push)
        if i < 7:
            even = even + even
            odd = odd + odd
        even = (0.5 * KEEP_EVEN) * (a + b) + even
        odd = (0.5 * KEEP_ODD) * (a - b) + odd
        out[i] = jnp.where(wall, b, even + odd)
        out[i + 1] = jnp.where(wall, a, even - odd)
    return out


def turn(value, amount, axis):
    if amount == 0:
        return value
    return pltpu.roll(value, int(amount) % value.shape[axis], axis)


def send(value, shape, target):
    def flat(at):
        return (at[0] * shape[1] + at[1]) * shape[2] + at[2]

    perm = [(flat(at), flat(target(*at))) for at in np.ndindex(*shape)]
    return lax.ppermute(value, ("slab", "col", "pair"), perm)


def send_slab(value, shape, which):
    def target(s, c, p):
        return ((s + (1 if s % 2 == which else -1)) % shape[0], c, p)

    return send(value, shape, target)


def odd_slab():
    return lax.rem(lax.axis_index("slab"), 2) == 1


def rank_among(member):
    count = member.shape[1]
    earlier = (iota((count, count), 0) < iota((count, count), 1)).astype(F32).astype(BF16)
    return lax.dot_general(member.astype(BF16), earlier, NN, preferred_element_type=F32)


def x_pair(i):
    return ENTER[0][0 if STEP[i, 0] == 1 else 1].index(i)


def patch_x(value, i, column):
    side = 0 if STEP[i, 0] == 1 else value.shape[1] - 1
    return jnp.where(iota(value.shape, 1) == side, column, value)


def x_place(i):
    group = 0 if STEP[i, 0] == 1 else 1
    place = ENTER[0][group].index(i)
    return place // 4, (place % 4) * 32 + 1 - group


def x_entering(face, k, z):
    tile = face[k // 4]
    return pltpu.roll(tile, tile.shape[1] - ((k % 4) * 32 + 2 * z + 1), 1)


def x_ends(planes):
    lane = lax.shift_right_logical(iota(planes[0].shape, 1), 1)
    tile = jnp.ones(planes[0].shape, F32)
    for z, value in enumerate(planes):
        tile = jnp.where(lane == z, pltpu.roll(value, 2 * z + 1, 1), tile)
    return tile


def pack_kernel(
    steps, owner_ref, base_ref, offset_ref, velocity_ref, target_ref, out_ref, table
):
    count = owner_ref.shape[1]
    step = 0 if steps == 1 else pl.program_id(0)
    local = owner_ref[...] - step * GROUP
    member = (iota((GROUP, count), 0) == local).astype(F32)
    rank = jnp.sum(member * rank_among(member), axis=0, keepdims=True).astype(jnp.int32)
    inside = (local >= 0) & (local < GROUP)
    target = jnp.where(inside, local * CAP + rank, -1)
    whole_target = jnp.where(inside, owner_ref[...] * CAP + rank, -1)

    if steps == 1:
        target_ref[...] = whole_target
    else:
        known = jnp.where(step == 0, -1, target_ref[...])
        target_ref[...] = jnp.maximum(known, whole_target)

    choose = (iota((GROUP * CAP, count), 0) == target).astype(F32).astype(BF16)
    table[...] = jnp.zeros_like(table)
    table[0:3] = base_ref[...].astype(F32) + 1.0
    table[8:11] = offset_ref[...]
    table[16:19] = velocity_ref[...]
    packed = dot_select(table[...], choose, NT)
    blank = jnp.zeros((8, CAP), F32)
    for r in range(GROUP):
        lanes = slice(r * CAP, (r + 1) * CAP)
        out_ref[r] = jnp.concatenate(
            [packed[0:8, lanes], packed[8:16, lanes], packed[16:24, lanes], blank], axis=1
        )


def pack(owners, owner, base, offset, velocity):
    count, steps = owner.shape[0], owners // GROUP
    args = (owner.reshape(1, count), base, offset, velocity)
    blocks = {}
    if steps > 1:
        blocks = dict(
            grid=(steps,),
            in_specs=[pl.BlockSpec(a.shape, lambda k: (0, 0)) for a in args],
            out_specs=[
                pl.BlockSpec((1, count), lambda k: (0, 0)),
                pl.BlockSpec((GROUP, 8, 128), lambda k: (k, 0, 0)),
            ],
            compiler_params=pltpu.CompilerParams(vmem_limit_bytes=48 << 20),
        )
    return pl.pallas_call(
        functools.partial(pack_kernel, steps),
        out_shape=[
            jax.ShapeDtypeStruct((1, count), jnp.int32),
            jax.ShapeDtypeStruct((owners, 8, 128), F32),
        ],
        scratch_shapes=[pltpu.VMEM((24, count), F32)],
        name="pack",
        **blocks,
    )(*args)


def moments_kernel(
    pops_ref, solid_ref, high_ref, low_ref, column_ref, side_ref, wall_ref, held, held_solid, flow, sem
):
    depth, rows, width = pops_ref.shape[1:]
    chunks = 4
    span = depth // chunks
    copies = [pltpu.make_async_copy(solid_ref, held_solid, sem.at[chunks])]
    for k in range(chunks):
        part = pl.ds(k * span, span)
        copies.append(
            pltpu.make_async_copy(pops_ref.at[:, part], held.at[:, part], sem.at[k])
        )
    for copy in copies:
        copy.start()

    def plane(z, carry):
        pops = [held[i, z] for i in range(19)]
        density, momentum = density_momentum(pops)
        inverse = 1.0 / density
        for axis in range(3):
            flow[axis, pl.ds(pl.multiple_of(z * rows, rows), rows)] = momentum[axis] * inverse
        return carry

    for k in range(chunks):
        copies[1 + k].wait()
        lax.fori_loop(k * span, (k + 1) * span, plane, 0, unroll=2)
    copies[0].wait()
    for axis in range(3):
        at = slice(axis * width, (axis + 1) * width)
        high_ref[at], low_ref[at] = high_low(flow[axis].T)
    for i in range(19):
        column_ref[i] = x_ends([held[i, z] for z in range(depth)])
        side_ref[i, 0] = held[i, :, 0, :]
        side_ref[i, 1] = held[i, :, rows - 1, :]
    wall_ref[0] = held_solid[:, 0, :]
    wall_ref[1] = held_solid[:, rows - 1, :]
    column_ref[19] = x_ends([held_solid[z].astype(F32) for z in range(depth)])


def moments(pops, solid):
    _, depth, rows, width = pops.shape
    hbm = pl.BlockSpec(memory_space=pltpu.HBM)
    return pl.pallas_call(
        moments_kernel,
        out_shape=[
            jax.ShapeDtypeStruct((3 * width, depth * rows), BF16),
            jax.ShapeDtypeStruct((3 * width, depth * rows), BF16),
            jax.ShapeDtypeStruct((20, rows, 128), F32),
            jax.ShapeDtypeStruct((19, 2, depth, width), F32),
            jax.ShapeDtypeStruct((2, depth, width), jnp.int32),
        ],
        in_specs=[hbm, hbm],
        scratch_shapes=[
            pltpu.VMEM(pops.shape, F32),
            pltpu.VMEM(solid.shape, jnp.int32),
            pltpu.VMEM((3, depth * rows, width), F32),
            pltpu.SemaphoreType.DMA((5,)),
        ],
        compiler_params=pltpu.CompilerParams(vmem_limit_bytes=54000000),
        cost_estimate=pl.CostEstimate(flops=3000000, bytes_accessed=4000000, transcendentals=0),
        name="moments",
    )(pops, solid)


def unpack(tiles):
    return [
        jnp.concatenate([t[:, g * CAP : (g + 1) * CAP] for t in tiles], axis=1) for g in range(3)
    ]


def couple_group(base, part, velocity, flow, depth, rows, width):
    slots = GROUP * CAP
    start = base.astype(jnp.int32) - 1

    def hat(axis, length):
        cell = iota((length, slots), 0)
        low, share = start[axis : axis + 1], part[axis : axis + 1]
        return jnp.where(cell == low, 1.0 - share, 0.0) + jnp.where(cell == low + 1, share, 0.0)

    hat_x, hat_y, hat_z = hat(0, width), hat(1, rows), hat(2, depth)
    weight = high_low((hat_z[:, None, :] * hat_y[None, :, :]).reshape(depth * rows, slots))
    across = dot_split(flow, weight, NN)
    drag = []
    for d in range(3):
        sampled = jnp.sum(across[d * width : (d + 1) * width] * hat_x, axis=0, keepdims=True)
        drag.append(DRAG_COEF * (sampled - velocity[d : d + 1]))
    spread = jnp.concatenate([hat_x * (-drag[d]) for d in range(3)], axis=0)
    return drag, dot_split(weight, high_low(spread), NT)


def couple_kernel(shape, n_drags, beads_ref, high_ref, low_ref, *refs):
    slabs, cols, _ = shape
    column_ref, side_ref, wall_ref, pops_ref, solid_ref, *refs = refs
    force_ref, face_ref, first_ref, second_ref, draft_ref, *refs = refs
    drag_refs, token_ref = refs[:-1], refs[-1]
    token_ref[...] = jnp.zeros_like(token_ref)
    depth, rows, width = pops_ref.shape[1:]
    flow = (high_ref[...], low_ref[...])

    def grid(force):
        return [
            force[:, d * width : (d + 1) * width].reshape(depth, rows, width) for d in range(3)
        ]

    hollow = jnp.zeros((5, GROUP * CAP), F32)

    if n_drags == 2:
        slab, col = lax.axis_index("slab"), lax.axis_index("col")
        got = []
        for r in range(GROUP):
            there = [a - b for a, b in zip((slab, col), divmod(r, cols))]
            there = [jnp.where(a < 0, a + n, a) for a, n in zip(there, (slabs, cols))]
            got.append(beads_ref[there[0] * cols + there[1]])
        drag, force = couple_group(*unpack(got), flow, depth, rows, width)
        for d, value in enumerate(grid(force)):
            force_ref[d] = value
        stacked = jnp.concatenate(drag + [hollow], axis=0)
        lanes = cols * CAP
        blank = jnp.zeros((8, 128 - lanes), F32)
        for dz in range(slabs):
            tile = jnp.concatenate([stacked[:, dz * lanes : (dz + 1) * lanes], blank], axis=1)
            drag_refs[0][dz] = tile
            if dz == 2:
                drag_refs[1][...] = tile
            if dz == 1:
                down = tile
        up = tile
    else:
        force_ref[...] = jnp.zeros_like(force_ref)
        blank = jnp.zeros((8, 128 - CAP), F32)

        def group(k, carry):
            got = [beads_ref[k * GROUP + r] for r in range(GROUP)]
            drag, force = couple_group(*unpack(got), flow, depth, rows, width)
            for d, value in enumerate(grid(force)):
                force_ref[d] += value
            stacked = jnp.concatenate(drag + [hollow], axis=0)
            for r in range(GROUP):
                drag_refs[0][k * GROUP + r] = jnp.concatenate(
                    [stacked[:, r * CAP : (r + 1) * CAP], blank], axis=1
                )
            return carry

        lax.fori_loop(0, beads_ref.shape[0] // GROUP, group, 0)

    force = [x_ends([force_ref[d, z] for z in range(depth)]) for d in range(3)]
    out = collide([column_ref[i] for i in range(19)], column_ref[19] == 1.0, force)
    high = lax.rem(iota((rows, 128), 1), 2) == 0
    ends = [
        jnp.where(high, turn(out[j], -1, 1), turn(out[i], 1, 1))[:, 0:32]
        for i, j in zip(*ENTER[0])
    ]
    face_ref[0] = jnp.concatenate(ends[0:4], axis=1)
    face_ref[1] = jnp.concatenate([ends[4], jnp.zeros((rows, 96), F32)], axis=1)
    odd = odd_slab()
    leaving = []
    for group, z in ((0, depth - 1), (1, 0)):
        out = collide(
            [pops_ref[i, z] for i in range(19)],
            solid_ref[z] == 1,
            [force_ref[d, z] for d in range(3)],
        )
        leaving.append([turn(out[i], STEP[i, 0], 1) for i in ENTER[2][group]])
    if n_drags == 2:
        leaving[0].append(up)
        leaving[1].append(down)
    row = 0
    for a, b in zip(*leaving):
        at = slice(row, row + a.shape[0])
        first_ref[at] = jnp.where(odd, a, b)
        second_ref[at] = jnp.where(odd, b, a)
        row += a.shape[0]
    for group in range(2):
        force = [force_ref[d, :, 0 if group else rows - 1, :] for d in range(3)]
        out = collide([side_ref[i, 1 - group] for i in range(19)], wall_ref[1 - group] == 1, force)
        for k, i in enumerate(ENTER[1][group]):
            row = (group * 5 + k) * depth
            value = turn(out[i], STEP[i, 0], 1)
            draft_ref[row : row + depth] = turn(value, STEP[i, 2], 0)


def couple(shape, beads, flow, columns, sides, walls, pops, solid):
    _, depth, rows, width = pops.shape
    single = beads.shape[0] == GROUP
    tile = jax.ShapeDtypeStruct((8, 128), F32)
    drags = [jax.ShapeDtypeStruct((shape[0], 8, 128), F32), tile] if single else [beads]
    message = jax.ShapeDtypeStruct((5 * rows + (8 if single else 0), width), F32)
    return pl.pallas_call(
        functools.partial(couple_kernel, shape, len(drags)),
        out_shape=[
            jax.ShapeDtypeStruct((3, depth, rows, width), F32),
            jax.ShapeDtypeStruct((2, rows, 128), F32),
            message,
            message,
            jax.ShapeDtypeStruct((10 * depth, width), F32),
        ]
        + [jax.ShapeDtypeStruct(d.shape, F32) for d in drags]
        + [TOKEN],
        compiler_params=pltpu.CompilerParams(vmem_limit_bytes=ROOM),
        name="couple",
    )(beads, *flow, columns, sides, walls, pops, solid)


def entered_z(first_ref, second_ref, side, rows):
    odd = odd_slab() if side == 0 else jnp.logical_not(odd_slab())
    return jnp.where(odd, second_ref[rows], first_ref[rows])


X_EDGES = [i for side in range(2) for i in ENTER[2][side] if STEP[i, 0] != 0]


def rows_kernel(depth, rows, draft_ref, face_ref, first_ref, second_ref, *refs):
    refs, (cross_ref, token_ref, turned) = refs[:-3], refs[-3:]
    token_ref[...] = jnp.zeros_like(token_ref)
    own_ref, outs = (refs[0], refs[1:]) if len(refs) == 2 and refs[0].shape[-2] == 8 else (None, refs)
    for n in range(2):
        turned[n] = face_ref[n].T
    for group in range(2):
        out_ref = outs[0] if len(outs) == 1 else outs[group]
        base = group * 5 * depth if len(outs) == 1 else 0
        y = rows - 1 if group == 0 else 0
        for k, i in enumerate(ENTER[1][group]):
            at = base + k * depth
            value = draft_ref[(group * 5 + k) * depth : (group * 5 + k + 1) * depth]
            if STEP[i, 0] != 0:
                tile, lane = x_place(i)
                column = turned[tile, pl.ds(lane, depth, stride=2), :][:, y : y + 1]
                value = patch_x(value, i, jnp.broadcast_to(column, value.shape))
            out_ref[at : at + depth] = value
            if STEP[i, 2] != 0:
                side = 0 if STEP[i, 2] == 1 else 1
                z = 0 if side == 0 else depth - 1
                row = ENTER[2][side].index(i) * rows + y
                out_ref[at + z : at + z + 1] = entered_z(
                    first_ref, second_ref, side, slice(row, row + 1)
                )
    if own_ref is not None:
        came = arrived_drag(own_ref, None, first_ref, second_ref, 5 * rows)
        outs[0][10 * depth : 10 * depth + 8] = one_tile(came, 1)
    for k, i in enumerate(X_EDGES):
        side = 0 if STEP[i, 2] == 1 else 1
        at = ENTER[2][side].index(i) * rows
        cross_ref[k * rows : (k + 1) * rows] = entered_z(
            first_ref, second_ref, side, slice(at, at + rows)
        )


def arrived_drag(own_ref, far_ref, first_ref, second_ref, tail):
    at = slice(tail, tail + 8)
    up, down = [entered_z(first_ref, second_ref, side, at) for side in range(2)]
    return [own_ref[0], down, jnp.zeros_like(up) if far_ref is None else far_ref[...], up]


def one_tile(tiles, col):
    return jnp.concatenate([t[:, col * CAP : (col + 1) * CAP] for t in tiles], axis=1)


def leaving_rows(depth, rows, draft, face, first, second, drags):
    width = draft.shape[1]
    sizes = [10 * depth + 8] if drags else [5 * depth] * 2
    return pl.pallas_call(
        functools.partial(rows_kernel, depth, rows),
        out_shape=[jax.ShapeDtypeStruct((n, width), F32) for n in sizes + [4 * rows]] + [TOKEN],
        scratch_shapes=[pltpu.VMEM((2, 128, rows), F32)],
        compiler_params=pltpu.CompilerParams(vmem_limit_bytes=ROOM),
        name="rows",
    )(draft, face, first, second, *drags)


def pass_kernel(before_ref, value_ref, out_ref, token_ref):
    out_ref[...] = value_ref[...]
    token_ref[...] = jnp.zeros_like(token_ref)


def pass_on(before, value):
    return pl.pallas_call(
        pass_kernel,
        out_shape=[jax.ShapeDtypeStruct(value.shape, F32), TOKEN],
        in_specs=[pl.BlockSpec(memory_space=pl.ANY), pl.BlockSpec(memory_space=pltpu.VMEM)],
        compiler_params=pltpu.CompilerParams(vmem_limit_bytes=ROOM),
        name="pass_on",
    )(before, value)


def runs(members):
    found = []
    for i in members:
        if found and found[-1][1] == i and STEP[i, 2] == STEP[i - 1, 2]:
            found[-1] = (found[-1][0], i + 1)
        else:
            found.append((i, i + 1))
    return found


def stream_planes(low, high, faces, pops_ref, solid_ref, force_ref, held):
    def plane(z, faces):
        out = collide(
            [pops_ref[i, z] for i in range(19)],
            solid_ref[z] == 1,
            [force_ref[d, z] for d in range(3)],
        )
        for i in range(19):
            value = turn(out[i], STEP[i, 0], 1)
            if STEP[i, 0] != 0 and faces:
                value = patch_x(value, i, faces[x_pair(i)])
            held[i, z] = turn(value, STEP[i, 1], 0)
        return tuple(pltpu.roll(f, 126, 1) for f in faces)

    return lax.fori_loop(low, high, plane, faces, unroll=2)


def lower_kernel(before_ref, pops_ref, solid_ref, force_ref, held, token_ref):
    token_ref[...] = jnp.zeros_like(token_ref)
    stream_planes(0, held.shape[1], (), pops_ref, solid_ref, force_ref, held)


def upper_kernel(
    before_ref, lower_ref, pops_ref, solid_ref, force_ref, face_ref, out_ref, tile_ref, held, sem
):
    depth, rows, width = pops_ref.shape[1:]
    half = lower_ref.shape[1]
    copies = []

    def leave(source, members, low, high):
        for a, b in runs(members):
            step = int(STEP[a, 2])
            start, stop = max(low + step, 0), min(high + step, depth)
            copy = pltpu.make_async_copy(
                source.at[a:b, start - step : stop - step],
                out_ref.at[a:b, start:stop],
                sem.at[len(copies)],
            )
            copy.start()
            copies.append(copy)

    straight = [i for i in range(19) if STEP[i, 0] == 0]
    across = [i for i in range(19) if STEP[i, 0] != 0]
    leave(lower_ref, straight, 0, half)
    face = (face_ref[0], face_ref[1])
    for k, pair in enumerate(zip(*ENTER[0])):
        for z in range(half):
            column = x_entering(face, k, z)
            for i in pair:
                held[i, z] = patch_x(lower_ref[i, z], i, turn(column, STEP[i, 1], 0))
    leave(held, across, 0, half)
    faces = tuple(x_entering(face, k, half) for k in range(5))
    marks = upper_marks(half, depth)
    for low, high in zip(marks, marks[1:]):
        faces = stream_planes(low, high, faces, pops_ref, solid_ref, force_ref, held)
        leave(held, range(19), low, high)
    for group in range(2):
        first = slice(0, 8) if group == 0 else slice(rows - 8, rows)
        for k, i in enumerate(ENTER[1][group]):
            source = lower_ref if i in straight else held
            tile_ref[group * 5 + k, 0:half] = source[i, 0:half, first, :]
            tile_ref[group * 5 + k, half:depth] = held[i, half:depth, first, :]
    for copy in copies:
        copy.wait()


def upper_marks(half, depth):
    return list(range(half, depth - 2, 4)) + ([depth - 2] if (depth - half) % 4 else []) + [depth]


def stream_lower(half, before, pops, solid, force):
    _, _, rows, width = pops.shape
    vmem = pl.BlockSpec(memory_space=pltpu.VMEM)
    return pl.pallas_call(
        lower_kernel,
        out_shape=[jax.ShapeDtypeStruct((19, half, rows, width), F32), TOKEN],
        in_specs=[pl.BlockSpec(memory_space=pl.ANY)] + [vmem] * 3,
        compiler_params=pltpu.CompilerParams(vmem_limit_bytes=ROOM),
        cost_estimate=LONG,
        name="lower",
    )(before, pops, solid, force)


def stream_upper(before, lower, pops, solid, force, face):
    _, depth, rows, width = pops.shape
    vmem = pl.BlockSpec(memory_space=pltpu.VMEM)
    return pl.pallas_call(
        upper_kernel,
        out_shape=[
            jax.ShapeDtypeStruct(pops.shape, F32),
            jax.ShapeDtypeStruct((10, depth, 8, width), F32),
        ],
        in_specs=[pl.BlockSpec(memory_space=pl.ANY)] + [vmem] * 5,
        out_specs=[pl.BlockSpec(memory_space=pltpu.HBM), vmem],
        scratch_shapes=[
            pltpu.VMEM(pops.shape, F32),
            pltpu.SemaphoreType.DMA((20 * len(upper_marks(lower.shape[1], depth)),)),
        ],
        compiler_params=pltpu.CompilerParams(vmem_limit_bytes=ROOM),
        cost_estimate=LONG,
        name="upper",
    )(before, lower, pops, solid, force, face)


def finish_kernel(shape, n_rows, whole_ref, target_ref, tile_ref, first_ref, second_ref, *refs):
    row_refs, cross_ref, refs = refs[:n_rows], refs[n_rows], refs[n_rows + 1 :]
    drag_refs, (out_ref, bead_ref, planes, tiles, bead, sem) = refs[:-6], refs[-6:]
    depth, rows, width = whole_ref.shape[1:]

    def entering(group, k):
        at = (group * 5 + k) * depth if n_rows == 1 else k * depth
        return row_refs[group % n_rows][at : at + depth]

    copies = []

    def leave(source, target):
        copy = pltpu.make_async_copy(source, target, sem.at[len(copies)])
        copy.start()
        copies.append(copy)

    for group in range(2):
        z = 0 if group == 0 else depth - 1
        for k, i in enumerate(ENTER[2][group]):
            value = entered_z(first_ref, second_ref, group, slice(k * rows, (k + 1) * rows))
            if STEP[i, 1] != 0:
                side = 0 if STEP[i, 1] == 1 else 1
                y = 0 if side == 0 else rows - 1
                row = entering(side, ENTER[1][side].index(i))[z : z + 1]
                value = jnp.where(
                    iota((rows, width), 0) == y,
                    jnp.broadcast_to(row, (rows, width)),
                    turn(value, STEP[i, 1], 0),
                )
            if STEP[i, 0] != 0:
                at = X_EDGES.index(i) * rows
                value = patch_x(value, i, cross_ref[at : at + rows])
            n = group * 5 + k
            planes[n] = value
            leave(planes.at[n], out_ref.at[i, z])
    for group in range(2):
        first = 0 if group == 0 else rows - 8
        for k, i in enumerate(ENTER[1][group]):
            n = group * 5 + k
            step = int(STEP[i, 2])
            tiles[n, 1 + step : 1 + step + depth] = tile_ref[n]
            tiles[n, 1 : 1 + depth, 0 if group == 0 else 7, :] = entering(group, k)
            low, high = max(step, 0), min(depth + step, depth)
            leave(tiles.at[n, 1 + low : 1 + high], out_ref.at[i, low:high, first : first + 8])

    count = target_ref.shape[1]
    target = target_ref[...]
    if len(drag_refs) == 3:
        slabs, cols, _ = shape
        own_ref, far_ref, passed_ref = drag_refs
        came = arrived_drag(own_ref, far_ref, first_ref, second_ref, 5 * rows)
        passed = row_refs[0][10 * depth : 10 * depth + 8]
        passed = jnp.concatenate(
            [passed[:, 0 : 2 * CAP], passed_ref[:, CAP : 2 * CAP], passed[:, 3 * CAP : 4 * CAP]],
            axis=1,
        )
        table = jnp.concatenate([one_tile(came, 0), passed], axis=1)
        owner = lax.shift_right_logical(target, 5)
        owner_slab = lax.shift_right_logical(owner, cols.bit_length() - 1)
        away_col = owner - owner_slab * cols - lax.axis_index("col")
        away_col = jnp.where(away_col < 0, away_col + cols, away_col)
        away_slab = owner_slab - lax.axis_index("slab")
        away_slab = jnp.where(away_slab < 0, away_slab + slabs, away_slab)
        place = away_col * 128 + away_slab * CAP + target - owner * CAP
        choose = (iota((256, count), 0) == place).astype(F32).astype(BF16)
        total = dot_select(table, choose, NN)
    else:
        back_ref = drag_refs[0]

        def group(k, total):
            got = [back_ref[k * GROUP + r] for r in range(GROUP)]
            slots = jnp.concatenate([t[:, 0:CAP] for t in got], axis=1)
            first = k * (GROUP * CAP)
            choose = (iota((GROUP * CAP, count), 0) + first == target).astype(F32)
            return total + dot_select(slots, choose.astype(BF16), NN)

        total = lax.fori_loop(
            0, back_ref.shape[0] // GROUP, group, jnp.zeros((8, count), F32)
        )
    bead[...] = total[0:3]
    leave(bead, bead_ref)
    for copy in copies:
        copy.wait()


def finish(shape, whole, target, tiles, first, second, entered, cross, drags):
    _, depth, rows, width = whole.shape
    vmem = pl.BlockSpec(memory_space=pltpu.VMEM)
    hbm = pl.BlockSpec(memory_space=pltpu.HBM)
    args = [whole, target, tiles, first, second, *entered, cross, *drags]
    return pl.pallas_call(
        functools.partial(finish_kernel, shape, len(entered)),
        out_shape=[
            jax.ShapeDtypeStruct(whole.shape, F32),
            jax.ShapeDtypeStruct((3, target.shape[1]), F32),
        ],
        in_specs=[hbm] + [vmem] * (len(args) - 1),
        out_specs=[hbm, hbm],
        scratch_shapes=[
            pltpu.VMEM((10, rows, width), F32),
            pltpu.VMEM((10, depth + 2, 8, width), F32),
            pltpu.VMEM((3, target.shape[1]), F32),
            pltpu.SemaphoreType.DMA((21,)),
        ],
        input_output_aliases={0: 0},
        compiler_params=pltpu.CompilerParams(vmem_limit_bytes=ROOM),
        name="finish",
    )(*args)


def shards(populations, solid_mask, bead_owner, bead_base, bead_offset, bead_velocity):
    slabs, cols, pairs = shape = tuple(lax.axis_size(a) for a in ("slab", "col", "pair"))
    owners = slabs * cols
    depth, rows = populations.shape[1:3]
    single = owners == GROUP and slabs == 4
    swap = functools.partial(
        lax.all_to_all, axis_name=("slab", "col"), split_axis=0, concat_axis=0, tiled=True
    )

    target, messages = pack(owners, bead_owner, bead_base, bead_offset, bead_velocity)
    messages = swap(messages)
    *flow, columns, sides, walls = moments(populations, solid_mask)
    force, face, first, second, draft, drag, *far, token = couple(
        shape, messages, flow, columns, sides, walls, populations, solid_mask
    )

    def send_pair(value):
        return send(value, shape, lambda s, c, p: (s, c, (p + 1) % pairs))

    def send_col(values):
        return [
            send(value, shape, lambda s, c, p, sign=sign: (s, (c + sign) % cols, p))
            for value, sign in zip(values, (1, -1))
        ]

    face = send_pair(face)
    first, second = send_slab(first, shape, 1), send_slab(second, shape, 0)
    if single:
        drags = [drag, send(far[0], shape, lambda s, c, p: ((s + 2) % slabs, c, p))]
    else:
        drags = []
        drag = swap(drag)
    fields = (populations, solid_mask, force)
    *leaving, cross, token = leaving_rows(depth, rows, draft, face, first, second, drags[:1])
    entered, cross = send_col(leaving), send_pair(cross)
    lower, token = stream_lower(6, token, *fields)
    if single:
        passed, token = pass_on(token, drags[1])
        drags += send_col([passed])
    whole, tiles = stream_upper(token, lower, *fields, face)
    return tuple(
        finish(shape, whole, target, tiles, first, second, entered, cross, drags or [drag])
    )


def solution(mesh):
    return jax.shard_map(
        shards,
        mesh=mesh,
        in_specs=(
            P(None, ("rep", "slab"), "col", "pair"),
            P(("rep", "slab"), "col", "pair"),
            P(("rep", "slab", "col", "pair")),
            P(None, ("rep", "slab", "col", "pair")),
            P(None, ("rep", "slab", "col", "pair")),
            P(None, ("rep", "slab", "col", "pair")),
        ),
        out_specs=(
            P(None, ("rep", "slab"), "col", "pair"),
            P(None, ("rep", "slab", "col", "pair")),
        ),
        check_vma=False,
    )
```

```python
import functools

import jax
import jax.numpy as jnp
import numpy as np
from jax import lax
from jax.experimental import pallas as pl
from jax.experimental.pallas import tpu as pltpu
from jax.sharding import PartitionSpec as P

CAP = 32
GROUP = 8

STEP = np.array(
    [
        [0, 0, 0],
        [1, 0, 0],
        [-1, 0, 0],
        [0, 1, 0],
        [0, -1, 0],
        [0, 0, 1],
        [0, 0, -1],
        [1, 1, 0],
        [-1, -1, 0],
        [1, -1, 0],
        [-1, 1, 0],
        [1, 0, 1],
        [-1, 0, -1],
        [1, 0, -1],
        [-1, 0, 1],
        [0, 1, 1],
        [0, -1, -1],
        [0, 1, -1],
        [0, -1, 1],
    ],
    np.int32,
)
TAU_PLUS = 0.8
TAU_MINUS = 0.5 + (3.0 / 16.0) / (TAU_PLUS - 0.5)
KEEP_EVEN = 1.0 - 1.0 / TAU_PLUS
KEEP_ODD = 1.0 - 1.0 / TAU_MINUS
FORCE_GAIN = 1.0 - 0.5 / TAU_PLUS
DRAG_COEF = 2.0
F32 = jnp.float32
BF16 = jnp.bfloat16

ENTER = [[[i for i in range(19) if STEP[i, a] == sign] for sign in (1, -1)] for a in range(3)]
TOKEN = jax.ShapeDtypeStruct((8, 128), F32)
LONG = pl.CostEstimate(flops=5000000000, bytes_accessed=1000000000, transcendentals=0)
ROOM = 16 << 20
NT = (((1,), (1,)), ((), ()))
NN = (((1,), (0,)), ((), ()))


def iota(shape, dim):
    return lax.broadcasted_iota(jnp.int32, shape, dim)


def high_low(value):
    high = value.astype(BF16)
    return high, (value - high.astype(F32)).astype(BF16)


def dot_split(left, right, dims):
    (a, b), (c, d) = left, right
    mul = functools.partial(lax.dot_general, dimension_numbers=dims, preferred_element_type=F32)
    return mul(a, c) + (mul(a, d) + mul(b, c))


def dot_select(value, choose, dims):
    first = value.astype(BF16).astype(F32)
    rest = value - first
    second = rest.astype(BF16).astype(F32)
    stacked = jnp.concatenate([first, second, rest - second], axis=0).astype(BF16)
    got = lax.dot_general(stacked, choose, dimension_numbers=dims, preferred_element_type=F32)
    rows = value.shape[0]
    return got[0:rows] + got[rows : 2 * rows] + got[2 * rows : 3 * rows]


def density_momentum(pops):
    momentum = []
    for axis in range(3):
        plus = [pops[i] for i in range(19) if STEP[i, axis] == 1]
        minus = [pops[i] for i in range(19) if STEP[i, axis] == -1]
        momentum.append(sum(plus[1:], plus[0]) - sum(minus[1:], minus[0]))
    return sum(pops[1:], pops[0]), momentum


def along(step, vector):
    terms = None
    for axis in range(3):
        if step[axis] == 0:
            continue
        if terms is None:
            terms = vector[axis] if step[axis] == 1 else -vector[axis]
        else:
            terms = terms + vector[axis] if step[axis] == 1 else terms - vector[axis]
    return terms


def collide(pops, wall, force):
    density, momentum = density_momentum(pops)
    inverse = 1.0 / density
    carried = [m + 0.5 * f for m, f in zip(momentum, force)]
    speed = [m * inverse for m in carried]
    w = 1.0 / 36.0
    bend = [(4.5 * w / TAU_PLUS) * m + (9.0 * w * FORCE_GAIN) * f for m, f in zip(carried, force)]
    push = [(3.0 * w / TAU_MINUS) * m + (3.0 * w * FORCE_GAIN) * f for m, f in zip(carried, force)]
    drop = [(1.5 * w / TAU_PLUS) * m + (3.0 * w * FORCE_GAIN) * f for m, f in zip(carried, force)]
    rest = (w / TAU_PLUS) * density - sum(
        [u * d for u, d in zip(speed[1:], drop[1:])], speed[0] * drop[0]
    )
    out = [None] * 19
    out[0] = jnp.where(wall, pops[0], KEEP_EVEN * pops[0] + 12.0 * rest)
    for i in range(1, 19, 2):
        a, b = pops[i], pops[i + 1]
        step = STEP[i]
        even = rest + along(step, speed) * along(step, bend)
        odd = along(step, push)
        if i < 7:
            even = even + even
            odd = odd + odd
        even = (0.5 * KEEP_EVEN) * (a + b) + even
        odd = (0.5 * KEEP_ODD) * (a - b) + odd
        out[i] = jnp.where(wall, b, even + odd)
        out[i + 1] = jnp.where(wall, a, even - odd)
    return out


def turn(value, amount, axis):
    if amount == 0:
        return value
    return pltpu.roll(value, int(amount) % value.shape[axis], axis)


def send(value, shape, target):
    def flat(at):
        return (at[0] * shape[1] + at[1]) * shape[2] + at[2]

    perm = [(flat(at), flat(target(*at))) for at in np.ndindex(*shape)]
    return lax.ppermute(value, ("slab", "col", "pair"), perm)


def send_slab(value, shape, which):
    def target(s, c, p):
        return ((s + (1 if s % 2 == which else -1)) % shape[0], c, p)

    return send(value, shape, target)


def odd_slab():
    return lax.rem(lax.axis_index("slab"), 2) == 1


def rank_among(member):
    count = member.shape[1]
    earlier = (iota((count, count), 0) < iota((count, count), 1)).astype(F32).astype(BF16)
    return lax.dot_general(member.astype(BF16), earlier, NN, preferred_element_type=F32)


def spread_column(tile, lane):
    return jnp.broadcast_to(tile[:, lane : lane + 1], tile.shape)


def patch_x(value, i, column):
    side = 0 if STEP[i, 0] == 1 else value.shape[1] - 1
    return jnp.where(iota(value.shape, 1) == side, column, value)


def x_place(i):
    group = 0 if STEP[i, 0] == 1 else 1
    place = ENTER[0][group].index(i)
    return place // 4, (place % 4) * 32 + group


def x_ends(planes):
    lane = lax.shift_right_logical(iota(planes[0].shape, 1), 1)
    tile = jnp.ones(planes[0].shape, F32)
    for z, value in enumerate(planes):
        tile = jnp.where(lane == z, pltpu.roll(value, 2 * z + 1, 1), tile)
    return tile


def pack_kernel(shape, steps, owner_ref, base_ref, offset_ref, velocity_ref, target_ref, *refs):
    outs, table = refs[:-1], refs[-1]
    count = owner_ref.shape[1]
    owner = owner_ref[...]
    if len(outs) == 2:
        cols = shape[1]
        slab, col = lax.axis_index("slab"), lax.axis_index("col")
        to_slab = lax.shift_right_logical(owner, cols.bit_length() - 1)
        to_col = owner - to_slab * cols
        away = to_slab - slab
        away = jnp.where(away < 0, away + shape[0], away)
        up = jnp.where(odd_slab(), 1, 2)
        place = jnp.where(away == 1, up, jnp.where(away == 3, 3 - up, jnp.where(away == 2, 3, 0)))
        local = jnp.where(to_col == col, 0, 4) + place
    else:
        local = owner - (0 if steps == 1 else pl.program_id(0)) * GROUP
    member = (iota((GROUP, count), 0) == local).astype(F32)
    rank = jnp.sum(member * rank_among(member), axis=0, keepdims=True).astype(jnp.int32)
    inside = (local >= 0) & (local < GROUP)
    target = jnp.where(inside, local * CAP + rank, -1)
    whole_target = jnp.where(inside, owner * CAP + rank, -1)
    if steps == 1:
        target_ref[...] = whole_target
    else:
        known = jnp.where(pl.program_id(0) == 0, -1, target_ref[...])
        target_ref[...] = jnp.maximum(known, whole_target)
    choose = (iota((GROUP * CAP, count), 0) == target).astype(F32).astype(BF16)
    table[...] = jnp.zeros_like(table)
    table[0:3] = base_ref[...].astype(F32) + 1.0
    table[8:11] = offset_ref[...]
    table[16:19] = velocity_ref[...]
    packed = dot_select(table[...], choose, NT)
    blank = jnp.zeros((8, CAP), F32)
    for r in range(GROUP):
        lanes = slice(r * CAP, (r + 1) * CAP)
        tile = jnp.concatenate(
            [packed[0:8, lanes], packed[8:16, lanes], packed[16:24, lanes], blank], axis=1
        )
        if len(outs) == 2:
            outs[r // 4][(r % 4) * 8 : (r % 4) * 8 + 8] = tile
        else:
            outs[0][r] = tile


def pack(shape, single, owner, base, offset, velocity):
    owners = shape[0] * shape[1]
    count, steps = owner.shape[0], owners // GROUP
    args = (owner.reshape(1, count), base, offset, velocity)
    blocks = {}
    if single:
        tiles = [jax.ShapeDtypeStruct((32, 128), F32)] * 2
    else:
        tiles = [jax.ShapeDtypeStruct((owners, 8, 128), F32)]
        blocks = dict(
            grid=(steps,),
            in_specs=[pl.BlockSpec(a.shape, lambda k: (0, 0)) for a in args],
            out_specs=[
                pl.BlockSpec((1, count), lambda k: (0, 0)),
                pl.BlockSpec((GROUP, 8, 128), lambda k: (k, 0, 0)),
            ],
            compiler_params=pltpu.CompilerParams(vmem_limit_bytes=48 << 20),
        )
    return pl.pallas_call(
        functools.partial(pack_kernel, shape, steps),
        out_shape=[jax.ShapeDtypeStruct((1, count), jnp.int32), *tiles],
        scratch_shapes=[pltpu.VMEM((24, count), F32)],
        name="pack",
        **blocks,
    )(*args)


def join_kernel(before_ref, own_ref, came_ref, *refs):
    outs, token_ref = refs[:-1], refs[-1]
    token_ref[...] = jnp.zeros_like(token_ref)
    for k, out_ref in enumerate(outs):
        out_ref[0:8] = own_ref[8 * k : 8 * k + 8]
        out_ref[8:16] = came_ref[8 * k : 8 * k + 8]


def join(before, own, came):
    vmem = pl.BlockSpec(memory_space=pltpu.VMEM)
    return pl.pallas_call(
        join_kernel,
        out_shape=[jax.ShapeDtypeStruct((16, 128), F32)] * 4 + [TOKEN],
        in_specs=[pl.BlockSpec(memory_space=pl.ANY), vmem, vmem],
        compiler_params=pltpu.CompilerParams(vmem_limit_bytes=ROOM),
        name="join",
    )(before, own, came)


def moments_kernel(
    before_ref, pops_ref, high_ref, low_ref, column_ref, side_ref, token_ref, held, flow, sem
):
    depth, rows, width = pops_ref.shape[1:]
    chunks = 4
    span = depth // chunks
    copies = []
    token_ref[...] = jnp.zeros_like(token_ref)
    for k in range(chunks):
        part = pl.ds(k * span, span)
        copies.append(
            pltpu.make_async_copy(pops_ref.at[:, part], held.at[:, part], sem.at[k])
        )
    for copy in copies:
        copy.start()

    def plane(z, carry):
        pops = [held[i, z] for i in range(19)]
        density, momentum = density_momentum(pops)
        inverse = 1.0 / density
        for axis in range(3):
            flow[axis, pl.ds(pl.multiple_of(z * rows, rows), rows)] = momentum[axis] * inverse
        return carry

    for k in range(chunks):
        copies[k].wait()
        lax.fori_loop(k * span, (k + 1) * span, plane, 0, unroll=2)
    for axis in range(3):
        at = slice(axis * width, (axis + 1) * width)
        high_ref[at], low_ref[at] = high_low(flow[axis].T)
    for i in range(19):
        column_ref[i] = x_ends([held[i, z] for z in range(depth)])
        side_ref[i, 0] = held[i, :, 0, :]
        side_ref[i, 1] = held[i, :, rows - 1, :]


def moments(before, pops):
    _, depth, rows, width = pops.shape
    return pl.pallas_call(
        moments_kernel,
        out_shape=[
            jax.ShapeDtypeStruct((3 * width, depth * rows), BF16),
            jax.ShapeDtypeStruct((3 * width, depth * rows), BF16),
            jax.ShapeDtypeStruct((19, rows, 128), F32),
            jax.ShapeDtypeStruct((19, 2, depth, width), F32),
            TOKEN,
        ],
        in_specs=[pl.BlockSpec(memory_space=pl.ANY), pl.BlockSpec(memory_space=pltpu.HBM)],
        scratch_shapes=[
            pltpu.VMEM(pops.shape, F32),
            pltpu.VMEM((3, depth * rows, width), F32),
            pltpu.SemaphoreType.DMA((4,)),
        ],
        compiler_params=pltpu.CompilerParams(vmem_limit_bytes=54000000),
        cost_estimate=LONG,
        name="moments",
    )(before, pops)


def walls_kernel(before_ref, solid_ref, column_ref, wall_ref):
    depth, rows = solid_ref.shape[0:2]
    column_ref[...] = x_ends([solid_ref[z].astype(F32) for z in range(depth)])
    wall_ref[0] = solid_ref[:, 0, :]
    wall_ref[1] = solid_ref[:, rows - 1, :]


def wall_faces(before, solid):
    depth, rows, width = solid.shape
    return pl.pallas_call(
        walls_kernel,
        out_shape=[
            jax.ShapeDtypeStruct((rows, 128), F32),
            jax.ShapeDtypeStruct((2, depth, width), jnp.int32),
        ],
        in_specs=[pl.BlockSpec(memory_space=pl.ANY), pl.BlockSpec(memory_space=pltpu.VMEM)],
        compiler_params=pltpu.CompilerParams(vmem_limit_bytes=ROOM),
        cost_estimate=LONG,
        name="walls",
    )(before, solid)


def unpack(tiles):
    return [
        jnp.concatenate([t[:, g * CAP : (g + 1) * CAP] for t in tiles], axis=1) for g in range(3)
    ]


def couple_group(base, part, velocity, flow, depth, rows, width):
    slots = GROUP * CAP
    start = base.astype(jnp.int32) - 1

    def hat(axis, length):
        cell = iota((length, slots), 0)
        low, share = start[axis : axis + 1], part[axis : axis + 1]
        return jnp.where(cell == low, 1.0 - share, 0.0) + jnp.where(cell == low + 1, share, 0.0)

    hat_x, hat_y, hat_z = hat(0, width), hat(1, rows), hat(2, depth)
    weight = high_low((hat_z[:, None, :] * hat_y[None, :, :]).reshape(depth * rows, slots))
    across = dot_split(flow, weight, NN)
    drag = []
    for d in range(3):
        sampled = jnp.sum(across[d * width : (d + 1) * width] * hat_x, axis=0, keepdims=True)
        drag.append(DRAG_COEF * (sampled - velocity[d : d + 1]))
    spread = jnp.concatenate([hat_x * (-drag[d]) for d in range(3)], axis=0)
    return drag, dot_split(weight, high_low(spread), NT)


def couple_kernel(shape, n_beads, n_drags, *refs):
    slabs, cols, _ = shape
    bead_refs, refs = refs[:n_beads], refs[n_beads:]
    high_ref, low_ref, column_ref, wall_ref, pops_ref, solid_ref, *refs = refs
    force_ref, face_ref, first_ref, second_ref, *refs = refs
    drag_refs, token_ref = refs[:-1], refs[-1]
    token_ref[...] = jnp.zeros_like(token_ref)
    depth, rows, width = pops_ref.shape[1:]
    flow = (high_ref[...], low_ref[...])

    def grid(force):
        return [
            force[:, d * width : (d + 1) * width].reshape(depth, rows, width) for d in range(3)
        ]

    hollow = jnp.zeros((5, GROUP * CAP), F32)

    if n_drags == 2:
        got = [ref[k : k + 8] for ref in bead_refs for k in (0, 8)]
        drag, force = couple_group(*unpack(got), flow, depth, rows, width)
        for d, value in enumerate(grid(force)):
            force_ref[d] = value
        stacked = jnp.concatenate(drag + [hollow], axis=0)
        lanes = cols * CAP
        blank = jnp.zeros((8, 128 - lanes), F32)
        own, near, next_, far = [
            jnp.concatenate([stacked[:, k * lanes : (k + 1) * lanes], blank], axis=1)
            for k in range(slabs)
        ]
        odd = odd_slab()
        down, up = jnp.where(odd, next_, near), jnp.where(odd, near, next_)
        for dz, tile in enumerate([own, down, far, up]):
            drag_refs[0][dz] = tile
        drag_refs[1][...] = far
    else:
        force_ref[...] = jnp.zeros_like(force_ref)
        blank = jnp.zeros((8, 128 - CAP), F32)

        def group(k, carry):
            got = [bead_refs[0][k * GROUP + r] for r in range(GROUP)]
            drag, force = couple_group(*unpack(got), flow, depth, rows, width)
            for d, value in enumerate(grid(force)):
                force_ref[d] += value
            stacked = jnp.concatenate(drag + [hollow], axis=0)
            for r in range(GROUP):
                drag_refs[0][k * GROUP + r] = jnp.concatenate(
                    [stacked[:, r * CAP : (r + 1) * CAP], blank], axis=1
                )
            return carry

        lax.fori_loop(0, bead_refs[0].shape[0] // GROUP, group, 0)

    force = [x_ends([force_ref[d, z] for z in range(depth)]) for d in range(3)]
    out = collide([column_ref[i] for i in range(19)], wall_ref[...] == 1.0, force)
    high = lax.rem(iota((rows, 128), 1), 2) == 0
    ends = [jnp.where(high, out[i], out[j])[:, 0:32] for i, j in zip(*ENTER[0])]
    face_ref[0] = jnp.concatenate(ends[0:4], axis=1)
    face_ref[1] = jnp.concatenate([ends[4], jnp.zeros((rows, 96), F32)], axis=1)
    odd = odd_slab()
    leaving = []
    for group, z in ((0, depth - 1), (1, 0)):
        out = collide(
            [pops_ref[i, z] for i in range(19)],
            solid_ref[z] == 1,
            [force_ref[d, z] for d in range(3)],
        )
        leaving.append([turn(out[i], STEP[i, 0], 1) for i in ENTER[2][group]])
    if n_drags == 2:
        leaving[0].append(up)
        leaving[1].append(down)
    row = 0
    for a, b in zip(*leaving):
        at = slice(row, row + a.shape[0])
        first_ref[at] = jnp.where(odd, a, b)
        second_ref[at] = jnp.where(odd, b, a)
        row += a.shape[0]


def couple(single, shape, beads, flow, columns, wall, pops, solid):
    _, depth, rows, width = pops.shape
    tile = jax.ShapeDtypeStruct((8, 128), F32)
    drags = [jax.ShapeDtypeStruct((shape[0], 8, 128), F32), tile] if single else beads
    message = jax.ShapeDtypeStruct((5 * rows + (8 if single else 0), width), F32)
    return pl.pallas_call(
        functools.partial(couple_kernel, shape, len(beads), len(drags)),
        out_shape=[
            jax.ShapeDtypeStruct((3, depth, rows, width), F32),
            jax.ShapeDtypeStruct((2, rows, 128), F32),
            message,
            message,
        ]
        + [jax.ShapeDtypeStruct(d.shape, F32) for d in drags]
        + [TOKEN],
        compiler_params=pltpu.CompilerParams(vmem_limit_bytes=ROOM),
        name="couple",
    )(*beads, *flow, columns, wall, pops, solid)


def entered_z(first_ref, second_ref, side, rows):
    odd = odd_slab() if side == 0 else jnp.logical_not(odd_slab())
    return jnp.where(odd, second_ref[rows], first_ref[rows])


X_EDGES = [i for side in range(2) for i in ENTER[2][side] if STEP[i, 0] != 0]


def rows_kernel(depth, rows, before_ref, draft_ref, face_ref, first_ref, second_ref, *refs):
    refs, (cross_ref, token_ref, turned) = refs[:-3], refs[-3:]
    token_ref[...] = jnp.zeros_like(token_ref)
    outs = refs[-1:] if len(refs) == 3 else refs
    for n in range(2):
        turned[n] = face_ref[n].T
    for group in range(2):
        out_ref = outs[0] if len(outs) == 1 else outs[group]
        base = group * 5 * depth if len(outs) == 1 else 0
        y = rows - 1 if group == 0 else 0
        for k, i in enumerate(ENTER[1][group]):
            at = base + k * depth
            value = draft_ref[(group * 5 + k) * depth : (group * 5 + k + 1) * depth]
            if STEP[i, 0] != 0:
                tile, lane = x_place(i)
                column = turned[tile, pl.ds(lane, depth, stride=2), :][:, y : y + 1]
                value = patch_x(value, i, jnp.broadcast_to(column, value.shape))
            out_ref[at : at + depth] = value
            if STEP[i, 2] != 0:
                side = 0 if STEP[i, 2] == 1 else 1
                z = 0 if side == 0 else depth - 1
                row = ENTER[2][side].index(i) * rows + y
                out_ref[at + z : at + z + 1] = entered_z(
                    first_ref, second_ref, side, slice(row, row + 1)
                )
    if len(refs) == 3:
        own_ref, far_ref, out_ref = refs
        came = arrived_drag(own_ref, far_ref, first_ref, second_ref, 5 * rows)
        out_ref[10 * depth : 10 * depth + 8] = one_tile(came, 1)
    for k, i in enumerate(X_EDGES):
        side = 0 if STEP[i, 2] == 1 else 1
        at = ENTER[2][side].index(i) * rows
        cross_ref[k * rows : (k + 1) * rows] = entered_z(
            first_ref, second_ref, side, slice(at, at + rows)
        )


def arrived_drag(own_ref, far_ref, first_ref, second_ref, tail):
    at = slice(tail, tail + 8)
    up, down = [entered_z(first_ref, second_ref, side, at) for side in range(2)]
    return [own_ref[0], down, far_ref[...], up]


def one_tile(tiles, col):
    return jnp.concatenate([t[:, col * CAP : (col + 1) * CAP] for t in tiles], axis=1)


def leaving_rows(depth, rows, before, draft, face, first, second, drags):
    width = draft.shape[1]
    if drags:
        sizes = [10 * depth + 8]
    else:
        sizes = [5 * depth] * 2
    args = (draft, face, first, second, *drags)
    return pl.pallas_call(
        functools.partial(rows_kernel, depth, rows),
        out_shape=[jax.ShapeDtypeStruct((n, width), F32) for n in sizes + [4 * rows]] + [TOKEN],
        in_specs=[pl.BlockSpec(memory_space=pl.ANY)]
        + [pl.BlockSpec(memory_space=pltpu.VMEM)] * len(args),
        scratch_shapes=[pltpu.VMEM((2, 128, rows), F32)],
        compiler_params=pltpu.CompilerParams(vmem_limit_bytes=ROOM),
        name="rows",
    )(before, *args)


def runs(members):
    found = []
    for i in members:
        if found and found[-1][1] == i and STEP[i, 2] == STEP[i - 1, 2]:
            found[-1] = (found[-1][0], i + 1)
        else:
            found.append((i, i + 1))
    return found


def stream_planes(low, high, faces, pops_ref, solid_ref, force_ref, held):
    def plane(z, faces):
        out = collide(
            [pops_ref[i, z] for i in range(19)],
            solid_ref[z] == 1,
            [force_ref[d, z] for d in range(3)],
        )
        for i in range(19):
            value = turn(out[i], STEP[i, 0], 1)
            if STEP[i, 0] != 0 and faces:
                tile, lane = x_place(i)
                value = patch_x(value, i, spread_column(faces[tile], lane))
            held[i, z] = turn(value, STEP[i, 1], 0)
        return tuple(pltpu.roll(f, 126, 1) for f in faces)

    return lax.fori_loop(low, high, plane, faces, unroll=2)


def lower_kernel(
    before_ref, pops_ref, solid_ref, force_ref, side_ref, wall_ref, held, draft_ref, token_ref
):
    depth, rows, _ = pops_ref.shape[1:]
    token_ref[...] = jnp.zeros_like(token_ref)
    for group in range(2):
        force = [force_ref[d, :, 0 if group else rows - 1, :] for d in range(3)]
        out = collide([side_ref[i, 1 - group] for i in range(19)], wall_ref[1 - group] == 1, force)
        for k, i in enumerate(ENTER[1][group]):
            row = (group * 5 + k) * depth
            value = turn(out[i], STEP[i, 0], 1)
            draft_ref[row : row + depth] = turn(value, STEP[i, 2], 0)
    stream_planes(0, held.shape[1], (), pops_ref, solid_ref, force_ref, held)


def upper_kernel(
    before_ref, lower_ref, pops_ref, solid_ref, force_ref, face_ref, out_ref, tile_ref, held, sem
):
    depth, rows, width = pops_ref.shape[1:]
    half = lower_ref.shape[1]
    copies = []

    def leave(source, members, low, high):
        for a, b in runs(members):
            step = int(STEP[a, 2])
            start, stop = max(low + step, 0), min(high + step, depth)
            copy = pltpu.make_async_copy(
                source.at[a:b, start - step : stop - step],
                out_ref.at[a:b, start:stop],
                sem.at[len(copies)],
            )
            copy.start()
            copies.append(copy)

    straight = [i for i in range(19) if STEP[i, 0] == 0]
    across = [i for i in range(19) if STEP[i, 0] != 0]
    leave(lower_ref, straight, 0, half)
    faces = (face_ref[0], face_ref[1])
    for i in across:
        tile, lane = x_place(i)
        for z in range(half):
            column = turn(spread_column(faces[tile], lane + 2 * z), STEP[i, 1], 0)
            held[i, z] = patch_x(lower_ref[i, z], i, column)
    leave(held, across, 0, half)
    faces = tuple(pltpu.roll(f, 128 - 2 * half, 1) for f in faces)
    marks = upper_marks(half, depth)
    for low, high in zip(marks, marks[1:]):
        faces = stream_planes(low, high, faces, pops_ref, solid_ref, force_ref, held)
        leave(held, range(19), low, high)
    for group in range(2):
        first = slice(0, 8) if group == 0 else slice(rows - 8, rows)
        for k, i in enumerate(ENTER[1][group]):
            source = lower_ref if i in straight else held
            tile_ref[group * 5 + k, 0:half] = source[i, 0:half, first, :]
            tile_ref[group * 5 + k, half:depth] = held[i, half:depth, first, :]
    for copy in copies:
        copy.wait()


def upper_marks(half, depth):
    return list(range(half, depth - 2, 4)) + ([depth - 2] if (depth - half) % 4 else []) + [depth]


def stream_lower(half, before, pops, solid, force, sides, walls):
    _, depth, rows, width = pops.shape
    vmem = pl.BlockSpec(memory_space=pltpu.VMEM)
    return pl.pallas_call(
        lower_kernel,
        out_shape=[
            jax.ShapeDtypeStruct((19, half, rows, width), F32),
            jax.ShapeDtypeStruct((10 * depth, width), F32),
            TOKEN,
        ],
        in_specs=[pl.BlockSpec(memory_space=pl.ANY)] + [vmem] * 5,
        compiler_params=pltpu.CompilerParams(vmem_limit_bytes=ROOM),
        cost_estimate=pl.CostEstimate(flops=3000000, bytes_accessed=2000000, transcendentals=0),
        name="lower",
    )(before, pops, solid, force, sides, walls)


def stream_upper(before, lower, pops, solid, force, face):
    _, depth, rows, width = pops.shape
    vmem = pl.BlockSpec(memory_space=pltpu.VMEM)
    return pl.pallas_call(
        upper_kernel,
        out_shape=[
            jax.ShapeDtypeStruct(pops.shape, F32),
            jax.ShapeDtypeStruct((10, depth, 8, width), F32),
        ],
        in_specs=[pl.BlockSpec(memory_space=pl.ANY)] + [vmem] * 5,
        out_specs=[pl.BlockSpec(memory_space=pltpu.HBM), vmem],
        scratch_shapes=[
            pltpu.VMEM(pops.shape, F32),
            pltpu.SemaphoreType.DMA((20 * len(upper_marks(lower.shape[1], depth)),)),
        ],
        compiler_params=pltpu.CompilerParams(vmem_limit_bytes=ROOM),
        cost_estimate=pl.CostEstimate(flops=5000000, bytes_accessed=3000000, transcendentals=0),
        name="upper",
    )(before, lower, pops, solid, force, face)


def finish_kernel(shape, n_rows, whole_ref, target_ref, tile_ref, first_ref, second_ref, *refs):
    row_refs, cross_ref, refs = refs[:n_rows], refs[n_rows], refs[n_rows + 1 :]
    drag_refs, (out_ref, bead_ref, planes, tiles, bead, sem) = refs[:-6], refs[-6:]
    depth, rows, width = whole_ref.shape[1:]

    def entering(group, k):
        at = (group * 5 + k) * depth if n_rows == 1 else k * depth
        return row_refs[group % n_rows][at : at + depth]

    copies = []

    def leave(source, target):
        copy = pltpu.make_async_copy(source, target, sem.at[len(copies)])
        copy.start()
        copies.append(copy)

    for group in range(2):
        z = 0 if group == 0 else depth - 1
        for k, i in enumerate(ENTER[2][group]):
            value = entered_z(first_ref, second_ref, group, slice(k * rows, (k + 1) * rows))
            if STEP[i, 1] != 0:
                side = 0 if STEP[i, 1] == 1 else 1
                y = 0 if side == 0 else rows - 1
                row = entering(side, ENTER[1][side].index(i))[z : z + 1]
                value = jnp.where(
                    iota((rows, width), 0) == y,
                    jnp.broadcast_to(row, (rows, width)),
                    turn(value, STEP[i, 1], 0),
                )
            if STEP[i, 0] != 0:
                at = X_EDGES.index(i) * rows
                value = patch_x(value, i, cross_ref[at : at + rows])
            n = group * 5 + k
            planes[n] = value
            leave(planes.at[n], out_ref.at[i, z])
    for group in range(2):
        first = 0 if group == 0 else rows - 8
        for k, i in enumerate(ENTER[1][group]):
            n = group * 5 + k
            step = int(STEP[i, 2])
            tiles[n, 1 + step : 1 + step + depth] = tile_ref[n]
            tiles[n, 1 : 1 + depth, 0 if group == 0 else 7, :] = entering(group, k)
            low, high = max(step, 0), min(depth + step, depth)
            leave(tiles.at[n, 1 + low : 1 + high], out_ref.at[i, low:high, first : first + 8])

    count = target_ref.shape[1]
    target = target_ref[...]
    if len(drag_refs) == 2:
        slabs, cols, _ = shape
        came = arrived_drag(*drag_refs, first_ref, second_ref, 5 * rows)
        passed = row_refs[0][10 * depth : 10 * depth + 8]
        table = jnp.concatenate([one_tile(came, 0), passed], axis=1)
        owner = lax.shift_right_logical(target, 5)
        owner_slab = lax.shift_right_logical(owner, cols.bit_length() - 1)
        away_col = owner - owner_slab * cols - lax.axis_index("col")
        away_col = jnp.where(away_col < 0, away_col + cols, away_col)
        away_slab = owner_slab - lax.axis_index("slab")
        away_slab = jnp.where(away_slab < 0, away_slab + slabs, away_slab)
        place = away_col * 128 + away_slab * CAP + target - owner * CAP
        choose = (iota((256, count), 0) == place).astype(F32).astype(BF16)
        total = dot_select(table, choose, NN)
    else:
        back_ref = drag_refs[0]

        def group(k, total):
            got = [back_ref[k * GROUP + r] for r in range(GROUP)]
            slots = jnp.concatenate([t[:, 0:CAP] for t in got], axis=1)
            first = k * (GROUP * CAP)
            choose = (iota((GROUP * CAP, count), 0) + first == target).astype(F32)
            return total + dot_select(slots, choose.astype(BF16), NN)

        total = lax.fori_loop(
            0, back_ref.shape[0] // GROUP, group, jnp.zeros((8, count), F32)
        )
    bead[...] = total[0:3]
    leave(bead, bead_ref)
    for copy in copies:
        copy.wait()


def finish(shape, whole, target, tiles, first, second, entered, cross, drags):
    _, depth, rows, width = whole.shape
    vmem = pl.BlockSpec(memory_space=pltpu.VMEM)
    hbm = pl.BlockSpec(memory_space=pltpu.HBM)
    args = [whole, target, tiles, first, second, *entered, cross, *drags]
    return pl.pallas_call(
        functools.partial(finish_kernel, shape, len(entered)),
        out_shape=[
            jax.ShapeDtypeStruct(whole.shape, F32),
            jax.ShapeDtypeStruct((3, target.shape[1]), F32),
        ],
        in_specs=[hbm] + [vmem] * (len(args) - 1),
        out_specs=[hbm, hbm],
        scratch_shapes=[
            pltpu.VMEM((10, rows, width), F32),
            pltpu.VMEM((10, depth + 2, 8, width), F32),
            pltpu.VMEM((3, target.shape[1]), F32),
            pltpu.SemaphoreType.DMA((21,)),
        ],
        input_output_aliases={0: 0},
        compiler_params=pltpu.CompilerParams(vmem_limit_bytes=ROOM),
        name="finish",
    )(*args)


def shards(populations, solid_mask, bead_owner, bead_base, bead_offset, bead_velocity):
    slabs, cols, pairs = shape = tuple(lax.axis_size(a) for a in ("slab", "col", "pair"))
    owners = slabs * cols
    depth, rows = populations.shape[1:3]
    single = owners == GROUP and slabs == 4
    swap = functools.partial(
        lax.all_to_all, axis_name=("slab", "col"), split_axis=0, concat_axis=0, tiled=True
    )

    target, *tiles = pack(shape, single, bead_owner, bead_base, bead_offset, bead_velocity)

    def send_far(value):
        return send(value, shape, lambda s, c, p: ((s + 2) % slabs, c, p))

    *flow, columns, sides, token = moments(tiles[0], populations)
    if single:
        came = send(tiles[1], shape, lambda s, c, p: (s, (c + 1) % cols, p))
        own, near, next_, far, token = join(token, tiles[0], came)
        beads = [own, send_slab(near, shape, 1), send_slab(next_, shape, 0), send_far(far)]
    else:
        beads = [swap(tiles[0])]
    wall, walls = wall_faces(token, solid_mask)
    force, face, first, second, drag, *far, token = couple(
        single, shape, beads, flow, columns, wall, populations, solid_mask
    )

    def send_pair(value):
        return send(value, shape, lambda s, c, p: (s, c, (p + 1) % pairs))

    def send_col(values):
        return [
            send(value, shape, lambda s, c, p, sign=sign: (s, (c + sign) % cols, p))
            for value, sign in zip(values, (1, -1))
        ]

    face = send_pair(face)
    first, second = send_slab(first, shape, 1), send_slab(second, shape, 0)
    if single:
        drags = [drag, send_far(far[0])]
    else:
        drags = []
        drag = swap(drag)
    fields = (populations, solid_mask, force)
    lower, draft, token = stream_lower(10, token, *fields, sides, walls)
    *leaving, cross, token = leaving_rows(depth, rows, token, draft, face, first, second, drags)
    entered, cross = send_col(leaving), send_pair(cross)
    whole, tiles = stream_upper(token, lower, *fields, face)
    return tuple(
        finish(shape, whole, target, tiles, first, second, entered, cross, drags or [drag])
    )


def solution(mesh):
    return jax.shard_map(
        shards,
        mesh=mesh,
        in_specs=(
            P(None, ("rep", "slab"), "col", "pair"),
            P(("rep", "slab"), "col", "pair"),
            P(("rep", "slab", "col", "pair")),
            P(None, ("rep", "slab", "col", "pair")),
            P(None, ("rep", "slab", "col", "pair")),
            P(None, ("rep", "slab", "col", "pair")),
        ),
        out_specs=(
            P(None, ("rep", "slab"), "col", "pair"),
            P(None, ("rep", "slab", "col", "pair")),
        ),
        check_vma=False,
    )
```

```python
import functools

import jax
import jax.numpy as jnp
import numpy as np
from jax import lax
from jax.experimental import pallas as pl
from jax.experimental.pallas import tpu as pltpu
from jax.sharding import PartitionSpec as P

CAP = 32
GROUP = 8

STEP = np.array(
    [
        [0, 0, 0],
        [1, 0, 0],
        [-1, 0, 0],
        [0, 1, 0],
        [0, -1, 0],
        [0, 0, 1],
        [0, 0, -1],
        [1, 1, 0],
        [-1, -1, 0],
        [1, -1, 0],
        [-1, 1, 0],
        [1, 0, 1],
        [-1, 0, -1],
        [1, 0, -1],
        [-1, 0, 1],
        [0, 1, 1],
        [0, -1, -1],
        [0, 1, -1],
        [0, -1, 1],
    ],
    np.int32,
)
TAU_PLUS = 0.8
TAU_MINUS = 0.5 + (3.0 / 16.0) / (TAU_PLUS - 0.5)
KEEP_EVEN = 1.0 - 1.0 / TAU_PLUS
KEEP_ODD = 1.0 - 1.0 / TAU_MINUS
FORCE_GAIN = 1.0 - 0.5 / TAU_PLUS
DRAG_COEF = 2.0
F32 = jnp.float32
BF16 = jnp.bfloat16

ENTER = [[[i for i in range(19) if STEP[i, a] == sign] for sign in (1, -1)] for a in range(3)]
TOKEN = jax.ShapeDtypeStruct((8, 128), F32)
ROOM = 16 << 20
NT = (((1,), (1,)), ((), ()))
NN = (((1,), (0,)), ((), ()))


def iota(shape, dim):
    return lax.broadcasted_iota(jnp.int32, shape, dim)


def high_low(value):
    high = value.astype(BF16)
    return high, (value - high.astype(F32)).astype(BF16)


def dot_split(left, right, dims):
    (a, b), (c, d) = left, right
    mul = functools.partial(lax.dot_general, dimension_numbers=dims, preferred_element_type=F32)
    return mul(a, c) + (mul(a, d) + mul(b, c))


def dot_select(value, choose, dims):
    first = value.astype(BF16).astype(F32)
    rest = value - first
    second = rest.astype(BF16).astype(F32)
    stacked = jnp.concatenate([first, second, rest - second], axis=0).astype(BF16)
    got = lax.dot_general(stacked, choose, dimension_numbers=dims, preferred_element_type=F32)
    rows = value.shape[0]
    return got[0:rows] + got[rows : 2 * rows] + got[2 * rows : 3 * rows]


def density_momentum(pops):
    momentum = []
    for axis in range(3):
        plus = [pops[i] for i in range(19) if STEP[i, axis] == 1]
        minus = [pops[i] for i in range(19) if STEP[i, axis] == -1]
        momentum.append(sum(plus[1:], plus[0]) - sum(minus[1:], minus[0]))
    return sum(pops[1:], pops[0]), momentum


def along(step, vector):
    terms = None
    for axis in range(3):
        if step[axis] == 0:
            continue
        if terms is None:
            terms = vector[axis] if step[axis] == 1 else -vector[axis]
        else:
            terms = terms + vector[axis] if step[axis] == 1 else terms - vector[axis]
    return terms


def collide(pops, wall, force):
    density, momentum = density_momentum(pops)
    inverse = 1.0 / density
    carried = [m + 0.5 * f for m, f in zip(momentum, force)]
    speed = [m * inverse for m in carried]
    w = 1.0 / 36.0
    bend = [(4.5 * w / TAU_PLUS) * m + (9.0 * w * FORCE_GAIN) * f for m, f in zip(carried, force)]
    push = [(3.0 * w / TAU_MINUS) * m + (3.0 * w * FORCE_GAIN) * f for m, f in zip(carried, force)]
    drop = [(1.5 * w / TAU_PLUS) * m + (3.0 * w * FORCE_GAIN) * f for m, f in zip(carried, force)]
    rest = (w / TAU_PLUS) * density - sum(
        [u * d for u, d in zip(speed[1:], drop[1:])], speed[0] * drop[0]
    )
    out = [None] * 19
    out[0] = jnp.where(wall, pops[0], KEEP_EVEN * pops[0] + 12.0 * rest)
    for i in range(1, 19, 2):
        a, b = pops[i], pops[i + 1]
        step = STEP[i]
        even = rest + along(step, speed) * along(step, bend)
        odd = along(step, push)
        if i < 7:
            even = even + even
            odd = odd + odd
        even = (0.5 * KEEP_EVEN) * (a + b) + even
        odd = (0.5 * KEEP_ODD) * (a - b) + odd
        out[i] = jnp.where(wall, b, even + odd)
        out[i + 1] = jnp.where(wall, a, even - odd)
    return out


def turn(value, amount, axis):
    if amount == 0:
        return value
    return pltpu.roll(value, int(amount) % value.shape[axis], axis)


def send(value, shape, target):
    def flat(at):
        return (at[0] * shape[1] + at[1]) * shape[2] + at[2]

    perm = [(flat(at), flat(target(*at))) for at in np.ndindex(*shape)]
    return lax.ppermute(value, ("slab", "col", "pair"), perm)


def send_slab(value, shape, which):
    def target(s, c, p):
        return ((s + (1 if s % 2 == which else -1)) % shape[0], c, p)

    return send(value, shape, target)


def odd_slab():
    return lax.rem(lax.axis_index("slab"), 2) == 1


def rank_among(member):
    count = member.shape[1]
    earlier = (iota((count, count), 0) < iota((count, count), 1)).astype(F32).astype(BF16)
    return lax.dot_general(member.astype(BF16), earlier, NN, preferred_element_type=F32)


def patch_x(value, i, column):
    side = 0 if STEP[i, 0] == 1 else value.shape[1] - 1
    return jnp.where(iota(value.shape, 1) == side, column, value)


def x_pair(i):
    return ENTER[0][0 if STEP[i, 0] == 1 else 1].index(i)


def x_place(i):
    k = x_pair(i)
    return k // 4, (k % 4) * 32 + (1 if STEP[i, 0] == 1 else 0)


def x_entering(face, k, z):
    tile = face[k // 4]
    return pltpu.roll(tile, tile.shape[1] - ((k % 4) * 32 + 2 * z + 1), 1)


def x_ends(planes):
    lane = lax.shift_right_logical(iota(planes[0].shape, 1), 1)
    tile = jnp.ones(planes[0].shape, F32)
    for z, value in enumerate(planes):
        tile = jnp.where(lane == z, pltpu.roll(value, 2 * z + 1, 1), tile)
    return tile


def pack_kernel(
    steps, owner_ref, base_ref, offset_ref, velocity_ref, target_ref, out_ref, table
):
    count = owner_ref.shape[1]
    step = 0 if steps == 1 else pl.program_id(0)
    local = owner_ref[...] - step * GROUP
    member = (iota((GROUP, count), 0) == local).astype(F32)
    rank = jnp.sum(member * rank_among(member), axis=0, keepdims=True).astype(jnp.int32)
    inside = (local >= 0) & (local < GROUP)
    target = jnp.where(inside, local * CAP + rank, -1)
    whole_target = jnp.where(inside, owner_ref[...] * CAP + rank, -1)

    if steps == 1:
        target_ref[...] = whole_target
    else:
        known = jnp.where(step == 0, -1, target_ref[...])
        target_ref[...] = jnp.maximum(known, whole_target)

    choose = (iota((GROUP * CAP, count), 0) == target).astype(F32).astype(BF16)
    table[...] = jnp.zeros_like(table)
    table[0:3] = base_ref[...].astype(F32) + 1.0
    table[8:11] = offset_ref[...]
    table[16:19] = velocity_ref[...]
    packed = dot_select(table[...], choose, NT)
    blank = jnp.zeros((8, CAP), F32)
    for r in range(GROUP):
        lanes = slice(r * CAP, (r + 1) * CAP)
        out_ref[r] = jnp.concatenate(
            [packed[0:8, lanes], packed[8:16, lanes], packed[16:24, lanes], blank], axis=1
        )


def pack(owners, owner, base, offset, velocity):
    count, steps = owner.shape[0], owners // GROUP
    args = (owner.reshape(1, count), base, offset, velocity)
    blocks = {}
    if steps > 1:
        blocks = dict(
            grid=(steps,),
            in_specs=[pl.BlockSpec(a.shape, lambda k: (0, 0)) for a in args],
            out_specs=[
                pl.BlockSpec((1, count), lambda k: (0, 0)),
                pl.BlockSpec((GROUP, 8, 128), lambda k: (k, 0, 0)),
            ],
            compiler_params=pltpu.CompilerParams(vmem_limit_bytes=48 << 20),
        )
    return pl.pallas_call(
        functools.partial(pack_kernel, steps),
        out_shape=[
            jax.ShapeDtypeStruct((1, count), jnp.int32),
            jax.ShapeDtypeStruct((owners, 8, 128), F32),
        ],
        scratch_shapes=[pltpu.VMEM((24, count), F32)],
        name="pack",
        **blocks,
    )(*args)


def moments_kernel(
    pops_ref, solid_ref, high_ref, low_ref, column_ref, side_ref, wall_ref, held, held_solid, flow, sem
):
    depth, rows, width = pops_ref.shape[1:]
    chunks = 4
    span = depth // chunks
    copies = [pltpu.make_async_copy(solid_ref, held_solid, sem.at[chunks])]
    for k in range(chunks):
        part = pl.ds(k * span, span)
        copies.append(
            pltpu.make_async_copy(pops_ref.at[:, part], held.at[:, part], sem.at[k])
        )
    for copy in copies:
        copy.start()

    def plane(z, carry):
        pops = [held[i, z] for i in range(19)]
        density, momentum = density_momentum(pops)
        inverse = 1.0 / density
        for axis in range(3):
            flow[axis, pl.ds(pl.multiple_of(z * rows, rows), rows)] = momentum[axis] * inverse
        return carry

    for k in range(chunks):
        copies[1 + k].wait()
        lax.fori_loop(k * span, (k + 1) * span, plane, 0, unroll=2)
    copies[0].wait()
    for axis in range(3):
        at = slice(axis * width, (axis + 1) * width)
        high_ref[at], low_ref[at] = high_low(flow[axis].T)
    for i in range(19):
        column_ref[i] = x_ends([held[i, z] for z in range(depth)])
        side_ref[i, 0] = held[i, :, 0, :]
        side_ref[i, 1] = held[i, :, rows - 1, :]
    wall_ref[0] = held_solid[:, 0, :]
    wall_ref[1] = held_solid[:, rows - 1, :]
    column_ref[19] = x_ends([held_solid[z].astype(F32) for z in range(depth)])


def moments(pops, solid):
    _, depth, rows, width = pops.shape
    hbm = pl.BlockSpec(memory_space=pltpu.HBM)
    return pl.pallas_call(
        moments_kernel,
        out_shape=[
            jax.ShapeDtypeStruct((3 * width, depth * rows), BF16),
            jax.ShapeDtypeStruct((3 * width, depth * rows), BF16),
            jax.ShapeDtypeStruct((20, rows, 128), F32),
            jax.ShapeDtypeStruct((19, 2, depth, width), F32),
            jax.ShapeDtypeStruct((2, depth, width), jnp.int32),
        ],
        in_specs=[hbm, hbm],
        scratch_shapes=[
            pltpu.VMEM(pops.shape, F32),
            pltpu.VMEM(solid.shape, jnp.int32),
            pltpu.VMEM((3, depth * rows, width), F32),
            pltpu.SemaphoreType.DMA((5,)),
        ],
        compiler_params=pltpu.CompilerParams(vmem_limit_bytes=54000000),
        cost_estimate=pl.CostEstimate(flops=3000000, bytes_accessed=4000000, transcendentals=0),
        name="moments",
    )(pops, solid)


def unpack(tiles):
    return [
        jnp.concatenate([t[:, g * CAP : (g + 1) * CAP] for t in tiles], axis=1) for g in range(3)
    ]


def couple_group(base, part, velocity, flow, depth, rows, width):
    slots = GROUP * CAP
    start = base.astype(jnp.int32) - 1

    def hat(axis, length):
        cell = iota((length, slots), 0)
        low, share = start[axis : axis + 1], part[axis : axis + 1]
        return jnp.where(cell == low, 1.0 - share, 0.0) + jnp.where(cell == low + 1, share, 0.0)

    hat_x, hat_y, hat_z = hat(0, width), hat(1, rows), hat(2, depth)
    weight = high_low((hat_z[:, None, :] * hat_y[None, :, :]).reshape(depth * rows, slots))
    across = dot_split(flow, weight, NN)
    drag = []
    for d in range(3):
        sampled = jnp.sum(across[d * width : (d + 1) * width] * hat_x, axis=0, keepdims=True)
        drag.append(DRAG_COEF * (sampled - velocity[d : d + 1]))
    spread = jnp.concatenate([hat_x * (-drag[d]) for d in range(3)], axis=0)
    return drag, dot_split(weight, high_low(spread), NT)


def couple_kernel(shape, n_drags, beads_ref, high_ref, low_ref, *refs):
    slabs, cols, _ = shape
    column_ref, pops_ref, solid_ref, force_ref, face_ref, first_ref, second_ref, *refs = refs
    drag_refs, token_ref = refs[:-1], refs[-1]
    token_ref[...] = jnp.zeros_like(token_ref)
    depth, rows, width = pops_ref.shape[1:]
    flow = (high_ref[...], low_ref[...])

    def grid(force):
        return [
            force[:, d * width : (d + 1) * width].reshape(depth, rows, width) for d in range(3)
        ]

    hollow = jnp.zeros((5, GROUP * CAP), F32)

    if n_drags == 2:
        slab, col = lax.axis_index("slab"), lax.axis_index("col")
        got = []
        for r in range(GROUP):
            there = [a - b for a, b in zip((slab, col), divmod(r, cols))]
            there = [jnp.where(a < 0, a + n, a) for a, n in zip(there, (slabs, cols))]
            got.append(beads_ref[there[0] * cols + there[1]])
        drag, force = couple_group(*unpack(got), flow, depth, rows, width)
        for d, value in enumerate(grid(force)):
            force_ref[d] = value
        stacked = jnp.concatenate(drag + [hollow], axis=0)
        lanes = cols * CAP
        blank = jnp.zeros((8, 128 - lanes), F32)
        for dz in range(slabs):
            tile = jnp.concatenate([stacked[:, dz * lanes : (dz + 1) * lanes], blank], axis=1)
            drag_refs[0][dz] = tile
            if dz == 2:
                drag_refs[1][...] = tile
            if dz == 1:
                down = tile
        up = tile
    else:
        force_ref[...] = jnp.zeros_like(force_ref)
        blank = jnp.zeros((8, 128 - CAP), F32)

        def group(k, carry):
            got = [beads_ref[k * GROUP + r] for r in range(GROUP)]
            drag, force = couple_group(*unpack(got), flow, depth, rows, width)
            for d, value in enumerate(grid(force)):
                force_ref[d] += value
            stacked = jnp.concatenate(drag + [hollow], axis=0)
            for r in range(GROUP):
                drag_refs[0][k * GROUP + r] = jnp.concatenate(
                    [stacked[:, r * CAP : (r + 1) * CAP], blank], axis=1
                )
            return carry

        lax.fori_loop(0, beads_ref.shape[0] // GROUP, group, 0)

    force = [x_ends([force_ref[d, z] for z in range(depth)]) for d in range(3)]
    out = collide([column_ref[i] for i in range(19)], column_ref[19] == 1.0, force)
    high = lax.rem(iota((rows, 128), 1), 2) == 0
    ends = [
        jnp.where(high, turn(out[j], -1, 1), turn(out[i], 1, 1))[:, 0:32]
        for i, j in zip(*ENTER[0])
    ]
    face_ref[0] = jnp.concatenate(ends[0:4], axis=1)
    face_ref[1] = jnp.concatenate([ends[4], jnp.zeros((rows, 96), F32)], axis=1)
    odd = odd_slab()
    leaving = []
    for group, z in ((0, depth - 1), (1, 0)):
        out = collide(
            [pops_ref[i, z] for i in range(19)],
            solid_ref[z] == 1,
            [force_ref[d, z] for d in range(3)],
        )
        leaving.append([turn(out[i], STEP[i, 0], 1) for i in ENTER[2][group]])
    if n_drags == 2:
        leaving[0].append(up)
        leaving[1].append(down)
    row = 0
    for a, b in zip(*leaving):
        at = slice(row, row + a.shape[0])
        first_ref[at] = jnp.where(odd, a, b)
        second_ref[at] = jnp.where(odd, b, a)
        row += a.shape[0]


def couple(shape, beads, flow, columns, pops, solid):
    _, depth, rows, width = pops.shape
    single = beads.shape[0] == GROUP
    tile = jax.ShapeDtypeStruct((8, 128), F32)
    drags = [jax.ShapeDtypeStruct((shape[0], 8, 128), F32), tile] if single else [beads]
    message = jax.ShapeDtypeStruct((5 * rows + (8 if single else 0), width), F32)
    return pl.pallas_call(
        functools.partial(couple_kernel, shape, len(drags)),
        out_shape=[
            jax.ShapeDtypeStruct((3, depth, rows, width), F32),
            jax.ShapeDtypeStruct((2, rows, 128), F32),
            message,
            message,
        ]
        + [jax.ShapeDtypeStruct(d.shape, F32) for d in drags]
        + [TOKEN],
        compiler_params=pltpu.CompilerParams(vmem_limit_bytes=ROOM),
        name="couple",
    )(beads, *flow, columns, pops, solid)


def entered_z(first_ref, second_ref, side, rows):
    odd = odd_slab() if side == 0 else jnp.logical_not(odd_slab())
    return jnp.where(odd, second_ref[rows], first_ref[rows])


X_EDGES = [i for side in range(2) for i in ENTER[2][side] if STEP[i, 0] != 0]


def rows_kernel(depth, rows, before_ref, draft_ref, first_ref, second_ref, *refs):
    refs, (cross_ref, token_ref) = refs[:-2], refs[-2:]
    token_ref[...] = jnp.zeros_like(token_ref)
    outs = refs[-1:] if len(refs) == 3 else refs
    for group in range(2):
        out_ref = outs[0] if len(outs) == 1 else outs[group]
        base = group * 5 * depth if len(outs) == 1 else 0
        y = rows - 1 if group == 0 else 0
        out_ref[base : base + 5 * depth] = draft_ref[group * 5 * depth : (group + 1) * 5 * depth]
        for k, i in enumerate(ENTER[1][group]):
            at = base + k * depth
            if STEP[i, 2] != 0:
                side = 0 if STEP[i, 2] == 1 else 1
                z = 0 if side == 0 else depth - 1
                row = ENTER[2][side].index(i) * rows + y
                out_ref[at + z : at + z + 1] = entered_z(
                    first_ref, second_ref, side, slice(row, row + 1)
                )
    if len(refs) == 3:
        own_ref, far_ref, out_ref = refs
        came = arrived_drag(own_ref, far_ref, first_ref, second_ref, 5 * rows)
        out_ref[10 * depth : 10 * depth + 8] = one_tile(came, 1)
    for k, i in enumerate(X_EDGES):
        side = 0 if STEP[i, 2] == 1 else 1
        at = ENTER[2][side].index(i) * rows
        cross_ref[k * rows : (k + 1) * rows] = entered_z(
            first_ref, second_ref, side, slice(at, at + rows)
        )


def arrived_drag(own_ref, far_ref, first_ref, second_ref, tail):
    at = slice(tail, tail + 8)
    up, down = [entered_z(first_ref, second_ref, side, at) for side in range(2)]
    return [own_ref[0], down, far_ref[...], up]


def one_tile(tiles, col):
    return jnp.concatenate([t[:, col * CAP : (col + 1) * CAP] for t in tiles], axis=1)


def leaving_rows(depth, rows, before, draft, first, second, drags):
    width = draft.shape[1]
    if drags:
        sizes = [10 * depth + 8]
    else:
        sizes = [5 * depth] * 2
    args = (draft, first, second, *drags)
    return pl.pallas_call(
        functools.partial(rows_kernel, depth, rows),
        out_shape=[jax.ShapeDtypeStruct((n, width), F32) for n in sizes + [4 * rows]] + [TOKEN],
        in_specs=[pl.BlockSpec(memory_space=pl.ANY)]
        + [pl.BlockSpec(memory_space=pltpu.VMEM)] * len(args),
        compiler_params=pltpu.CompilerParams(vmem_limit_bytes=ROOM),
        name="rows",
    )(before, *args)


def runs(members):
    found = []
    for i in members:
        if found and found[-1][1] == i and STEP[i, 2] == STEP[i - 1, 2]:
            found[-1] = (found[-1][0], i + 1)
        else:
            found.append((i, i + 1))
    return found


def stream_planes(low, high, faces, pops_ref, solid_ref, force_ref, held):
    def plane(z, faces):
        out = collide(
            [pops_ref[i, z] for i in range(19)],
            solid_ref[z] == 1,
            [force_ref[d, z] for d in range(3)],
        )
        for i in range(19):
            value = turn(out[i], STEP[i, 0], 1)
            if STEP[i, 0] != 0:
                value = patch_x(value, i, faces[x_pair(i)])
            held[i, z] = turn(value, STEP[i, 1], 0)
        return tuple(pltpu.roll(f, 126, 1) for f in faces)

    return lax.fori_loop(low, high, plane, faces, unroll=2)


def lower_kernel(
    before_ref, pops_ref, solid_ref, force_ref, side_ref, wall_ref, face_ref, *refs
):
    held, draft_ref, token_ref, turned = refs
    depth, rows, _ = pops_ref.shape[1:]
    token_ref[...] = jnp.zeros_like(token_ref)
    for n in range(2):
        turned[n] = face_ref[n].T
    for group in range(2):
        y = 0 if group else rows - 1
        force = [force_ref[d, :, y, :] for d in range(3)]
        out = collide([side_ref[i, 1 - group] for i in range(19)], wall_ref[1 - group] == 1, force)
        for k, i in enumerate(ENTER[1][group]):
            row = (group * 5 + k) * depth
            value = turn(out[i], STEP[i, 0], 1)
            if STEP[i, 0] != 0:
                tile, lane = x_place(i)
                column = turned[tile, pl.ds(lane, depth, stride=2), :][:, y : y + 1]
                value = patch_x(value, i, jnp.broadcast_to(column, value.shape))
            draft_ref[row : row + depth] = turn(value, STEP[i, 2], 0)
    face = (face_ref[0], face_ref[1])
    faces = tuple(x_entering(face, k, 0) for k in range(5))
    stream_planes(0, held.shape[1], faces, pops_ref, solid_ref, force_ref, held)


def upper_kernel(
    before_ref, lower_ref, pops_ref, solid_ref, force_ref, face_ref, out_ref, tile_ref, held, sem
):
    depth, rows, width = pops_ref.shape[1:]
    half = lower_ref.shape[1]
    copies = []

    def leave(source, members, low, high):
        for a, b in runs(members):
            step = int(STEP[a, 2])
            start, stop = max(low + step, 0), min(high + step, depth)
            copy = pltpu.make_async_copy(
                source.at[a:b, start - step : stop - step],
                out_ref.at[a:b, start:stop],
                sem.at[len(copies)],
            )
            copy.start()
            copies.append(copy)

    leave(lower_ref, range(19), 0, half)
    face = (face_ref[0], face_ref[1])
    faces = tuple(x_entering(face, k, half) for k in range(5))
    marks = upper_marks(half, depth)
    for low, high in zip(marks, marks[1:]):
        faces = stream_planes(low, high, faces, pops_ref, solid_ref, force_ref, held)
        leave(held, range(19), low, high)
    for group in range(2):
        first = slice(0, 8) if group == 0 else slice(rows - 8, rows)
        for k, i in enumerate(ENTER[1][group]):
            tile_ref[group * 5 + k, 0:half] = lower_ref[i, :, first, :]
            tile_ref[group * 5 + k, half:depth] = held[i, half:depth, first, :]
    for copy in copies:
        copy.wait()


def upper_marks(half, depth):
    return list(range(half, depth - 2, 4)) + ([depth - 2] if (depth - half) % 4 else []) + [depth]


def stream_lower(half, before, pops, solid, force, sides, walls, face):
    _, depth, rows, width = pops.shape
    vmem = pl.BlockSpec(memory_space=pltpu.VMEM)
    return pl.pallas_call(
        lower_kernel,
        out_shape=[
            jax.ShapeDtypeStruct((19, half, rows, width), F32),
            jax.ShapeDtypeStruct((10 * depth, width), F32),
            TOKEN,
        ],
        in_specs=[pl.BlockSpec(memory_space=pl.ANY)] + [vmem] * 6,
        scratch_shapes=[pltpu.VMEM((2, 128, rows), F32)],
        compiler_params=pltpu.CompilerParams(vmem_limit_bytes=ROOM),
        cost_estimate=pl.CostEstimate(flops=3000000, bytes_accessed=2000000, transcendentals=0),
        name="lower",
    )(before, pops, solid, force, sides, walls, face)


def stream_upper(before, lower, pops, solid, force, face):
    _, depth, rows, width = pops.shape
    vmem = pl.BlockSpec(memory_space=pltpu.VMEM)
    return pl.pallas_call(
        upper_kernel,
        out_shape=[
            jax.ShapeDtypeStruct(pops.shape, F32),
            jax.ShapeDtypeStruct((10, depth, 8, width), F32),
        ],
        in_specs=[pl.BlockSpec(memory_space=pl.ANY)] + [vmem] * 5,
        out_specs=[pl.BlockSpec(memory_space=pltpu.HBM), vmem],
        scratch_shapes=[
            pltpu.VMEM(pops.shape, F32),
            pltpu.SemaphoreType.DMA((20 * len(upper_marks(lower.shape[1], depth)),)),
        ],
        compiler_params=pltpu.CompilerParams(vmem_limit_bytes=ROOM),
        cost_estimate=pl.CostEstimate(flops=5000000, bytes_accessed=3000000, transcendentals=0),
        name="upper",
    )(before, lower, pops, solid, force, face)


def choice_kernel(shape, before_ref, target_ref, choice_ref, token_ref):
    slabs, cols, _ = shape
    token_ref[...] = jnp.zeros_like(token_ref)
    target = target_ref[...]
    owner = lax.shift_right_logical(target, 5)
    owner_slab = lax.shift_right_logical(owner, cols.bit_length() - 1)
    away_col = owner - owner_slab * cols - lax.axis_index("col")
    away_col = jnp.where(away_col < 0, away_col + cols, away_col)
    away_slab = owner_slab - lax.axis_index("slab")
    away_slab = jnp.where(away_slab < 0, away_slab + slabs, away_slab)
    place = away_col * 128 + away_slab * CAP + target - owner * CAP
    choice_ref[...] = (iota(choice_ref.shape, 0) == place).astype(F32).astype(BF16)


def choice_of(shape, before, target):
    return pl.pallas_call(
        functools.partial(choice_kernel, shape),
        out_shape=[jax.ShapeDtypeStruct((256, target.shape[1]), BF16), TOKEN],
        in_specs=[pl.BlockSpec(memory_space=pl.ANY), pl.BlockSpec(memory_space=pltpu.VMEM)],
        compiler_params=pltpu.CompilerParams(vmem_limit_bytes=ROOM),
        name="choice",
    )(before, target)


def finish_kernel(shape, n_rows, whole_ref, target_ref, tile_ref, first_ref, second_ref, *refs):
    row_refs, cross_ref, refs = refs[:n_rows], refs[n_rows], refs[n_rows + 1 :]
    drag_refs, (out_ref, bead_ref, planes, tiles, bead, sem) = refs[:-6], refs[-6:]
    depth, rows, width = whole_ref.shape[1:]

    def entering(group, k):
        at = (group * 5 + k) * depth if n_rows == 1 else k * depth
        return row_refs[group % n_rows][at : at + depth]

    copies = []

    def leave(source, target):
        copy = pltpu.make_async_copy(source, target, sem.at[len(copies)])
        copy.start()
        copies.append(copy)

    count = target_ref.shape[1]
    if len(drag_refs) == 2:
        came = arrived_drag(*drag_refs, first_ref, second_ref, 5 * rows)
        passed = row_refs[0][10 * depth : 10 * depth + 8]
        table = jnp.concatenate([one_tile(came, 0), passed], axis=1)
        total = dot_select(table, target_ref[...], NN)
    else:
        back_ref = drag_refs[0]

        def group_share(k, total):
            got = [back_ref[k * GROUP + r] for r in range(GROUP)]
            slots = jnp.concatenate([t[:, 0:CAP] for t in got], axis=1)
            first = k * (GROUP * CAP)
            choose = (iota((GROUP * CAP, count), 0) + first == target_ref[...]).astype(F32)
            return total + dot_select(slots, choose.astype(BF16), NN)

        total = lax.fori_loop(
            0, back_ref.shape[0] // GROUP, group_share, jnp.zeros((8, count), F32)
        )
    bead[...] = total[0:3]

    for group in range(2):
        z = 0 if group == 0 else depth - 1
        for k, i in enumerate(ENTER[2][group]):
            value = entered_z(first_ref, second_ref, group, slice(k * rows, (k + 1) * rows))
            if STEP[i, 1] != 0:
                side = 0 if STEP[i, 1] == 1 else 1
                y = 0 if side == 0 else rows - 1
                row = entering(side, ENTER[1][side].index(i))[z : z + 1]
                value = jnp.where(
                    iota((rows, width), 0) == y,
                    jnp.broadcast_to(row, (rows, width)),
                    turn(value, STEP[i, 1], 0),
                )
            if STEP[i, 0] != 0:
                at = X_EDGES.index(i) * rows
                value = patch_x(value, i, cross_ref[at : at + rows])
            n = group * 5 + k
            planes[n] = value
            leave(planes.at[n], out_ref.at[i, z])
    leave(bead, bead_ref)
    for group in range(2):
        first = 0 if group == 0 else rows - 8
        for k, i in enumerate(ENTER[1][group]):
            n = group * 5 + k
            step = int(STEP[i, 2])
            tiles[n, 1 + step : 1 + step + depth] = tile_ref[n]
            tiles[n, 1 : 1 + depth, 0 if group == 0 else 7, :] = entering(group, k)
            low, high = max(step, 0), min(depth + step, depth)
            leave(tiles.at[n, 1 + low : 1 + high], out_ref.at[i, low:high, first : first + 8])

    for copy in copies:
        copy.wait()


def finish(shape, whole, target, tiles, first, second, entered, cross, drags):
    _, depth, rows, width = whole.shape
    vmem = pl.BlockSpec(memory_space=pltpu.VMEM)
    hbm = pl.BlockSpec(memory_space=pltpu.HBM)
    args = [whole, target, tiles, first, second, *entered, cross, *drags]
    return pl.pallas_call(
        functools.partial(finish_kernel, shape, len(entered)),
        out_shape=[
            jax.ShapeDtypeStruct(whole.shape, F32),
            jax.ShapeDtypeStruct((3, target.shape[1]), F32),
        ],
        in_specs=[hbm] + [vmem] * (len(args) - 1),
        out_specs=[hbm, hbm],
        scratch_shapes=[
            pltpu.VMEM((10, rows, width), F32),
            pltpu.VMEM((10, depth + 2, 8, width), F32),
            pltpu.VMEM((3, target.shape[1]), F32),
            pltpu.SemaphoreType.DMA((21,)),
        ],
        input_output_aliases={0: 0},
        compiler_params=pltpu.CompilerParams(vmem_limit_bytes=ROOM),
        name="finish",
    )(*args)


def shards(populations, solid_mask, bead_owner, bead_base, bead_offset, bead_velocity):
    slabs, cols, pairs = shape = tuple(lax.axis_size(a) for a in ("slab", "col", "pair"))
    owners = slabs * cols
    depth, rows = populations.shape[1:3]
    single = owners == GROUP and slabs == 4
    swap = functools.partial(
        lax.all_to_all, axis_name=("slab", "col"), split_axis=0, concat_axis=0, tiled=True
    )

    target, messages = pack(owners, bead_owner, bead_base, bead_offset, bead_velocity)
    messages = swap(messages)
    *flow, columns, sides, walls = moments(populations, solid_mask)
    force, face, first, second, drag, *far, token = couple(
        shape, messages, flow, columns, populations, solid_mask
    )

    def send_pair(value):
        return send(value, shape, lambda s, c, p: (s, c, (p + 1) % pairs))

    def send_col(values):
        return [
            send(value, shape, lambda s, c, p, sign=sign: (s, (c + sign) % cols, p))
            for value, sign in zip(values, (1, -1))
        ]

    face = send_pair(face)
    first, second = send_slab(first, shape, 1), send_slab(second, shape, 0)
    if single:
        drags = [drag, send(far[0], shape, lambda s, c, p: ((s + 2) % slabs, c, p))]
    else:
        drags = []
        drag = swap(drag)
    fields = (populations, solid_mask, force)
    lower, draft, token = stream_lower(depth // 2, token, *fields, sides, walls, face)
    *leaving, cross, token = leaving_rows(depth, rows, token, draft, first, second, drags)
    entered, cross = send_col(leaving), send_pair(cross)
    if single:
        target, token = choice_of(shape, token, target)
    whole, tiles = stream_upper(token, lower, *fields, face)
    return tuple(
        finish(shape, whole, target, tiles, first, second, entered, cross, drags or [drag])
    )


def solution(mesh):
    return jax.shard_map(
        shards,
        mesh=mesh,
        in_specs=(
            P(None, ("rep", "slab"), "col", "pair"),
            P(("rep", "slab"), "col", "pair"),
            P(("rep", "slab", "col", "pair")),
            P(None, ("rep", "slab", "col", "pair")),
            P(None, ("rep", "slab", "col", "pair")),
            P(None, ("rep", "slab", "col", "pair")),
        ),
        out_specs=(
            P(None, ("rep", "slab"), "col", "pair"),
            P(None, ("rep", "slab", "col", "pair")),
        ),
        check_vma=False,
    )
```

```python
import functools

import jax
import jax.numpy as jnp
import numpy as np
from jax import lax
from jax.experimental import pallas as pl
from jax.experimental.pallas import tpu as pltpu
from jax.sharding import PartitionSpec as P

CAP = 32
GROUP = 8

STEP = np.array(
    [
        [0, 0, 0],
        [1, 0, 0],
        [-1, 0, 0],
        [0, 1, 0],
        [0, -1, 0],
        [0, 0, 1],
        [0, 0, -1],
        [1, 1, 0],
        [-1, -1, 0],
        [1, -1, 0],
        [-1, 1, 0],
        [1, 0, 1],
        [-1, 0, -1],
        [1, 0, -1],
        [-1, 0, 1],
        [0, 1, 1],
        [0, -1, -1],
        [0, 1, -1],
        [0, -1, 1],
    ],
    np.int32,
)
TAU_PLUS = 0.8
TAU_MINUS = 0.5 + (3.0 / 16.0) / (TAU_PLUS - 0.5)
KEEP_EVEN = 1.0 - 1.0 / TAU_PLUS
KEEP_ODD = 1.0 - 1.0 / TAU_MINUS
FORCE_GAIN = 1.0 - 0.5 / TAU_PLUS
DRAG_COEF = 2.0
F32 = jnp.float32
BF16 = jnp.bfloat16

ENTER = [[[i for i in range(19) if STEP[i, a] == sign] for sign in (1, -1)] for a in range(3)]
TOKEN = jax.ShapeDtypeStruct((8, 128), F32)
ROOM = 16 << 20
NT = (((1,), (1,)), ((), ()))
NN = (((1,), (0,)), ((), ()))


def iota(shape, dim):
    return lax.broadcasted_iota(jnp.int32, shape, dim)


def high_low(value):
    high = value.astype(BF16)
    return high, (value - high.astype(F32)).astype(BF16)


def dot_split(left, right, dims):
    (a, b), (c, d) = left, right
    mul = functools.partial(lax.dot_general, dimension_numbers=dims, preferred_element_type=F32)
    return mul(a, c) + (mul(a, d) + mul(b, c))


def dot_select(value, choose, dims):
    first = value.astype(BF16).astype(F32)
    rest = value - first
    second = rest.astype(BF16).astype(F32)
    stacked = jnp.concatenate([first, second, rest - second], axis=0).astype(BF16)
    got = lax.dot_general(stacked, choose, dimension_numbers=dims, preferred_element_type=F32)
    rows = value.shape[0]
    return got[0:rows] + got[rows : 2 * rows] + got[2 * rows : 3 * rows]


def density_momentum(pops):
    momentum = []
    for axis in range(3):
        plus = [pops[i] for i in range(19) if STEP[i, axis] == 1]
        minus = [pops[i] for i in range(19) if STEP[i, axis] == -1]
        momentum.append(sum(plus[1:], plus[0]) - sum(minus[1:], minus[0]))
    return sum(pops[1:], pops[0]), momentum


def along(step, vector):
    terms = None
    for axis in range(3):
        if step[axis] == 0:
            continue
        if terms is None:
            terms = vector[axis] if step[axis] == 1 else -vector[axis]
        else:
            terms = terms + vector[axis] if step[axis] == 1 else terms - vector[axis]
    return terms


def collide(pops, wall, force):
    density, momentum = density_momentum(pops)
    inverse = 1.0 / density
    carried = [m + 0.5 * f for m, f in zip(momentum, force)]
    speed = [m * inverse for m in carried]
    w = 1.0 / 36.0
    bend = [(4.5 * w / TAU_PLUS) * m + (9.0 * w * FORCE_GAIN) * f for m, f in zip(carried, force)]
    push = [(3.0 * w / TAU_MINUS) * m + (3.0 * w * FORCE_GAIN) * f for m, f in zip(carried, force)]
    drop = [(1.5 * w / TAU_PLUS) * m + (3.0 * w * FORCE_GAIN) * f for m, f in zip(carried, force)]
    rest = (w / TAU_PLUS) * density - sum(
        [u * d for u, d in zip(speed[1:], drop[1:])], speed[0] * drop[0]
    )
    out = [None] * 19
    out[0] = jnp.where(wall, pops[0], KEEP_EVEN * pops[0] + 12.0 * rest)
    for i in range(1, 19, 2):
        a, b = pops[i], pops[i + 1]
        step = STEP[i]
        even = rest + along(step, speed) * along(step, bend)
        odd = along(step, push)
        if i < 7:
            even = even + even
            odd = odd + odd
        even = (0.5 * KEEP_EVEN) * (a + b) + even
        odd = (0.5 * KEEP_ODD) * (a - b) + odd
        out[i] = jnp.where(wall, b, even + odd)
        out[i + 1] = jnp.where(wall, a, even - odd)
    return out


def turn(value, amount, axis):
    if amount == 0:
        return value
    return pltpu.roll(value, int(amount) % value.shape[axis], axis)


def send(value, shape, target):
    def flat(at):
        return (at[0] * shape[1] + at[1]) * shape[2] + at[2]

    perm = [(flat(at), flat(target(*at))) for at in np.ndindex(*shape)]
    return lax.ppermute(value, ("slab", "col", "pair"), perm)


def send_slab(value, shape, which):
    def target(s, c, p):
        return ((s + (1 if s % 2 == which else -1)) % shape[0], c, p)

    return send(value, shape, target)


def odd_slab():
    return lax.rem(lax.axis_index("slab"), 2) == 1


def rank_among(member):
    count = member.shape[1]
    earlier = (iota((count, count), 0) < iota((count, count), 1)).astype(F32).astype(BF16)
    return lax.dot_general(member.astype(BF16), earlier, NN, preferred_element_type=F32)


def patch_x(value, i, column):
    side = 0 if STEP[i, 0] == 1 else value.shape[1] - 1
    return jnp.where(iota(value.shape, 1) == side, column, value)


def x_pair(i):
    return ENTER[0][0 if STEP[i, 0] == 1 else 1].index(i)


def x_place(i):
    k = x_pair(i)
    return k // 4, (k % 4) * 32 + (1 if STEP[i, 0] == 1 else 0)


def x_arrived(face_ref):
    even = lax.rem(iota(face_ref.shape[1:], 1), 2) == 0
    return [jnp.where(even, turn(face_ref[n], -1, 1), turn(face_ref[n], 1, 1)) for n in range(2)]


def x_entering(face, k, z):
    tile = face[k // 4]
    return pltpu.roll(tile, tile.shape[1] - ((k % 4) * 32 + 2 * z + 1), 1)


def x_ends(planes):
    lane = lax.shift_right_logical(iota(planes[0].shape, 1), 1)
    tile = jnp.ones(planes[0].shape, F32)
    for z, value in enumerate(planes):
        tile = jnp.where(lane == z, pltpu.roll(value, 2 * z + 1, 1), tile)
    return tile


def pack_kernel(
    steps, owner_ref, base_ref, offset_ref, velocity_ref, target_ref, out_ref, table
):
    count = owner_ref.shape[1]
    step = 0 if steps == 1 else pl.program_id(0)
    local = owner_ref[...] - step * GROUP
    member = (iota((GROUP, count), 0) == local).astype(F32)
    rank = jnp.sum(member * rank_among(member), axis=0, keepdims=True).astype(jnp.int32)
    inside = (local >= 0) & (local < GROUP)
    target = jnp.where(inside, local * CAP + rank, -1)
    whole_target = jnp.where(inside, owner_ref[...] * CAP + rank, -1)

    if steps == 1:
        target_ref[...] = whole_target
    else:
        known = jnp.where(step == 0, -1, target_ref[...])
        target_ref[...] = jnp.maximum(known, whole_target)

    choose = (iota((GROUP * CAP, count), 0) == target).astype(F32).astype(BF16)
    table[...] = jnp.zeros_like(table)
    table[0:3] = base_ref[...].astype(F32) + 1.0
    table[8:11] = offset_ref[...]
    table[16:19] = velocity_ref[...]
    packed = dot_select(table[...], choose, NT)
    blank = jnp.zeros((8, CAP), F32)
    for r in range(GROUP):
        lanes = slice(r * CAP, (r + 1) * CAP)
        out_ref[r] = jnp.concatenate(
            [packed[0:8, lanes], packed[8:16, lanes], packed[16:24, lanes], blank], axis=1
        )


def pack(owners, owner, base, offset, velocity):
    count, steps = owner.shape[0], owners // GROUP
    args = (owner.reshape(1, count), base, offset, velocity)
    blocks = {}
    if steps > 1:
        blocks = dict(
            grid=(steps,),
            in_specs=[pl.BlockSpec(a.shape, lambda k: (0, 0)) for a in args],
            out_specs=[
                pl.BlockSpec((1, count), lambda k: (0, 0)),
                pl.BlockSpec((GROUP, 8, 128), lambda k: (k, 0, 0)),
            ],
            compiler_params=pltpu.CompilerParams(vmem_limit_bytes=48 << 20),
        )
    return pl.pallas_call(
        functools.partial(pack_kernel, steps),
        out_shape=[
            jax.ShapeDtypeStruct((1, count), jnp.int32),
            jax.ShapeDtypeStruct((owners, 8, 128), F32),
        ],
        scratch_shapes=[pltpu.VMEM((24, count), F32)],
        name="pack",
        **blocks,
    )(*args)


def moments_kernel(
    pops_ref, solid_ref, high_ref, low_ref, column_ref, side_ref, wall_ref, held, held_solid, flow, sem
):
    depth, rows, width = pops_ref.shape[1:]
    chunks = 4
    span = depth // chunks
    copies = [pltpu.make_async_copy(solid_ref, held_solid, sem.at[chunks])]
    for k in range(chunks):
        part = pl.ds(k * span, span)
        copies.append(
            pltpu.make_async_copy(pops_ref.at[:, part], held.at[:, part], sem.at[k])
        )
    for copy in copies:
        copy.start()

    def plane(z, carry):
        pops = [held[i, z] for i in range(19)]
        density, momentum = density_momentum(pops)
        inverse = 1.0 / density
        for axis in range(3):
            flow[axis, pl.ds(pl.multiple_of(z * rows, rows), rows)] = momentum[axis] * inverse
        return carry

    for k in range(chunks):
        copies[1 + k].wait()
        lax.fori_loop(k * span, (k + 1) * span, plane, 0, unroll=2)
    copies[0].wait()
    for axis in range(3):
        at = slice(axis * width, (axis + 1) * width)
        high_ref[at], low_ref[at] = high_low(flow[axis].T)
    for i in range(19):
        column_ref[i] = x_ends([held[i, z] for z in range(depth)])
        side_ref[i, 0] = held[i, :, 0, :]
        side_ref[i, 1] = held[i, :, rows - 1, :]
    wall_ref[0] = held_solid[:, 0, :]
    wall_ref[1] = held_solid[:, rows - 1, :]
    column_ref[19] = x_ends([held_solid[z].astype(F32) for z in range(depth)])


def moments(pops, solid):
    _, depth, rows, width = pops.shape
    hbm = pl.BlockSpec(memory_space=pltpu.HBM)
    return pl.pallas_call(
        moments_kernel,
        out_shape=[
            jax.ShapeDtypeStruct((3 * width, depth * rows), BF16),
            jax.ShapeDtypeStruct((3 * width, depth * rows), BF16),
            jax.ShapeDtypeStruct((20, rows, 128), F32),
            jax.ShapeDtypeStruct((19, 2, depth, width), F32),
            jax.ShapeDtypeStruct((2, depth, width), jnp.int32),
        ],
        in_specs=[hbm, hbm],
        scratch_shapes=[
            pltpu.VMEM(pops.shape, F32),
            pltpu.VMEM(solid.shape, jnp.int32),
            pltpu.VMEM((3, depth * rows, width), F32),
            pltpu.SemaphoreType.DMA((5,)),
        ],
        compiler_params=pltpu.CompilerParams(vmem_limit_bytes=54000000),
        cost_estimate=pl.CostEstimate(flops=3000000, bytes_accessed=4000000, transcendentals=0),
        name="moments",
    )(pops, solid)


def unpack(tiles):
    return [
        jnp.concatenate([t[:, g * CAP : (g + 1) * CAP] for t in tiles], axis=1) for g in range(3)
    ]


def couple_group(base, part, velocity, flow, depth, rows, width):
    slots = GROUP * CAP
    start = base.astype(jnp.int32) - 1

    def hat(axis, length):
        cell = iota((length, slots), 0)
        low, share = start[axis : axis + 1], part[axis : axis + 1]
        return jnp.where(cell == low, 1.0 - share, 0.0) + jnp.where(cell == low + 1, share, 0.0)

    hat_x, hat_y, hat_z = hat(0, width), hat(1, rows), hat(2, depth)
    weight = high_low((hat_z[:, None, :] * hat_y[None, :, :]).reshape(depth * rows, slots))
    across = dot_split(flow, weight, NN)
    drag = []
    for d in range(3):
        sampled = jnp.sum(across[d * width : (d + 1) * width] * hat_x, axis=0, keepdims=True)
        drag.append(DRAG_COEF * (sampled - velocity[d : d + 1]))
    spread = jnp.concatenate([hat_x * (-drag[d]) for d in range(3)], axis=0)
    return drag, dot_split(weight, high_low(spread), NT)


def couple_kernel(shape, n_drags, beads_ref, high_ref, low_ref, *refs):
    slabs, cols, _ = shape
    column_ref, pops_ref, solid_ref, force_ref, face_ref, first_ref, second_ref, *refs = refs
    drag_refs, token_ref = refs[:-1], refs[-1]
    token_ref[...] = jnp.zeros_like(token_ref)
    depth, rows, width = pops_ref.shape[1:]
    flow = (high_ref[...], low_ref[...])

    def grid(force):
        return [
            force[:, d * width : (d + 1) * width].reshape(depth, rows, width) for d in range(3)
        ]

    hollow = jnp.zeros((5, GROUP * CAP), F32)

    if n_drags == 2:
        slab, col = lax.axis_index("slab"), lax.axis_index("col")
        got = []
        for r in range(GROUP):
            there = [a - b for a, b in zip((slab, col), divmod(r, cols))]
            there = [jnp.where(a < 0, a + n, a) for a, n in zip(there, (slabs, cols))]
            got.append(beads_ref[there[0] * cols + there[1]])
        drag, force = couple_group(*unpack(got), flow, depth, rows, width)
        for d, value in enumerate(grid(force)):
            force_ref[d] = value
        stacked = jnp.concatenate(drag + [hollow], axis=0)
        lanes = cols * CAP
        blank = jnp.zeros((8, 128 - lanes), F32)
        for dz in range(slabs):
            tile = jnp.concatenate([stacked[:, dz * lanes : (dz + 1) * lanes], blank], axis=1)
            drag_refs[0][dz] = tile
            if dz == 2:
                drag_refs[1][...] = tile
            if dz == 1:
                down = tile
        up = tile
    else:
        force_ref[...] = jnp.zeros_like(force_ref)
        blank = jnp.zeros((8, 128 - CAP), F32)

        def group(k, carry):
            got = [beads_ref[k * GROUP + r] for r in range(GROUP)]
            drag, force = couple_group(*unpack(got), flow, depth, rows, width)
            for d, value in enumerate(grid(force)):
                force_ref[d] += value
            stacked = jnp.concatenate(drag + [hollow], axis=0)
            for r in range(GROUP):
                drag_refs[0][k * GROUP + r] = jnp.concatenate(
                    [stacked[:, r * CAP : (r + 1) * CAP], blank], axis=1
                )
            return carry

        lax.fori_loop(0, beads_ref.shape[0] // GROUP, group, 0)

    force = [x_ends([force_ref[d, z] for z in range(depth)]) for d in range(3)]
    out = collide([column_ref[i] for i in range(19)], column_ref[19] == 1.0, force)
    high = lax.rem(iota((rows, 128), 1), 2) == 0
    ends = [jnp.where(high, out[i], out[j])[:, 0:32] for i, j in zip(*ENTER[0])]
    face_ref[0] = jnp.concatenate(ends[0:4], axis=1)
    face_ref[1] = jnp.concatenate([ends[4], jnp.zeros((rows, 96), F32)], axis=1)
    odd = odd_slab()
    leaving = []
    for group, z in ((0, depth - 1), (1, 0)):
        out = collide(
            [pops_ref[i, z] for i in range(19)],
            solid_ref[z] == 1,
            [force_ref[d, z] for d in range(3)],
        )
        leaving.append([turn(out[i], STEP[i, 0], 1) for i in ENTER[2][group]])
    if n_drags == 2:
        leaving[0].append(up)
        leaving[1].append(down)
    row = 0
    for a, b in zip(*leaving):
        at = slice(row, row + a.shape[0])
        first_ref[at] = jnp.where(odd, a, b)
        second_ref[at] = jnp.where(odd, b, a)
        row += a.shape[0]


def couple(shape, beads, flow, columns, pops, solid):
    _, depth, rows, width = pops.shape
    single = beads.shape[0] == GROUP
    tile = jax.ShapeDtypeStruct((8, 128), F32)
    drags = [jax.ShapeDtypeStruct((shape[0], 8, 128), F32), tile] if single else [beads]
    message = jax.ShapeDtypeStruct((5 * rows + (8 if single else 0), width), F32)
    return pl.pallas_call(
        functools.partial(couple_kernel, shape, len(drags)),
        out_shape=[
            jax.ShapeDtypeStruct((3, depth, rows, width), F32),
            jax.ShapeDtypeStruct((2, rows, 128), F32),
            message,
            message,
        ]
        + [jax.ShapeDtypeStruct(d.shape, F32) for d in drags]
        + [TOKEN],
        compiler_params=pltpu.CompilerParams(vmem_limit_bytes=ROOM),
        name="couple",
    )(beads, *flow, columns, pops, solid)


def entered_z(first_ref, second_ref, side, rows):
    odd = odd_slab() if side == 0 else jnp.logical_not(odd_slab())
    return jnp.where(odd, second_ref[rows], first_ref[rows])


X_EDGES = [i for side in range(2) for i in ENTER[2][side] if STEP[i, 0] != 0]


def rows_kernel(depth, rows, before_ref, draft_ref, first_ref, second_ref, *refs):
    refs, (cross_ref, token_ref) = refs[:-2], refs[-2:]
    token_ref[...] = jnp.zeros_like(token_ref)
    outs = refs[-1:] if len(refs) == 3 else refs
    for group in range(2):
        out_ref = outs[0] if len(outs) == 1 else outs[group]
        base = group * 5 * depth if len(outs) == 1 else 0
        y = rows - 1 if group == 0 else 0
        out_ref[base : base + 5 * depth] = draft_ref[group * 5 * depth : (group + 1) * 5 * depth]
        for k, i in enumerate(ENTER[1][group]):
            at = base + k * depth
            if STEP[i, 2] != 0:
                side = 0 if STEP[i, 2] == 1 else 1
                z = 0 if side == 0 else depth - 1
                row = ENTER[2][side].index(i) * rows + y
                out_ref[at + z : at + z + 1] = entered_z(
                    first_ref, second_ref, side, slice(row, row + 1)
                )
    if len(refs) == 3:
        own_ref, far_ref, out_ref = refs
        came = arrived_drag(own_ref, far_ref, first_ref, second_ref, 5 * rows)
        out_ref[10 * depth : 10 * depth + 8] = one_tile(came, 1)
    for k, i in enumerate(X_EDGES):
        side = 0 if STEP[i, 2] == 1 else 1
        at = ENTER[2][side].index(i) * rows
        cross_ref[k * rows : (k + 1) * rows] = entered_z(
            first_ref, second_ref, side, slice(at, at + rows)
        )


def arrived_drag(own_ref, far_ref, first_ref, second_ref, tail):
    at = slice(tail, tail + 8)
    up, down = [entered_z(first_ref, second_ref, side, at) for side in range(2)]
    return [own_ref[0], down, far_ref[...], up]


def one_tile(tiles, col):
    return jnp.concatenate([t[:, col * CAP : (col + 1) * CAP] for t in tiles], axis=1)


def leaving_rows(depth, rows, before, draft, first, second, drags):
    width = draft.shape[1]
    if drags:
        sizes = [10 * depth + 8]
    else:
        sizes = [5 * depth] * 2
    args = (draft, first, second, *drags)
    return pl.pallas_call(
        functools.partial(rows_kernel, depth, rows),
        out_shape=[jax.ShapeDtypeStruct((n, width), F32) for n in sizes + [4 * rows]] + [TOKEN],
        in_specs=[pl.BlockSpec(memory_space=pl.ANY)]
        + [pl.BlockSpec(memory_space=pltpu.VMEM)] * len(args),
        compiler_params=pltpu.CompilerParams(vmem_limit_bytes=ROOM),
        name="rows",
    )(before, *args)


def runs(members):
    found = []
    for i in members:
        if found and found[-1][1] == i and STEP[i, 2] == STEP[i - 1, 2]:
            found[-1] = (found[-1][0], i + 1)
        else:
            found.append((i, i + 1))
    return found


def stream_planes(low, high, faces, pops_ref, solid_ref, force_ref, held):
    def plane(z, faces):
        out = collide(
            [pops_ref[i, z] for i in range(19)],
            solid_ref[z] == 1,
            [force_ref[d, z] for d in range(3)],
        )
        for i in range(19):
            value = turn(out[i], STEP[i, 0], 1)
            if STEP[i, 0] != 0:
                value = patch_x(value, i, faces[x_pair(i)])
            held[i, z] = turn(value, STEP[i, 1], 0)
        return tuple(pltpu.roll(f, 126, 1) for f in faces)

    return lax.fori_loop(low, high, plane, faces, unroll=2)


def lower_kernel(
    before_ref, pops_ref, solid_ref, force_ref, side_ref, wall_ref, face_ref, *refs
):
    held, draft_ref, token_ref, turned = refs
    depth, rows, _ = pops_ref.shape[1:]
    token_ref[...] = jnp.zeros_like(token_ref)
    face = x_arrived(face_ref)
    for n in range(2):
        turned[n] = face[n].T
    for group in range(2):
        y = 0 if group else rows - 1
        force = [force_ref[d, :, y, :] for d in range(3)]
        out = collide([side_ref[i, 1 - group] for i in range(19)], wall_ref[1 - group] == 1, force)
        for k, i in enumerate(ENTER[1][group]):
            row = (group * 5 + k) * depth
            value = turn(out[i], STEP[i, 0], 1)
            if STEP[i, 0] != 0:
                tile, lane = x_place(i)
                column = turned[tile, pl.ds(lane, depth, stride=2), :][:, y : y + 1]
                value = patch_x(value, i, jnp.broadcast_to(column, value.shape))
            draft_ref[row : row + depth] = turn(value, STEP[i, 2], 0)
    faces = tuple(x_entering(face, k, 0) for k in range(5))
    stream_planes(0, held.shape[1], faces, pops_ref, solid_ref, force_ref, held)


def upper_kernel(
    before_ref, lower_ref, pops_ref, solid_ref, force_ref, face_ref, out_ref, tile_ref, held, sem
):
    depth, rows, width = pops_ref.shape[1:]
    half = lower_ref.shape[1]
    copies = []

    def leave(source, members, low, high):
        for a, b in runs(members):
            step = int(STEP[a, 2])
            start, stop = max(low + step, 0), min(high + step, depth)
            copy = pltpu.make_async_copy(
                source.at[a:b, start - step : stop - step],
                out_ref.at[a:b, start:stop],
                sem.at[len(copies)],
            )
            copy.start()
            copies.append(copy)

    leave(lower_ref, range(19), 0, half)
    face = x_arrived(face_ref)
    faces = tuple(x_entering(face, k, half) for k in range(5))
    marks = upper_marks(half, depth)
    for low, high in zip(marks, marks[1:]):
        faces = stream_planes(low, high, faces, pops_ref, solid_ref, force_ref, held)
        leave(held, range(19), low, high)
    for group in range(2):
        first = slice(0, 8) if group == 0 else slice(rows - 8, rows)
        for k, i in enumerate(ENTER[1][group]):
            tile_ref[group * 5 + k, 0:half] = lower_ref[i, :, first, :]
            tile_ref[group * 5 + k, half:depth] = held[i, half:depth, first, :]
    for copy in copies:
        copy.wait()


def upper_marks(half, depth):
    return list(range(half, depth - 2, 4)) + ([depth - 2] if (depth - half) % 4 else []) + [depth]


def stream_lower(half, before, pops, solid, force, sides, walls, face):
    _, depth, rows, width = pops.shape
    vmem = pl.BlockSpec(memory_space=pltpu.VMEM)
    return pl.pallas_call(
        lower_kernel,
        out_shape=[
            jax.ShapeDtypeStruct((19, half, rows, width), F32),
            jax.ShapeDtypeStruct((10 * depth, width), F32),
            TOKEN,
        ],
        in_specs=[pl.BlockSpec(memory_space=pl.ANY)] + [vmem] * 6,
        scratch_shapes=[pltpu.VMEM((2, 128, rows), F32)],
        compiler_params=pltpu.CompilerParams(vmem_limit_bytes=ROOM),
        cost_estimate=pl.CostEstimate(flops=3000000, bytes_accessed=2000000, transcendentals=0),
        name="lower",
    )(before, pops, solid, force, sides, walls, face)


def stream_upper(before, lower, pops, solid, force, face):
    _, depth, rows, width = pops.shape
    vmem = pl.BlockSpec(memory_space=pltpu.VMEM)
    return pl.pallas_call(
        upper_kernel,
        out_shape=[
            jax.ShapeDtypeStruct(pops.shape, F32),
            jax.ShapeDtypeStruct((10, depth, 8, width), F32),
        ],
        in_specs=[pl.BlockSpec(memory_space=pl.ANY)] + [vmem] * 5,
        out_specs=[pl.BlockSpec(memory_space=pltpu.HBM), vmem],
        scratch_shapes=[
            pltpu.VMEM(pops.shape, F32),
            pltpu.SemaphoreType.DMA((20 * len(upper_marks(lower.shape[1], depth)),)),
        ],
        compiler_params=pltpu.CompilerParams(vmem_limit_bytes=ROOM),
        cost_estimate=pl.CostEstimate(flops=5000000, bytes_accessed=3000000, transcendentals=0),
        name="upper",
    )(before, lower, pops, solid, force, face)


def choice_kernel(shape, before_ref, target_ref, choice_ref, token_ref):
    slabs, cols, _ = shape
    token_ref[...] = jnp.zeros_like(token_ref)
    target = target_ref[...]
    owner = lax.shift_right_logical(target, 5)
    owner_slab = lax.shift_right_logical(owner, cols.bit_length() - 1)
    away_col = owner - owner_slab * cols - lax.axis_index("col")
    away_col = jnp.where(away_col < 0, away_col + cols, away_col)
    away_slab = owner_slab - lax.axis_index("slab")
    away_slab = jnp.where(away_slab < 0, away_slab + slabs, away_slab)
    place = away_col * 128 + away_slab * CAP + target - owner * CAP
    choice_ref[...] = (iota(choice_ref.shape, 0) == place).astype(F32).astype(BF16)


def choice_of(shape, before, target):
    return pl.pallas_call(
        functools.partial(choice_kernel, shape),
        out_shape=[jax.ShapeDtypeStruct((256, target.shape[1]), BF16), TOKEN],
        in_specs=[pl.BlockSpec(memory_space=pl.ANY), pl.BlockSpec(memory_space=pltpu.VMEM)],
        compiler_params=pltpu.CompilerParams(vmem_limit_bytes=ROOM),
        name="choice",
    )(before, target)


def finish_kernel(shape, n_rows, whole_ref, target_ref, tile_ref, first_ref, second_ref, *refs):
    row_refs, cross_ref, refs = refs[:n_rows], refs[n_rows], refs[n_rows + 1 :]
    drag_refs, (out_ref, bead_ref, planes, tiles, bead, sem) = refs[:-6], refs[-6:]
    depth, rows, width = whole_ref.shape[1:]

    def entering(group, k):
        at = (group * 5 + k) * depth if n_rows == 1 else k * depth
        return row_refs[group % n_rows][at : at + depth]

    copies = []

    def leave(source, target):
        copy = pltpu.make_async_copy(source, target, sem.at[len(copies)])
        copy.start()
        copies.append(copy)

    for group in range(2):
        z = 0 if group == 0 else depth - 1
        for k, i in enumerate(ENTER[2][group]):
            value = entered_z(first_ref, second_ref, group, slice(k * rows, (k + 1) * rows))
            if STEP[i, 1] != 0:
                side = 0 if STEP[i, 1] == 1 else 1
                y = 0 if side == 0 else rows - 1
                row = entering(side, ENTER[1][side].index(i))[z : z + 1]
                value = jnp.where(
                    iota((rows, width), 0) == y,
                    jnp.broadcast_to(row, (rows, width)),
                    turn(value, STEP[i, 1], 0),
                )
            if STEP[i, 0] != 0:
                at = X_EDGES.index(i) * rows
                value = patch_x(value, i, cross_ref[at : at + rows])
            n = group * 5 + k
            planes[n] = value
            leave(planes.at[n], out_ref.at[i, z])
    for group in range(2):
        first = 0 if group == 0 else rows - 8
        for k, i in enumerate(ENTER[1][group]):
            n = group * 5 + k
            step = int(STEP[i, 2])
            tiles[n, 1 + step : 1 + step + depth] = tile_ref[n]
            tiles[n, 1 : 1 + depth, 0 if group == 0 else 7, :] = entering(group, k)
            low, high = max(step, 0), min(depth + step, depth)
            leave(tiles.at[n, 1 + low : 1 + high], out_ref.at[i, low:high, first : first + 8])

    count = target_ref.shape[1]
    if len(drag_refs) == 2:
        came = arrived_drag(*drag_refs, first_ref, second_ref, 5 * rows)
        passed = row_refs[0][10 * depth : 10 * depth + 8]
        table = jnp.concatenate([one_tile(came, 0), passed], axis=1)
        total = dot_select(table, target_ref[...], NN)
    else:
        back_ref = drag_refs[0]

        def group_share(k, total):
            got = [back_ref[k * GROUP + r] for r in range(GROUP)]
            slots = jnp.concatenate([t[:, 0:CAP] for t in got], axis=1)
            first = k * (GROUP * CAP)
            choose = (iota((GROUP * CAP, count), 0) + first == target_ref[...]).astype(F32)
            return total + dot_select(slots, choose.astype(BF16), NN)

        total = lax.fori_loop(
            0, back_ref.shape[0] // GROUP, group_share, jnp.zeros((8, count), F32)
        )
    bead[...] = total[0:3]
    leave(bead, bead_ref)
    for copy in copies:
        copy.wait()


def finish(shape, whole, target, tiles, first, second, entered, cross, drags):
    _, depth, rows, width = whole.shape
    vmem = pl.BlockSpec(memory_space=pltpu.VMEM)
    hbm = pl.BlockSpec(memory_space=pltpu.HBM)
    args = [whole, target, tiles, first, second, *entered, cross, *drags]
    return pl.pallas_call(
        functools.partial(finish_kernel, shape, len(entered)),
        out_shape=[
            jax.ShapeDtypeStruct(whole.shape, F32),
            jax.ShapeDtypeStruct((3, target.shape[1]), F32),
        ],
        in_specs=[hbm] + [vmem] * (len(args) - 1),
        out_specs=[hbm, hbm],
        scratch_shapes=[
            pltpu.VMEM((10, rows, width), F32),
            pltpu.VMEM((10, depth + 2, 8, width), F32),
            pltpu.VMEM((3, target.shape[1]), F32),
            pltpu.SemaphoreType.DMA((21,)),
        ],
        input_output_aliases={0: 0},
        compiler_params=pltpu.CompilerParams(vmem_limit_bytes=ROOM),
        name="finish",
    )(*args)


def shards(populations, solid_mask, bead_owner, bead_base, bead_offset, bead_velocity):
    slabs, cols, pairs = shape = tuple(lax.axis_size(a) for a in ("slab", "col", "pair"))
    owners = slabs * cols
    depth, rows = populations.shape[1:3]
    single = owners == GROUP and slabs == 4
    swap = functools.partial(
        lax.all_to_all, axis_name=("slab", "col"), split_axis=0, concat_axis=0, tiled=True
    )

    target, messages = pack(owners, bead_owner, bead_base, bead_offset, bead_velocity)
    messages = swap(messages)
    *flow, columns, sides, walls = moments(populations, solid_mask)
    force, face, first, second, drag, *far, token = couple(
        shape, messages, flow, columns, populations, solid_mask
    )

    def send_pair(value):
        return send(value, shape, lambda s, c, p: (s, c, (p + 1) % pairs))

    def send_col(values):
        return [
            send(value, shape, lambda s, c, p, sign=sign: (s, (c + sign) % cols, p))
            for value, sign in zip(values, (1, -1))
        ]

    face = send_pair(face)
    first, second = send_slab(first, shape, 1), send_slab(second, shape, 0)
    if single:
        drags = [drag, send(far[0], shape, lambda s, c, p: ((s + 2) % slabs, c, p))]
    else:
        drags = []
        drag = swap(drag)
    fields = (populations, solid_mask, force)
    lower, draft, token = stream_lower(depth // 2, token, *fields, sides, walls, face)
    *leaving, cross, token = leaving_rows(depth, rows, token, draft, first, second, drags)
    entered, cross = send_col(leaving), send_pair(cross)
    if single:
        target, token = choice_of(shape, token, target)
    whole, tiles = stream_upper(token, lower, *fields, face)
    return tuple(
        finish(shape, whole, target, tiles, first, second, entered, cross, drags or [drag])
    )


def solution(mesh):
    return jax.shard_map(
        shards,
        mesh=mesh,
        in_specs=(
            P(None, ("rep", "slab"), "col", "pair"),
            P(("rep", "slab"), "col", "pair"),
            P(("rep", "slab", "col", "pair")),
            P(None, ("rep", "slab", "col", "pair")),
            P(None, ("rep", "slab", "col", "pair")),
            P(None, ("rep", "slab", "col", "pair")),
        ),
        out_specs=(
            P(None, ("rep", "slab"), "col", "pair"),
            P(None, ("rep", "slab", "col", "pair")),
        ),
        check_vma=False,
    )
```

```python
import functools

import jax
import jax.numpy as jnp
import numpy as np
from jax import lax
from jax.experimental import pallas as pl
from jax.experimental.pallas import tpu as pltpu
from jax.sharding import PartitionSpec as P

CAP = 32
GROUP = 8

STEP = np.array(
    [
        [0, 0, 0],
        [1, 0, 0],
        [-1, 0, 0],
        [0, 1, 0],
        [0, -1, 0],
        [0, 0, 1],
        [0, 0, -1],
        [1, 1, 0],
        [-1, -1, 0],
        [1, -1, 0],
        [-1, 1, 0],
        [1, 0, 1],
        [-1, 0, -1],
        [1, 0, -1],
        [-1, 0, 1],
        [0, 1, 1],
        [0, -1, -1],
        [0, 1, -1],
        [0, -1, 1],
    ],
    np.int32,
)
TAU_PLUS = 0.8
TAU_MINUS = 0.5 + (3.0 / 16.0) / (TAU_PLUS - 0.5)
KEEP_EVEN = 1.0 - 1.0 / TAU_PLUS
KEEP_ODD = 1.0 - 1.0 / TAU_MINUS
FORCE_GAIN = 1.0 - 0.5 / TAU_PLUS
DRAG_COEF = 2.0
F32 = jnp.float32
BF16 = jnp.bfloat16

ENTER = [[[i for i in range(19) if STEP[i, a] == sign] for sign in (1, -1)] for a in range(3)]
TOKEN = jax.ShapeDtypeStruct((8, 128), F32)
ROOM = 16 << 20
NT = (((1,), (1,)), ((), ()))
NN = (((1,), (0,)), ((), ()))


def iota(shape, dim):
    return lax.broadcasted_iota(jnp.int32, shape, dim)


def high_low(value):
    high = value.astype(BF16)
    return high, (value - high.astype(F32)).astype(BF16)


def dot_split(left, right, dims):
    (a, b), (c, d) = left, right
    mul = functools.partial(lax.dot_general, dimension_numbers=dims, preferred_element_type=F32)
    return mul(a, c) + (mul(a, d) + mul(b, c))


def dot_select(value, choose, dims):
    first = value.astype(BF16).astype(F32)
    rest = value - first
    second = rest.astype(BF16).astype(F32)
    stacked = jnp.concatenate([first, second, rest - second], axis=0).astype(BF16)
    got = lax.dot_general(stacked, choose, dimension_numbers=dims, preferred_element_type=F32)
    rows = value.shape[0]
    return got[0:rows] + got[rows : 2 * rows] + got[2 * rows : 3 * rows]


def density_momentum(pops):
    momentum = []
    for axis in range(3):
        plus = [pops[i] for i in range(19) if STEP[i, axis] == 1]
        minus = [pops[i] for i in range(19) if STEP[i, axis] == -1]
        momentum.append(sum(plus[1:], plus[0]) - sum(minus[1:], minus[0]))
    return sum(pops[1:], pops[0]), momentum


def along(step, vector):
    terms = None
    for axis in range(3):
        if step[axis] == 0:
            continue
        if terms is None:
            terms = vector[axis] if step[axis] == 1 else -vector[axis]
        else:
            terms = terms + vector[axis] if step[axis] == 1 else terms - vector[axis]
    return terms


def collide(pops, wall, force):
    density, momentum = density_momentum(pops)
    inverse = 1.0 / density
    carried = [m + 0.5 * f for m, f in zip(momentum, force)]
    speed = [m * inverse for m in carried]
    w = 1.0 / 36.0
    bend = [(4.5 * w / TAU_PLUS) * m + (9.0 * w * FORCE_GAIN) * f for m, f in zip(carried, force)]
    push = [(3.0 * w / TAU_MINUS) * m + (3.0 * w * FORCE_GAIN) * f for m, f in zip(carried, force)]
    drop = [(1.5 * w / TAU_PLUS) * m + (3.0 * w * FORCE_GAIN) * f for m, f in zip(carried, force)]
    rest = (w / TAU_PLUS) * density - sum(
        [u * d for u, d in zip(speed[1:], drop[1:])], speed[0] * drop[0]
    )
    out = [None] * 19
    out[0] = jnp.where(wall, pops[0], KEEP_EVEN * pops[0] + 12.0 * rest)
    for i in range(1, 19, 2):
        a, b = pops[i], pops[i + 1]
        step = STEP[i]
        even = rest + along(step, speed) * along(step, bend)
        odd = along(step, push)
        if i < 7:
            even = even + even
            odd = odd + odd
        even = (0.5 * KEEP_EVEN) * (a + b) + even
        odd = (0.5 * KEEP_ODD) * (a - b) + odd
        out[i] = jnp.where(wall, b, even + odd)
        out[i + 1] = jnp.where(wall, a, even - odd)
    return out


def turn(value, amount, axis):
    if amount == 0:
        return value
    return pltpu.roll(value, int(amount) % value.shape[axis], axis)


def send(value, shape, target):
    def flat(at):
        return (at[0] * shape[1] + at[1]) * shape[2] + at[2]

    perm = [(flat(at), flat(target(*at))) for at in np.ndindex(*shape)]
    return lax.ppermute(value, ("slab", "col", "pair"), perm)


def send_slab(value, shape, which):
    def target(s, c, p):
        return ((s + (1 if s % 2 == which else -1)) % shape[0], c, p)

    return send(value, shape, target)


def odd_slab():
    return lax.rem(lax.axis_index("slab"), 2) == 1


def rank_among(member):
    count = member.shape[1]
    earlier = (iota((count, count), 0) < iota((count, count), 1)).astype(F32).astype(BF16)
    return lax.dot_general(member.astype(BF16), earlier, NN, preferred_element_type=F32)


def patch_x(value, i, column):
    side = 0 if STEP[i, 0] == 1 else value.shape[1] - 1
    return jnp.where(iota(value.shape, 1) == side, column, value)


def x_pair(i):
    return ENTER[0][0 if STEP[i, 0] == 1 else 1].index(i)


def x_place(i):
    k = x_pair(i)
    return k // 4, (k % 4) * 32 + (1 if STEP[i, 0] == 1 else 0)


def x_arrived(face_ref):
    even = lax.rem(iota(face_ref.shape[1:], 1), 2) == 0
    return [jnp.where(even, turn(face_ref[n], -1, 1), turn(face_ref[n], 1, 1)) for n in range(2)]


def x_entering(face, k, z):
    tile = face[k // 4]
    return pltpu.roll(tile, tile.shape[1] - ((k % 4) * 32 + 2 * z + 1), 1)


def x_ends(planes):
    lane = lax.shift_right_logical(iota(planes[0].shape, 1), 1)
    tile = jnp.ones(planes[0].shape, F32)
    for z, value in enumerate(planes):
        tile = jnp.where(lane == z, pltpu.roll(value, 2 * z + 1, 1), tile)
    return tile


def pack_kernel(
    steps, owner_ref, base_ref, offset_ref, velocity_ref, target_ref, out_ref, table
):
    count = owner_ref.shape[1]
    step = 0 if steps == 1 else pl.program_id(0)
    local = owner_ref[...] - step * GROUP
    member = (iota((GROUP, count), 0) == local).astype(F32)
    rank = jnp.sum(member * rank_among(member), axis=0, keepdims=True).astype(jnp.int32)
    inside = (local >= 0) & (local < GROUP)
    target = jnp.where(inside, local * CAP + rank, -1)
    whole_target = jnp.where(inside, owner_ref[...] * CAP + rank, -1)

    if steps == 1:
        target_ref[...] = whole_target
    else:
        known = jnp.where(step == 0, -1, target_ref[...])
        target_ref[...] = jnp.maximum(known, whole_target)

    choose = (iota((GROUP * CAP, count), 0) == target).astype(F32).astype(BF16)
    table[...] = jnp.zeros_like(table)
    table[0:3] = base_ref[...].astype(F32) + 1.0
    table[8:11] = offset_ref[...]
    table[16:19] = velocity_ref[...]
    packed = dot_select(table[...], choose, NT)
    blank = jnp.zeros((8, CAP), F32)
    for r in range(GROUP):
        lanes = slice(r * CAP, (r + 1) * CAP)
        out_ref[r * 8 : r * 8 + 8] = jnp.concatenate(
            [packed[0:8, lanes], packed[8:16, lanes], packed[16:24, lanes], blank], axis=1
        )


def pack(owners, owner, base, offset, velocity):
    count, steps = owner.shape[0], owners // GROUP
    args = (owner.reshape(1, count), base, offset, velocity)
    blocks = {}
    if steps > 1:
        blocks = dict(
            grid=(steps,),
            in_specs=[pl.BlockSpec(a.shape, lambda k: (0, 0)) for a in args],
            out_specs=[
                pl.BlockSpec((1, count), lambda k: (0, 0)),
                pl.BlockSpec((GROUP * 8, 128), lambda k: (k, 0)),
            ],
            compiler_params=pltpu.CompilerParams(vmem_limit_bytes=48 << 20),
        )
    target, tiles = pl.pallas_call(
        functools.partial(pack_kernel, steps),
        out_shape=[
            jax.ShapeDtypeStruct((1, count), jnp.int32),
            jax.ShapeDtypeStruct((owners * 8, 128), F32),
        ],
        scratch_shapes=[pltpu.VMEM((24, count), F32)],
        name="pack",
        **blocks,
    )(*args)
    return target, tiles.reshape(owners, 8, 128)


def moments_kernel(
    pops_ref, solid_ref, high_ref, low_ref, column_ref, side_ref, wall_ref, held, held_solid, flow, sem
):
    depth, rows, width = pops_ref.shape[1:]
    chunks = 4
    span = depth // chunks
    copies = [pltpu.make_async_copy(solid_ref, held_solid, sem.at[chunks])]
    for k in range(chunks):
        part = pl.ds(k * span, span)
        copies.append(
            pltpu.make_async_copy(pops_ref.at[:, part], held.at[:, part], sem.at[k])
        )
    for copy in copies:
        copy.start()

    def plane(z, carry):
        pops = [held[i, z] for i in range(19)]
        density, momentum = density_momentum(pops)
        inverse = 1.0 / density
        for axis in range(3):
            flow[axis, pl.ds(pl.multiple_of(z * rows, rows), rows)] = momentum[axis] * inverse
        return carry

    for k in range(chunks):
        copies[1 + k].wait()
        lax.fori_loop(k * span, (k + 1) * span, plane, 0, unroll=2)
    copies[0].wait()
    for axis in range(3):
        at = slice(axis * width, (axis + 1) * width)
        high_ref[at], low_ref[at] = high_low(flow[axis].T)
    for i in range(19):
        column_ref[i] = x_ends([held[i, z] for z in range(depth)])
        side_ref[i, 0] = held[i, :, 0, :]
        side_ref[i, 1] = held[i, :, rows - 1, :]
    wall_ref[0] = held_solid[:, 0, :]
    wall_ref[1] = held_solid[:, rows - 1, :]
    column_ref[19] = x_ends([held_solid[z].astype(F32) for z in range(depth)])


def moments(pops, solid):
    _, depth, rows, width = pops.shape
    hbm = pl.BlockSpec(memory_space=pltpu.HBM)
    return pl.pallas_call(
        moments_kernel,
        out_shape=[
            jax.ShapeDtypeStruct((3 * width, depth * rows), BF16),
            jax.ShapeDtypeStruct((3 * width, depth * rows), BF16),
            jax.ShapeDtypeStruct((20, rows, 128), F32),
            jax.ShapeDtypeStruct((19, 2, depth, width), F32),
            jax.ShapeDtypeStruct((2, depth, width), jnp.int32),
        ],
        in_specs=[hbm, hbm],
        scratch_shapes=[
            pltpu.VMEM(pops.shape, F32),
            pltpu.VMEM(solid.shape, jnp.int32),
            pltpu.VMEM((3, depth * rows, width), F32),
            pltpu.SemaphoreType.DMA((5,)),
        ],
        compiler_params=pltpu.CompilerParams(vmem_limit_bytes=54000000),
        cost_estimate=pl.CostEstimate(flops=3000000, bytes_accessed=4000000, transcendentals=0),
        name="moments",
    )(pops, solid)


def unpack(tiles):
    return [
        jnp.concatenate([t[:, g * CAP : (g + 1) * CAP] for t in tiles], axis=1) for g in range(3)
    ]


def couple_group(base, part, velocity, flow, depth, rows, width):
    slots = GROUP * CAP
    start = base.astype(jnp.int32) - 1

    def hat(axis, length):
        cell = iota((length, slots), 0)
        low, share = start[axis : axis + 1], part[axis : axis + 1]
        return jnp.where(cell == low, 1.0 - share, 0.0) + jnp.where(cell == low + 1, share, 0.0)

    hat_x, hat_y, hat_z = hat(0, width), hat(1, rows), hat(2, depth)
    weight = high_low((hat_z[:, None, :] * hat_y[None, :, :]).reshape(depth * rows, slots))
    across = dot_split(flow, weight, NN)
    drag = []
    for d in range(3):
        sampled = jnp.sum(across[d * width : (d + 1) * width] * hat_x, axis=0, keepdims=True)
        drag.append(DRAG_COEF * (sampled - velocity[d : d + 1]))
    spread = jnp.concatenate([hat_x * (-drag[d]) for d in range(3)], axis=0)
    return drag, dot_split(weight, high_low(spread), NT)


def couple_kernel(shape, n_drags, beads_ref, high_ref, low_ref, *refs):
    slabs, cols, _ = shape
    column_ref, pops_ref, solid_ref, force_ref, face_ref, first_ref, second_ref, *refs = refs
    drag_refs, token_ref = refs[:-1], refs[-1]
    token_ref[...] = jnp.zeros_like(token_ref)
    depth, rows, width = pops_ref.shape[1:]
    flow = (high_ref[...], low_ref[...])

    def grid(force):
        return [
            force[:, d * width : (d + 1) * width].reshape(depth, rows, width) for d in range(3)
        ]

    hollow = jnp.zeros((5, GROUP * CAP), F32)

    if n_drags == 2:
        slab, col = lax.axis_index("slab"), lax.axis_index("col")
        got = []
        for r in range(GROUP):
            there = [a - b for a, b in zip((slab, col), divmod(r, cols))]
            there = [jnp.where(a < 0, a + n, a) for a, n in zip(there, (slabs, cols))]
            got.append(beads_ref[there[0] * cols + there[1]])
        drag, force = couple_group(*unpack(got), flow, depth, rows, width)
        for d, value in enumerate(grid(force)):
            force_ref[d] = value
        stacked = jnp.concatenate(drag + [hollow], axis=0)
        lanes = cols * CAP
        blank = jnp.zeros((8, 128 - lanes), F32)
        for dz in range(slabs):
            tile = jnp.concatenate([stacked[:, dz * lanes : (dz + 1) * lanes], blank], axis=1)
            drag_refs[0][dz] = tile
            if dz == 2:
                drag_refs[1][...] = tile
            if dz == 1:
                down = tile
        up = tile
    else:
        force_ref[...] = jnp.zeros_like(force_ref)
        blank = jnp.zeros((8, 128 - CAP), F32)

        def group(k, carry):
            got = [beads_ref[k * GROUP + r] for r in range(GROUP)]
            drag, force = couple_group(*unpack(got), flow, depth, rows, width)
            for d, value in enumerate(grid(force)):
                force_ref[d] += value
            stacked = jnp.concatenate(drag + [hollow], axis=0)
            for r in range(GROUP):
                drag_refs[0][k * GROUP + r] = jnp.concatenate(
                    [stacked[:, r * CAP : (r + 1) * CAP], blank], axis=1
                )
            return carry

        lax.fori_loop(0, beads_ref.shape[0] // GROUP, group, 0)

    force = [x_ends([force_ref[d, z] for z in range(depth)]) for d in range(3)]
    out = collide([column_ref[i] for i in range(19)], column_ref[19] == 1.0, force)
    high = lax.rem(iota((rows, 128), 1), 2) == 0
    ends = [jnp.where(high, out[i], out[j])[:, 0:32] for i, j in zip(*ENTER[0])]
    face_ref[0] = jnp.concatenate(ends[0:4], axis=1)
    face_ref[1] = jnp.concatenate([ends[4], jnp.zeros((rows, 96), F32)], axis=1)
    odd = odd_slab()
    leaving = []
    for group, z in ((0, depth - 1), (1, 0)):
        out = collide(
            [pops_ref[i, z] for i in range(19)],
            solid_ref[z] == 1,
            [force_ref[d, z] for d in range(3)],
        )
        leaving.append([turn(out[i], STEP[i, 0], 1) for i in ENTER[2][group]])
    if n_drags == 2:
        leaving[0].append(up)
        leaving[1].append(down)
    row = 0
    for a, b in zip(*leaving):
        at = slice(row, row + a.shape[0])
        first_ref[at] = jnp.where(odd, a, b)
        second_ref[at] = jnp.where(odd, b, a)
        row += a.shape[0]


def couple(shape, beads, flow, columns, pops, solid):
    _, depth, rows, width = pops.shape
    single = beads.shape[0] == GROUP
    tile = jax.ShapeDtypeStruct((8, 128), F32)
    drags = [jax.ShapeDtypeStruct((shape[0], 8, 128), F32), tile] if single else [beads]
    message = jax.ShapeDtypeStruct((5 * rows + (8 if single else 0), width), F32)
    return pl.pallas_call(
        functools.partial(couple_kernel, shape, len(drags)),
        out_shape=[
            jax.ShapeDtypeStruct((3, depth, rows, width), F32),
            jax.ShapeDtypeStruct((2, rows, 128), F32),
            message,
            message,
        ]
        + [jax.ShapeDtypeStruct(d.shape, F32) for d in drags]
        + [TOKEN],
        compiler_params=pltpu.CompilerParams(vmem_limit_bytes=ROOM),
        name="couple",
    )(beads, *flow, columns, pops, solid)


def entered_z(first_ref, second_ref, side, rows):
    odd = odd_slab() if side == 0 else jnp.logical_not(odd_slab())
    return jnp.where(odd, second_ref[rows], first_ref[rows])


X_EDGES = [i for side in range(2) for i in ENTER[2][side] if STEP[i, 0] != 0]


def rows_kernel(depth, rows, before_ref, draft_ref, first_ref, second_ref, *refs):
    refs, (cross_ref, token_ref) = refs[:-2], refs[-2:]
    token_ref[...] = jnp.zeros_like(token_ref)
    outs = refs[-1:] if len(refs) == 3 else refs
    for group in range(2):
        out_ref = outs[0] if len(outs) == 1 else outs[group]
        base = group * 5 * depth if len(outs) == 1 else 0
        y = rows - 1 if group == 0 else 0
        out_ref[base : base + 5 * depth] = draft_ref[group * 5 * depth : (group + 1) * 5 * depth]
        for k, i in enumerate(ENTER[1][group]):
            at = base + k * depth
            if STEP[i, 2] != 0:
                side = 0 if STEP[i, 2] == 1 else 1
                z = 0 if side == 0 else depth - 1
                row = ENTER[2][side].index(i) * rows + y
                out_ref[at + z : at + z + 1] = entered_z(
                    first_ref, second_ref, side, slice(row, row + 1)
                )
    if len(refs) == 3:
        own_ref, far_ref, out_ref = refs
        came = arrived_drag(own_ref, far_ref, first_ref, second_ref, 5 * rows)
        out_ref[10 * depth : 10 * depth + 8] = one_tile(came, 1)
    for k, i in enumerate(X_EDGES):
        side = 0 if STEP[i, 2] == 1 else 1
        at = ENTER[2][side].index(i) * rows
        cross_ref[k * rows : (k + 1) * rows] = entered_z(
            first_ref, second_ref, side, slice(at, at + rows)
        )


def arrived_drag(own_ref, far_ref, first_ref, second_ref, tail):
    at = slice(tail, tail + 8)
    up, down = [entered_z(first_ref, second_ref, side, at) for side in range(2)]
    return [own_ref[0], down, far_ref[...], up]


def one_tile(tiles, col):
    return jnp.concatenate([t[:, col * CAP : (col + 1) * CAP] for t in tiles], axis=1)


def leaving_rows(depth, rows, before, draft, first, second, drags):
    width = draft.shape[1]
    if drags:
        sizes = [10 * depth + 8]
    else:
        sizes = [5 * depth] * 2
    args = (draft, first, second, *drags)
    return pl.pallas_call(
        functools.partial(rows_kernel, depth, rows),
        out_shape=[jax.ShapeDtypeStruct((n, width), F32) for n in sizes + [4 * rows]] + [TOKEN],
        in_specs=[pl.BlockSpec(memory_space=pl.ANY)]
        + [pl.BlockSpec(memory_space=pltpu.VMEM)] * len(args),
        compiler_params=pltpu.CompilerParams(vmem_limit_bytes=ROOM),
        name="rows",
    )(before, *args)


def runs(members):
    found = []
    for i in members:
        if found and found[-1][1] == i and STEP[i, 2] == STEP[i - 1, 2]:
            found[-1] = (found[-1][0], i + 1)
        else:
            found.append((i, i + 1))
    return found


def stream_planes(low, high, faces, pops_ref, solid_ref, force_ref, held):
    def plane(z, faces):
        out = collide(
            [pops_ref[i, z] for i in range(19)],
            solid_ref[z] == 1,
            [force_ref[d, z] for d in range(3)],
        )
        for i in range(19):
            value = turn(out[i], STEP[i, 0], 1)
            if STEP[i, 0] != 0:
                value = patch_x(value, i, faces[x_pair(i)])
            held[i, z] = turn(value, STEP[i, 1], 0)
        return tuple(pltpu.roll(f, 126, 1) for f in faces)

    return lax.fori_loop(low, high, plane, faces, unroll=2)


def lower_kernel(
    before_ref, pops_ref, solid_ref, force_ref, side_ref, wall_ref, face_ref, *refs
):
    held, draft_ref, token_ref, turned = refs
    depth, rows, _ = pops_ref.shape[1:]
    token_ref[...] = jnp.zeros_like(token_ref)
    face = x_arrived(face_ref)
    for n in range(2):
        turned[n] = face[n].T
    for group in range(2):
        y = 0 if group else rows - 1
        force = [force_ref[d, :, y, :] for d in range(3)]
        out = collide([side_ref[i, 1 - group] for i in range(19)], wall_ref[1 - group] == 1, force)
        for k, i in enumerate(ENTER[1][group]):
            row = (group * 5 + k) * depth
            value = turn(out[i], STEP[i, 0], 1)
            if STEP[i, 0] != 0:
                tile, lane = x_place(i)
                column = turned[tile, pl.ds(lane, depth, stride=2), :][:, y : y + 1]
                value = patch_x(value, i, jnp.broadcast_to(column, value.shape))
            draft_ref[row : row + depth] = turn(value, STEP[i, 2], 0)
    faces = tuple(x_entering(face, k, 0) for k in range(5))
    stream_planes(0, held.shape[1], faces, pops_ref, solid_ref, force_ref, held)


def upper_kernel(
    before_ref, lower_ref, pops_ref, solid_ref, force_ref, face_ref, out_ref, tile_ref, held, sem
):
    depth, rows, width = pops_ref.shape[1:]
    half = lower_ref.shape[1]
    copies = []

    def leave(source, members, low, high):
        for a, b in runs(members):
            step = int(STEP[a, 2])
            start, stop = max(low + step, 0), min(high + step, depth)
            copy = pltpu.make_async_copy(
                source.at[a:b, start - step : stop - step],
                out_ref.at[a:b, start:stop],
                sem.at[len(copies)],
            )
            copy.start()
            copies.append(copy)

    leave(lower_ref, range(19), 0, half)
    face = x_arrived(face_ref)
    faces = tuple(x_entering(face, k, half) for k in range(5))
    marks = upper_marks(half, depth)
    for low, high in zip(marks, marks[1:]):
        faces = stream_planes(low, high, faces, pops_ref, solid_ref, force_ref, held)
        leave(held, range(19), low, high)
    for group in range(2):
        first = slice(0, 8) if group == 0 else slice(rows - 8, rows)
        for k, i in enumerate(ENTER[1][group]):
            tile_ref[group * 5 + k, 0:half] = lower_ref[i, :, first, :]
            tile_ref[group * 5 + k, half:depth] = held[i, half:depth, first, :]
    for copy in copies:
        copy.wait()


def upper_marks(half, depth):
    return list(range(half, depth - 2, 4)) + ([depth - 2] if (depth - half) % 4 else []) + [depth]


def stream_lower(half, before, pops, solid, force, sides, walls, face):
    _, depth, rows, width = pops.shape
    vmem = pl.BlockSpec(memory_space=pltpu.VMEM)
    return pl.pallas_call(
        lower_kernel,
        out_shape=[
            jax.ShapeDtypeStruct((19, half, rows, width), F32),
            jax.ShapeDtypeStruct((10 * depth, width), F32),
            TOKEN,
        ],
        in_specs=[pl.BlockSpec(memory_space=pl.ANY)] + [vmem] * 6,
        scratch_shapes=[pltpu.VMEM((2, 128, rows), F32)],
        compiler_params=pltpu.CompilerParams(vmem_limit_bytes=ROOM),
        cost_estimate=pl.CostEstimate(flops=3000000, bytes_accessed=2000000, transcendentals=0),
        name="lower",
    )(before, pops, solid, force, sides, walls, face)


def stream_upper(before, lower, pops, solid, force, face):
    _, depth, rows, width = pops.shape
    vmem = pl.BlockSpec(memory_space=pltpu.VMEM)
    return pl.pallas_call(
        upper_kernel,
        out_shape=[
            jax.ShapeDtypeStruct(pops.shape, F32),
            jax.ShapeDtypeStruct((10, depth, 8, width), F32),
        ],
        in_specs=[pl.BlockSpec(memory_space=pl.ANY)] + [vmem] * 5,
        out_specs=[pl.BlockSpec(memory_space=pltpu.HBM), vmem],
        scratch_shapes=[
            pltpu.VMEM(pops.shape, F32),
            pltpu.SemaphoreType.DMA((20 * len(upper_marks(lower.shape[1], depth)),)),
        ],
        compiler_params=pltpu.CompilerParams(vmem_limit_bytes=ROOM),
        cost_estimate=pl.CostEstimate(flops=5000000, bytes_accessed=3000000, transcendentals=0),
        name="upper",
    )(before, lower, pops, solid, force, face)


def choice_kernel(shape, before_ref, target_ref, choice_ref, token_ref):
    slabs, cols, _ = shape
    token_ref[...] = jnp.zeros_like(token_ref)
    target = target_ref[...]
    owner = lax.shift_right_logical(target, 5)
    owner_slab = lax.shift_right_logical(owner, cols.bit_length() - 1)
    away_col = owner - owner_slab * cols - lax.axis_index("col")
    away_col = jnp.where(away_col < 0, away_col + cols, away_col)
    away_slab = owner_slab - lax.axis_index("slab")
    away_slab = jnp.where(away_slab < 0, away_slab + slabs, away_slab)
    place = away_col * 128 + away_slab * CAP + target - owner * CAP
    choice_ref[...] = (iota(choice_ref.shape, 0) == place).astype(F32).astype(BF16)


def choice_of(shape, before, target):
    return pl.pallas_call(
        functools.partial(choice_kernel, shape),
        out_shape=[jax.ShapeDtypeStruct((256, target.shape[1]), BF16), TOKEN],
        in_specs=[pl.BlockSpec(memory_space=pl.ANY), pl.BlockSpec(memory_space=pltpu.VMEM)],
        compiler_params=pltpu.CompilerParams(vmem_limit_bytes=ROOM),
        name="choice",
    )(before, target)


def finish_kernel(shape, n_rows, whole_ref, target_ref, tile_ref, first_ref, second_ref, *refs):
    row_refs, cross_ref, refs = refs[:n_rows], refs[n_rows], refs[n_rows + 1 :]
    drag_refs, (out_ref, bead_ref, planes, tiles, bead, sem) = refs[:-6], refs[-6:]
    depth, rows, width = whole_ref.shape[1:]

    def entering(group, k):
        at = (group * 5 + k) * depth if n_rows == 1 else k * depth
        return row_refs[group % n_rows][at : at + depth]

    copies = []

    def leave(source, target):
        copy = pltpu.make_async_copy(source, target, sem.at[len(copies)])
        copy.start()
        copies.append(copy)

    for group in range(2):
        z = 0 if group == 0 else depth - 1
        for k, i in enumerate(ENTER[2][group]):
            value = entered_z(first_ref, second_ref, group, slice(k * rows, (k + 1) * rows))
            if STEP[i, 1] != 0:
                side = 0 if STEP[i, 1] == 1 else 1
                y = 0 if side == 0 else rows - 1
                row = entering(side, ENTER[1][side].index(i))[z : z + 1]
                value = jnp.where(
                    iota((rows, width), 0) == y,
                    jnp.broadcast_to(row, (rows, width)),
                    turn(value, STEP[i, 1], 0),
                )
            if STEP[i, 0] != 0:
                at = X_EDGES.index(i) * rows
                value = patch_x(value, i, cross_ref[at : at + rows])
            n = group * 5 + k
            planes[n] = value
            leave(planes.at[n], out_ref.at[i, z])
    for group in range(2):
        first = 0 if group == 0 else rows - 8
        for k, i in enumerate(ENTER[1][group]):
            n = group * 5 + k
            step = int(STEP[i, 2])
            tiles[n, 1 + step : 1 + step + depth] = tile_ref[n]
            tiles[n, 1 : 1 + depth, 0 if group == 0 else 7, :] = entering(group, k)
            low, high = max(step, 0), min(depth + step, depth)
            leave(tiles.at[n, 1 + low : 1 + high], out_ref.at[i, low:high, first : first + 8])

    count = target_ref.shape[1]
    if len(drag_refs) == 2:
        came = arrived_drag(*drag_refs, first_ref, second_ref, 5 * rows)
        passed = row_refs[0][10 * depth : 10 * depth + 8]
        table = jnp.concatenate([one_tile(came, 0), passed], axis=1)
        total = dot_select(table, target_ref[...], NN)
    else:
        back_ref = drag_refs[0]

        def group_share(k, total):
            got = [back_ref[k * GROUP + r] for r in range(GROUP)]
            slots = jnp.concatenate([t[:, 0:CAP] for t in got], axis=1)
            first = k * (GROUP * CAP)
            choose = (iota((GROUP * CAP, count), 0) + first == target_ref[...]).astype(F32)
            return total + dot_select(slots, choose.astype(BF16), NN)

        total = lax.fori_loop(
            0, back_ref.shape[0] // GROUP, group_share, jnp.zeros((8, count), F32)
        )
    bead[...] = total[0:3]
    leave(bead, bead_ref)
    for copy in copies:
        copy.wait()


def finish(shape, whole, target, tiles, first, second, entered, cross, drags):
    _, depth, rows, width = whole.shape
    vmem = pl.BlockSpec(memory_space=pltpu.VMEM)
    hbm = pl.BlockSpec(memory_space=pltpu.HBM)
    args = [whole, target, tiles, first, second, *entered, cross, *drags]
    return pl.pallas_call(
        functools.partial(finish_kernel, shape, len(entered)),
        out_shape=[
            jax.ShapeDtypeStruct(whole.shape, F32),
            jax.ShapeDtypeStruct((3, target.shape[1]), F32),
        ],
        in_specs=[hbm] + [vmem] * (len(args) - 1),
        out_specs=[hbm, hbm],
        scratch_shapes=[
            pltpu.VMEM((10, rows, width), F32),
            pltpu.VMEM((10, depth + 2, 8, width), F32),
            pltpu.VMEM((3, target.shape[1]), F32),
            pltpu.SemaphoreType.DMA((21,)),
        ],
        input_output_aliases={0: 0},
        compiler_params=pltpu.CompilerParams(vmem_limit_bytes=ROOM),
        name="finish",
    )(*args)


def shards(populations, solid_mask, bead_owner, bead_base, bead_offset, bead_velocity):
    slabs, cols, pairs = shape = tuple(lax.axis_size(a) for a in ("slab", "col", "pair"))
    owners = slabs * cols
    depth, rows = populations.shape[1:3]
    single = owners == GROUP and slabs == 4
    swap = functools.partial(
        lax.all_to_all, axis_name=("slab", "col"), split_axis=0, concat_axis=0, tiled=True
    )

    target, messages = pack(owners, bead_owner, bead_base, bead_offset, bead_velocity)
    messages = swap(messages)
    *flow, columns, sides, walls = moments(populations, solid_mask)
    force, face, first, second, drag, *far, token = couple(
        shape, messages, flow, columns, populations, solid_mask
    )

    def send_pair(value):
        return send(value, shape, lambda s, c, p: (s, c, (p + 1) % pairs))

    def send_col(values):
        return [
            send(value, shape, lambda s, c, p, sign=sign: (s, (c + sign) % cols, p))
            for value, sign in zip(values, (1, -1))
        ]

    face = send_pair(face)
    first, second = send_slab(first, shape, 1), send_slab(second, shape, 0)
    if single:
        drags = [drag, send(far[0], shape, lambda s, c, p: ((s + 2) % slabs, c, p))]
    else:
        drags = []
        drag = swap(drag)
    fields = (populations, solid_mask, force)
    lower, draft, token = stream_lower(depth // 2, token, *fields, sides, walls, face)
    *leaving, cross, token = leaving_rows(depth, rows, token, draft, first, second, drags)
    entered, cross = send_col(leaving), send_pair(cross)
    if single:
        target, token = choice_of(shape, token, target)
    whole, tiles = stream_upper(token, lower, *fields, face)
    return tuple(
        finish(shape, whole, target, tiles, first, second, entered, cross, drags or [drag])
    )


def solution(mesh):
    return jax.shard_map(
        shards,
        mesh=mesh,
        in_specs=(
            P(None, ("rep", "slab"), "col", "pair"),
            P(("rep", "slab"), "col", "pair"),
            P(("rep", "slab", "col", "pair")),
            P(None, ("rep", "slab", "col", "pair")),
            P(None, ("rep", "slab", "col", "pair")),
            P(None, ("rep", "slab", "col", "pair")),
        ),
        out_specs=(
            P(None, ("rep", "slab"), "col", "pair"),
            P(None, ("rep", "slab", "col", "pair")),
        ),
        check_vma=False,
    )
```

```python
import functools

import jax
import jax.numpy as jnp
import numpy as np
from jax import lax
from jax.experimental import pallas as pl
from jax.experimental.pallas import tpu as pltpu
from jax.sharding import PartitionSpec as P

CAP = 32
GROUP = 8

STEP = np.array(
    [
        [0, 0, 0],
        [1, 0, 0],
        [-1, 0, 0],
        [0, 1, 0],
        [0, -1, 0],
        [0, 0, 1],
        [0, 0, -1],
        [1, 1, 0],
        [-1, -1, 0],
        [1, -1, 0],
        [-1, 1, 0],
        [1, 0, 1],
        [-1, 0, -1],
        [1, 0, -1],
        [-1, 0, 1],
        [0, 1, 1],
        [0, -1, -1],
        [0, 1, -1],
        [0, -1, 1],
    ],
    np.int32,
)
TAU_PLUS = 0.8
TAU_MINUS = 0.5 + (3.0 / 16.0) / (TAU_PLUS - 0.5)
KEEP_EVEN = 1.0 - 1.0 / TAU_PLUS
KEEP_ODD = 1.0 - 1.0 / TAU_MINUS
FORCE_GAIN = 1.0 - 0.5 / TAU_PLUS
DRAG_COEF = 2.0
F32 = jnp.float32
BF16 = jnp.bfloat16

ENTER = [[[i for i in range(19) if STEP[i, a] == sign] for sign in (1, -1)] for a in range(3)]
TOKEN = jax.ShapeDtypeStruct((8, 128), F32)
ROOM = 16 << 20
NT = (((1,), (1,)), ((), ()))
NN = (((1,), (0,)), ((), ()))


def iota(shape, dim):
    return lax.broadcasted_iota(jnp.int32, shape, dim)


def high_low(value):
    high = value.astype(BF16)
    return high, (value - high.astype(F32)).astype(BF16)


def dot_split(left, right, dims):
    (a, b), (c, d) = left, right
    mul = functools.partial(lax.dot_general, dimension_numbers=dims, preferred_element_type=F32)
    return mul(a, c) + (mul(a, d) + mul(b, c))


def dot_select(value, choose, dims):
    first = value.astype(BF16).astype(F32)
    rest = value - first
    second = rest.astype(BF16).astype(F32)
    stacked = jnp.concatenate([first, second, rest - second], axis=0).astype(BF16)
    got = lax.dot_general(stacked, choose, dimension_numbers=dims, preferred_element_type=F32)
    rows = value.shape[0]
    return got[0:rows] + got[rows : 2 * rows] + got[2 * rows : 3 * rows]


def density_momentum(pops):
    momentum = []
    for axis in range(3):
        plus = [pops[i] for i in range(19) if STEP[i, axis] == 1]
        minus = [pops[i] for i in range(19) if STEP[i, axis] == -1]
        momentum.append(sum(plus[1:], plus[0]) - sum(minus[1:], minus[0]))
    return sum(pops[1:], pops[0]), momentum


def along(step, vector):
    terms = None
    for axis in range(3):
        if step[axis] == 0:
            continue
        if terms is None:
            terms = vector[axis] if step[axis] == 1 else -vector[axis]
        else:
            terms = terms + vector[axis] if step[axis] == 1 else terms - vector[axis]
    return terms


def collide(pops, wall, force):
    density, momentum = density_momentum(pops)
    inverse = 1.0 / density
    carried = [m + 0.5 * f for m, f in zip(momentum, force)]
    speed = [m * inverse for m in carried]
    w = 1.0 / 36.0
    bend = [(4.5 * w / TAU_PLUS) * m + (9.0 * w * FORCE_GAIN) * f for m, f in zip(carried, force)]
    push = [(3.0 * w / TAU_MINUS) * m + (3.0 * w * FORCE_GAIN) * f for m, f in zip(carried, force)]
    drop = [(1.5 * w / TAU_PLUS) * m + (3.0 * w * FORCE_GAIN) * f for m, f in zip(carried, force)]
    rest = (w / TAU_PLUS) * density - sum(
        [u * d for u, d in zip(speed[1:], drop[1:])], speed[0] * drop[0]
    )
    out = [None] * 19
    out[0] = jnp.where(wall, pops[0], KEEP_EVEN * pops[0] + 12.0 * rest)
    for i in range(1, 19, 2):
        a, b = pops[i], pops[i + 1]
        step = STEP[i]
        even = rest + along(step, speed) * along(step, bend)
        odd = along(step, push)
        if i < 7:
            even = even + even
            odd = odd + odd
        even = (0.5 * KEEP_EVEN) * (a + b) + even
        odd = (0.5 * KEEP_ODD) * (a - b) + odd
        out[i] = jnp.where(wall, b, even + odd)
        out[i + 1] = jnp.where(wall, a, even - odd)
    return out


def turn(value, amount, axis):
    if amount == 0:
        return value
    return pltpu.roll(value, int(amount) % value.shape[axis], axis)


def send(value, shape, target):
    def flat(at):
        return (at[0] * shape[1] + at[1]) * shape[2] + at[2]

    perm = [(flat(at), flat(target(*at))) for at in np.ndindex(*shape)]
    return lax.ppermute(value, ("slab", "col", "pair"), perm)


def send_slab(value, shape, which):
    def target(s, c, p):
        return ((s + (1 if s % 2 == which else -1)) % shape[0], c, p)

    return send(value, shape, target)


def odd_slab():
    return lax.rem(lax.axis_index("slab"), 2) == 1


def rank_among(member):
    count = member.shape[1]
    earlier = (iota((count, count), 0) < iota((count, count), 1)).astype(F32).astype(BF16)
    return lax.dot_general(member.astype(BF16), earlier, NN, preferred_element_type=F32)


def patch_x(value, i, column):
    side = 0 if STEP[i, 0] == 1 else value.shape[1] - 1
    return jnp.where(iota(value.shape, 1) == side, column, value)


def x_pair(i):
    return ENTER[0][0 if STEP[i, 0] == 1 else 1].index(i)


def x_place(i):
    k = x_pair(i)
    return k // 4, (k % 4) * 32 + (1 if STEP[i, 0] == 1 else 0)


def x_arrived(face_ref):
    even = lax.rem(iota(face_ref.shape[1:], 1), 2) == 0
    return [jnp.where(even, turn(face_ref[n], -1, 1), turn(face_ref[n], 1, 1)) for n in range(2)]


def x_entering(face, k, z):
    tile = face[k // 4]
    return pltpu.roll(tile, tile.shape[1] - ((k % 4) * 32 + 2 * z + 1), 1)


def x_ends(planes):
    lane = lax.shift_right_logical(iota(planes[0].shape, 1), 1)
    tile = jnp.ones(planes[0].shape, F32)
    for z, value in enumerate(planes):
        tile = jnp.where(lane == z, pltpu.roll(value, 2 * z + 1, 1), tile)
    return tile


def pack_kernel(steps, *refs):
    sources, (target_ref, out_ref, table, *held) = refs[:4], refs[4:]
    copies = []
    if steps == 1:
        *held, sem = held
        for k, (source, place) in enumerate(zip(sources, held)):
            copies.append(pltpu.make_async_copy(source, place, sem.at[k]))
            copies[-1].start()
        copies[0].wait()
        sources = held
    owner_ref, base_ref, offset_ref, velocity_ref = sources
    count = owner_ref.shape[1]
    step = 0 if steps == 1 else pl.program_id(0)
    local = owner_ref[...] - step * GROUP
    member = (iota((GROUP, count), 0) == local).astype(F32)
    rank = jnp.sum(member * rank_among(member), axis=0, keepdims=True).astype(jnp.int32)
    inside = (local >= 0) & (local < GROUP)
    target = jnp.where(inside, local * CAP + rank, -1)
    whole_target = jnp.where(inside, owner_ref[...] * CAP + rank, -1)

    if steps == 1:
        target_ref[...] = whole_target
    else:
        known = jnp.where(step == 0, -1, target_ref[...])
        target_ref[...] = jnp.maximum(known, whole_target)

    choose = (iota((GROUP * CAP, count), 0) == target).astype(F32).astype(BF16)
    table[...] = jnp.zeros_like(table)
    for copy in copies[1:]:
        copy.wait()
    table[0:3] = base_ref[...].astype(F32) + 1.0
    table[8:11] = offset_ref[...]
    table[16:19] = velocity_ref[...]
    packed = dot_select(table[...], choose, NT)
    blank = jnp.zeros((8, CAP), F32)
    for r in range(GROUP):
        lanes = slice(r * CAP, (r + 1) * CAP)
        out_ref[r * 8 : r * 8 + 8] = jnp.concatenate(
            [packed[0:8, lanes], packed[8:16, lanes], packed[16:24, lanes], blank], axis=1
        )


def pack(owners, owner, base, offset, velocity):
    count, steps = owner.shape[0], owners // GROUP
    args = (owner.reshape(1, count), base, offset, velocity)
    scratch = [pltpu.VMEM((24, count), F32)]
    if steps == 1:
        blocks = dict(in_specs=[pl.BlockSpec(memory_space=pl.ANY)] * 4)
        scratch += [pltpu.VMEM(a.shape, a.dtype) for a in args] + [pltpu.SemaphoreType.DMA((4,))]
    else:
        blocks = dict(
            grid=(steps,),
            in_specs=[pl.BlockSpec(a.shape, lambda k: (0, 0)) for a in args],
            out_specs=[
                pl.BlockSpec((1, count), lambda k: (0, 0)),
                pl.BlockSpec((GROUP * 8, 128), lambda k: (k, 0)),
            ],
            compiler_params=pltpu.CompilerParams(vmem_limit_bytes=48 << 20),
        )
    target, tiles = pl.pallas_call(
        functools.partial(pack_kernel, steps),
        out_shape=[
            jax.ShapeDtypeStruct((1, count), jnp.int32),
            jax.ShapeDtypeStruct((owners * 8, 128), F32),
        ],
        scratch_shapes=scratch,
        name="pack",
        **blocks,
    )(*args)
    return target, tiles.reshape(owners, 8, 128)


def moments_kernel(
    pops_ref, solid_ref, high_ref, low_ref, column_ref, side_ref, wall_ref, held, held_solid, flow, sem
):
    depth, rows, width = pops_ref.shape[1:]
    chunks = 4
    span = depth // chunks
    copies = [pltpu.make_async_copy(solid_ref, held_solid, sem.at[chunks])]
    for k in range(chunks):
        part = pl.ds(k * span, span)
        copies.append(
            pltpu.make_async_copy(pops_ref.at[:, part], held.at[:, part], sem.at[k])
        )
    for copy in copies:
        copy.start()

    def plane(z, carry):
        pops = [held[i, z] for i in range(19)]
        density, momentum = density_momentum(pops)
        inverse = 1.0 / density
        for axis in range(3):
            flow[axis, pl.ds(pl.multiple_of(z * rows, rows), rows)] = momentum[axis] * inverse
        return carry

    for k in range(chunks):
        copies[1 + k].wait()
        lax.fori_loop(k * span, (k + 1) * span, plane, 0, unroll=2)
    copies[0].wait()
    for axis in range(3):
        at = slice(axis * width, (axis + 1) * width)
        high_ref[at], low_ref[at] = high_low(flow[axis].T)
    for i in range(19):
        column_ref[i] = x_ends([held[i, z] for z in range(depth)])
        side_ref[i, 0] = held[i, :, 0, :]
        side_ref[i, 1] = held[i, :, rows - 1, :]
    wall_ref[0] = held_solid[:, 0, :]
    wall_ref[1] = held_solid[:, rows - 1, :]
    column_ref[19] = x_ends([held_solid[z].astype(F32) for z in range(depth)])


def moments(pops, solid):
    _, depth, rows, width = pops.shape
    hbm = pl.BlockSpec(memory_space=pltpu.HBM)
    return pl.pallas_call(
        moments_kernel,
        out_shape=[
            jax.ShapeDtypeStruct((3 * width, depth * rows), BF16),
            jax.ShapeDtypeStruct((3 * width, depth * rows), BF16),
            jax.ShapeDtypeStruct((20, rows, 128), F32),
            jax.ShapeDtypeStruct((19, 2, depth, width), F32),
            jax.ShapeDtypeStruct((2, depth, width), jnp.int32),
        ],
        in_specs=[hbm, hbm],
        scratch_shapes=[
            pltpu.VMEM(pops.shape, F32),
            pltpu.VMEM(solid.shape, jnp.int32),
            pltpu.VMEM((3, depth * rows, width), F32),
            pltpu.SemaphoreType.DMA((5,)),
        ],
        compiler_params=pltpu.CompilerParams(vmem_limit_bytes=54000000),
        cost_estimate=pl.CostEstimate(flops=3000000, bytes_accessed=4000000, transcendentals=0),
        name="moments",
    )(pops, solid)


def unpack(tiles):
    return [
        jnp.concatenate([t[:, g * CAP : (g + 1) * CAP] for t in tiles], axis=1) for g in range(3)
    ]


def couple_group(base, part, velocity, flow, depth, rows, width):
    slots = GROUP * CAP
    start = base.astype(jnp.int32) - 1

    def hat(axis, length):
        cell = iota((length, slots), 0)
        low, share = start[axis : axis + 1], part[axis : axis + 1]
        return jnp.where(cell == low, 1.0 - share, 0.0) + jnp.where(cell == low + 1, share, 0.0)

    hat_x, hat_y, hat_z = hat(0, width), hat(1, rows), hat(2, depth)
    weight = high_low((hat_z[:, None, :] * hat_y[None, :, :]).reshape(depth * rows, slots))
    across = dot_split(flow, weight, NN)
    drag = []
    for d in range(3):
        sampled = jnp.sum(across[d * width : (d + 1) * width] * hat_x, axis=0, keepdims=True)
        drag.append(DRAG_COEF * (sampled - velocity[d : d + 1]))
    spread = jnp.concatenate([hat_x * (-drag[d]) for d in range(3)], axis=0)
    return drag, dot_split(weight, high_low(spread), NT)


def couple_kernel(shape, n_drags, beads_ref, high_ref, low_ref, *refs):
    slabs, cols, _ = shape
    column_ref, pops_ref, solid_ref, force_ref, face_ref, first_ref, second_ref, *refs = refs
    drag_refs, token_ref = refs[:-1], refs[-1]
    token_ref[...] = jnp.zeros_like(token_ref)
    depth, rows, width = pops_ref.shape[1:]
    flow = (high_ref[...], low_ref[...])

    def grid(force):
        return [
            force[:, d * width : (d + 1) * width].reshape(depth, rows, width) for d in range(3)
        ]

    hollow = jnp.zeros((5, GROUP * CAP), F32)

    if n_drags == 2:
        slab, col = lax.axis_index("slab"), lax.axis_index("col")
        got = []
        for r in range(GROUP):
            there = [a - b for a, b in zip((slab, col), divmod(r, cols))]
            there = [jnp.where(a < 0, a + n, a) for a, n in zip(there, (slabs, cols))]
            got.append(beads_ref[there[0] * cols + there[1]])
        drag, force = couple_group(*unpack(got), flow, depth, rows, width)
        for d, value in enumerate(grid(force)):
            force_ref[d] = value
        stacked = jnp.concatenate(drag + [hollow], axis=0)
        lanes = cols * CAP
        blank = jnp.zeros((8, 128 - lanes), F32)
        for dz in range(slabs):
            tile = jnp.concatenate([stacked[:, dz * lanes : (dz + 1) * lanes], blank], axis=1)
            drag_refs[0][dz] = tile
            if dz == 2:
                drag_refs[1][...] = tile
            if dz == 1:
                down = tile
        up = tile
    else:
        force_ref[...] = jnp.zeros_like(force_ref)
        blank = jnp.zeros((8, 128 - CAP), F32)

        def group(k, carry):
            got = [beads_ref[k * GROUP + r] for r in range(GROUP)]
            drag, force = couple_group(*unpack(got), flow, depth, rows, width)
            for d, value in enumerate(grid(force)):
                force_ref[d] += value
            stacked = jnp.concatenate(drag + [hollow], axis=0)
            for r in range(GROUP):
                drag_refs[0][k * GROUP + r] = jnp.concatenate(
                    [stacked[:, r * CAP : (r + 1) * CAP], blank], axis=1
                )
            return carry

        lax.fori_loop(0, beads_ref.shape[0] // GROUP, group, 0)

    force = [x_ends([force_ref[d, z] for z in range(depth)]) for d in range(3)]
    out = collide([column_ref[i] for i in range(19)], column_ref[19] == 1.0, force)
    high = lax.rem(iota((rows, 128), 1), 2) == 0
    ends = [jnp.where(high, out[i], out[j])[:, 0:32] for i, j in zip(*ENTER[0])]
    face_ref[0] = jnp.concatenate(ends[0:4], axis=1)
    face_ref[1] = jnp.concatenate([ends[4], jnp.zeros((rows, 96), F32)], axis=1)
    odd = odd_slab()
    leaving = []
    for group, z in ((0, depth - 1), (1, 0)):
        out = collide(
            [pops_ref[i, z] for i in range(19)],
            solid_ref[z] == 1,
            [force_ref[d, z] for d in range(3)],
        )
        leaving.append([turn(out[i], STEP[i, 0], 1) for i in ENTER[2][group]])
    if n_drags == 2:
        leaving[0].append(up)
        leaving[1].append(down)
    row = 0
    for a, b in zip(*leaving):
        at = slice(row, row + a.shape[0])
        first_ref[at] = jnp.where(odd, a, b)
        second_ref[at] = jnp.where(odd, b, a)
        row += a.shape[0]


def couple(shape, beads, flow, columns, pops, solid):
    _, depth, rows, width = pops.shape
    single = beads.shape[0] == GROUP
    tile = jax.ShapeDtypeStruct((8, 128), F32)
    drags = [jax.ShapeDtypeStruct((shape[0], 8, 128), F32), tile] if single else [beads]
    message = jax.ShapeDtypeStruct((5 * rows + (8 if single else 0), width), F32)
    return pl.pallas_call(
        functools.partial(couple_kernel, shape, len(drags)),
        out_shape=[
            jax.ShapeDtypeStruct((3, depth, rows, width), F32),
            jax.ShapeDtypeStruct((2, rows, 128), F32),
            message,
            message,
        ]
        + [jax.ShapeDtypeStruct(d.shape, F32) for d in drags]
        + [TOKEN],
        compiler_params=pltpu.CompilerParams(vmem_limit_bytes=ROOM),
        name="couple",
    )(beads, *flow, columns, pops, solid)


def entered_z(first_ref, second_ref, side, rows):
    odd = odd_slab() if side == 0 else jnp.logical_not(odd_slab())
    return jnp.where(odd, second_ref[rows], first_ref[rows])


X_EDGES = [i for side in range(2) for i in ENTER[2][side] if STEP[i, 0] != 0]


def rows_kernel(depth, rows, before_ref, draft_ref, first_ref, second_ref, *refs):
    refs, (cross_ref, token_ref) = refs[:-2], refs[-2:]
    token_ref[...] = jnp.zeros_like(token_ref)
    outs = refs[-1:] if len(refs) == 3 else refs
    for group in range(2):
        out_ref = outs[0] if len(outs) == 1 else outs[group]
        base = group * 5 * depth if len(outs) == 1 else 0
        y = rows - 1 if group == 0 else 0
        out_ref[base : base + 5 * depth] = draft_ref[group * 5 * depth : (group + 1) * 5 * depth]
        for k, i in enumerate(ENTER[1][group]):
            at = base + k * depth
            if STEP[i, 2] != 0:
                side = 0 if STEP[i, 2] == 1 else 1
                z = 0 if side == 0 else depth - 1
                row = ENTER[2][side].index(i) * rows + y
                out_ref[at + z : at + z + 1] = entered_z(
                    first_ref, second_ref, side, slice(row, row + 1)
                )
    if len(refs) == 3:
        own_ref, far_ref, out_ref = refs
        came = arrived_drag(own_ref, far_ref, first_ref, second_ref, 5 * rows)
        out_ref[10 * depth : 10 * depth + 8] = one_tile(came, 1)
    for k, i in enumerate(X_EDGES):
        side = 0 if STEP[i, 2] == 1 else 1
        at = ENTER[2][side].index(i) * rows
        cross_ref[k * rows : (k + 1) * rows] = entered_z(
            first_ref, second_ref, side, slice(at, at + rows)
        )


def arrived_drag(own_ref, far_ref, first_ref, second_ref, tail):
    at = slice(tail, tail + 8)
    up, down = [entered_z(first_ref, second_ref, side, at) for side in range(2)]
    return [own_ref[0], down, far_ref[...], up]


def one_tile(tiles, col):
    return jnp.concatenate([t[:, col * CAP : (col + 1) * CAP] for t in tiles], axis=1)


def leaving_rows(depth, rows, before, draft, first, second, drags):
    width = draft.shape[1]
    if drags:
        sizes = [10 * depth + 8]
    else:
        sizes = [5 * depth] * 2
    args = (draft, first, second, *drags)
    return pl.pallas_call(
        functools.partial(rows_kernel, depth, rows),
        out_shape=[jax.ShapeDtypeStruct((n, width), F32) for n in sizes + [4 * rows]] + [TOKEN],
        in_specs=[pl.BlockSpec(memory_space=pl.ANY)]
        + [pl.BlockSpec(memory_space=pltpu.VMEM)] * len(args),
        compiler_params=pltpu.CompilerParams(vmem_limit_bytes=ROOM),
        name="rows",
    )(before, *args)


def runs(members):
    found = []
    for i in members:
        if found and found[-1][1] == i and STEP[i, 2] == STEP[i - 1, 2]:
            found[-1] = (found[-1][0], i + 1)
        else:
            found.append((i, i + 1))
    return found


def stream_planes(low, high, faces, pops_ref, solid_ref, force_ref, held):
    def plane(z, faces):
        out = collide(
            [pops_ref[i, z] for i in range(19)],
            solid_ref[z] == 1,
            [force_ref[d, z] for d in range(3)],
        )
        for i in range(19):
            value = turn(out[i], STEP[i, 0], 1)
            if STEP[i, 0] != 0:
                value = patch_x(value, i, faces[x_pair(i)])
            held[i, z] = turn(value, STEP[i, 1], 0)
        return tuple(pltpu.roll(f, 126, 1) for f in faces)

    return lax.fori_loop(low, high, plane, faces, unroll=2)


def lower_kernel(
    before_ref, pops_ref, solid_ref, force_ref, side_ref, wall_ref, face_ref, *refs
):
    held, draft_ref, token_ref, turned = refs
    depth, rows, _ = pops_ref.shape[1:]
    token_ref[...] = jnp.zeros_like(token_ref)
    face = x_arrived(face_ref)
    for n in range(2):
        turned[n] = face[n].T
    for group in range(2):
        y = 0 if group else rows - 1
        force = [force_ref[d, :, y, :] for d in range(3)]
        out = collide([side_ref[i, 1 - group] for i in range(19)], wall_ref[1 - group] == 1, force)
        for k, i in enumerate(ENTER[1][group]):
            row = (group * 5 + k) * depth
            value = turn(out[i], STEP[i, 0], 1)
            if STEP[i, 0] != 0:
                tile, lane = x_place(i)
                column = turned[tile, pl.ds(lane, depth, stride=2), :][:, y : y + 1]
                value = patch_x(value, i, jnp.broadcast_to(column, value.shape))
            draft_ref[row : row + depth] = turn(value, STEP[i, 2], 0)
    faces = tuple(x_entering(face, k, 0) for k in range(5))
    stream_planes(0, held.shape[1], faces, pops_ref, solid_ref, force_ref, held)


def upper_kernel(
    before_ref, lower_ref, pops_ref, solid_ref, force_ref, face_ref, out_ref, tile_ref, held, sem
):
    depth, rows, width = pops_ref.shape[1:]
    half = lower_ref.shape[1]
    copies = []

    def leave(source, members, low, high):
        for a, b in runs(members):
            step = int(STEP[a, 2])
            start, stop = max(low + step, 0), min(high + step, depth)
            copy = pltpu.make_async_copy(
                source.at[a:b, start - step : stop - step],
                out_ref.at[a:b, start:stop],
                sem.at[len(copies)],
            )
            copy.start()
            copies.append(copy)

    leave(lower_ref, range(19), 0, half)
    face = x_arrived(face_ref)
    faces = tuple(x_entering(face, k, half) for k in range(5))
    marks = upper_marks(half, depth)
    for low, high in zip(marks, marks[1:]):
        faces = stream_planes(low, high, faces, pops_ref, solid_ref, force_ref, held)
        leave(held, range(19), low, high)
    for group in range(2):
        first = slice(0, 8) if group == 0 else slice(rows - 8, rows)
        for k, i in enumerate(ENTER[1][group]):
            tile_ref[group * 5 + k, 0:half] = lower_ref[i, :, first, :]
            tile_ref[group * 5 + k, half:depth] = held[i, half:depth, first, :]
    for copy in copies:
        copy.wait()


def upper_marks(half, depth):
    return list(range(half, depth - 2, 4)) + ([depth - 2] if (depth - half) % 4 else []) + [depth]


def stream_lower(half, before, pops, solid, force, sides, walls, face):
    _, depth, rows, width = pops.shape
    vmem = pl.BlockSpec(memory_space=pltpu.VMEM)
    return pl.pallas_call(
        lower_kernel,
        out_shape=[
            jax.ShapeDtypeStruct((19, half, rows, width), F32),
            jax.ShapeDtypeStruct((10 * depth, width), F32),
            TOKEN,
        ],
        in_specs=[pl.BlockSpec(memory_space=pl.ANY)] + [vmem] * 6,
        scratch_shapes=[pltpu.VMEM((2, 128, rows), F32)],
        compiler_params=pltpu.CompilerParams(vmem_limit_bytes=ROOM),
        cost_estimate=pl.CostEstimate(flops=3000000, bytes_accessed=2000000, transcendentals=0),
        name="lower",
    )(before, pops, solid, force, sides, walls, face)


def stream_upper(before, lower, pops, solid, force, face):
    _, depth, rows, width = pops.shape
    vmem = pl.BlockSpec(memory_space=pltpu.VMEM)
    return pl.pallas_call(
        upper_kernel,
        out_shape=[
            jax.ShapeDtypeStruct(pops.shape, F32),
            jax.ShapeDtypeStruct((10, depth, 8, width), F32),
        ],
        in_specs=[pl.BlockSpec(memory_space=pl.ANY)] + [vmem] * 5,
        out_specs=[pl.BlockSpec(memory_space=pltpu.HBM), vmem],
        scratch_shapes=[
            pltpu.VMEM(pops.shape, F32),
            pltpu.SemaphoreType.DMA((20 * len(upper_marks(lower.shape[1], depth)),)),
        ],
        compiler_params=pltpu.CompilerParams(vmem_limit_bytes=ROOM),
        cost_estimate=pl.CostEstimate(flops=5000000, bytes_accessed=3000000, transcendentals=0),
        name="upper",
    )(before, lower, pops, solid, force, face)


def choice_kernel(shape, before_ref, target_ref, choice_ref, token_ref):
    slabs, cols, _ = shape
    token_ref[...] = jnp.zeros_like(token_ref)
    target = target_ref[...]
    owner = lax.shift_right_logical(target, 5)
    owner_slab = lax.shift_right_logical(owner, cols.bit_length() - 1)
    away_col = owner - owner_slab * cols - lax.axis_index("col")
    away_col = jnp.where(away_col < 0, away_col + cols, away_col)
    away_slab = owner_slab - lax.axis_index("slab")
    away_slab = jnp.where(away_slab < 0, away_slab + slabs, away_slab)
    place = away_col * 128 + away_slab * CAP + target - owner * CAP
    choice_ref[...] = (iota(choice_ref.shape, 0) == place).astype(F32).astype(BF16)


def choice_of(shape, before, target):
    return pl.pallas_call(
        functools.partial(choice_kernel, shape),
        out_shape=[jax.ShapeDtypeStruct((256, target.shape[1]), BF16), TOKEN],
        in_specs=[pl.BlockSpec(memory_space=pl.ANY), pl.BlockSpec(memory_space=pltpu.VMEM)],
        compiler_params=pltpu.CompilerParams(vmem_limit_bytes=ROOM),
        name="choice",
    )(before, target)


def finish_kernel(shape, n_rows, whole_ref, target_ref, tile_ref, first_ref, second_ref, *refs):
    row_refs, cross_ref, refs = refs[:n_rows], refs[n_rows], refs[n_rows + 1 :]
    drag_refs, (out_ref, bead_ref, planes, tiles, bead, sem) = refs[:-6], refs[-6:]
    depth, rows, width = whole_ref.shape[1:]

    def entering(group, k):
        at = (group * 5 + k) * depth if n_rows == 1 else k * depth
        return row_refs[group % n_rows][at : at + depth]

    copies = []

    def leave(source, target):
        copy = pltpu.make_async_copy(source, target, sem.at[len(copies)])
        copy.start()
        copies.append(copy)

    for group in range(2):
        z = 0 if group == 0 else depth - 1
        for k, i in enumerate(ENTER[2][group]):
            value = entered_z(first_ref, second_ref, group, slice(k * rows, (k + 1) * rows))
            if STEP[i, 1] != 0:
                side = 0 if STEP[i, 1] == 1 else 1
                y = 0 if side == 0 else rows - 1
                row = entering(side, ENTER[1][side].index(i))[z : z + 1]
                value = jnp.where(
                    iota((rows, width), 0) == y,
                    jnp.broadcast_to(row, (rows, width)),
                    turn(value, STEP[i, 1], 0),
                )
            if STEP[i, 0] != 0:
                at = X_EDGES.index(i) * rows
                value = patch_x(value, i, cross_ref[at : at + rows])
            n = group * 5 + k
            planes[n] = value
            leave(planes.at[n], out_ref.at[i, z])
    for group in range(2):
        first = 0 if group == 0 else rows - 8
        for k, i in enumerate(ENTER[1][group]):
            n = group * 5 + k
            step = int(STEP[i, 2])
            tiles[n, 1 + step : 1 + step + depth] = tile_ref[n]
            tiles[n, 1 : 1 + depth, 0 if group == 0 else 7, :] = entering(group, k)
            low, high = max(step, 0), min(depth + step, depth)
            leave(tiles.at[n, 1 + low : 1 + high], out_ref.at[i, low:high, first : first + 8])

    count = target_ref.shape[1]
    if len(drag_refs) == 2:
        came = arrived_drag(*drag_refs, first_ref, second_ref, 5 * rows)
        passed = row_refs[0][10 * depth : 10 * depth + 8]
        table = jnp.concatenate([one_tile(came, 0), passed], axis=1)
        total = dot_select(table, target_ref[...], NN)
    else:
        back_ref = drag_refs[0]

        def group_share(k, total):
            got = [back_ref[k * GROUP + r] for r in range(GROUP)]
            slots = jnp.concatenate([t[:, 0:CAP] for t in got], axis=1)
            first = k * (GROUP * CAP)
            choose = (iota((GROUP * CAP, count), 0) + first == target_ref[...]).astype(F32)
            return total + dot_select(slots, choose.astype(BF16), NN)

        total = lax.fori_loop(
            0, back_ref.shape[0] // GROUP, group_share, jnp.zeros((8, count), F32)
        )
    bead[...] = total[0:3]
    leave(bead, bead_ref)
    for copy in copies:
        copy.wait()


def finish(shape, whole, target, tiles, first, second, entered, cross, drags):
    _, depth, rows, width = whole.shape
    vmem = pl.BlockSpec(memory_space=pltpu.VMEM)
    hbm = pl.BlockSpec(memory_space=pltpu.HBM)
    args = [whole, target, tiles, first, second, *entered, cross, *drags]
    return pl.pallas_call(
        functools.partial(finish_kernel, shape, len(entered)),
        out_shape=[
            jax.ShapeDtypeStruct(whole.shape, F32),
            jax.ShapeDtypeStruct((3, target.shape[1]), F32),
        ],
        in_specs=[hbm] + [vmem] * (len(args) - 1),
        out_specs=[hbm, hbm],
        scratch_shapes=[
            pltpu.VMEM((10, rows, width), F32),
            pltpu.VMEM((10, depth + 2, 8, width), F32),
            pltpu.VMEM((3, target.shape[1]), F32),
            pltpu.SemaphoreType.DMA((21,)),
        ],
        input_output_aliases={0: 0},
        compiler_params=pltpu.CompilerParams(vmem_limit_bytes=ROOM),
        name="finish",
    )(*args)


def shards(populations, solid_mask, bead_owner, bead_base, bead_offset, bead_velocity):
    slabs, cols, pairs = shape = tuple(lax.axis_size(a) for a in ("slab", "col", "pair"))
    owners = slabs * cols
    depth, rows = populations.shape[1:3]
    single = owners == GROUP and slabs == 4
    swap = functools.partial(
        lax.all_to_all, axis_name=("slab", "col"), split_axis=0, concat_axis=0, tiled=True
    )

    target, messages = pack(owners, bead_owner, bead_base, bead_offset, bead_velocity)
    messages = swap(messages)
    *flow, columns, sides, walls = moments(populations, solid_mask)
    force, face, first, second, drag, *far, token = couple(
        shape, messages, flow, columns, populations, solid_mask
    )

    def send_pair(value):
        return send(value, shape, lambda s, c, p: (s, c, (p + 1) % pairs))

    def send_col(values):
        return [
            send(value, shape, lambda s, c, p, sign=sign: (s, (c + sign) % cols, p))
            for value, sign in zip(values, (1, -1))
        ]

    face = send_pair(face)
    first, second = send_slab(first, shape, 1), send_slab(second, shape, 0)
    if single:
        drags = [drag, send(far[0], shape, lambda s, c, p: ((s + 2) % slabs, c, p))]
    else:
        drags = []
        drag = swap(drag)
    fields = (populations, solid_mask, force)
    lower, draft, token = stream_lower(depth // 2, token, *fields, sides, walls, face)
    *leaving, cross, token = leaving_rows(depth, rows, token, draft, first, second, drags)
    entered, cross = send_col(leaving), send_pair(cross)
    if single:
        target, token = choice_of(shape, token, target)
    whole, tiles = stream_upper(token, lower, *fields, face)
    return tuple(
        finish(shape, whole, target, tiles, first, second, entered, cross, drags or [drag])
    )


def solution(mesh):
    return jax.shard_map(
        shards,
        mesh=mesh,
        in_specs=(
            P(None, ("rep", "slab"), "col", "pair"),
            P(("rep", "slab"), "col", "pair"),
            P(("rep", "slab", "col", "pair")),
            P(None, ("rep", "slab", "col", "pair")),
            P(None, ("rep", "slab", "col", "pair")),
            P(None, ("rep", "slab", "col", "pair")),
        ),
        out_specs=(
            P(None, ("rep", "slab"), "col", "pair"),
            P(None, ("rep", "slab", "col", "pair")),
        ),
        check_vma=False,
    )
```

```python
import functools

import jax
import jax.numpy as jnp
import numpy as np
from jax import lax
from jax.experimental import pallas as pl
from jax.experimental.pallas import tpu as pltpu
from jax.sharding import PartitionSpec as P

CAP = 32
GROUP = 8

STEP = np.array(
    [
        [0, 0, 0],
        [1, 0, 0],
        [-1, 0, 0],
        [0, 1, 0],
        [0, -1, 0],
        [0, 0, 1],
        [0, 0, -1],
        [1, 1, 0],
        [-1, -1, 0],
        [1, -1, 0],
        [-1, 1, 0],
        [1, 0, 1],
        [-1, 0, -1],
        [1, 0, -1],
        [-1, 0, 1],
        [0, 1, 1],
        [0, -1, -1],
        [0, 1, -1],
        [0, -1, 1],
    ],
    np.int32,
)
TAU_PLUS = 0.8
TAU_MINUS = 0.5 + (3.0 / 16.0) / (TAU_PLUS - 0.5)
KEEP_EVEN = 1.0 - 1.0 / TAU_PLUS
KEEP_ODD = 1.0 - 1.0 / TAU_MINUS
FORCE_GAIN = 1.0 - 0.5 / TAU_PLUS
DRAG_COEF = 2.0
F32 = jnp.float32
BF16 = jnp.bfloat16

ENTER = [[[i for i in range(19) if STEP[i, a] == sign] for sign in (1, -1)] for a in range(3)]
TOKEN = jax.ShapeDtypeStruct((8, 128), F32)
ROOM = 16 << 20
NT = (((1,), (1,)), ((), ()))
NN = (((1,), (0,)), ((), ()))


def iota(shape, dim):
    return lax.broadcasted_iota(jnp.int32, shape, dim)


def high_low(value):
    high = value.astype(BF16)
    return high, (value - high.astype(F32)).astype(BF16)


def dot_split(left, right, dims):
    (a, b), (c, d) = left, right
    mul = functools.partial(lax.dot_general, dimension_numbers=dims, preferred_element_type=F32)
    return mul(a, c) + (mul(a, d) + mul(b, c))


def dot_select(value, choose, dims):
    first = value.astype(BF16).astype(F32)
    rest = value - first
    second = rest.astype(BF16).astype(F32)
    stacked = jnp.concatenate([first, second, rest - second], axis=0).astype(BF16)
    got = lax.dot_general(stacked, choose, dimension_numbers=dims, preferred_element_type=F32)
    rows = value.shape[0]
    return got[0:rows] + got[rows : 2 * rows] + got[2 * rows : 3 * rows]


def density_momentum(pops):
    momentum = []
    for axis in range(3):
        plus = [pops[i] for i in range(19) if STEP[i, axis] == 1]
        minus = [pops[i] for i in range(19) if STEP[i, axis] == -1]
        momentum.append(sum(plus[1:], plus[0]) - sum(minus[1:], minus[0]))
    return sum(pops[1:], pops[0]), momentum


def along(step, vector):
    terms = None
    for axis in range(3):
        if step[axis] == 0:
            continue
        if terms is None:
            terms = vector[axis] if step[axis] == 1 else -vector[axis]
        else:
            terms = terms + vector[axis] if step[axis] == 1 else terms - vector[axis]
    return terms


def collide(pops, wall, force):
    density, momentum = density_momentum(pops)
    inverse = 1.0 / density
    carried = [m + 0.5 * f for m, f in zip(momentum, force)]
    speed = [m * inverse for m in carried]
    w = 1.0 / 36.0
    bend = [(4.5 * w / TAU_PLUS) * m + (9.0 * w * FORCE_GAIN) * f for m, f in zip(carried, force)]
    push = [(3.0 * w / TAU_MINUS) * m + (3.0 * w * FORCE_GAIN) * f for m, f in zip(carried, force)]
    drop = [(1.5 * w / TAU_PLUS) * m + (3.0 * w * FORCE_GAIN) * f for m, f in zip(carried, force)]
    rest = (w / TAU_PLUS) * density - sum(
        [u * d for u, d in zip(speed[1:], drop[1:])], speed[0] * drop[0]
    )
    out = [None] * 19
    out[0] = jnp.where(wall, pops[0], KEEP_EVEN * pops[0] + 12.0 * rest)
    for i in range(1, 19, 2):
        a, b = pops[i], pops[i + 1]
        step = STEP[i]
        even = rest + along(step, speed) * along(step, bend)
        odd = along(step, push)
        if i < 7:
            even = even + even
            odd = odd + odd
        even = (0.5 * KEEP_EVEN) * (a + b) + even
        odd = (0.5 * KEEP_ODD) * (a - b) + odd
        out[i] = jnp.where(wall, b, even + odd)
        out[i + 1] = jnp.where(wall, a, even - odd)
    return out


def turn(value, amount, axis):
    if amount == 0:
        return value
    return pltpu.roll(value, int(amount) % value.shape[axis], axis)


def send(value, shape, target):
    def flat(at):
        return (at[0] * shape[1] + at[1]) * shape[2] + at[2]

    perm = [(flat(at), flat(target(*at))) for at in np.ndindex(*shape)]
    return lax.ppermute(value, ("slab", "col", "pair"), perm)


def send_slab(value, shape, which):
    def target(s, c, p):
        return ((s + (1 if s % 2 == which else -1)) % shape[0], c, p)

    return send(value, shape, target)


def odd_slab():
    return lax.rem(lax.axis_index("slab"), 2) == 1


def rank_among(member):
    count = member.shape[1]
    earlier = (iota((count, count), 0) < iota((count, count), 1)).astype(F32).astype(BF16)
    return lax.dot_general(member.astype(BF16), earlier, NN, preferred_element_type=F32)


def patch_x(value, i, column):
    side = 0 if STEP[i, 0] == 1 else value.shape[1] - 1
    return jnp.where(iota(value.shape, 1) == side, column, value)


def x_pair(i):
    return ENTER[0][0 if STEP[i, 0] == 1 else 1].index(i)


def x_place(i):
    k = x_pair(i)
    return k // 4, (k % 4) * 32 + (1 if STEP[i, 0] == 1 else 0)


def x_arrived(face_ref):
    even = lax.rem(iota(face_ref.shape[1:], 1), 2) == 0
    return [jnp.where(even, turn(face_ref[n], -1, 1), turn(face_ref[n], 1, 1)) for n in range(2)]


def x_entering(face, k, z):
    tile = face[k // 4]
    return pltpu.roll(tile, tile.shape[1] - ((k % 4) * 32 + 2 * z + 1), 1)


def x_ends(planes):
    lane = lax.shift_right_logical(iota(planes[0].shape, 1), 1)
    tile = jnp.ones(planes[0].shape, F32)
    for z, value in enumerate(planes):
        tile = jnp.where(lane == z, pltpu.roll(value, 2 * z + 1, 1), tile)
    return tile


def pack_kernel(steps, *refs):
    sources, (target_ref, out_ref, table, *held) = refs[:4], refs[4:]
    copies = []
    if steps == 1:
        *held, sem = held
        for k, (source, place) in enumerate(zip(sources, held)):
            copies.append(pltpu.make_async_copy(source, place, sem.at[k]))
            copies[-1].start()
        copies[0].wait()
        sources = held
    owner_ref, base_ref, offset_ref, velocity_ref = sources
    count = owner_ref.shape[1]
    step = 0 if steps == 1 else pl.program_id(0)
    local = owner_ref[...] - step * GROUP
    member = (iota((GROUP, count), 0) == local).astype(F32)
    rank = jnp.sum(member * rank_among(member), axis=0, keepdims=True).astype(jnp.int32)
    inside = (local >= 0) & (local < GROUP)
    target = jnp.where(inside, local * CAP + rank, -1)
    whole_target = jnp.where(inside, owner_ref[...] * CAP + rank, -1)

    if steps == 1:
        target_ref[...] = whole_target
    else:
        known = jnp.where(step == 0, -1, target_ref[...])
        target_ref[...] = jnp.maximum(known, whole_target)

    choose = (iota((GROUP * CAP, count), 0) == target).astype(F32).astype(BF16)
    table[...] = jnp.zeros_like(table)
    for copy in copies[1:]:
        copy.wait()
    table[0:3] = base_ref[...].astype(F32) + 1.0
    table[8:11] = offset_ref[...]
    table[16:19] = velocity_ref[...]
    packed = dot_select(table[...], choose, NT)
    blank = jnp.zeros((8, CAP), F32)
    for r in range(GROUP):
        lanes = slice(r * CAP, (r + 1) * CAP)
        out_ref[r * 8 : r * 8 + 8] = jnp.concatenate(
            [packed[0:8, lanes], packed[8:16, lanes], packed[16:24, lanes], blank], axis=1
        )


def pack(owners, owner, base, offset, velocity):
    count, steps = owner.shape[0], owners // GROUP
    args = (owner.reshape(1, count), base, offset, velocity)
    scratch = [pltpu.VMEM((24, count), F32)]
    if steps == 1:
        blocks = dict(in_specs=[pl.BlockSpec(memory_space=pl.ANY)] * 4)
        scratch += [pltpu.VMEM(a.shape, a.dtype) for a in args] + [pltpu.SemaphoreType.DMA((4,))]
    else:
        blocks = dict(
            grid=(steps,),
            in_specs=[pl.BlockSpec(a.shape, lambda k: (0, 0)) for a in args],
            out_specs=[
                pl.BlockSpec((1, count), lambda k: (0, 0)),
                pl.BlockSpec((GROUP * 8, 128), lambda k: (k, 0)),
            ],
            compiler_params=pltpu.CompilerParams(vmem_limit_bytes=48 << 20),
        )
    target, tiles = pl.pallas_call(
        functools.partial(pack_kernel, steps),
        out_shape=[
            jax.ShapeDtypeStruct((1, count), jnp.int32),
            jax.ShapeDtypeStruct((owners * 8, 128), F32),
        ],
        scratch_shapes=scratch,
        name="pack",
        **blocks,
    )(*args)
    return target, tiles.reshape(owners, 8, 128)


def moments_kernel(
    pops_ref, solid_ref, high_ref, low_ref, column_ref, side_ref, wall_ref, held, held_solid, flow, sem
):
    depth, rows, width = pops_ref.shape[1:]
    chunks = 4
    span = depth // chunks
    copies = [pltpu.make_async_copy(solid_ref, held_solid, sem.at[chunks])]
    for k in range(chunks):
        part = pl.ds(k * span, span)
        copies.append(
            pltpu.make_async_copy(pops_ref.at[:, part], held.at[:, part], sem.at[k])
        )
    for copy in copies:
        copy.start()

    def plane(z, carry):
        pops = [held[i, z] for i in range(19)]
        density, momentum = density_momentum(pops)
        inverse = 1.0 / density
        for axis in range(3):
            flow[axis, pl.ds(pl.multiple_of(z * rows, rows), rows)] = momentum[axis] * inverse
        return carry

    for k in range(chunks):
        copies[1 + k].wait()
        lax.fori_loop(k * span, (k + 1) * span, plane, 0, unroll=2)
    copies[0].wait()
    for axis in range(3):
        at = slice(axis * width, (axis + 1) * width)
        high_ref[at], low_ref[at] = high_low(flow[axis].T)
    for i in range(19):
        column_ref[i] = x_ends([held[i, z] for z in range(depth)])
        side_ref[i, 0] = held[i, :, 0, :]
        side_ref[i, 1] = held[i, :, rows - 1, :]
    wall_ref[0] = held_solid[:, 0, :]
    wall_ref[1] = held_solid[:, rows - 1, :]
    column_ref[19] = x_ends([held_solid[z].astype(F32) for z in range(depth)])


def moments(pops, solid):
    _, depth, rows, width = pops.shape
    hbm = pl.BlockSpec(memory_space=pltpu.HBM)
    return pl.pallas_call(
        moments_kernel,
        out_shape=[
            jax.ShapeDtypeStruct((3 * width, depth * rows), BF16),
            jax.ShapeDtypeStruct((3 * width, depth * rows), BF16),
            jax.ShapeDtypeStruct((20, rows, 128), F32),
            jax.ShapeDtypeStruct((19, 2, depth, width), F32),
            jax.ShapeDtypeStruct((2, depth, width), jnp.int32),
        ],
        in_specs=[hbm, hbm],
        scratch_shapes=[
            pltpu.VMEM(pops.shape, F32),
            pltpu.VMEM(solid.shape, jnp.int32),
            pltpu.VMEM((3, depth * rows, width), F32),
            pltpu.SemaphoreType.DMA((5,)),
        ],
        compiler_params=pltpu.CompilerParams(vmem_limit_bytes=54000000),
        cost_estimate=pl.CostEstimate(flops=3000000, bytes_accessed=4000000, transcendentals=0),
        name="moments",
    )(pops, solid)


def unpack(tiles):
    return [
        jnp.concatenate([t[:, g * CAP : (g + 1) * CAP] for t in tiles], axis=1) for g in range(3)
    ]


def couple_group(base, part, velocity, flow, depth, rows, width):
    slots = GROUP * CAP
    start = base.astype(jnp.int32) - 1

    def hat(axis, length):
        cell = iota((length, slots), 0)
        low, share = start[axis : axis + 1], part[axis : axis + 1]
        return jnp.where(cell == low, 1.0 - share, 0.0) + jnp.where(cell == low + 1, share, 0.0)

    hat_x, hat_y, hat_z = hat(0, width), hat(1, rows), hat(2, depth)
    weight = high_low((hat_z[:, None, :] * hat_y[None, :, :]).reshape(depth * rows, slots))
    across = dot_split(flow, weight, NN)
    drag = []
    for d in range(3):
        sampled = jnp.sum(across[d * width : (d + 1) * width] * hat_x, axis=0, keepdims=True)
        drag.append(DRAG_COEF * (sampled - velocity[d : d + 1]))
    spread = jnp.concatenate([hat_x * (-drag[d]) for d in range(3)], axis=0)
    return drag, dot_split(weight, high_low(spread), NT)


def couple_kernel(shape, n_drags, beads_ref, high_ref, low_ref, *refs):
    slabs, cols, _ = shape
    column_ref, pops_ref, solid_ref, force_ref, face_ref, first_ref, second_ref, *refs = refs
    drag_refs, token_ref = refs[:-1], refs[-1]
    token_ref[...] = jnp.zeros_like(token_ref)
    depth, rows, width = pops_ref.shape[1:]
    flow = (high_ref[...], low_ref[...])

    def grid(force):
        return [
            force[:, d * width : (d + 1) * width].reshape(depth, rows, width) for d in range(3)
        ]

    hollow = jnp.zeros((5, GROUP * CAP), F32)

    if n_drags == 2:
        slab, col = lax.axis_index("slab"), lax.axis_index("col")
        got = []
        for r in range(GROUP):
            there = [a - b for a, b in zip((slab, col), divmod(r, cols))]
            there = [jnp.where(a < 0, a + n, a) for a, n in zip(there, (slabs, cols))]
            got.append(beads_ref[there[0] * cols + there[1]])
        drag, force = couple_group(*unpack(got), flow, depth, rows, width)
        for d, value in enumerate(grid(force)):
            force_ref[d] = value
        stacked = jnp.concatenate(drag + [hollow], axis=0)
        lanes = cols * CAP
        blank = jnp.zeros((8, 128 - lanes), F32)
        for dz in range(slabs):
            tile = jnp.concatenate([stacked[:, dz * lanes : (dz + 1) * lanes], blank], axis=1)
            drag_refs[0][dz] = tile
            if dz == 2:
                drag_refs[1][...] = tile
            if dz == 1:
                down = tile
        up = tile
    else:
        force_ref[...] = jnp.zeros_like(force_ref)
        blank = jnp.zeros((8, 128 - CAP), F32)

        def group(k, carry):
            got = [beads_ref[k * GROUP + r] for r in range(GROUP)]
            drag, force = couple_group(*unpack(got), flow, depth, rows, width)
            for d, value in enumerate(grid(force)):
                force_ref[d] += value
            stacked = jnp.concatenate(drag + [hollow], axis=0)
            for r in range(GROUP):
                drag_refs[0][k * GROUP + r] = jnp.concatenate(
                    [stacked[:, r * CAP : (r + 1) * CAP], blank], axis=1
                )
            return carry

        lax.fori_loop(0, beads_ref.shape[0] // GROUP, group, 0)

    force = [x_ends([force_ref[d, z] for z in range(depth)]) for d in range(3)]
    out = collide([column_ref[i] for i in range(19)], column_ref[19] == 1.0, force)
    high = lax.rem(iota((rows, 128), 1), 2) == 0
    ends = [jnp.where(high, out[i], out[j])[:, 0:32] for i, j in zip(*ENTER[0])]
    face_ref[0] = jnp.concatenate(ends[0:4], axis=1)
    face_ref[1] = jnp.concatenate([ends[4], jnp.zeros((rows, 96), F32)], axis=1)
    odd = odd_slab()
    leaving = []
    for group, z in ((0, depth - 1), (1, 0)):
        out = collide(
            [pops_ref[i, z] for i in range(19)],
            solid_ref[z] == 1,
            [force_ref[d, z] for d in range(3)],
        )
        leaving.append([turn(out[i], STEP[i, 0], 1) for i in ENTER[2][group]])
    if n_drags == 2:
        leaving[0].append(up)
        leaving[1].append(down)
    row = 0
    for a, b in zip(*leaving):
        at = slice(row, row + a.shape[0])
        first_ref[at] = jnp.where(odd, a, b)
        second_ref[at] = jnp.where(odd, b, a)
        row += a.shape[0]


def couple(shape, beads, flow, columns, pops, solid):
    _, depth, rows, width = pops.shape
    single = beads.shape[0] == GROUP
    tile = jax.ShapeDtypeStruct((8, 128), F32)
    drags = [jax.ShapeDtypeStruct((shape[0], 8, 128), F32), tile] if single else [beads]
    message = jax.ShapeDtypeStruct((5 * rows + (8 if single else 0), width), F32)
    return pl.pallas_call(
        functools.partial(couple_kernel, shape, len(drags)),
        out_shape=[
            jax.ShapeDtypeStruct((3, depth, rows, width), F32),
            jax.ShapeDtypeStruct((2, rows, 128), F32),
            message,
            message,
        ]
        + [jax.ShapeDtypeStruct(d.shape, F32) for d in drags]
        + [TOKEN],
        compiler_params=pltpu.CompilerParams(vmem_limit_bytes=ROOM),
        name="couple",
    )(beads, *flow, columns, pops, solid)


def entered_z(first_ref, second_ref, side, rows):
    odd = odd_slab() if side == 0 else jnp.logical_not(odd_slab())
    return jnp.where(odd, second_ref[rows], first_ref[rows])


X_EDGES = [i for side in range(2) for i in ENTER[2][side] if STEP[i, 0] != 0]


def rows_kernel(depth, rows, before_ref, draft_ref, first_ref, second_ref, *refs):
    refs, (cross_ref, token_ref) = refs[:-2], refs[-2:]
    token_ref[...] = jnp.zeros_like(token_ref)
    outs = refs[-1:] if len(refs) == 3 else refs
    for group in range(2):
        out_ref = outs[0] if len(outs) == 1 else outs[group]
        base = group * 5 * depth if len(outs) == 1 else 0
        y = rows - 1 if group == 0 else 0
        out_ref[base : base + 5 * depth] = draft_ref[group * 5 * depth : (group + 1) * 5 * depth]
        for k, i in enumerate(ENTER[1][group]):
            at = base + k * depth
            if STEP[i, 2] != 0:
                side = 0 if STEP[i, 2] == 1 else 1
                z = 0 if side == 0 else depth - 1
                row = ENTER[2][side].index(i) * rows + y
                out_ref[at + z : at + z + 1] = entered_z(
                    first_ref, second_ref, side, slice(row, row + 1)
                )
    if len(refs) == 3:
        own_ref, far_ref, out_ref = refs
        came = arrived_drag(own_ref, far_ref, first_ref, second_ref, 5 * rows)
        out_ref[10 * depth : 10 * depth + 8] = one_tile(came, 1)
    for k, i in enumerate(X_EDGES):
        side = 0 if STEP[i, 2] == 1 else 1
        at = ENTER[2][side].index(i) * rows
        cross_ref[k * rows : (k + 1) * rows] = entered_z(
            first_ref, second_ref, side, slice(at, at + rows)
        )


def arrived_drag(own_ref, far_ref, first_ref, second_ref, tail):
    at = slice(tail, tail + 8)
    up, down = [entered_z(first_ref, second_ref, side, at) for side in range(2)]
    return [own_ref[0], down, far_ref[...], up]


def one_tile(tiles, col):
    return jnp.concatenate([t[:, col * CAP : (col + 1) * CAP] for t in tiles], axis=1)


def leaving_rows(depth, rows, before, draft, first, second, drags):
    width = draft.shape[1]
    if drags:
        sizes = [10 * depth + 8]
    else:
        sizes = [5 * depth] * 2
    args = (draft, first, second, *drags)
    return pl.pallas_call(
        functools.partial(rows_kernel, depth, rows),
        out_shape=[jax.ShapeDtypeStruct((n, width), F32) for n in sizes + [4 * rows]] + [TOKEN],
        in_specs=[pl.BlockSpec(memory_space=pl.ANY)]
        + [pl.BlockSpec(memory_space=pltpu.VMEM)] * len(args),
        compiler_params=pltpu.CompilerParams(vmem_limit_bytes=ROOM),
        name="rows",
    )(before, *args)


def runs(members):
    found = []
    for i in members:
        if found and found[-1][1] == i and STEP[i, 2] == STEP[i - 1, 2]:
            found[-1] = (found[-1][0], i + 1)
        else:
            found.append((i, i + 1))
    return found


def stream_planes(low, high, faces, pops_ref, solid_ref, force_ref, held):
    def plane(z, faces):
        out = collide(
            [pops_ref[i, z] for i in range(19)],
            solid_ref[z] == 1,
            [force_ref[d, z] for d in range(3)],
        )
        for i in range(19):
            value = turn(out[i], STEP[i, 0], 1)
            if STEP[i, 0] != 0:
                value = patch_x(value, i, faces[x_pair(i)])
            held[i, z] = turn(value, STEP[i, 1], 0)
        return tuple(pltpu.roll(f, 126, 1) for f in faces)

    return lax.fori_loop(low, high, plane, faces, unroll=2)


def lower_kernel(
    before_ref, pops_ref, solid_ref, force_ref, side_ref, wall_ref, face_ref, *refs
):
    held, draft_ref, token_ref, turned = refs
    depth, rows, _ = pops_ref.shape[1:]
    token_ref[...] = jnp.zeros_like(token_ref)
    face = x_arrived(face_ref)
    for n in range(2):
        turned[n] = face[n].T
    for group in range(2):
        y = 0 if group else rows - 1
        force = [force_ref[d, :, y, :] for d in range(3)]
        out = collide([side_ref[i, 1 - group] for i in range(19)], wall_ref[1 - group] == 1, force)
        for k, i in enumerate(ENTER[1][group]):
            row = (group * 5 + k) * depth
            value = turn(out[i], STEP[i, 0], 1)
            if STEP[i, 0] != 0:
                tile, lane = x_place(i)
                column = turned[tile, pl.ds(lane, depth, stride=2), :][:, y : y + 1]
                value = patch_x(value, i, jnp.broadcast_to(column, value.shape))
            draft_ref[row : row + depth] = turn(value, STEP[i, 2], 0)
    faces = tuple(x_entering(face, k, 0) for k in range(5))
    stream_planes(0, held.shape[1], faces, pops_ref, solid_ref, force_ref, held)


def upper_kernel(
    before_ref, lower_ref, pops_ref, solid_ref, force_ref, face_ref, out_ref, tile_ref, held, sem
):
    depth, rows, width = pops_ref.shape[1:]
    half = lower_ref.shape[1]
    copies = []

    def leave(source, members, low, high):
        for a, b in runs(members):
            step = int(STEP[a, 2])
            start, stop = max(low + step, 0), min(high + step, depth)
            copy = pltpu.make_async_copy(
                source.at[a:b, start - step : stop - step],
                out_ref.at[a:b, start:stop],
                sem.at[len(copies)],
            )
            copy.start()
            copies.append(copy)

    leave(lower_ref, range(19), 0, half)
    face = x_arrived(face_ref)
    faces = tuple(x_entering(face, k, half) for k in range(5))
    marks = upper_marks(half, depth)
    for low, high in zip(marks, marks[1:]):
        faces = stream_planes(low, high, faces, pops_ref, solid_ref, force_ref, held)
        leave(held, range(19), low, high)
    for group in range(2):
        first = slice(0, 8) if group == 0 else slice(rows - 8, rows)
        for k, i in enumerate(ENTER[1][group]):
            tile_ref[group * 5 + k, 0:half] = lower_ref[i, :, first, :]
            tile_ref[group * 5 + k, half:depth] = held[i, half:depth, first, :]
    for copy in copies:
        copy.wait()


def upper_marks(half, depth):
    return list(range(half, depth - 2, 4)) + ([depth - 2] if (depth - half) % 4 else []) + [depth]


def stream_lower(half, before, pops, solid, force, sides, walls, face):
    _, depth, rows, width = pops.shape
    vmem = pl.BlockSpec(memory_space=pltpu.VMEM)
    return pl.pallas_call(
        lower_kernel,
        out_shape=[
            jax.ShapeDtypeStruct((19, half, rows, width), F32),
            jax.ShapeDtypeStruct((10 * depth, width), F32),
            TOKEN,
        ],
        in_specs=[pl.BlockSpec(memory_space=pl.ANY)] + [vmem] * 6,
        scratch_shapes=[pltpu.VMEM((2, 128, rows), F32)],
        compiler_params=pltpu.CompilerParams(vmem_limit_bytes=ROOM),
        cost_estimate=pl.CostEstimate(flops=3000000, bytes_accessed=2000000, transcendentals=0),
        name="lower",
    )(before, pops, solid, force, sides, walls, face)


def stream_upper(before, lower, pops, solid, force, face):
    _, depth, rows, width = pops.shape
    vmem = pl.BlockSpec(memory_space=pltpu.VMEM)
    return pl.pallas_call(
        upper_kernel,
        out_shape=[
            jax.ShapeDtypeStruct(pops.shape, F32),
            jax.ShapeDtypeStruct((10, depth, 8, width), F32),
        ],
        in_specs=[pl.BlockSpec(memory_space=pl.ANY)] + [vmem] * 5,
        out_specs=[pl.BlockSpec(memory_space=pltpu.HBM), vmem],
        scratch_shapes=[
            pltpu.VMEM(pops.shape, F32),
            pltpu.SemaphoreType.DMA((20 * len(upper_marks(lower.shape[1], depth)),)),
        ],
        compiler_params=pltpu.CompilerParams(vmem_limit_bytes=ROOM),
        cost_estimate=pl.CostEstimate(flops=5000000, bytes_accessed=3000000, transcendentals=0),
        name="upper",
    )(before, lower, pops, solid, force, face)


def choice_kernel(shape, before_ref, target_ref, choice_ref, token_ref):
    slabs, cols, _ = shape
    token_ref[...] = jnp.zeros_like(token_ref)
    target = target_ref[...]
    owner = lax.shift_right_logical(target, 5)
    owner_slab = lax.shift_right_logical(owner, cols.bit_length() - 1)
    away_col = owner - owner_slab * cols - lax.axis_index("col")
    away_col = jnp.where(away_col < 0, away_col + cols, away_col)
    away_slab = owner_slab - lax.axis_index("slab")
    away_slab = jnp.where(away_slab < 0, away_slab + slabs, away_slab)
    place = away_col * 128 + away_slab * CAP + target - owner * CAP
    choice_ref[...] = (iota(choice_ref.shape, 0) == place).astype(F32).astype(BF16)


def choice_of(shape, before, target):
    return pl.pallas_call(
        functools.partial(choice_kernel, shape),
        out_shape=[jax.ShapeDtypeStruct((256, target.shape[1]), BF16), TOKEN],
        in_specs=[pl.BlockSpec(memory_space=pl.ANY), pl.BlockSpec(memory_space=pltpu.VMEM)],
        compiler_params=pltpu.CompilerParams(vmem_limit_bytes=ROOM),
        name="choice",
    )(before, target)


def finish_kernel(shape, n_rows, whole_ref, target_ref, tile_ref, first_ref, second_ref, *refs):
    row_refs, cross_ref, refs = refs[:n_rows], refs[n_rows], refs[n_rows + 1 :]
    drag_refs, (out_ref, bead_ref, planes, tiles, bead, sem) = refs[:-6], refs[-6:]
    depth, rows, width = whole_ref.shape[1:]

    def entering(group, k):
        at = (group * 5 + k) * depth if n_rows == 1 else k * depth
        return row_refs[group % n_rows][at : at + depth]

    copies = []

    def leave(source, target):
        copy = pltpu.make_async_copy(source, target, sem.at[len(copies)])
        copy.start()
        copies.append(copy)

    for group in range(2):
        first = 0 if group == 0 else rows - 8
        for k, i in enumerate(ENTER[1][group]):
            n = group * 5 + k
            step = int(STEP[i, 2])
            tiles[n, 1 + step : 1 + step + depth] = tile_ref[n]
            tiles[n, 1 : 1 + depth, 0 if group == 0 else 7, :] = entering(group, k)
            low, high = max(step, 0), min(depth + step, depth)
            leave(tiles.at[n, 1 + low : 1 + high], out_ref.at[i, low:high, first : first + 8])
    for group in range(2):
        z = 0 if group == 0 else depth - 1
        for k, i in enumerate(ENTER[2][group]):
            value = entered_z(first_ref, second_ref, group, slice(k * rows, (k + 1) * rows))
            if STEP[i, 1] != 0:
                side = 0 if STEP[i, 1] == 1 else 1
                y = 0 if side == 0 else rows - 1
                row = entering(side, ENTER[1][side].index(i))[z : z + 1]
                value = jnp.where(
                    iota((rows, width), 0) == y,
                    jnp.broadcast_to(row, (rows, width)),
                    turn(value, STEP[i, 1], 0),
                )
            if STEP[i, 0] != 0:
                at = X_EDGES.index(i) * rows
                value = patch_x(value, i, cross_ref[at : at + rows])
            n = group * 5 + k
            planes[n] = value
            leave(planes.at[n], out_ref.at[i, z])

    count = target_ref.shape[1]
    if len(drag_refs) == 2:
        came = arrived_drag(*drag_refs, first_ref, second_ref, 5 * rows)
        passed = row_refs[0][10 * depth : 10 * depth + 8]
        table = jnp.concatenate([one_tile(came, 0), passed], axis=1)
        total = dot_select(table, target_ref[...], NN)
    else:
        back_ref = drag_refs[0]

        def group_share(k, total):
            got = [back_ref[k * GROUP + r] for r in range(GROUP)]
            slots = jnp.concatenate([t[:, 0:CAP] for t in got], axis=1)
            first = k * (GROUP * CAP)
            choose = (iota((GROUP * CAP, count), 0) + first == target_ref[...]).astype(F32)
            return total + dot_select(slots, choose.astype(BF16), NN)

        total = lax.fori_loop(
            0, back_ref.shape[0] // GROUP, group_share, jnp.zeros((8, count), F32)
        )
    bead[...] = total[0:3]
    leave(bead, bead_ref)
    for copy in copies:
        copy.wait()


def finish(shape, whole, target, tiles, first, second, entered, cross, drags):
    _, depth, rows, width = whole.shape
    vmem = pl.BlockSpec(memory_space=pltpu.VMEM)
    hbm = pl.BlockSpec(memory_space=pltpu.HBM)
    args = [whole, target, tiles, first, second, *entered, cross, *drags]
    return pl.pallas_call(
        functools.partial(finish_kernel, shape, len(entered)),
        out_shape=[
            jax.ShapeDtypeStruct(whole.shape, F32),
            jax.ShapeDtypeStruct((3, target.shape[1]), F32),
        ],
        in_specs=[hbm] + [vmem] * (len(args) - 1),
        out_specs=[hbm, hbm],
        scratch_shapes=[
            pltpu.VMEM((10, rows, width), F32),
            pltpu.VMEM((10, depth + 2, 8, width), F32),
            pltpu.VMEM((3, target.shape[1]), F32),
            pltpu.SemaphoreType.DMA((21,)),
        ],
        input_output_aliases={0: 0},
        compiler_params=pltpu.CompilerParams(vmem_limit_bytes=ROOM),
        name="finish",
    )(*args)


def shards(populations, solid_mask, bead_owner, bead_base, bead_offset, bead_velocity):
    slabs, cols, pairs = shape = tuple(lax.axis_size(a) for a in ("slab", "col", "pair"))
    owners = slabs * cols
    depth, rows = populations.shape[1:3]
    single = owners == GROUP and slabs == 4
    swap = functools.partial(
        lax.all_to_all, axis_name=("slab", "col"), split_axis=0, concat_axis=0, tiled=True
    )

    target, messages = pack(owners, bead_owner, bead_base, bead_offset, bead_velocity)
    messages = swap(messages)
    *flow, columns, sides, walls = moments(populations, solid_mask)
    force, face, first, second, drag, *far, token = couple(
        shape, messages, flow, columns, populations, solid_mask
    )

    def send_pair(value):
        return send(value, shape, lambda s, c, p: (s, c, (p + 1) % pairs))

    def send_col(values):
        return [
            send(value, shape, lambda s, c, p, sign=sign: (s, (c + sign) % cols, p))
            for value, sign in zip(values, (1, -1))
        ]

    face = send_pair(face)
    first, second = send_slab(first, shape, 1), send_slab(second, shape, 0)
    if single:
        drags = [drag, send(far[0], shape, lambda s, c, p: ((s + 2) % slabs, c, p))]
    else:
        drags = []
        drag = swap(drag)
    fields = (populations, solid_mask, force)
    lower, draft, token = stream_lower(depth // 2, token, *fields, sides, walls, face)
    *leaving, cross, token = leaving_rows(depth, rows, token, draft, first, second, drags)
    entered, cross = send_col(leaving), send_pair(cross)
    if single:
        target, token = choice_of(shape, token, target)
    whole, tiles = stream_upper(token, lower, *fields, face)
    return tuple(
        finish(shape, whole, target, tiles, first, second, entered, cross, drags or [drag])
    )


def solution(mesh):
    return jax.shard_map(
        shards,
        mesh=mesh,
        in_specs=(
            P(None, ("rep", "slab"), "col", "pair"),
            P(("rep", "slab"), "col", "pair"),
            P(("rep", "slab", "col", "pair")),
            P(None, ("rep", "slab", "col", "pair")),
            P(None, ("rep", "slab", "col", "pair")),
            P(None, ("rep", "slab", "col", "pair")),
        ),
        out_specs=(
            P(None, ("rep", "slab"), "col", "pair"),
            P(None, ("rep", "slab", "col", "pair")),
        ),
        check_vma=False,
    )
```

```python
import functools

import jax
import jax.numpy as jnp
import numpy as np
from jax import lax
from jax.experimental import pallas as pl
from jax.experimental.pallas import tpu as pltpu
from jax.sharding import PartitionSpec as P

CAP = 32
GROUP = 8

STEP = np.array(
    [
        [0, 0, 0],
        [1, 0, 0],
        [-1, 0, 0],
        [0, 1, 0],
        [0, -1, 0],
        [0, 0, 1],
        [0, 0, -1],
        [1, 1, 0],
        [-1, -1, 0],
        [1, -1, 0],
        [-1, 1, 0],
        [1, 0, 1],
        [-1, 0, -1],
        [1, 0, -1],
        [-1, 0, 1],
        [0, 1, 1],
        [0, -1, -1],
        [0, 1, -1],
        [0, -1, 1],
    ],
    np.int32,
)
TAU_PLUS = 0.8
TAU_MINUS = 0.5 + (3.0 / 16.0) / (TAU_PLUS - 0.5)
KEEP_EVEN = 1.0 - 1.0 / TAU_PLUS
KEEP_ODD = 1.0 - 1.0 / TAU_MINUS
FORCE_GAIN = 1.0 - 0.5 / TAU_PLUS
DRAG_COEF = 2.0
F32 = jnp.float32
BF16 = jnp.bfloat16

ENTER = [[[i for i in range(19) if STEP[i, a] == sign] for sign in (1, -1)] for a in range(3)]
TOKEN = jax.ShapeDtypeStruct((8, 128), F32)
ROOM = 16 << 20
NT = (((1,), (1,)), ((), ()))
NN = (((1,), (0,)), ((), ()))


def iota(shape, dim):
    return lax.broadcasted_iota(jnp.int32, shape, dim)


def high_low(value):
    high = value.astype(BF16)
    return high, (value - high.astype(F32)).astype(BF16)


def dot_split(left, right, dims):
    (a, b), (c, d) = left, right
    mul = functools.partial(lax.dot_general, dimension_numbers=dims, preferred_element_type=F32)
    return mul(a, c) + (mul(a, d) + mul(b, c))


def dot_select(value, choose, dims):
    first = value.astype(BF16).astype(F32)
    rest = value - first
    second = rest.astype(BF16).astype(F32)
    stacked = jnp.concatenate([first, second, rest - second], axis=0).astype(BF16)
    got = lax.dot_general(stacked, choose, dimension_numbers=dims, preferred_element_type=F32)
    rows = value.shape[0]
    return got[0:rows] + got[rows : 2 * rows] + got[2 * rows : 3 * rows]


def density_momentum(pops):
    momentum = []
    for axis in range(3):
        plus = [pops[i] for i in range(19) if STEP[i, axis] == 1]
        minus = [pops[i] for i in range(19) if STEP[i, axis] == -1]
        momentum.append(sum(plus[1:], plus[0]) - sum(minus[1:], minus[0]))
    return sum(pops[1:], pops[0]), momentum


def along(step, vector):
    terms = None
    for axis in range(3):
        if step[axis] == 0:
            continue
        if terms is None:
            terms = vector[axis] if step[axis] == 1 else -vector[axis]
        else:
            terms = terms + vector[axis] if step[axis] == 1 else terms - vector[axis]
    return terms


def collide(pops, wall, force):
    density, momentum = density_momentum(pops)
    inverse = 1.0 / density
    carried = [m + 0.5 * f for m, f in zip(momentum, force)]
    speed = [m * inverse for m in carried]
    w = 1.0 / 36.0
    bend = [(4.5 * w / TAU_PLUS) * m + (9.0 * w * FORCE_GAIN) * f for m, f in zip(carried, force)]
    push = [(3.0 * w / TAU_MINUS) * m + (3.0 * w * FORCE_GAIN) * f for m, f in zip(carried, force)]
    drop = [(1.5 * w / TAU_PLUS) * m + (3.0 * w * FORCE_GAIN) * f for m, f in zip(carried, force)]
    rest = (w / TAU_PLUS) * density - sum(
        [u * d for u, d in zip(speed[1:], drop[1:])], speed[0] * drop[0]
    )
    out = [None] * 19
    out[0] = jnp.where(wall, pops[0], KEEP_EVEN * pops[0] + 12.0 * rest)
    for i in range(1, 19, 2):
        a, b = pops[i], pops[i + 1]
        step = STEP[i]
        even = rest + along(step, speed) * along(step, bend)
        odd = along(step, push)
        if i < 7:
            even = even + even
            odd = odd + odd
        even = (0.5 * KEEP_EVEN) * (a + b) + even
        odd = (0.5 * KEEP_ODD) * (a - b) + odd
        out[i] = jnp.where(wall, b, even + odd)
        out[i + 1] = jnp.where(wall, a, even - odd)
    return out


def turn(value, amount, axis):
    if amount == 0:
        return value
    return pltpu.roll(value, int(amount) % value.shape[axis], axis)


def send(value, shape, target):
    def flat(at):
        return (at[0] * shape[1] + at[1]) * shape[2] + at[2]

    perm = [(flat(at), flat(target(*at))) for at in np.ndindex(*shape)]
    return lax.ppermute(value, ("slab", "col", "pair"), perm)


def send_slab(value, shape, which):
    def target(s, c, p):
        return ((s + (1 if s % 2 == which else -1)) % shape[0], c, p)

    return send(value, shape, target)


def odd_slab():
    return lax.rem(lax.axis_index("slab"), 2) == 1


def rank_among(member):
    count = member.shape[1]
    earlier = (iota((count, count), 0) < iota((count, count), 1)).astype(F32).astype(BF16)
    return lax.dot_general(member.astype(BF16), earlier, NN, preferred_element_type=F32)


def patch_x(value, i, column):
    side = 0 if STEP[i, 0] == 1 else value.shape[1] - 1
    return jnp.where(iota(value.shape, 1) == side, column, value)


def x_pair(i):
    return ENTER[0][0 if STEP[i, 0] == 1 else 1].index(i)


def x_place(i):
    k = x_pair(i)
    return k // 4, (k % 4) * 32 + (1 if STEP[i, 0] == 1 else 0)


def x_arrived(face_ref):
    even = lax.rem(iota(face_ref.shape[1:], 1), 2) == 0
    return [jnp.where(even, turn(face_ref[n], -1, 1), turn(face_ref[n], 1, 1)) for n in range(2)]


def x_entering(face, k, z):
    tile = face[k // 4]
    return pltpu.roll(tile, tile.shape[1] - ((k % 4) * 32 + 2 * z + 1), 1)


def x_ends(planes):
    lane = lax.shift_right_logical(iota(planes[0].shape, 1), 1)
    tile = jnp.ones(planes[0].shape, F32)
    for z, value in enumerate(planes):
        tile = jnp.where(lane == z, pltpu.roll(value, 2 * z + 1, 1), tile)
    return tile


def pack_kernel(steps, *refs):
    sources, (target_ref, out_ref, table, *held) = refs[:4], refs[4:]
    copies = []
    if steps == 1:
        *held, slots, tiles, sem = held
        outputs = (target_ref, out_ref)
        target_ref, out_ref = slots, tiles
        for k, (source, place) in enumerate(zip(sources, held)):
            copies.append(pltpu.make_async_copy(source, place, sem.at[k]))
            copies[-1].start()
        copies[0].wait()
        sources = held
    owner_ref, base_ref, offset_ref, velocity_ref = sources
    count = owner_ref.shape[1]
    step = 0 if steps == 1 else pl.program_id(0)
    local = owner_ref[...] - step * GROUP
    member = (iota((GROUP, count), 0) == local).astype(F32)
    rank = jnp.sum(member * rank_among(member), axis=0, keepdims=True).astype(jnp.int32)
    inside = (local >= 0) & (local < GROUP)
    target = jnp.where(inside, local * CAP + rank, -1)
    whole_target = jnp.where(inside, owner_ref[...] * CAP + rank, -1)

    if steps == 1:
        target_ref[...] = whole_target
        leaving = [pltpu.make_async_copy(target_ref, outputs[0], sem.at[4])]
        leaving[0].start()
    else:
        known = jnp.where(step == 0, -1, target_ref[...])
        target_ref[...] = jnp.maximum(known, whole_target)

    choose = (iota((GROUP * CAP, count), 0) == target).astype(F32).astype(BF16)
    table[...] = jnp.zeros_like(table)
    for copy in copies[1:]:
        copy.wait()
    table[0:3] = base_ref[...].astype(F32) + 1.0
    table[8:11] = offset_ref[...]
    table[16:19] = velocity_ref[...]
    packed = dot_select(table[...], choose, NT)
    blank = jnp.zeros((8, CAP), F32)
    for r in range(GROUP):
        lanes = slice(r * CAP, (r + 1) * CAP)
        out_ref[r * 8 : r * 8 + 8] = jnp.concatenate(
            [packed[0:8, lanes], packed[8:16, lanes], packed[16:24, lanes], blank], axis=1
        )
        if steps == 1 and r % 4 == 3:
            part = slice((r - 3) * 8, (r + 1) * 8)
            leaving.append(
                pltpu.make_async_copy(out_ref.at[part], outputs[1].at[part], sem.at[5 + r // 4])
            )
            leaving[-1].start()
    if steps == 1:
        for copy in leaving:
            copy.wait()


def pack(owners, owner, base, offset, velocity):
    count, steps = owner.shape[0], owners // GROUP
    args = (owner.reshape(1, count), base, offset, velocity)
    scratch = [pltpu.VMEM((24, count), F32)]
    if steps == 1:
        far = pl.BlockSpec(memory_space=pl.ANY)
        blocks = dict(in_specs=[far] * 4, out_specs=[far] * 2)
        scratch += [pltpu.VMEM(a.shape, a.dtype) for a in args]
        scratch += [pltpu.VMEM((1, count), jnp.int32), pltpu.VMEM((owners * 8, 128), F32)]
        scratch += [pltpu.SemaphoreType.DMA((7,))]
    else:
        blocks = dict(
            grid=(steps,),
            in_specs=[pl.BlockSpec(a.shape, lambda k: (0, 0)) for a in args],
            out_specs=[
                pl.BlockSpec((1, count), lambda k: (0, 0)),
                pl.BlockSpec((GROUP * 8, 128), lambda k: (k, 0)),
            ],
            compiler_params=pltpu.CompilerParams(vmem_limit_bytes=48 << 20),
        )
    target, tiles = pl.pallas_call(
        functools.partial(pack_kernel, steps),
        out_shape=[
            jax.ShapeDtypeStruct((1, count), jnp.int32),
            jax.ShapeDtypeStruct((owners * 8, 128), F32),
        ],
        scratch_shapes=scratch,
        name="pack",
        **blocks,
    )(*args)
    return target, tiles.reshape(owners, 8, 128)


def moments_kernel(
    pops_ref, solid_ref, high_ref, low_ref, column_ref, side_ref, wall_ref, held, held_solid, flow, sem
):
    depth, rows, width = pops_ref.shape[1:]
    chunks = 4
    span = depth // chunks
    copies = [pltpu.make_async_copy(solid_ref, held_solid, sem.at[chunks])]
    for k in range(chunks):
        part = pl.ds(k * span, span)
        copies.append(
            pltpu.make_async_copy(pops_ref.at[:, part], held.at[:, part], sem.at[k])
        )
    for copy in copies:
        copy.start()

    def plane(z, carry):
        pops = [held[i, z] for i in range(19)]
        density, momentum = density_momentum(pops)
        inverse = 1.0 / density
        for axis in range(3):
            flow[axis, pl.ds(pl.multiple_of(z * rows, rows), rows)] = momentum[axis] * inverse
        return carry

    for k in range(chunks):
        copies[1 + k].wait()
        lax.fori_loop(k * span, (k + 1) * span, plane, 0, unroll=2)
    copies[0].wait()
    for axis in range(3):
        at = slice(axis * width, (axis + 1) * width)
        high_ref[at], low_ref[at] = high_low(flow[axis].T)
    for i in range(19):
        column_ref[i] = x_ends([held[i, z] for z in range(depth)])
        side_ref[i, 0] = held[i, :, 0, :]
        side_ref[i, 1] = held[i, :, rows - 1, :]
    wall_ref[0] = held_solid[:, 0, :]
    wall_ref[1] = held_solid[:, rows - 1, :]
    column_ref[19] = x_ends([held_solid[z].astype(F32) for z in range(depth)])


def moments(pops, solid):
    _, depth, rows, width = pops.shape
    hbm = pl.BlockSpec(memory_space=pltpu.HBM)
    return pl.pallas_call(
        moments_kernel,
        out_shape=[
            jax.ShapeDtypeStruct((3 * width, depth * rows), BF16),
            jax.ShapeDtypeStruct((3 * width, depth * rows), BF16),
            jax.ShapeDtypeStruct((20, rows, 128), F32),
            jax.ShapeDtypeStruct((19, 2, depth, width), F32),
            jax.ShapeDtypeStruct((2, depth, width), jnp.int32),
        ],
        in_specs=[hbm, hbm],
        scratch_shapes=[
            pltpu.VMEM(pops.shape, F32),
            pltpu.VMEM(solid.shape, jnp.int32),
            pltpu.VMEM((3, depth * rows, width), F32),
            pltpu.SemaphoreType.DMA((5,)),
        ],
        compiler_params=pltpu.CompilerParams(vmem_limit_bytes=54000000),
        cost_estimate=pl.CostEstimate(flops=3000000, bytes_accessed=4000000, transcendentals=0),
        name="moments",
    )(pops, solid)


def unpack(tiles):
    return [
        jnp.concatenate([t[:, g * CAP : (g + 1) * CAP] for t in tiles], axis=1) for g in range(3)
    ]


def couple_group(base, part, velocity, flow, depth, rows, width):
    slots = GROUP * CAP
    start = base.astype(jnp.int32) - 1

    def hat(axis, length):
        cell = iota((length, slots), 0)
        low, share = start[axis : axis + 1], part[axis : axis + 1]
        return jnp.where(cell == low, 1.0 - share, 0.0) + jnp.where(cell == low + 1, share, 0.0)

    hat_x, hat_y, hat_z = hat(0, width), hat(1, rows), hat(2, depth)
    weight = high_low((hat_z[:, None, :] * hat_y[None, :, :]).reshape(depth * rows, slots))
    across = dot_split(flow, weight, NN)
    drag = []
    for d in range(3):
        sampled = jnp.sum(across[d * width : (d + 1) * width] * hat_x, axis=0, keepdims=True)
        drag.append(DRAG_COEF * (sampled - velocity[d : d + 1]))
    spread = jnp.concatenate([hat_x * (-drag[d]) for d in range(3)], axis=0)
    return drag, dot_split(weight, high_low(spread), NT)


def couple_kernel(shape, n_drags, beads_ref, high_ref, low_ref, *refs):
    slabs, cols, _ = shape
    column_ref, pops_ref, solid_ref, force_ref, face_ref, first_ref, second_ref, *refs = refs
    drag_refs, token_ref = refs[:-1], refs[-1]
    token_ref[...] = jnp.zeros_like(token_ref)
    depth, rows, width = pops_ref.shape[1:]
    flow = (high_ref[...], low_ref[...])

    def grid(force):
        return [
            force[:, d * width : (d + 1) * width].reshape(depth, rows, width) for d in range(3)
        ]

    hollow = jnp.zeros((5, GROUP * CAP), F32)

    if n_drags == 2:
        slab, col = lax.axis_index("slab"), lax.axis_index("col")
        got = []
        for r in range(GROUP):
            there = [a - b for a, b in zip((slab, col), divmod(r, cols))]
            there = [jnp.where(a < 0, a + n, a) for a, n in zip(there, (slabs, cols))]
            got.append(beads_ref[there[0] * cols + there[1]])
        drag, force = couple_group(*unpack(got), flow, depth, rows, width)
        for d, value in enumerate(grid(force)):
            force_ref[d] = value
        stacked = jnp.concatenate(drag + [hollow], axis=0)
        lanes = cols * CAP
        blank = jnp.zeros((8, 128 - lanes), F32)
        for dz in range(slabs):
            tile = jnp.concatenate([stacked[:, dz * lanes : (dz + 1) * lanes], blank], axis=1)
            drag_refs[0][dz] = tile
            if dz == 2:
                drag_refs[1][...] = tile
            if dz == 1:
                down = tile
        up = tile
    else:
        force_ref[...] = jnp.zeros_like(force_ref)
        blank = jnp.zeros((8, 128 - CAP), F32)

        def group(k, carry):
            got = [beads_ref[k * GROUP + r] for r in range(GROUP)]
            drag, force = couple_group(*unpack(got), flow, depth, rows, width)
            for d, value in enumerate(grid(force)):
                force_ref[d] += value
            stacked = jnp.concatenate(drag + [hollow], axis=0)
            for r in range(GROUP):
                drag_refs[0][k * GROUP + r] = jnp.concatenate(
                    [stacked[:, r * CAP : (r + 1) * CAP], blank], axis=1
                )
            return carry

        lax.fori_loop(0, beads_ref.shape[0] // GROUP, group, 0)

    force = [x_ends([force_ref[d, z] for z in range(depth)]) for d in range(3)]
    out = collide([column_ref[i] for i in range(19)], column_ref[19] == 1.0, force)
    high = lax.rem(iota((rows, 128), 1), 2) == 0
    ends = [jnp.where(high, out[i], out[j])[:, 0:32] for i, j in zip(*ENTER[0])]
    face_ref[0] = jnp.concatenate(ends[0:4], axis=1)
    face_ref[1] = jnp.concatenate([ends[4], jnp.zeros((rows, 96), F32)], axis=1)
    odd = odd_slab()
    leaving = []
    for group, z in ((0, depth - 1), (1, 0)):
        out = collide(
            [pops_ref[i, z] for i in range(19)],
            solid_ref[z] == 1,
            [force_ref[d, z] for d in range(3)],
        )
        leaving.append([turn(out[i], STEP[i, 0], 1) for i in ENTER[2][group]])
    if n_drags == 2:
        leaving[0].append(up)
        leaving[1].append(down)
    row = 0
    for a, b in zip(*leaving):
        at = slice(row, row + a.shape[0])
        first_ref[at] = jnp.where(odd, a, b)
        second_ref[at] = jnp.where(odd, b, a)
        row += a.shape[0]


def couple(shape, beads, flow, columns, pops, solid):
    _, depth, rows, width = pops.shape
    single = beads.shape[0] == GROUP
    tile = jax.ShapeDtypeStruct((8, 128), F32)
    drags = [jax.ShapeDtypeStruct((shape[0], 8, 128), F32), tile] if single else [beads]
    message = jax.ShapeDtypeStruct((5 * rows + (8 if single else 0), width), F32)
    return pl.pallas_call(
        functools.partial(couple_kernel, shape, len(drags)),
        out_shape=[
            jax.ShapeDtypeStruct((3, depth, rows, width), F32),
            jax.ShapeDtypeStruct((2, rows, 128), F32),
            message,
            message,
        ]
        + [jax.ShapeDtypeStruct(d.shape, F32) for d in drags]
        + [TOKEN],
        compiler_params=pltpu.CompilerParams(vmem_limit_bytes=ROOM),
        name="couple",
    )(beads, *flow, columns, pops, solid)


def entered_z(first_ref, second_ref, side, rows):
    odd = odd_slab() if side == 0 else jnp.logical_not(odd_slab())
    return jnp.where(odd, second_ref[rows], first_ref[rows])


X_EDGES = [i for side in range(2) for i in ENTER[2][side] if STEP[i, 0] != 0]


def rows_kernel(depth, rows, before_ref, draft_ref, first_ref, second_ref, *refs):
    refs, (cross_ref, token_ref) = refs[:-2], refs[-2:]
    token_ref[...] = jnp.zeros_like(token_ref)
    outs = refs[-1:] if len(refs) == 3 else refs
    for group in range(2):
        out_ref = outs[0] if len(outs) == 1 else outs[group]
        base = group * 5 * depth if len(outs) == 1 else 0
        y = rows - 1 if group == 0 else 0
        out_ref[base : base + 5 * depth] = draft_ref[group * 5 * depth : (group + 1) * 5 * depth]
        for k, i in enumerate(ENTER[1][group]):
            at = base + k * depth
            if STEP[i, 2] != 0:
                side = 0 if STEP[i, 2] == 1 else 1
                z = 0 if side == 0 else depth - 1
                row = ENTER[2][side].index(i) * rows + y
                out_ref[at + z : at + z + 1] = entered_z(
                    first_ref, second_ref, side, slice(row, row + 1)
                )
    if len(refs) == 3:
        own_ref, far_ref, out_ref = refs
        came = arrived_drag(own_ref, far_ref, first_ref, second_ref, 5 * rows)
        out_ref[10 * depth : 10 * depth + 8] = one_tile(came, 1)
    for k, i in enumerate(X_EDGES):
        side = 0 if STEP[i, 2] == 1 else 1
        at = ENTER[2][side].index(i) * rows
        cross_ref[k * rows : (k + 1) * rows] = entered_z(
            first_ref, second_ref, side, slice(at, at + rows)
        )


def arrived_drag(own_ref, far_ref, first_ref, second_ref, tail):
    at = slice(tail, tail + 8)
    up, down = [entered_z(first_ref, second_ref, side, at) for side in range(2)]
    return [own_ref[0], down, far_ref[...], up]


def one_tile(tiles, col):
    return jnp.concatenate([t[:, col * CAP : (col + 1) * CAP] for t in tiles], axis=1)


def leaving_rows(depth, rows, before, draft, first, second, drags):
    width = draft.shape[1]
    if drags:
        sizes = [10 * depth + 8]
    else:
        sizes = [5 * depth] * 2
    args = (draft, first, second, *drags)
    return pl.pallas_call(
        functools.partial(rows_kernel, depth, rows),
        out_shape=[jax.ShapeDtypeStruct((n, width), F32) for n in sizes + [4 * rows]] + [TOKEN],
        in_specs=[pl.BlockSpec(memory_space=pl.ANY)]
        + [pl.BlockSpec(memory_space=pltpu.VMEM)] * len(args),
        compiler_params=pltpu.CompilerParams(vmem_limit_bytes=ROOM),
        name="rows",
    )(before, *args)


def runs(members):
    found = []
    for i in members:
        if found and found[-1][1] == i and STEP[i, 2] == STEP[i - 1, 2]:
            found[-1] = (found[-1][0], i + 1)
        else:
            found.append((i, i + 1))
    return found


def stream_planes(low, high, faces, pops_ref, solid_ref, force_ref, held):
    def plane(z, faces):
        out = collide(
            [pops_ref[i, z] for i in range(19)],
            solid_ref[z] == 1,
            [force_ref[d, z] for d in range(3)],
        )
        for i in range(19):
            value = turn(out[i], STEP[i, 0], 1)
            if STEP[i, 0] != 0:
                value = patch_x(value, i, faces[x_pair(i)])
            held[i, z] = turn(value, STEP[i, 1], 0)
        return tuple(pltpu.roll(f, 126, 1) for f in faces)

    return lax.fori_loop(low, high, plane, faces, unroll=2)


def lower_kernel(
    before_ref, pops_ref, solid_ref, force_ref, side_ref, wall_ref, face_ref, *refs
):
    held, draft_ref, token_ref, turned = refs
    depth, rows, _ = pops_ref.shape[1:]
    token_ref[...] = jnp.zeros_like(token_ref)
    face = x_arrived(face_ref)
    for n in range(2):
        turned[n] = face[n].T
    for group in range(2):
        y = 0 if group else rows - 1
        force = [force_ref[d, :, y, :] for d in range(3)]
        out = collide([side_ref[i, 1 - group] for i in range(19)], wall_ref[1 - group] == 1, force)
        for k, i in enumerate(ENTER[1][group]):
            row = (group * 5 + k) * depth
            value = turn(out[i], STEP[i, 0], 1)
            if STEP[i, 0] != 0:
                tile, lane = x_place(i)
                column = turned[tile, pl.ds(lane, depth, stride=2), :][:, y : y + 1]
                value = patch_x(value, i, jnp.broadcast_to(column, value.shape))
            draft_ref[row : row + depth] = turn(value, STEP[i, 2], 0)
    faces = tuple(x_entering(face, k, 0) for k in range(5))
    stream_planes(0, held.shape[1], faces, pops_ref, solid_ref, force_ref, held)


def upper_kernel(
    before_ref, lower_ref, pops_ref, solid_ref, force_ref, face_ref, out_ref, tile_ref, held, sem
):
    depth, rows, width = pops_ref.shape[1:]
    half = lower_ref.shape[1]
    copies = []

    def leave(source, members, low, high):
        for a, b in runs(members):
            step = int(STEP[a, 2])
            start, stop = max(low + step, 0), min(high + step, depth)
            copy = pltpu.make_async_copy(
                source.at[a:b, start - step : stop - step],
                out_ref.at[a:b, start:stop],
                sem.at[len(copies)],
            )
            copy.start()
            copies.append(copy)

    leave(lower_ref, range(19), 0, half)
    face = x_arrived(face_ref)
    faces = tuple(x_entering(face, k, half) for k in range(5))
    marks = upper_marks(half, depth)
    for low, high in zip(marks, marks[1:]):
        faces = stream_planes(low, high, faces, pops_ref, solid_ref, force_ref, held)
        leave(held, range(19), low, high)
    for group in range(2):
        first = slice(0, 8) if group == 0 else slice(rows - 8, rows)
        for k, i in enumerate(ENTER[1][group]):
            tile_ref[group * 5 + k, 0:half] = lower_ref[i, :, first, :]
            tile_ref[group * 5 + k, half:depth] = held[i, half:depth, first, :]
    for copy in copies:
        copy.wait()


def upper_marks(half, depth):
    return list(range(half, depth - 2, 4)) + ([depth - 2] if (depth - half) % 4 else []) + [depth]


def stream_lower(half, before, pops, solid, force, sides, walls, face):
    _, depth, rows, width = pops.shape
    vmem = pl.BlockSpec(memory_space=pltpu.VMEM)
    return pl.pallas_call(
        lower_kernel,
        out_shape=[
            jax.ShapeDtypeStruct((19, half, rows, width), F32),
            jax.ShapeDtypeStruct((10 * depth, width), F32),
            TOKEN,
        ],
        in_specs=[pl.BlockSpec(memory_space=pl.ANY)] + [vmem] * 6,
        scratch_shapes=[pltpu.VMEM((2, 128, rows), F32)],
        compiler_params=pltpu.CompilerParams(vmem_limit_bytes=ROOM),
        cost_estimate=pl.CostEstimate(flops=3000000, bytes_accessed=2000000, transcendentals=0),
        name="lower",
    )(before, pops, solid, force, sides, walls, face)


def stream_upper(before, lower, pops, solid, force, face):
    _, depth, rows, width = pops.shape
    vmem = pl.BlockSpec(memory_space=pltpu.VMEM)
    return pl.pallas_call(
        upper_kernel,
        out_shape=[
            jax.ShapeDtypeStruct(pops.shape, F32),
            jax.ShapeDtypeStruct((10, depth, 8, width), F32),
        ],
        in_specs=[pl.BlockSpec(memory_space=pl.ANY)] + [vmem] * 5,
        out_specs=[pl.BlockSpec(memory_space=pltpu.HBM), vmem],
        scratch_shapes=[
            pltpu.VMEM(pops.shape, F32),
            pltpu.SemaphoreType.DMA((20 * len(upper_marks(lower.shape[1], depth)),)),
        ],
        compiler_params=pltpu.CompilerParams(vmem_limit_bytes=ROOM),
        cost_estimate=pl.CostEstimate(flops=5000000, bytes_accessed=3000000, transcendentals=0),
        name="upper",
    )(before, lower, pops, solid, force, face)


def choice_kernel(shape, before_ref, target_ref, choice_ref, token_ref):
    slabs, cols, _ = shape
    token_ref[...] = jnp.zeros_like(token_ref)
    target = target_ref[...]
    owner = lax.shift_right_logical(target, 5)
    owner_slab = lax.shift_right_logical(owner, cols.bit_length() - 1)
    away_col = owner - owner_slab * cols - lax.axis_index("col")
    away_col = jnp.where(away_col < 0, away_col + cols, away_col)
    away_slab = owner_slab - lax.axis_index("slab")
    away_slab = jnp.where(away_slab < 0, away_slab + slabs, away_slab)
    place = away_col * 128 + away_slab * CAP + target - owner * CAP
    choice_ref[...] = (iota(choice_ref.shape, 0) == place).astype(F32).astype(BF16)


def choice_of(shape, before, target):
    return pl.pallas_call(
        functools.partial(choice_kernel, shape),
        out_shape=[jax.ShapeDtypeStruct((256, target.shape[1]), BF16), TOKEN],
        in_specs=[pl.BlockSpec(memory_space=pl.ANY), pl.BlockSpec(memory_space=pltpu.VMEM)],
        compiler_params=pltpu.CompilerParams(vmem_limit_bytes=ROOM),
        name="choice",
    )(before, target)


def finish_kernel(shape, n_rows, whole_ref, target_ref, tile_ref, first_ref, second_ref, *refs):
    row_refs, cross_ref, refs = refs[:n_rows], refs[n_rows], refs[n_rows + 1 :]
    drag_refs, (out_ref, bead_ref, planes, tiles, bead, sem) = refs[:-6], refs[-6:]
    depth, rows, width = whole_ref.shape[1:]

    def entering(group, k):
        at = (group * 5 + k) * depth if n_rows == 1 else k * depth
        return row_refs[group % n_rows][at : at + depth]

    copies = []

    def leave(source, target):
        copy = pltpu.make_async_copy(source, target, sem.at[len(copies)])
        copy.start()
        copies.append(copy)

    for group in range(2):
        z = 0 if group == 0 else depth - 1
        for k, i in enumerate(ENTER[2][group]):
            value = entered_z(first_ref, second_ref, group, slice(k * rows, (k + 1) * rows))
            if STEP[i, 1] != 0:
                side = 0 if STEP[i, 1] == 1 else 1
                y = 0 if side == 0 else rows - 1
                row = entering(side, ENTER[1][side].index(i))[z : z + 1]
                value = jnp.where(
                    iota((rows, width), 0) == y,
                    jnp.broadcast_to(row, (rows, width)),
                    turn(value, STEP[i, 1], 0),
                )
            if STEP[i, 0] != 0:
                at = X_EDGES.index(i) * rows
                value = patch_x(value, i, cross_ref[at : at + rows])
            n = group * 5 + k
            planes[n] = value
            leave(planes.at[n], out_ref.at[i, z])
    for group in range(2):
        first = 0 if group == 0 else rows - 8
        for k, i in enumerate(ENTER[1][group]):
            n = group * 5 + k
            step = int(STEP[i, 2])
            tiles[n, 1 + step : 1 + step + depth] = tile_ref[n]
            tiles[n, 1 : 1 + depth, 0 if group == 0 else 7, :] = entering(group, k)
            low, high = max(step, 0), min(depth + step, depth)
            leave(tiles.at[n, 1 + low : 1 + high], out_ref.at[i, low:high, first : first + 8])

    count = target_ref.shape[1]
    if len(drag_refs) == 2:
        came = arrived_drag(*drag_refs, first_ref, second_ref, 5 * rows)
        passed = row_refs[0][10 * depth : 10 * depth + 8]
        table = jnp.concatenate([one_tile(came, 0), passed], axis=1)
        total = dot_select(table, target_ref[...], NN)
    else:
        back_ref = drag_refs[0]

        def group_share(k, total):
            got = [back_ref[k * GROUP + r] for r in range(GROUP)]
            slots = jnp.concatenate([t[:, 0:CAP] for t in got], axis=1)
            first = k * (GROUP * CAP)
            choose = (iota((GROUP * CAP, count), 0) + first == target_ref[...]).astype(F32)
            return total + dot_select(slots, choose.astype(BF16), NN)

        total = lax.fori_loop(
            0, back_ref.shape[0] // GROUP, group_share, jnp.zeros((8, count), F32)
        )
    bead[...] = total[0:3]
    leave(bead, bead_ref)
    for copy in copies:
        copy.wait()


def finish(shape, whole, target, tiles, first, second, entered, cross, drags):
    _, depth, rows, width = whole.shape
    vmem = pl.BlockSpec(memory_space=pltpu.VMEM)
    hbm = pl.BlockSpec(memory_space=pltpu.HBM)
    args = [whole, target, tiles, first, second, *entered, cross, *drags]
    return pl.pallas_call(
        functools.partial(finish_kernel, shape, len(entered)),
        out_shape=[
            jax.ShapeDtypeStruct(whole.shape, F32),
            jax.ShapeDtypeStruct((3, target.shape[1]), F32),
        ],
        in_specs=[hbm] + [vmem] * (len(args) - 1),
        out_specs=[hbm, hbm],
        scratch_shapes=[
            pltpu.VMEM((10, rows, width), F32),
            pltpu.VMEM((10, depth + 2, 8, width), F32),
            pltpu.VMEM((3, target.shape[1]), F32),
            pltpu.SemaphoreType.DMA((21,)),
        ],
        input_output_aliases={0: 0},
        compiler_params=pltpu.CompilerParams(vmem_limit_bytes=ROOM),
        name="finish",
    )(*args)


def shards(populations, solid_mask, bead_owner, bead_base, bead_offset, bead_velocity):
    slabs, cols, pairs = shape = tuple(lax.axis_size(a) for a in ("slab", "col", "pair"))
    owners = slabs * cols
    depth, rows = populations.shape[1:3]
    single = owners == GROUP and slabs == 4
    swap = functools.partial(
        lax.all_to_all, axis_name=("slab", "col"), split_axis=0, concat_axis=0, tiled=True
    )

    target, messages = pack(owners, bead_owner, bead_base, bead_offset, bead_velocity)
    messages = swap(messages)
    *flow, columns, sides, walls = moments(populations, solid_mask)
    force, face, first, second, drag, *far, token = couple(
        shape, messages, flow, columns, populations, solid_mask
    )

    def send_pair(value):
        return send(value, shape, lambda s, c, p: (s, c, (p + 1) % pairs))

    def send_col(values):
        return [
            send(value, shape, lambda s, c, p, sign=sign: (s, (c + sign) % cols, p))
            for value, sign in zip(values, (1, -1))
        ]

    face = send_pair(face)
    first, second = send_slab(first, shape, 1), send_slab(second, shape, 0)
    if single:
        drags = [drag, send(far[0], shape, lambda s, c, p: ((s + 2) % slabs, c, p))]
    else:
        drags = []
        drag = swap(drag)
    fields = (populations, solid_mask, force)
    lower, draft, token = stream_lower(depth // 2, token, *fields, sides, walls, face)
    *leaving, cross, token = leaving_rows(depth, rows, token, draft, first, second, drags)
    entered, cross = send_col(leaving), send_pair(cross)
    if single:
        target, token = choice_of(shape, token, target)
    whole, tiles = stream_upper(token, lower, *fields, face)
    return tuple(
        finish(shape, whole, target, tiles, first, second, entered, cross, drags or [drag])
    )


def solution(mesh):
    return jax.shard_map(
        shards,
        mesh=mesh,
        in_specs=(
            P(None, ("rep", "slab"), "col", "pair"),
            P(("rep", "slab"), "col", "pair"),
            P(("rep", "slab", "col", "pair")),
            P(None, ("rep", "slab", "col", "pair")),
            P(None, ("rep", "slab", "col", "pair")),
            P(None, ("rep", "slab", "col", "pair")),
        ),
        out_specs=(
            P(None, ("rep", "slab"), "col", "pair"),
            P(None, ("rep", "slab", "col", "pair")),
        ),
        check_vma=False,
    )
```

```python
import functools

import jax
import jax.numpy as jnp
import numpy as np
from jax import lax
from jax.experimental import pallas as pl
from jax.experimental.pallas import tpu as pltpu
from jax.sharding import PartitionSpec as P

CAP = 32
GROUP = 8

STEP = np.array(
    [
        [0, 0, 0],
        [1, 0, 0],
        [-1, 0, 0],
        [0, 1, 0],
        [0, -1, 0],
        [0, 0, 1],
        [0, 0, -1],
        [1, 1, 0],
        [-1, -1, 0],
        [1, -1, 0],
        [-1, 1, 0],
        [1, 0, 1],
        [-1, 0, -1],
        [1, 0, -1],
        [-1, 0, 1],
        [0, 1, 1],
        [0, -1, -1],
        [0, 1, -1],
        [0, -1, 1],
    ],
    np.int32,
)
TAU_PLUS = 0.8
TAU_MINUS = 0.5 + (3.0 / 16.0) / (TAU_PLUS - 0.5)
KEEP_EVEN = 1.0 - 1.0 / TAU_PLUS
KEEP_ODD = 1.0 - 1.0 / TAU_MINUS
FORCE_GAIN = 1.0 - 0.5 / TAU_PLUS
DRAG_COEF = 2.0
F32 = jnp.float32
BF16 = jnp.bfloat16

ENTER = [[[i for i in range(19) if STEP[i, a] == sign] for sign in (1, -1)] for a in range(3)]
TOKEN = jax.ShapeDtypeStruct((8, 128), F32)
ROOM = 16 << 20
NT = (((1,), (1,)), ((), ()))
NN = (((1,), (0,)), ((), ()))


def iota(shape, dim):
    return lax.broadcasted_iota(jnp.int32, shape, dim)


def high_low(value):
    high = value.astype(BF16)
    return high, (value - high.astype(F32)).astype(BF16)


def dot_split(left, right, dims):
    (a, b), (c, d) = left, right
    mul = functools.partial(lax.dot_general, dimension_numbers=dims, preferred_element_type=F32)
    return mul(a, c) + (mul(a, d) + mul(b, c))


def dot_select(value, choose, dims):
    first = value.astype(BF16).astype(F32)
    rest = value - first
    second = rest.astype(BF16).astype(F32)
    stacked = jnp.concatenate([first, second, rest - second], axis=0).astype(BF16)
    got = lax.dot_general(stacked, choose, dimension_numbers=dims, preferred_element_type=F32)
    rows = value.shape[0]
    return got[0:rows] + got[rows : 2 * rows] + got[2 * rows : 3 * rows]


def density_momentum(pops):
    momentum = []
    for axis in range(3):
        plus = [pops[i] for i in range(19) if STEP[i, axis] == 1]
        minus = [pops[i] for i in range(19) if STEP[i, axis] == -1]
        momentum.append(sum(plus[1:], plus[0]) - sum(minus[1:], minus[0]))
    return sum(pops[1:], pops[0]), momentum


def along(step, vector):
    terms = None
    for axis in range(3):
        if step[axis] == 0:
            continue
        if terms is None:
            terms = vector[axis] if step[axis] == 1 else -vector[axis]
        else:
            terms = terms + vector[axis] if step[axis] == 1 else terms - vector[axis]
    return terms


def collide(pops, wall, force):
    density, momentum = density_momentum(pops)
    inverse = 1.0 / density
    carried = [m + 0.5 * f for m, f in zip(momentum, force)]
    speed = [m * inverse for m in carried]
    w = 1.0 / 36.0
    bend = [(4.5 * w / TAU_PLUS) * m + (9.0 * w * FORCE_GAIN) * f for m, f in zip(carried, force)]
    push = [(3.0 * w / TAU_MINUS) * m + (3.0 * w * FORCE_GAIN) * f for m, f in zip(carried, force)]
    drop = [(1.5 * w / TAU_PLUS) * m + (3.0 * w * FORCE_GAIN) * f for m, f in zip(carried, force)]
    rest = (w / TAU_PLUS) * density - sum(
        [u * d for u, d in zip(speed[1:], drop[1:])], speed[0] * drop[0]
    )
    out = [None] * 19
    out[0] = jnp.where(wall, pops[0], KEEP_EVEN * pops[0] + 12.0 * rest)
    for i in range(1, 19, 2):
        a, b = pops[i], pops[i + 1]
        step = STEP[i]
        even = rest + along(step, speed) * along(step, bend)
        odd = along(step, push)
        if i < 7:
            even = even + even
            odd = odd + odd
        even = (0.5 * KEEP_EVEN) * (a + b) + even
        odd = (0.5 * KEEP_ODD) * (a - b) + odd
        out[i] = jnp.where(wall, b, even + odd)
        out[i + 1] = jnp.where(wall, a, even - odd)
    return out


def turn(value, amount, axis):
    if amount == 0:
        return value
    return pltpu.roll(value, int(amount) % value.shape[axis], axis)


def send(value, shape, target):
    def flat(at):
        return (at[0] * shape[1] + at[1]) * shape[2] + at[2]

    perm = [(flat(at), flat(target(*at))) for at in np.ndindex(*shape)]
    return lax.ppermute(value, ("slab", "col", "pair"), perm)


def send_slab(value, shape, which):
    def target(s, c, p):
        return ((s + (1 if s % 2 == which else -1)) % shape[0], c, p)

    return send(value, shape, target)


def odd_slab():
    return lax.rem(lax.axis_index("slab"), 2) == 1


def rank_among(member):
    count = member.shape[1]
    earlier = (iota((count, count), 0) < iota((count, count), 1)).astype(F32).astype(BF16)
    return lax.dot_general(member.astype(BF16), earlier, NN, preferred_element_type=F32)


def patch_x(value, i, column):
    side = 0 if STEP[i, 0] == 1 else value.shape[1] - 1
    return jnp.where(iota(value.shape, 1) == side, column, value)


def x_pair(i):
    return ENTER[0][0 if STEP[i, 0] == 1 else 1].index(i)


def x_place(i):
    k = x_pair(i)
    return k // 4, (k % 4) * 32 + (1 if STEP[i, 0] == 1 else 0)


def x_arrived(face_ref):
    even = lax.rem(iota(face_ref.shape[1:], 1), 2) == 0
    return [jnp.where(even, turn(face_ref[n], -1, 1), turn(face_ref[n], 1, 1)) for n in range(2)]


def x_entering(face, k, z):
    tile = face[k // 4]
    return pltpu.roll(tile, tile.shape[1] - ((k % 4) * 32 + 2 * z + 1), 1)


def x_ends(planes):
    lane = lax.shift_right_logical(iota(planes[0].shape, 1), 1)
    tile = jnp.ones(planes[0].shape, F32)
    for z, value in enumerate(planes):
        tile = jnp.where(lane == z, pltpu.roll(value, 2 * z + 1, 1), tile)
    return tile


def pack_kernel(steps, *refs):
    sources, (target_ref, out_ref, table, *held) = refs[:4], refs[4:]
    copies = []
    if steps == 1:
        *held, sem = held
        for k, (source, place) in enumerate(zip(sources, held)):
            copies.append(pltpu.make_async_copy(source, place, sem.at[k]))
            copies[-1].start()
        copies[0].wait()
        sources = held
    owner_ref, base_ref, offset_ref, velocity_ref = sources
    count = owner_ref.shape[1]
    step = 0 if steps == 1 else pl.program_id(0)
    local = owner_ref[...] - step * GROUP
    member = (iota((GROUP, count), 0) == local).astype(F32)
    rank = jnp.sum(member * rank_among(member), axis=0, keepdims=True).astype(jnp.int32)
    inside = (local >= 0) & (local < GROUP)
    target = jnp.where(inside, local * CAP + rank, -1)
    whole_target = jnp.where(inside, owner_ref[...] * CAP + rank, -1)

    if steps == 1:
        target_ref[...] = whole_target
    else:
        known = jnp.where(step == 0, -1, target_ref[...])
        target_ref[...] = jnp.maximum(known, whole_target)

    choose = (iota((GROUP * CAP, count), 0) == target).astype(F32).astype(BF16)
    table[...] = jnp.zeros_like(table)
    for copy in copies[1:]:
        copy.wait()
    table[0:3] = base_ref[...].astype(F32) + 1.0
    table[8:11] = offset_ref[...]
    table[16:19] = velocity_ref[...]
    packed = dot_select(table[...], choose, NT)
    blank = jnp.zeros((8, CAP), F32)
    for r in range(GROUP):
        lanes = slice(r * CAP, (r + 1) * CAP)
        out_ref[r * 8 : r * 8 + 8] = jnp.concatenate(
            [packed[0:8, lanes], packed[8:16, lanes], packed[16:24, lanes], blank], axis=1
        )


def pack(owners, owner, base, offset, velocity):
    count, steps = owner.shape[0], owners // GROUP
    args = (owner.reshape(1, count), base, offset, velocity)
    scratch = [pltpu.VMEM((24, count), F32)]
    if steps == 1:
        blocks = dict(in_specs=[pl.BlockSpec(memory_space=pl.ANY)] * 4)
        scratch += [pltpu.VMEM(a.shape, a.dtype) for a in args] + [pltpu.SemaphoreType.DMA((4,))]
    else:
        blocks = dict(
            grid=(steps,),
            in_specs=[pl.BlockSpec(a.shape, lambda k: (0, 0)) for a in args],
            out_specs=[
                pl.BlockSpec((1, count), lambda k: (0, 0)),
                pl.BlockSpec((GROUP * 8, 128), lambda k: (k, 0)),
            ],
            compiler_params=pltpu.CompilerParams(vmem_limit_bytes=48 << 20),
        )
    target, tiles = pl.pallas_call(
        functools.partial(pack_kernel, steps),
        out_shape=[
            jax.ShapeDtypeStruct((1, count), jnp.int32),
            jax.ShapeDtypeStruct((owners * 8, 128), F32),
        ],
        scratch_shapes=scratch,
        name="pack",
        **blocks,
    )(*args)
    return target, tiles.reshape(owners, 8, 128)


def moments_kernel(
    pops_ref, solid_ref, high_ref, low_ref, column_ref, side_ref, wall_ref, held, held_solid, flow, sem
):
    depth, rows, width = pops_ref.shape[1:]
    chunks = 4
    span = depth // chunks
    copies = [pltpu.make_async_copy(solid_ref, held_solid, sem.at[chunks])]
    for k in range(chunks):
        part = pl.ds(k * span, span)
        copies.append(
            pltpu.make_async_copy(pops_ref.at[:, part], held.at[:, part], sem.at[k])
        )
    for copy in copies:
        copy.start()

    def plane(z, carry):
        pops = [held[i, z] for i in range(19)]
        density, momentum = density_momentum(pops)
        inverse = 1.0 / density
        for axis in range(3):
            flow[axis, pl.ds(pl.multiple_of(z * rows, rows), rows)] = momentum[axis] * inverse
        return carry

    for k in range(chunks):
        copies[1 + k].wait()
        lax.fori_loop(k * span, (k + 1) * span, plane, 0, unroll=2)
    copies[0].wait()
    for axis in range(3):
        at = slice(axis * width, (axis + 1) * width)
        high_ref[at], low_ref[at] = high_low(flow[axis].T)
    for i in range(19):
        column_ref[i] = x_ends([held[i, z] for z in range(depth)])
        side_ref[i, 0] = held[i, :, 0, :]
        side_ref[i, 1] = held[i, :, rows - 1, :]
    wall_ref[0] = held_solid[:, 0, :]
    wall_ref[1] = held_solid[:, rows - 1, :]
    column_ref[19] = x_ends([held_solid[z].astype(F32) for z in range(depth)])


def moments(pops, solid):
    _, depth, rows, width = pops.shape
    hbm = pl.BlockSpec(memory_space=pltpu.HBM)
    return pl.pallas_call(
        moments_kernel,
        out_shape=[
            jax.ShapeDtypeStruct((3 * width, depth * rows), BF16),
            jax.ShapeDtypeStruct((3 * width, depth * rows), BF16),
            jax.ShapeDtypeStruct((20, rows, 128), F32),
            jax.ShapeDtypeStruct((19, 2, depth, width), F32),
            jax.ShapeDtypeStruct((2, depth, width), jnp.int32),
        ],
        in_specs=[hbm, hbm],
        scratch_shapes=[
            pltpu.VMEM(pops.shape, F32),
            pltpu.VMEM(solid.shape, jnp.int32),
            pltpu.VMEM((3, depth * rows, width), F32),
            pltpu.SemaphoreType.DMA((5,)),
        ],
        compiler_params=pltpu.CompilerParams(vmem_limit_bytes=54000000),
        cost_estimate=pl.CostEstimate(flops=3000000, bytes_accessed=4000000, transcendentals=0),
        name="moments",
    )(pops, solid)


def unpack(tiles):
    return [
        jnp.concatenate([t[:, g * CAP : (g + 1) * CAP] for t in tiles], axis=1) for g in range(3)
    ]


def couple_group(base, part, velocity, flow, depth, rows, width):
    slots = GROUP * CAP
    start = base.astype(jnp.int32) - 1

    def hat(axis, length):
        cell = iota((length, slots), 0)
        low, share = start[axis : axis + 1], part[axis : axis + 1]
        return jnp.where(cell == low, 1.0 - share, 0.0) + jnp.where(cell == low + 1, share, 0.0)

    hat_x, hat_y, hat_z = hat(0, width), hat(1, rows), hat(2, depth)
    weight = high_low((hat_z[:, None, :] * hat_y[None, :, :]).reshape(depth * rows, slots))
    across = dot_split(flow, weight, NN)
    drag = []
    for d in range(3):
        sampled = jnp.sum(across[d * width : (d + 1) * width] * hat_x, axis=0, keepdims=True)
        drag.append(DRAG_COEF * (sampled - velocity[d : d + 1]))
    spread = jnp.concatenate([hat_x * (-drag[d]) for d in range(3)], axis=0)
    return drag, dot_split(weight, high_low(spread), NT)


def couple_kernel(shape, n_drags, beads_ref, high_ref, low_ref, *refs):
    slabs, cols, _ = shape
    column_ref, pops_ref, solid_ref, force_ref, face_ref, first_ref, second_ref, *refs = refs
    drag_refs, token_ref = refs[:-1], refs[-1]
    token_ref[...] = jnp.zeros_like(token_ref)
    depth, rows, width = pops_ref.shape[1:]
    flow = (high_ref[...], low_ref[...])

    def grid(force):
        return [
            force[:, d * width : (d + 1) * width].reshape(depth, rows, width) for d in range(3)
        ]

    hollow = jnp.zeros((5, GROUP * CAP), F32)

    if n_drags == 2:
        slab, col = lax.axis_index("slab"), lax.axis_index("col")
        got = []
        for r in range(GROUP):
            there = [a - b for a, b in zip((slab, col), divmod(r, cols))]
            there = [jnp.where(a < 0, a + n, a) for a, n in zip(there, (slabs, cols))]
            got.append(beads_ref[there[0] * cols + there[1]])
        drag, force = couple_group(*unpack(got), flow, depth, rows, width)
        for d, value in enumerate(grid(force)):
            force_ref[d] = value
        stacked = jnp.concatenate(drag + [hollow], axis=0)
        lanes = cols * CAP
        blank = jnp.zeros((8, 128 - lanes), F32)
        for dz in range(slabs):
            tile = jnp.concatenate([stacked[:, dz * lanes : (dz + 1) * lanes], blank], axis=1)
            drag_refs[0][dz] = tile
            if dz == 2:
                drag_refs[1][...] = tile
            if dz == 1:
                down = tile
        up = tile
    else:
        force_ref[...] = jnp.zeros_like(force_ref)
        blank = jnp.zeros((8, 128 - CAP), F32)

        def group(k, carry):
            got = [beads_ref[k * GROUP + r] for r in range(GROUP)]
            drag, force = couple_group(*unpack(got), flow, depth, rows, width)
            for d, value in enumerate(grid(force)):
                force_ref[d] += value
            stacked = jnp.concatenate(drag + [hollow], axis=0)
            for r in range(GROUP):
                drag_refs[0][k * GROUP + r] = jnp.concatenate(
                    [stacked[:, r * CAP : (r + 1) * CAP], blank], axis=1
                )
            return carry

        lax.fori_loop(0, beads_ref.shape[0] // GROUP, group, 0)

    force = [x_ends([force_ref[d, z] for z in range(depth)]) for d in range(3)]
    out = collide([column_ref[i] for i in range(19)], column_ref[19] == 1.0, force)
    high = lax.rem(iota((rows, 128), 1), 2) == 0
    ends = [jnp.where(high, out[i], out[j])[:, 0:32] for i, j in zip(*ENTER[0])]
    face_ref[0] = jnp.concatenate(ends[0:4], axis=1)
    face_ref[1] = jnp.concatenate([ends[4], jnp.zeros((rows, 96), F32)], axis=1)
    odd = odd_slab()
    leaving = []
    for group, z in ((0, depth - 1), (1, 0)):
        out = collide(
            [pops_ref[i, z] for i in range(19)],
            solid_ref[z] == 1,
            [force_ref[d, z] for d in range(3)],
        )
        leaving.append([turn(out[i], STEP[i, 0], 1) for i in ENTER[2][group]])
    if n_drags == 2:
        leaving[0].append(up)
        leaving[1].append(down)
    row = 0
    for a, b in zip(*leaving):
        at = slice(row, row + a.shape[0])
        first_ref[at] = jnp.where(odd, a, b)
        second_ref[at] = jnp.where(odd, b, a)
        row += a.shape[0]


def couple(shape, beads, flow, columns, pops, solid):
    _, depth, rows, width = pops.shape
    single = beads.shape[0] == GROUP
    tile = jax.ShapeDtypeStruct((8, 128), F32)
    drags = [jax.ShapeDtypeStruct((shape[0], 8, 128), F32), tile] if single else [beads]
    message = jax.ShapeDtypeStruct((5 * rows + (8 if single else 0), width), F32)
    return pl.pallas_call(
        functools.partial(couple_kernel, shape, len(drags)),
        out_shape=[
            jax.ShapeDtypeStruct((3, depth, rows, width), F32),
            jax.ShapeDtypeStruct((2, rows, 128), F32),
            message,
            message,
        ]
        + [jax.ShapeDtypeStruct(d.shape, F32) for d in drags]
        + [TOKEN],
        compiler_params=pltpu.CompilerParams(vmem_limit_bytes=ROOM),
        name="couple",
    )(beads, *flow, columns, pops, solid)


def entered_z(first_ref, second_ref, side, rows):
    odd = odd_slab() if side == 0 else jnp.logical_not(odd_slab())
    return jnp.where(odd, second_ref[rows], first_ref[rows])


X_EDGES = [i for side in range(2) for i in ENTER[2][side] if STEP[i, 0] != 0]


def rows_kernel(depth, rows, before_ref, draft_ref, first_ref, second_ref, *refs):
    refs, (cross_ref, token_ref) = refs[:-2], refs[-2:]
    token_ref[...] = jnp.zeros_like(token_ref)
    outs = refs[-1:] if len(refs) == 3 else refs
    for group in range(2):
        out_ref = outs[0] if len(outs) == 1 else outs[group]
        base = group * 5 * depth if len(outs) == 1 else 0
        y = rows - 1 if group == 0 else 0
        out_ref[base : base + 5 * depth] = draft_ref[group * 5 * depth : (group + 1) * 5 * depth]
        for k, i in enumerate(ENTER[1][group]):
            at = base + k * depth
            if STEP[i, 2] != 0:
                side = 0 if STEP[i, 2] == 1 else 1
                z = 0 if side == 0 else depth - 1
                row = ENTER[2][side].index(i) * rows + y
                out_ref[at + z : at + z + 1] = entered_z(
                    first_ref, second_ref, side, slice(row, row + 1)
                )
    if len(refs) == 3:
        own_ref, far_ref, out_ref = refs
        came = arrived_drag(own_ref, far_ref, first_ref, second_ref, 5 * rows)
        out_ref[10 * depth : 10 * depth + 8] = one_tile(came, 1)
    for k, i in enumerate(X_EDGES):
        side = 0 if STEP[i, 2] == 1 else 1
        at = ENTER[2][side].index(i) * rows
        cross_ref[k * rows : (k + 1) * rows] = entered_z(
            first_ref, second_ref, side, slice(at, at + rows)
        )


def arrived_drag(own_ref, far_ref, first_ref, second_ref, tail):
    at = slice(tail, tail + 8)
    up, down = [entered_z(first_ref, second_ref, side, at) for side in range(2)]
    return [own_ref[0], down, far_ref[...], up]


def one_tile(tiles, col):
    return jnp.concatenate([t[:, col * CAP : (col + 1) * CAP] for t in tiles], axis=1)


def leaving_rows(depth, rows, before, draft, first, second, drags):
    width = draft.shape[1]
    if drags:
        sizes = [10 * depth + 8]
    else:
        sizes = [5 * depth] * 2
    args = (draft, first, second, *drags)
    return pl.pallas_call(
        functools.partial(rows_kernel, depth, rows),
        out_shape=[jax.ShapeDtypeStruct((n, width), F32) for n in sizes + [4 * rows]] + [TOKEN],
        in_specs=[pl.BlockSpec(memory_space=pl.ANY)]
        + [pl.BlockSpec(memory_space=pltpu.VMEM)] * len(args),
        compiler_params=pltpu.CompilerParams(vmem_limit_bytes=ROOM),
        name="rows",
    )(before, *args)


def runs(members):
    found = []
    for i in members:
        if found and found[-1][1] == i and STEP[i, 2] == STEP[i - 1, 2]:
            found[-1] = (found[-1][0], i + 1)
        else:
            found.append((i, i + 1))
    return found


def stream_planes(low, high, faces, pops_ref, solid_ref, force_ref, held):
    def plane(z, faces):
        out = collide(
            [pops_ref[i, z] for i in range(19)],
            solid_ref[z] == 1,
            [force_ref[d, z] for d in range(3)],
        )
        for i in range(19):
            value = turn(out[i], STEP[i, 0], 1)
            if STEP[i, 0] != 0:
                value = patch_x(value, i, faces[x_pair(i)])
            held[i, z] = turn(value, STEP[i, 1], 0)
        return tuple(pltpu.roll(f, 126, 1) for f in faces)

    return lax.fori_loop(low, high, plane, faces, unroll=2)


def lower_kernel(
    before_ref, pops_ref, solid_ref, force_ref, side_ref, wall_ref, face_ref, *refs
):
    held, draft_ref, token_ref, turned = refs
    depth, rows, _ = pops_ref.shape[1:]
    token_ref[...] = jnp.zeros_like(token_ref)
    face = x_arrived(face_ref)
    for n in range(2):
        turned[n] = face[n].T
    for group in range(2):
        y = 0 if group else rows - 1
        force = [force_ref[d, :, y, :] for d in range(3)]
        out = collide([side_ref[i, 1 - group] for i in range(19)], wall_ref[1 - group] == 1, force)
        for k, i in enumerate(ENTER[1][group]):
            row = (group * 5 + k) * depth
            value = turn(out[i], STEP[i, 0], 1)
            if STEP[i, 0] != 0:
                tile, lane = x_place(i)
                column = turned[tile, pl.ds(lane, depth, stride=2), :][:, y : y + 1]
                value = patch_x(value, i, jnp.broadcast_to(column, value.shape))
            draft_ref[row : row + depth] = turn(value, STEP[i, 2], 0)
    faces = tuple(x_entering(face, k, 0) for k in range(5))
    stream_planes(0, held.shape[1], faces, pops_ref, solid_ref, force_ref, held)


def upper_kernel(
    before_ref, lower_ref, pops_ref, solid_ref, force_ref, face_ref, out_ref, tile_ref, held, sem
):
    depth, rows, width = pops_ref.shape[1:]
    half = lower_ref.shape[1]
    copies = []

    def leave(source, members, low, high):
        for a, b in runs(members):
            step = int(STEP[a, 2])
            start, stop = max(low + step, 0), min(high + step, depth)
            copy = pltpu.make_async_copy(
                source.at[a:b, start - step : stop - step],
                out_ref.at[a:b, start:stop],
                sem.at[len(copies)],
            )
            copy.start()
            copies.append(copy)

    leave(lower_ref, range(19), 0, half)
    face = x_arrived(face_ref)
    faces = tuple(x_entering(face, k, half) for k in range(5))
    marks = upper_marks(half, depth)
    for low, high in zip(marks, marks[1:]):
        faces = stream_planes(low, high, faces, pops_ref, solid_ref, force_ref, held)
        leave(held, range(19), low, high)
    for group in range(2):
        first = slice(0, 8) if group == 0 else slice(rows - 8, rows)
        for k, i in enumerate(ENTER[1][group]):
            tile_ref[group * 5 + k, 0:half] = lower_ref[i, :, first, :]
            tile_ref[group * 5 + k, half:depth] = held[i, half:depth, first, :]
    for copy in copies:
        copy.wait()


def upper_marks(half, depth):
    return list(range(half, depth - 2, 4)) + ([depth - 2] if (depth - half) % 4 else []) + [depth]


def stream_lower(half, before, pops, solid, force, sides, walls, face):
    _, depth, rows, width = pops.shape
    vmem = pl.BlockSpec(memory_space=pltpu.VMEM)
    return pl.pallas_call(
        lower_kernel,
        out_shape=[
            jax.ShapeDtypeStruct((19, half, rows, width), F32),
            jax.ShapeDtypeStruct((10 * depth, width), F32),
            TOKEN,
        ],
        in_specs=[pl.BlockSpec(memory_space=pl.ANY)] + [vmem] * 6,
        scratch_shapes=[pltpu.VMEM((2, 128, rows), F32)],
        compiler_params=pltpu.CompilerParams(vmem_limit_bytes=ROOM),
        cost_estimate=pl.CostEstimate(flops=5000000000, bytes_accessed=1000000000, transcendentals=0),
        name="lower",
    )(before, pops, solid, force, sides, walls, face)


def stream_upper(before, lower, pops, solid, force, face):
    _, depth, rows, width = pops.shape
    vmem = pl.BlockSpec(memory_space=pltpu.VMEM)
    return pl.pallas_call(
        upper_kernel,
        out_shape=[
            jax.ShapeDtypeStruct(pops.shape, F32),
            jax.ShapeDtypeStruct((10, depth, 8, width), F32),
        ],
        in_specs=[pl.BlockSpec(memory_space=pl.ANY)] + [vmem] * 5,
        out_specs=[pl.BlockSpec(memory_space=pltpu.HBM), vmem],
        scratch_shapes=[
            pltpu.VMEM(pops.shape, F32),
            pltpu.SemaphoreType.DMA((20 * len(upper_marks(lower.shape[1], depth)),)),
        ],
        compiler_params=pltpu.CompilerParams(vmem_limit_bytes=ROOM),
        cost_estimate=pl.CostEstimate(flops=5000000, bytes_accessed=3000000, transcendentals=0),
        name="upper",
    )(before, lower, pops, solid, force, face)


def choice_kernel(shape, before_ref, target_ref, choice_ref, token_ref):
    slabs, cols, _ = shape
    token_ref[...] = jnp.zeros_like(token_ref)
    target = target_ref[...]
    owner = lax.shift_right_logical(target, 5)
    owner_slab = lax.shift_right_logical(owner, cols.bit_length() - 1)
    away_col = owner - owner_slab * cols - lax.axis_index("col")
    away_col = jnp.where(away_col < 0, away_col + cols, away_col)
    away_slab = owner_slab - lax.axis_index("slab")
    away_slab = jnp.where(away_slab < 0, away_slab + slabs, away_slab)
    place = away_col * 128 + away_slab * CAP + target - owner * CAP
    choice_ref[...] = (iota(choice_ref.shape, 0) == place).astype(F32).astype(BF16)


def choice_of(shape, before, target):
    return pl.pallas_call(
        functools.partial(choice_kernel, shape),
        out_shape=[jax.ShapeDtypeStruct((256, target.shape[1]), BF16), TOKEN],
        in_specs=[pl.BlockSpec(memory_space=pl.ANY), pl.BlockSpec(memory_space=pltpu.VMEM)],
        compiler_params=pltpu.CompilerParams(vmem_limit_bytes=ROOM),
        name="choice",
    )(before, target)


def finish_kernel(shape, n_rows, whole_ref, target_ref, tile_ref, first_ref, second_ref, *refs):
    row_refs, cross_ref, refs = refs[:n_rows], refs[n_rows], refs[n_rows + 1 :]
    drag_refs, (out_ref, bead_ref, planes, tiles, bead, sem) = refs[:-6], refs[-6:]
    depth, rows, width = whole_ref.shape[1:]

    def entering(group, k):
        at = (group * 5 + k) * depth if n_rows == 1 else k * depth
        return row_refs[group % n_rows][at : at + depth]

    copies = []

    def leave(source, target):
        copy = pltpu.make_async_copy(source, target, sem.at[len(copies)])
        copy.start()
        copies.append(copy)

    for group in range(2):
        z = 0 if group == 0 else depth - 1
        for k, i in enumerate(ENTER[2][group]):
            value = entered_z(first_ref, second_ref, group, slice(k * rows, (k + 1) * rows))
            if STEP[i, 1] != 0:
                side = 0 if STEP[i, 1] == 1 else 1
                y = 0 if side == 0 else rows - 1
                row = entering(side, ENTER[1][side].index(i))[z : z + 1]
                value = jnp.where(
                    iota((rows, width), 0) == y,
                    jnp.broadcast_to(row, (rows, width)),
                    turn(value, STEP[i, 1], 0),
                )
            if STEP[i, 0] != 0:
                at = X_EDGES.index(i) * rows
                value = patch_x(value, i, cross_ref[at : at + rows])
            n = group * 5 + k
            planes[n] = value
            leave(planes.at[n], out_ref.at[i, z])
    for group in range(2):
        first = 0 if group == 0 else rows - 8
        for k, i in enumerate(ENTER[1][group]):
            n = group * 5 + k
            step = int(STEP[i, 2])
            tiles[n, 1 + step : 1 + step + depth] = tile_ref[n]
            tiles[n, 1 : 1 + depth, 0 if group == 0 else 7, :] = entering(group, k)
            low, high = max(step, 0), min(depth + step, depth)
            leave(tiles.at[n, 1 + low : 1 + high], out_ref.at[i, low:high, first : first + 8])

    count = target_ref.shape[1]
    if len(drag_refs) == 2:
        came = arrived_drag(*drag_refs, first_ref, second_ref, 5 * rows)
        passed = row_refs[0][10 * depth : 10 * depth + 8]
        table = jnp.concatenate([one_tile(came, 0), passed], axis=1)
        total = dot_select(table, target_ref[...], NN)
    else:
        back_ref = drag_refs[0]

        def group_share(k, total):
            got = [back_ref[k * GROUP + r] for r in range(GROUP)]
            slots = jnp.concatenate([t[:, 0:CAP] for t in got], axis=1)
            first = k * (GROUP * CAP)
            choose = (iota((GROUP * CAP, count), 0) + first == target_ref[...]).astype(F32)
            return total + dot_select(slots, choose.astype(BF16), NN)

        total = lax.fori_loop(
            0, back_ref.shape[0] // GROUP, group_share, jnp.zeros((8, count), F32)
        )
    bead[...] = total[0:3]
    leave(bead, bead_ref)
    for copy in copies:
        copy.wait()


def finish(shape, whole, target, tiles, first, second, entered, cross, drags):
    _, depth, rows, width = whole.shape
    vmem = pl.BlockSpec(memory_space=pltpu.VMEM)
    hbm = pl.BlockSpec(memory_space=pltpu.HBM)
    args = [whole, target, tiles, first, second, *entered, cross, *drags]
    return pl.pallas_call(
        functools.partial(finish_kernel, shape, len(entered)),
        out_shape=[
            jax.ShapeDtypeStruct(whole.shape, F32),
            jax.ShapeDtypeStruct((3, target.shape[1]), F32),
        ],
        in_specs=[hbm] + [vmem] * (len(args) - 1),
        out_specs=[hbm, hbm],
        scratch_shapes=[
            pltpu.VMEM((10, rows, width), F32),
            pltpu.VMEM((10, depth + 2, 8, width), F32),
            pltpu.VMEM((3, target.shape[1]), F32),
            pltpu.SemaphoreType.DMA((21,)),
        ],
        input_output_aliases={0: 0},
        compiler_params=pltpu.CompilerParams(vmem_limit_bytes=ROOM),
        name="finish",
    )(*args)


def shards(populations, solid_mask, bead_owner, bead_base, bead_offset, bead_velocity):
    slabs, cols, pairs = shape = tuple(lax.axis_size(a) for a in ("slab", "col", "pair"))
    owners = slabs * cols
    depth, rows = populations.shape[1:3]
    single = owners == GROUP and slabs == 4
    swap = functools.partial(
        lax.all_to_all, axis_name=("slab", "col"), split_axis=0, concat_axis=0, tiled=True
    )

    target, messages = pack(owners, bead_owner, bead_base, bead_offset, bead_velocity)
    messages = swap(messages)
    *flow, columns, sides, walls = moments(populations, solid_mask)
    force, face, first, second, drag, *far, token = couple(
        shape, messages, flow, columns, populations, solid_mask
    )

    def send_pair(value):
        return send(value, shape, lambda s, c, p: (s, c, (p + 1) % pairs))

    def send_col(values):
        return [
            send(value, shape, lambda s, c, p, sign=sign: (s, (c + sign) % cols, p))
            for value, sign in zip(values, (1, -1))
        ]

    face = send_pair(face)
    first, second = send_slab(first, shape, 1), send_slab(second, shape, 0)
    if single:
        drags = [drag, send(far[0], shape, lambda s, c, p: ((s + 2) % slabs, c, p))]
    else:
        drags = []
        drag = swap(drag)
    fields = (populations, solid_mask, force)
    lower, draft, token = stream_lower(depth // 2, token, *fields, sides, walls, face)
    *leaving, cross, token = leaving_rows(depth, rows, token, draft, first, second, drags)
    entered, cross = send_col(leaving), send_pair(cross)
    if single:
        target, token = choice_of(shape, token, target)
    whole, tiles = stream_upper(token, lower, *fields, face)
    return tuple(
        finish(shape, whole, target, tiles, first, second, entered, cross, drags or [drag])
    )


def solution(mesh):
    return jax.shard_map(
        shards,
        mesh=mesh,
        in_specs=(
            P(None, ("rep", "slab"), "col", "pair"),
            P(("rep", "slab"), "col", "pair"),
            P(("rep", "slab", "col", "pair")),
            P(None, ("rep", "slab", "col", "pair")),
            P(None, ("rep", "slab", "col", "pair")),
            P(None, ("rep", "slab", "col", "pair")),
        ),
        out_specs=(
            P(None, ("rep", "slab"), "col", "pair"),
            P(None, ("rep", "slab", "col", "pair")),
        ),
        check_vma=False,
    )
```
